128 devices in a mesh: dp: 16 (over z, x_lo, core), tensor: 8 (over x_hi, y).
Axes of the slice: x: 4 (x_hi: 2, x_lo: 2; x = x_hi * 2 + x_lo), y: 4, z: 4, core: 2. Of those that a mesh axis runs over, the one named last changes fastest.
Arguments:
- tokens: bfloat16 [24576, 1536], P(('dp', 'tensor')), may hold values from -24 to 24
- gain_attn: float32 [1536], replicated, may hold values from 0.5 to 1.5
- gain_mlp: float32 [1536], replicated, may hold values from 0.5 to 1.5
- w_query: bfloat16 [1536, 1536], P('dp', 'tensor'), may hold values from -0.15625 to 0.15625
- w_key: bfloat16 [1536, 768], P('dp', 'tensor'), may hold values from -0.15625 to 0.15625
- w_value: bfloat16 [1536, 768], P('dp', 'tensor'), may hold values from -0.15625 to 0.15625
- w_out: bfloat16 [1536, 1536], P(('tensor', 'dp')), may hold values from -1.25 to 1.25
- w_gate: bfloat16 [1536, 4096], P('dp', 'tensor'), may hold values from -0.15625 to 0.15625
- w_up: bfloat16 [1536, 4096], P('dp', 'tensor'), may hold values from -0.15625 to 0.15625
- w_down: bfloat16 [4096, 1536], P(('tensor', 'dp')), may hold values from -0.09375 to 0.09375
- segments: int32 [24576], P('dp'), may hold values from 0 to 24575, as said below
- positions: int32 [24576], P('dp'), may hold values from 0 to 1999, as said below
- cotangent: bfloat16 [24576, 1536], P(('dp', 'tensor')), may hold values from -6 to 6
Outputs:
- result: bfloat16 [24576, 1536], P(('dp', 'tensor'))
- token_grad: bfloat16 [24576, 1536], P(('dp', 'tensor'))
- grad_gain_attn: float32 [1536], replicated
- grad_gain_mlp: float32 [1536], replicated
- grad_query: float32 [1536, 1536], P('dp', 'tensor')
- grad_key: float32 [1536, 768], P('dp', 'tensor')
- grad_value: float32 [1536, 768], P('dp', 'tensor')
- grad_out: float32 [1536, 1536], P(('tensor', 'dp'))
- grad_gate: float32 [1536, 4096], P('dp', 'tensor')
- grad_up: float32 [1536, 4096], P('dp', 'tensor')
- grad_down: float32 [4096, 1536], P(('tensor', 'dp'))
The draws below stay inside these ranges and needn't reach their ends.
Inputs may be any that keep to these rules, and one draw needn't show every extreme that they name: `segments`: segment labels never fall along the tokens; each run of equal labels is one document of 200 to 2000 tokens (the last one may be cut short), documents run on across sequences, and different documents have different labels. positions counts from 0 at the first token of each document and rises by one along it.
All inputs are finite; a program needn't handle non-finite values.
Results may differ from the reference program's by a relative error of at most 0.025.
Values may be sent and summed in bfloat16 or wider, within the bound.
A program may use at most 128 MiB of HBM per device.

```python
import math
import jax
import jax.numpy as jnp
from jax import lax

D = 1536
QH = 16
KVH = 8
HD = 96
FF = 4096
SEQ = 512
DOC_MIN = 200
DOC_MAX = 2000
SEQS = 3
TOKENS = 24576


def document_layout(key):
    doc_count = TOKENS // DOC_MIN + 1
    lengths = jax.random.randint(key, (doc_count,), DOC_MIN, DOC_MAX + 1, dtype=jnp.int32)
    lengths = lengths.at[0].set(DOC_MAX)
    doc_ends = jnp.cumsum(lengths).astype(jnp.int32)
    starts = doc_ends - lengths
    places = jnp.arange(TOKENS, dtype=jnp.int32)
    segment = jnp.sum((doc_ends[None, :] <= places[:, None]).astype(jnp.int32), axis=1).astype(jnp.int32)
    chosen = (jnp.arange(doc_count, dtype=jnp.int32)[None, :] == segment[:, None]).astype(jnp.int32)
    doc_start = jnp.sum(chosen * starts[None, :], axis=1).astype(jnp.int32)
    return (segment, doc_start, places - doc_start)


def draw_segments(key, part):
    segment, doc_start, offset = document_layout(key)
    final_label = jnp.full_like(doc_start, TOKENS - 1)
    return jnp.where(segment == segment[TOKENS - 1], final_label, doc_start).astype(jnp.int32)


def draw_positions(key, part):
    segment, doc_start, offset = document_layout(key)
    return offset


def strengthened(drawn, key, source, target, blocks, factor):
    owner, partner = [(jnp.arange(drawn.shape[axis_at]) // (drawn.shape[axis_at] // blocks)).reshape([-1 if axis == axis_at else 1 for axis in range(drawn.ndim)]) for axis_at in (source, target)]
    chosen = jax.random.permutation(key, blocks)[partner]
    strong = (owner == chosen) | (owner == (partner + blocks // 2) % blocks)
    return jnp.where(strong, factor * drawn, drawn)


def block_scale(rng, extent, shards, least, high):
    def one(dim, parts):
        draws = jax.random.uniform(jax.random.fold_in(jax.random.fold_in(rng, 6), dim), (parts,), jnp.float32, least / len(shards), high / len(shards))
        return jnp.repeat(jnp.exp(draws), extent[dim] // parts).reshape((-1,) + (1,) * (len(extent) - dim - 1))

    level = one(*shards[0])
    for cut in shards[1:]:
        level = level * one(*cut)
    return level


def bell_draw(own_key, extent, scale, most, cuts=(), held_as=jnp.bfloat16):
    factor_of = block_scale(own_key, extent, cuts, -0.22, 0.18) if cuts else 1.0
    values = jax.random.normal(own_key, extent, jnp.float32) * scale * factor_of
    return jnp.minimum(jnp.maximum(values, -most), most).astype(held_as)


def heavy_noise(stream_key, dims, deviation, most, split, heavy, held_as=jnp.bfloat16):
    values = deviation * jax.random.normal(stream_key, dims, jnp.float32)
    if split:
        values = values * block_scale(stream_key, dims, split, -0.22, 0.18)
    return jnp.clip(strengthened(values, jax.random.fold_in(stream_key, 3), *heavy), -most, most).astype(held_as)


def setup_inputs(seed: int = 0) -> dict:
    keys = jax.random.split(jax.random.key(seed), 14)
    tokens = heavy_noise(keys[0], (TOKENS, D), 1.0, 24.0, ((0, 128),), (0, 1, 128, 5.5))
    gain_attn = jnp.clip(1.0 + 0.1 * jax.random.normal(keys[1], (D,), jnp.float32), 0.5, 1.5)
    gain_mlp = jnp.clip(1.0 + 0.1 * jax.random.normal(keys[2], (D,), jnp.float32), 0.5, 1.5)
    w_query = bell_draw(keys[3], (D, QH * HD), D ** -0.5, 0.15625, ((0, 16), (1, 8)))
    w_key = bell_draw(keys[4], (D, KVH * HD), D ** -0.5, 0.15625, ((0, 16), (1, 8)))
    w_value = bell_draw(keys[5], (D, KVH * HD), D ** -0.5, 0.15625, ((0, 16), (1, 8)))
    w_out = bell_draw(keys[6], (QH * HD, D), (QH * HD // 64) ** -0.5, 1.25, ((0, 128),))
    w_gate = bell_draw(keys[7], (D, FF), D ** -0.5, 0.15625, ((0, 16), (1, 8)))
    w_up = bell_draw(keys[8], (D, FF), D ** -0.5, 0.15625, ((0, 16), (1, 8)))
    w_down = bell_draw(keys[9], (FF, D), FF ** -0.5, 0.09375, ((0, 128),))
    segments = draw_segments(jax.random.fold_in(keys[13], 71), 0)
    positions = draw_positions(jax.random.fold_in(keys[13], 71), 0)
    cotangent = bell_draw(keys[12], (TOKENS, D), 1.0, 6.0, ((0, 128),))
    return dict(tokens=tokens, gain_attn=gain_attn, gain_mlp=gain_mlp, w_query=w_query, w_key=w_key, w_value=w_value, w_out=w_out, w_gate=w_gate, w_up=w_up, w_down=w_down, segments=segments, positions=positions, cotangent=cotangent)


EPSILON = 1e-05
ROPE_BASE = 100000.0
MASKED = -1e+30

@jax.custom_vjp
def low(v):
    return lax.optimization_barrier(v.astype(jnp.bfloat16)).astype(jnp.float32)

@jax.custom_vjp
def low_back(v):
    return v

def low_keep(v):
    return (low(v), None)

def low_pass(kept, grad):
    return (grad,)

def back_keep(v):
    return (v, None)

def back_low(kept, grad):
    return (low(grad),)
low.defvjp(low_keep, low_pass)
low_back.defvjp(back_keep, back_low)

def exact_dot(left, right):
    return jnp.dot(left, right, precision=lax.Precision.HIGHEST, preferred_element_type=jnp.float32)

def root_norm(values, gain):
    inverse = lax.rsqrt(lax.optimization_barrier(jnp.mean(values * values, axis=-1, keepdims=True)) + EPSILON)
    return values * inverse * gain

def rotary_tables(places):
    half_size = HD // 2
    exponent = jnp.arange(half_size, dtype=jnp.float32) * (2.0 / HD)
    frequency = jnp.exp(-math.log(ROPE_BASE) * exponent)
    angles = places.astype(jnp.float32)[:, None] * frequency[None, :]
    return (jnp.cos(angles)[:, None, :], jnp.sin(angles)[:, None, :])

def rotate(values, cosine, sine):
    half_size = values.shape[-1] // 2
    front = values[..., :half_size]
    behind = values[..., half_size:]
    return jnp.concatenate([front * cosine - behind * sine, behind * cosine + front * sine], axis=-1)

def attend(pieces):
    query, keyed, valued, labels = pieces
    length = query.shape[0]
    grouped = query.reshape(length, KVH, QH // KVH, HD)
    scores = jnp.einsum('iard,jad->arij', grouped, keyed, precision=lax.Precision.HIGHEST) * HD ** (-0.5)
    scores = low_back(scores)
    places = jnp.arange(length)
    allowed = (labels[:, None] == labels[None, :]) & (places[None, :] <= places[:, None])
    scores = jnp.where(allowed, scores, MASKED)
    highest = lax.optimization_barrier(jnp.max(scores, axis=-1, keepdims=True))
    weights = jnp.exp(scores - highest)
    probability = low(weights / lax.optimization_barrier(jnp.sum(weights, axis=-1, keepdims=True)))
    mixed = jnp.einsum('arij,jad->iard', probability, valued, precision=lax.Precision.HIGHEST)
    return mixed.reshape(length, QH * HD)

def layer_forward(stream, labels, places, gain_attn, gain_mlp, w_query, w_key, w_value, w_out, w_gate, w_up, w_down):
    total_rows = stream.shape[0]
    seq_count = total_rows // SEQ
    cosine, sine = rotary_tables(places)
    normed = low(root_norm(stream, gain_attn))
    query = low_back(exact_dot(normed, w_query)).reshape(total_rows, QH, HD)
    keyed = low_back(exact_dot(normed, w_key)).reshape(total_rows, KVH, HD)
    query = low(rotate(query, cosine, sine))
    keyed = low(rotate(keyed, cosine, sine))
    valued = low(low_back(exact_dot(normed, w_value))).reshape(total_rows, KVH, HD)
    mixed = lax.map(jax.checkpoint(attend), (query.reshape(seq_count, SEQ, QH, HD), keyed.reshape(seq_count, SEQ, KVH, HD), valued.reshape(seq_count, SEQ, KVH, HD), labels.reshape(seq_count, SEQ)))
    mixed = low(low_back(mixed.reshape(total_rows, QH * HD)))
    middle = stream + low_back(exact_dot(mixed, w_out))
    second = low(root_norm(middle, gain_mlp))
    gate = low_back(exact_dot(second, w_gate))
    upward = low_back(exact_dot(second, w_up))
    hidden = low(jax.nn.silu(gate) * upward)
    return middle + low_back(exact_dot(hidden, w_down))

def reference(tokens, gain_attn, gain_mlp, w_query, w_key, w_value, w_out, w_gate, w_up, w_down, segments, positions, cotangent):
    params = tuple((member.astype(jnp.float32) for member in (gain_attn, gain_mlp, w_query, w_key, w_value, w_out, w_gate, w_up, w_down)))
    group_rows = SEQS * SEQ
    blocks = TOKENS // group_rows
    stream = tokens.astype(jnp.float32).reshape(blocks, group_rows, D)
    upstream_all = cotangent.astype(jnp.float32).reshape(blocks, group_rows, D)

    def one_block(totals, pieces):
        rows_in, labels, places, upstream = pieces

        def forward(rows_value, *weight_list):
            return layer_forward(rows_value, labels, places, *weight_list)
        output, pullback = jax.vjp(forward, rows_in, *params)
        gradients = pullback(upstream)
        totals = tuple((total + gradient for total, gradient in zip(totals, gradients[1:])))
        return (totals, (output.astype(jnp.bfloat16), gradients[0].astype(jnp.bfloat16)))
    zeros_start = tuple((jnp.zeros_like(member) for member in params))
    totals, (outputs, backs) = lax.scan(one_block, zeros_start, (stream, segments.reshape(blocks, group_rows), positions.reshape(blocks, group_rows), upstream_all))
    return (outputs.reshape(TOKENS, D), backs.reshape(TOKENS, D), totals[0], totals[1], totals[2], totals[3], totals[4], totals[5], totals[6], totals[7], totals[8])
```

```python
import functools
import math

import jax
import jax.numpy as jnp
from jax import lax
from jax.experimental import pallas as pl
from jax.experimental.pallas import tpu as pltpu
from jax.sharding import PartitionSpec as P

HD = 96
SEQ = 512
D = 1536
OWN = 192
HALF = 768
WIN = 256

EPSILON = 1e-05
ROPE_BASE = 100000.0
MASKED = -1e30
MESH = pl.DeviceIdType.MESH
ANY = pl.BlockSpec(memory_space=pl.ANY)
VMEM = pl.BlockSpec(memory_space=pltpu.VMEM)
BF16 = jnp.bfloat16
F32 = jnp.float32


def place():
    dp = lax.axis_index("dp")
    tensor = lax.axis_index("tensor")
    return (tensor // 4) * 2 + (dp // 2) % 2, tensor % 4, dp // 4, dp % 2


def device(x, y, z, c):
    return (z * 4 + (x % 2) * 2 + c, (x // 2) * 4 + y)


def turn(pos, by):
    return (pos + by + 4) % 4


class Spot:
    def __init__(self):
        x, y, z, c = place()
        self.x, self.y, self.z, self.c = x, y, z, c
        self.high, self.low = x // 2, x % 2
        self.quad = self.low * 2 + c
        self.sibling = device(x, y, z, 1 - c)
        self.partner = device(turn(x, 2), y, z, 1 - c)

    def along(self, axis, by):
        x, y, z, c = self.x, self.y, self.z, self.c
        if axis == "x":
            return device(turn(x, by), y, z, c)
        if axis == "y":
            return device(x, turn(y, by), z, c)
        return device(x, y, turn(z, by), c)

    def me(self, axis):
        return {"x": self.x, "y": self.y, "z": self.z}[axis]

    def in_quad(self, by):
        other = turn(self.quad, by)
        return other, device(self.high * 2 + other // 2, self.y, self.z, other % 2)


def greet(devices):
    barrier = pltpu.get_barrier_semaphore()
    for who in devices:
        pl.semaphore_signal(barrier, inc=1, device_id=who, device_id_type=MESH)
    pl.semaphore_wait(barrier, len(devices))


class Wires:
    def __init__(self, send_sem, recv_sem):
        self.send_sem, self.recv_sem = send_sem, recv_sem
        self.count = 0
        self.sent = []
        self.moved = []

    def send(self, src, dst, who):
        copy = pltpu.make_async_remote_copy(
            src_ref=src,
            dst_ref=dst,
            send_sem=self.send_sem.at[self.count],
            recv_sem=self.recv_sem.at[self.count],
            device_id=who,
            device_id_type=MESH,
        )
        self.count += 1
        copy.start()
        self.sent.append(copy)
        return copy

    def move(self, src, dst):
        copy = pltpu.make_async_copy(src, dst, self.send_sem.at[self.count])
        self.count += 1
        copy.start()
        return copy

    def close(self):
        for copy in self.sent:
            copy.wait_send()


def add_into(dst, *srcs, chunk=16):
    rows = dst.shape[-2]
    chunk = min(chunk, rows)

    def step(i, carry):
        span = pl.ds(pl.multiple_of(i * chunk, chunk), chunk)
        total = srcs[0][..., span, :].astype(F32)
        for src in srcs[1:]:
            total = total + src[..., span, :].astype(F32)
        dst[..., span, :] = total.astype(dst.dtype)
        return carry

    lax.fori_loop(0, rows // chunk, step, 0)


class RingGather:
    def __init__(self, wires, spot, axis, at):
        self.wires, self.at = wires, at
        self.me = spot.me(axis)
        self.next, self.prev = spot.along(axis, 1), spot.along(axis, -1)

    def start(self, own=None):
        own = own or (lambda half: self.at(self.me, half))
        send, at, me = self.wires.send, self.at, self.me
        self.right0 = send(own(0), at(me, 0), self.next)
        self.left1 = send(own(1), at(me, 1), self.prev)
        self.right1 = send(own(1), at(me, 1), self.next)
        self.left0 = send(own(0), at(me, 0), self.prev)

    def forward(self):
        send, at, me = self.wires.send, self.at, self.me
        self.right0.wait_recv()
        before = at(turn(me, -1), 0)
        self.pass0 = send(before, before, self.next)
        self.left1.wait_recv()
        after = at(turn(me, 1), 1)
        self.pass1 = send(after, after, self.prev)

    def near(self):
        self.right1.wait_recv()
        self.left0.wait_recv()

    def far(self):
        self.pass0.wait_recv()
        self.pass1.wait_recv()


class PairGather:
    def __init__(self, wires, spot, axis, out, own, start, size):
        self.wires, self.spot, self.out, self.own = wires, spot, out, own
        self.rows = pl.ds(start, size)
        cut = size // 2

        def half_rows(half):
            return pl.ds(start + half * cut, cut)

        self.half_rows = half_rows
        self.ring = RingGather(
            wires, spot, axis, lambda pos, half: out.at[spot.c, pos, half_rows(half)]
        )
        self.me = spot.me(axis)

    def share(self, pos):
        block = self.out.at[self.spot.c, pos, self.rows]
        return self.wires.send(block, block, self.spot.sibling)

    def start(self):
        self.ring.start(lambda half: self.own.at[self.half_rows(half)])
        mine = self.own.at[self.rows]
        place_of = self.out.at[self.spot.c, self.me, self.rows]
        self.shared = [self.wires.send(mine, place_of, self.spot.sibling)]
        self.kept = self.wires.move(mine, place_of)

    def forward(self):
        self.ring.forward()
        self.ring.near()
        self.shared.append(self.share(turn(self.me, -1)))
        self.shared.append(self.share(turn(self.me, 1)))

    def far(self):
        self.ring.far()
        self.shared.append(self.share(turn(self.me, 2)))

    def finish(self):
        for copy in self.shared:
            copy.wait_recv()
        self.kept.wait()


class PairScatter:
    def __init__(self, wires, spot, axis, part, got, passed, near, start, size):
        self.wires, self.spot = wires, spot
        self.me = spot.me(axis)
        self.next, self.prev = spot.along(axis, 1), spot.along(axis, -1)
        self.part, self.got, self.passed, self.near = part, got, passed, near
        self.start_row, self.size, self.cut = start, size, size // 2
        self.shared = {}

    def rows(self, half=None):
        if half is None:
            return pl.ds(self.start_row, self.size)
        return pl.ds(self.start_row + half * self.cut, self.cut)

    def share(self, by):
        pos = turn(self.me, by)
        self.shared[by] = self.wires.send(
            self.part.at[1 - self.spot.c, pos, self.rows()],
            self.got.at[pos, self.rows()],
            self.spot.sibling,
        )

    def first(self):
        self.shared[2].wait_recv()
        pos = turn(self.me, 2)
        mine = self.got.at[pos, self.rows()]
        add_into(mine, self.part.at[self.spot.c, pos, self.rows()], mine)
        self.pass0 = self.wires.send(
            self.got.at[pos, self.rows(0)], self.passed.at[0, self.rows(0)], self.next
        )
        self.pass1 = self.wires.send(
            self.got.at[pos, self.rows(1)], self.passed.at[1, self.rows(1)], self.prev
        )

    def second(self):
        self.arriving = []
        after, before = turn(self.me, 1), turn(self.me, -1)
        for by, half, who, side in ((1, 1, self.next, 0), (-1, 0, self.prev, 1)):
            pos = turn(self.me, by)
            self.shared[by].wait_recv()
            mine = self.got.at[pos, self.rows(half)]
            add_into(mine, self.part.at[self.spot.c, pos, self.rows(half)], mine)
            self.arriving.append(self.wires.send(mine, self.near.at[side, self.rows(half)], who))
        for pos, half, who, side, arrived in (
            (after, 0, self.next, 0, self.pass0),
            (before, 1, self.prev, 1, self.pass1),
        ):
            arrived.wait_recv()
            mine = self.got.at[pos, self.rows(half)]
            add_into(
                mine,
                self.part.at[self.spot.c, pos, self.rows(half)],
                mine,
                self.passed.at[side, self.rows(half)],
            )
            self.arriving.append(self.wires.send(mine, self.near.at[side, self.rows(half)], who))

    def arrive(self):
        self.shared[0].wait_recv()
        for copy in self.arriving:
            copy.wait_recv()

    def total(self, span):
        return (
            self.part[self.spot.c, self.me, span].astype(F32)
            + self.got[self.me, span].astype(F32)
            + self.near[0, span].astype(F32)
            + self.near[1, span].astype(F32)
        )


class LineScatter:
    def __init__(self, wires, spot, at, work, passed, near, cut):
        self.wires, self.spot, self.at = wires, spot, at
        self.me = spot.z
        self.next, self.prev = spot.along("z", 1), spot.along("z", -1)
        self.work, self.passed, self.near = work, passed, near
        rows = work.shape[-2]
        self.spans = (pl.ds(0, cut), pl.ds(cut, rows - cut))

    def half(self, ref, half):
        return ref.at[:, self.spans[half]]

    def first(self):
        far = self.at(turn(self.me, 2))
        self.pass0 = self.wires.send(self.half(far, 0), self.half(self.passed.at[0], 0), self.next)
        self.pass1 = self.wires.send(self.half(far, 1), self.half(self.passed.at[1], 1), self.prev)
        after, before = self.at(turn(self.me, 1)), self.at(turn(self.me, -1))
        self.arriving = [
            self.wires.send(self.half(after, 1), self.half(self.near.at[0], 1), self.next),
            self.wires.send(self.half(before, 0), self.half(self.near.at[1], 0), self.prev),
        ]

    def second(self):
        after, before = self.at(turn(self.me, 1)), self.at(turn(self.me, -1))
        for src, half, who, side, arrived in (
            (after, 0, self.next, 0, self.pass0),
            (before, 1, self.prev, 1, self.pass1),
        ):
            arrived.wait_recv()
            mine = self.half(self.work.at[side], half)
            add_into(mine, self.half(src, half), self.half(self.passed.at[side], half))
            self.arriving.append(self.wires.send(mine, self.half(self.near.at[side], half), who))

    def finish(self, out):
        for copy in self.arriving:
            copy.wait_recv()
        add_into(out, self.at(self.me), self.near.at[0], self.near.at[1])


def line_scratch(lines, rows, columns):
    shape = (2, lines, rows, columns)
    return [pltpu.VMEM(shape, BF16)] * 3 + [pltpu.VMEM((lines, rows, columns), BF16)]


def norm_scale(values):
    return lax.rsqrt(jnp.mean(values * values, axis=-1, keepdims=True) + EPSILON)


def norm_back(upstream, values, inverse, gain):
    scaled = upstream * gain
    inner = jnp.sum(scaled * values, axis=-1, keepdims=True)
    return scaled * inverse - values * inner * (inverse * inverse * inverse) / values.shape[-1]


def over_rows(start, size, step, chunk=16):
    def body(i, carry):
        step(pl.ds(pl.multiple_of(start + i * chunk, chunk), chunk))
        return carry

    lax.fori_loop(0, size // chunk, body, 0)


def fold(total, values):
    part = values[0:8]
    for first in range(8, values.shape[0], 8):
        part = part + values[first : first + 8]
    total[...] += part


SUBS = ((0, 96), (96, 96))


def gather_kernel(
    tokens, gain, cot, att, gu, dn, marks,
    normed_out, cot_out, att_out, gu_out, dn_out, marks_out,
    own, att_two, send_sem, recv_sem,
):
    spot = Spot()
    wires = Wires(send_sem, recv_sem)
    x, y, z, c = spot.x, spot.y, spot.z, spot.c
    near = [spot.along(a, by) for a in "xyz" for by in (1, -1)]
    greet(
        near
        + [spot.along("x", 2), spot.along("y", 2), spot.sibling, spot.partner]
        + [spot.in_quad(by)[1] for by in (1, 2, 3)]
    )
    att_keep = wires.move(att, att_two.at[0])
    att_swap = wires.send(att, att_two.at[1], spot.partner)
    gu_here = gu_out.at[y, z, pl.ds(pl.multiple_of(spot.quad * 96, 96), 96)]
    gu_kept = wires.move(gu.at[spot.quad], gu_here)
    gu_swap = []
    for by in (1, 2, 3):
        other, who = spot.in_quad(by)
        gu_swap.append(wires.send(gu.at[other], gu_here, who))
    dn_kept = wires.move(dn, dn_out.at[y, z])
    marks_kept = wires.move(marks, marks_out.at[c])
    marks_got = wires.send(marks, marks_out.at[c], spot.sibling)
    cots = [PairGather(wires, spot, "x", cot_out, cot, s, n) for s, n in SUBS]

    def normalise(span):
        rows = tokens[span, :].astype(F32)
        own[span, :] = (rows * norm_scale(rows) * gain[...]).astype(BF16)

    over_rows(0, OWN, normalise)
    rows_y = [PairGather(wires, spot, "y", normed_out, own, s, n) for s, n in SUBS]
    for g in rows_y:
        g.start()
    for g in cots:
        g.start()

    att_keep.wait()
    att_swap.wait_recv()
    slot = spot.low * 2 + spot.high
    mine = att_two.at[jnp.where(spot.high == c, 0, 1)]
    att_here = att_out.at[z, slot]
    att_moved = wires.move(mine, att_here)
    att_side = [wires.send(mine, att_here, spot.along("x", by)) for by in (1, -1, 2)]
    gu_kept.wait()
    dn_kept.wait()
    for copy in gu_swap:
        copy.wait_recv()
    side = []
    for by in (1, -1, 2):
        side.append(wires.send(gu_out.at[y, z], gu_out.at[y, z], spot.along("y", by)))
        side.append(wires.send(dn_out.at[y, z], dn_out.at[y, z], spot.along("y", by)))

    rows_y[0].forward()
    rows_y[1].forward()
    cots[0].forward()
    cots[1].forward()

    att_moved.wait()
    for copy in att_side:
        copy.wait_recv()
    att_line = RingGather(
        wires, spot, "z", lambda pos, h: att_out.at[pos, :, pl.ds((0, 80)[h], (80, 64)[h])]
    )
    att_line.start()
    for copy in side:
        copy.wait_recv()
    gu_line = RingGather(wires, spot, "z", lambda pos, h: gu_out.at[:, pos, pl.ds(h * 192, 192)])
    dn_line = RingGather(wires, spot, "z", lambda pos, h: dn_out.at[:, pos, pl.ds(h * 16, 16)])
    gu_line.start()
    dn_line.start()
    for g in rows_y + cots:
        g.far()
    for line in (att_line, gu_line, dn_line):
        line.forward()
    for g in rows_y + cots:
        g.finish()
    for line in (att_line, gu_line, dn_line):
        line.near()
        line.far()
    marks_kept.wait()
    marks_got.wait_recv()
    wires.close()


def gather_all(tokens, gain, cot, att, gu, dn, marks):
    shapes = (
        jax.ShapeDtypeStruct((2, 4, OWN, D), BF16),
        jax.ShapeDtypeStruct((2, 4, OWN, D), BF16),
        jax.ShapeDtypeStruct((4, 4, 144, 384), BF16),
        jax.ShapeDtypeStruct((4, 4, 384, 256), BF16),
        jax.ShapeDtypeStruct((4, 4, 32, D), BF16),
        jax.ShapeDtypeStruct((2, 2, D), jnp.int32),
    )
    sems = 96
    return pl.pallas_call(
        gather_kernel,
        out_shape=shapes,
        in_specs=[VMEM, VMEM, VMEM, VMEM, VMEM, VMEM, VMEM],
        out_specs=[ANY] * 6,
        scratch_shapes=[
            pltpu.VMEM((OWN, D), BF16),
            pltpu.VMEM((2, 144, 384), BF16),
            pltpu.SemaphoreType.DMA((sems,)),
            pltpu.SemaphoreType.DMA((sems,)),
        ],
        compiler_params=pltpu.CompilerParams(
            collective_id=1, has_side_effects=True, vmem_limit_bytes=48 << 20
        ),
        name="gather_all",
    )(tokens, gain, cot, att, gu, dn, marks)


def scatter_scratch():
    return [
        pltpu.VMEM((4, OWN, D), BF16),
        pltpu.VMEM((2, OWN, D), BF16),
        pltpu.VMEM((2, OWN, D), BF16),
    ]


def run_through(scatters, gathers, use):
    for by in (2, 1, -1, 0):
        for s in scatters:
            s.share(by)
    for s in scatters:
        s.first()
    for s in scatters:
        s.second()
    for s, g in zip(scatters, gathers):
        s.arrive()
        over_rows(s.start_row, s.size, lambda span, s=s: use(span, s.total(span)))
        g.start()
        g.forward()
    for g in gathers:
        g.far()
    for g in gathers:
        g.finish()


def around(spot, axes):
    return [spot.along(a, by) for a in axes for by in (1, -1)] + [spot.sibling]


def forward_kernel(
    part, tokens, gain, middle_out, second_out, own, got, passed, near, send_sem, recv_sem
):
    spot = Spot()
    wires = Wires(send_sem, recv_sem)
    greet(around(spot, "xy"))
    scatters = [
        PairScatter(wires, spot, "y", part, got, passed, near, s, n) for s, n in SUBS
    ]
    gathers = [PairGather(wires, spot, "x", second_out, own, s, n) for s, n in SUBS]

    def use(span, attn):
        middle = tokens[span, :].astype(F32) + attn
        middle_out[span, :] = middle
        own[span, :] = (middle * norm_scale(middle) * gain[...]).astype(BF16)

    run_through(scatters, gathers, use)
    wires.close()


def forward_exchange(part, tokens, gain):
    sems = 64
    return pl.pallas_call(
        forward_kernel,
        out_shape=(
            jax.ShapeDtypeStruct((OWN, D), F32),
            jax.ShapeDtypeStruct((2, 4, OWN, D), BF16),
        ),
        in_specs=[VMEM, VMEM, VMEM],
        out_specs=[VMEM, ANY],
        scratch_shapes=[pltpu.VMEM((OWN, D), BF16)]
        + scatter_scratch()
        + [pltpu.SemaphoreType.DMA((sems,)), pltpu.SemaphoreType.DMA((sems,))],
        compiler_params=pltpu.CompilerParams(
            collective_id=2, has_side_effects=True, vmem_limit_bytes=48 << 20
        ),
        name="forward_exchange",
    )(part, tokens, gain)


def backward_kernel(
    part, cot, middle, gain,
    back_out, grad_out, gain_out,
    own, got, passed, near, total, send_sem, recv_sem,
):
    spot = Spot()
    wires = Wires(send_sem, recv_sem)
    greet(around(spot, "xy"))
    scatters = [
        PairScatter(wires, spot, "x", part, got, passed, near, s, n) for s, n in SUBS
    ]
    gathers = [PairGather(wires, spot, "y", grad_out, own, s, n) for s, n in SUBS]
    total[...] = jnp.zeros_like(total)

    def use(span, grad_second):
        rows = middle[span, :]
        inverse = norm_scale(rows)
        back = cot[span, :].astype(F32) + norm_back(grad_second, rows, inverse, gain[...])
        back_out[span, :] = back
        own[span, :] = back.astype(BF16)
        fold(total, grad_second * rows * inverse)

    run_through(scatters, gathers, use)
    gain_out[...] = jnp.sum(total[...], axis=0, keepdims=True)
    wires.close()


def backward_exchange(part, cot, middle, gain):
    sems = 64
    return pl.pallas_call(
        backward_kernel,
        out_shape=(
            jax.ShapeDtypeStruct((OWN, D), F32),
            jax.ShapeDtypeStruct((2, 4, OWN, D), BF16),
            jax.ShapeDtypeStruct((1, D), F32),
        ),
        in_specs=[VMEM] * 4,
        out_specs=[VMEM, ANY, VMEM],
        scratch_shapes=[pltpu.VMEM((OWN, D), BF16)]
        + scatter_scratch()
        + [
            pltpu.VMEM((8, D), F32),
            pltpu.SemaphoreType.DMA((sems,)),
            pltpu.SemaphoreType.DMA((sems,)),
        ],
        compiler_params=pltpu.CompilerParams(
            collective_id=3, has_side_effects=True, vmem_limit_bytes=48 << 20
        ),
        name="backward_exchange",
    )(part, cot, middle, gain)


def final_kernel(
    normed_part, mlp_part, tokens, gain, back, middle, gain_two, d_att, d_gu, d_dn,
    result_out, token_out, gains_out, att_out, gu_out, dn_out,
    got_y, passed_y, near_y, got_x, passed_x, near_x,
    att_work, att_passed, att_near, att_line,
    gu_work, gu_passed, gu_near, gu_line,
    dn_work, dn_passed, dn_near, dn_line,
    att_in, gu_in, dn_in, att_two, gu_two, gain_c, gain_y, gain_x, gain_z, total,
    send_sem, recv_sem,
):
    spot = Spot()
    wires = Wires(send_sem, recv_sem)
    x, y, z, c = spot.x, spot.y, spot.z, spot.c
    greet(
        around(spot, "xyz")
        + [spot.along(a, 2) for a in "xyz"]
        + [spot.partner]
        + [spot.in_quad(by)[1] for by in (1, 2, 3)]
    )
    rows_y = [
        PairScatter(wires, spot, "y", normed_part, got_y, passed_y, near_y, s, n) for s, n in SUBS
    ]
    rows_x = [
        PairScatter(wires, spot, "x", mlp_part, got_x, passed_x, near_x, s, n) for s, n in SUBS
    ]
    lines = [
        LineScatter(wires, spot, lambda p: d_gu.at[:, p], gu_work, gu_passed, gu_near, 192),
        LineScatter(wires, spot, lambda p: d_dn.at[:, p], dn_work, dn_passed, dn_near, 16),
        LineScatter(wires, spot, lambda p: d_att.at[p], att_work, att_passed, att_near, 80),
    ]
    for line in lines:
        line.first()
    for by in (2, 1, -1, 0):
        for s in rows_y + rows_x:
            s.share(by)
    for s in rows_y + rows_x:
        s.first()
    for s in rows_y + rows_x:
        s.second()
    for line in lines:
        line.second()
    total[...] = jnp.zeros_like(total)

    def token_rows(s):
        def use(span):
            grad = s.total(span)
            rows = tokens[span, :].astype(F32)
            inverse = norm_scale(rows)
            out = back[span, :] + norm_back(grad, rows, inverse, gain[...])
            token_out[span, :] = out.astype(BF16)
            fold(total, grad * rows * inverse)

        return use

    def result_rows(s):
        def use(span):
            result_out[span, :] = (middle[span, :] + s.total(span)).astype(BF16)

        return use

    for s in rows_y:
        s.arrive()
        over_rows(s.start_row, s.size, token_rows(s))
    gain_c[c, 0:1] = jnp.sum(total[...], axis=0, keepdims=True)
    gain_c[c, 1:2] = gain_two[...]
    gain_got = [wires.send(gain_c.at[c], gain_c.at[c], spot.sibling)]
    for s in rows_x:
        s.arrive()
        over_rows(s.start_row, s.size, result_rows(s))

    held = gain_c
    for axis, into in (("y", gain_y), ("x", gain_x), ("z", gain_z), (None, None)):
        for copy in gain_got:
            copy.wait_recv()
        summed = held[0]
        for i in range(1, held.shape[0]):
            summed = summed + held[i]
        if into is None:
            gains_out[...] = summed
            break
        me = spot.me(axis)
        into[me] = summed
        gain_got = [
            wires.send(into.at[me], into.at[me], spot.along(axis, by)) for by in (1, -1, 2)
        ]
        held = into

    lines[0].finish(gu_line)
    gu_got = []
    for by in (1, -1, 2):
        gu_got.append(
            wires.send(gu_line.at[turn(y, by)], gu_in.at[y], spot.along("y", by))
        )
    lines[1].finish(dn_line)
    dn_got = []
    for by in (1, -1, 2):
        dn_got.append(
            wires.send(dn_line.at[turn(y, by)], dn_in.at[y], spot.along("y", by))
        )
    lines[2].finish(att_line)
    att_got = []
    for by in (1, -1, 2):
        far = turn(x, by)
        att_got.append(
            wires.send(
                att_line.at[(far % 2) * 2 + far // 2], att_in.at[x], spot.along("x", by)
            )
        )
    for copy in gu_got:
        copy.wait_recv()
    add_into(gu_line.at[y], gu_line.at[y], *[gu_in.at[turn(y, by)] for by in (1, -1, 2)])
    gu_done = []
    for by in (1, 2, 3):
        other, who = spot.in_quad(by)
        gu_done.append(
            wires.send(
                gu_line.at[y, pl.ds(pl.multiple_of(other * 96, 96), 96)],
                gu_two.at[spot.quad],
                who,
            )
        )
    for copy in att_got:
        copy.wait_recv()
    slot = spot.low * 2 + spot.high
    add_into(att_two.at[0], att_line.at[slot], *[att_in.at[turn(x, by)] for by in (1, -1, 2)])
    att_done = wires.send(att_two.at[0], att_two.at[1], spot.partner)
    for copy in dn_got:
        copy.wait_recv()
    add_into(dn_out, dn_line.at[y], *[dn_in.at[turn(y, by)] for by in (1, -1, 2)])
    own_rows = gu_line.at[y, pl.ds(pl.multiple_of(spot.quad * 96, 96), 96)]
    add_into(gu_out.at[spot.quad], own_rows)
    for copy in gu_done:
        copy.wait_recv()
    for by in (1, 2, 3):
        other = turn(spot.quad, by)
        add_into(gu_out.at[other], gu_two.at[other])
    att_done.wait_recv()
    add_into(att_out, att_two.at[jnp.where(spot.high == c, 0, 1)])
    wires.close()


def final_exchange(normed_part, mlp_part, tokens, gain, back, middle, gain_two, d_att, d_gu, d_dn):
    sems = 128
    return pl.pallas_call(
        final_kernel,
        out_shape=(
            jax.ShapeDtypeStruct((OWN, D), BF16),
            jax.ShapeDtypeStruct((OWN, D), BF16),
            jax.ShapeDtypeStruct((2, D), F32),
            jax.ShapeDtypeStruct((144, 384), F32),
            jax.ShapeDtypeStruct((4, 96, 256), F32),
            jax.ShapeDtypeStruct((32, D), F32),
        ),
        in_specs=[VMEM] * 10,
        out_specs=[VMEM] * 6,
        scratch_shapes=scatter_scratch()
        + scatter_scratch()
        + line_scratch(4, 144, 384)
        + line_scratch(4, 384, 256)
        + line_scratch(4, 32, D)
        + [
            pltpu.VMEM((4, 144, 384), BF16),
            pltpu.VMEM((4, 384, 256), BF16),
            pltpu.VMEM((4, 32, D), BF16),
            pltpu.VMEM((2, 144, 384), BF16),
            pltpu.VMEM((4, 96, 256), BF16),
            pltpu.VMEM((2, 2, D), F32),
            pltpu.VMEM((4, 2, D), F32),
            pltpu.VMEM((4, 2, D), F32),
            pltpu.VMEM((4, 2, D), F32),
            pltpu.VMEM((8, D), F32),
            pltpu.SemaphoreType.DMA((sems,)),
            pltpu.SemaphoreType.DMA((sems,)),
        ],
        compiler_params=pltpu.CompilerParams(
            collective_id=4, has_side_effects=True, vmem_limit_bytes=60 << 20
        ),
        name="final_exchange",
    )(normed_part, mlp_part, tokens, gain, back, middle, gain_two, d_att, d_gu, d_dn)


def rotary_tables(places):
    half_size = HD // 2
    exponent = jnp.arange(half_size, dtype=F32) * (2.0 / HD)
    frequency = jnp.exp(-math.log(ROPE_BASE) * exponent)
    angles = places.astype(F32)[:, None] * frequency[None, :]
    return (jnp.cos(angles)[:, None, :], jnp.sin(angles)[:, None, :])


def rotate(values, cosine, sine):
    half_size = values.shape[-1] // 2
    front = values[..., :half_size]
    behind = values[..., half_size:]
    return jnp.concatenate(
        [front * cosine - behind * sine, behind * cosine + front * sine], axis=-1
    )


def inner_rows(left, right):
    return lax.dot_general(left, right, (((0,), (0,)), ((), ())), preferred_element_type=F32)


def outer_cols(left, right):
    return lax.dot_general(left, right, (((1,), (1,)), ((), ())), preferred_element_type=F32)


def windows(blocks):
    return jnp.stack([blocks[:, i * WIN : i * WIN + SEQ] for i in range(3)], axis=1)


def unwindow(grads):
    none = jnp.zeros_like(grads[:, 0, :WIN])
    low = jnp.concatenate([grads[:, i, :WIN] for i in range(3)] + [none], axis=1)
    high = jnp.concatenate([none] + [grads[:, i, WIN:] for i in range(3)], axis=1)
    return low + high


def shards(
    tokens,
    gain_attn,
    gain_mlp,
    w_query,
    w_key,
    w_value,
    w_out,
    w_gate,
    w_up,
    w_down,
    segments,
    positions,
    cotangent,
):
    scale = HD ** (-0.5)
    rows = 8 * OWN
    half_way = [(t, (t + 4) % 8) for t in range(8)]
    high = lax.axis_index("tensor") // 4

    att = jnp.concatenate(
        [jnp.concatenate([w_query, w_key, w_value], axis=1), w_out.reshape(48, 384)], axis=0
    )

    def by_quad(w):
        return w.reshape(96, 4, 4, 32).transpose(2, 0, 1, 3).reshape(4, 96, 128)

    gu = jnp.concatenate([by_quad(w_gate), by_quad(w_up)], axis=-1)
    marks = jnp.stack([segments, positions])
    normed, cot_full, att_full, gu_full, dn_full, marks_full = gather_all(
        tokens, gain_attn[None], cotangent, att, gu, w_down, marks
    )
    normed = normed.reshape(rows, D)
    cot_full = cot_full.reshape(rows, D)
    qkv_w = att_full[:, :, :96].reshape(D, 384)
    out_w = att_full[:, :, 96:].reshape(OWN, D)
    gu_w = gu_full.reshape(4, D, 256)
    down_w = dn_full.reshape(512, D)

    labels = jnp.pad(marks_full[:, 0], ((0, 0), (WIN, 0)), constant_values=-1)
    labels = lax.dynamic_slice_in_dim(labels, high * HALF, HALF + WIN, axis=1)
    places = lax.dynamic_slice_in_dim(marks_full[:, 1], high * HALF, HALF, axis=1)
    cosine, sine = rotary_tables(places.reshape(rows))

    qkv = jnp.dot(normed, qkv_w, preferred_element_type=F32)
    query = rotate(qkv[:, :192].reshape(rows, 2, HD), cosine, sine).astype(BF16)
    key = rotate(qkv[:, 192:288].reshape(rows, 1, HD), cosine, sine).astype(BF16)
    key = key.reshape(2, HALF, HD)
    value = qkv[:, 288:].astype(BF16).reshape(2, HALF, HD)
    far = lax.ppermute(jnp.concatenate([key, value], axis=-1)[:, SEQ:], "tensor", half_way)
    keys = windows(jnp.concatenate([far[..., :HD], key], axis=1))
    values = windows(jnp.concatenate([far[..., HD:], value], axis=1))

    first = high * HALF + jnp.arange(3)[:, None, None] * WIN
    at_query = first + jnp.arange(WIN)[None, :, None]
    at_key = first - WIN + jnp.arange(SEQ)[None, None, :]
    allowed = (at_key >= 0) & (at_key <= at_query) & (at_key // SEQ == at_query // SEQ)
    mine = labels[:, WIN:].reshape(2, 3, WIN)
    allowed = allowed[None] & (mine[:, :, :, None] == windows(labels)[:, :, None, :])
    allowed = allowed[:, :, None]

    queries = query.reshape(2, 3, WIN, 2, HD)
    scores = jnp.einsum("btird,btjd->btrij", queries, keys, preferred_element_type=F32) * scale
    scores = jnp.where(allowed, scores, MASKED)
    highest = jnp.max(scores, axis=-1, keepdims=True)
    weights = jnp.exp(scores - highest)
    prob = weights / jnp.sum(weights, axis=-1, keepdims=True)
    prob_low = prob.astype(BF16)
    mixed = jnp.einsum("btrij,btjd->btird", prob_low, values, preferred_element_type=F32)
    mixed = mixed.astype(BF16).reshape(rows, 192)
    attn_part = jnp.dot(mixed, out_w, preferred_element_type=F32).astype(BF16)
    middle, second = forward_exchange(attn_part.reshape(2, 4, OWN, D), tokens, gain_mlp[None])
    second = second.reshape(rows, D)

    hidden, gate_acts, d_gu = [], [], []
    grad_second = jnp.zeros((rows, D), F32)
    for i in range(4):
        both = jnp.dot(second, gu_w[i], preferred_element_type=F32)
        gate, upward = both[:, :128], both[:, 128:]
        sigmoid_gate = jax.nn.sigmoid(gate)
        silu_gate = gate * sigmoid_gate
        hidden.append((silu_gate * upward).astype(BF16))
        grad_hidden = outer_cols(cot_full, down_w[i * 128 : (i + 1) * 128])
        slope = sigmoid_gate * (1.0 + gate * (1.0 - sigmoid_gate))
        acts = jnp.concatenate([grad_hidden * upward * slope, grad_hidden * silu_gate], axis=-1)
        acts = acts.astype(BF16)
        grad_second = grad_second + outer_cols(acts, gu_w[i])
        d_gu.append(inner_rows(second, acts).astype(BF16))
    hidden = jnp.concatenate(hidden, axis=-1)
    mlp_part = jnp.dot(hidden, down_w, preferred_element_type=F32).astype(BF16)
    d_dn = inner_rows(hidden, cot_full).astype(BF16)
    d_gu = jnp.stack(d_gu)
    back, grad_attn, gain_two = backward_exchange(
        grad_second.astype(BF16).reshape(2, 4, OWN, D), cotangent, middle, gain_mlp[None]
    )
    grad_attn = grad_attn.reshape(rows, D)

    d_out = inner_rows(mixed, grad_attn).astype(BF16)
    grad_mixed = outer_cols(grad_attn, out_w).astype(BF16).reshape(2, 3, WIN, 2, HD)
    grad_prob = jnp.einsum("btird,btjd->btrij", grad_mixed, values, preferred_element_type=F32)
    row_inner = jnp.sum(prob * grad_prob, axis=-1, keepdims=True)
    grad_scores = (prob * (grad_prob - row_inner)).astype(BF16)
    grad_query = (
        jnp.einsum("btrij,btjd->btird", grad_scores, keys, preferred_element_type=F32) * scale
    )
    grad_keys = (
        jnp.einsum("btrij,btird->btjd", grad_scores, queries, preferred_element_type=F32) * scale
    )
    grad_values = jnp.einsum("btrij,btird->btjd", prob_low, grad_mixed, preferred_element_type=F32)
    grad_kv = unwindow(jnp.concatenate([grad_keys, grad_values], axis=-1))
    far_back = lax.ppermute(grad_kv[:, :WIN].astype(BF16), "tensor", half_way).astype(F32)
    grad_kv = jnp.concatenate(
        [grad_kv[:, WIN : WIN + SEQ], grad_kv[:, WIN + SEQ :] + far_back], axis=1
    ).reshape(rows, 192)
    grad_query_act = rotate(grad_query.reshape(rows, 2, HD), cosine, -sine)
    grad_key_act = rotate(grad_kv[:, :HD].reshape(rows, 1, HD), cosine, -sine)
    acts = jnp.concatenate(
        [grad_query_act.reshape(rows, 192), grad_key_act.reshape(rows, HD), grad_kv[:, HD:]],
        axis=-1,
    ).astype(BF16)
    d_qkv = inner_rows(normed, acts).astype(BF16)
    grad_normed = outer_cols(acts, qkv_w).astype(BF16)

    d_att = jnp.concatenate([d_qkv.reshape(4, 4, 96, 384), d_out.reshape(4, 4, 48, 384)], axis=2)
    result, token_grad, gains, g_att, g_gu, g_dn = final_exchange(
        grad_normed.reshape(2, 4, OWN, D),
        mlp_part.reshape(2, 4, OWN, D),
        tokens,
        gain_attn[None],
        back,
        middle,
        gain_two,
        d_att,
        d_gu.reshape(4, 4, 384, 256),
        d_dn.reshape(4, 4, 32, D),
    )

    def from_quad(g):
        return g.reshape(4, 96, 4, 32).transpose(1, 2, 0, 3).reshape(96, 512)

    return (
        result,
        token_grad,
        gains[0],
        gains[1],
        g_att[:96, :192],
        g_att[:96, 192:288],
        g_att[:96, 288:],
        g_att[96:].reshape(12, D),
        from_quad(g_gu[..., :128]),
        from_quad(g_gu[..., 128:]),
        g_dn,
    )


def solution(mesh):
    placed = (
        P(("dp", "tensor"), None),
        P(),
        P(),
        P("dp", "tensor"),
        P("dp", "tensor"),
        P("dp", "tensor"),
        P(("tensor", "dp"), None),
        P("dp", "tensor"),
        P("dp", "tensor"),
        P(("tensor", "dp"), None),
        P("dp"),
        P("dp"),
        P(("dp", "tensor"), None),
    )
    return jax.shard_map(
        shards,
        mesh=mesh,
        in_specs=placed,
        out_specs=(
            P(("dp", "tensor"), None),
            P(("dp", "tensor"), None),
            P(),
            P(),
            P("dp", "tensor"),
            P("dp", "tensor"),
            P("dp", "tensor"),
            P(("tensor", "dp"), None),
            P("dp", "tensor"),
            P("dp", "tensor"),
            P(("tensor", "dp"), None),
        ),
        check_vma=False,
    )
```

```python
import functools
import math

import jax
import jax.numpy as jnp
from jax import lax
from jax.experimental import pallas as pl
from jax.experimental.pallas import tpu as pltpu
from jax.sharding import PartitionSpec as P

HD = 96
SEQ = 512
D = 1536
OWN = 192
HALF = 768
WIN = 256

EPSILON = 1e-05
ROPE_BASE = 100000.0
MASKED = -1e30
MESH = pl.DeviceIdType.MESH
ANY = pl.BlockSpec(memory_space=pl.ANY)
VMEM = pl.BlockSpec(memory_space=pltpu.VMEM)
BF16 = jnp.bfloat16
F32 = jnp.float32


def place():
    dp = lax.axis_index("dp")
    tensor = lax.axis_index("tensor")
    return (tensor // 4) * 2 + (dp // 2) % 2, tensor % 4, dp // 4, dp % 2


def device(x, y, z, c):
    return (z * 4 + (x % 2) * 2 + c, (x // 2) * 4 + y)


def turn(pos, by):
    return (pos + by + 4) % 4


class Spot:
    def __init__(self):
        x, y, z, c = place()
        self.x, self.y, self.z, self.c = x, y, z, c
        self.high, self.low = x // 2, x % 2
        self.quad = self.low * 2 + c
        self.sibling = device(x, y, z, 1 - c)
        self.partner = device(turn(x, 2), y, z, 1 - c)

    def along(self, axis, by):
        x, y, z, c = self.x, self.y, self.z, self.c
        if axis == "x":
            return device(turn(x, by), y, z, c)
        if axis == "y":
            return device(x, turn(y, by), z, c)
        return device(x, y, turn(z, by), c)

    def me(self, axis):
        return {"x": self.x, "y": self.y, "z": self.z}[axis]

    def in_quad(self, by):
        other = turn(self.quad, by)
        return other, device(self.high * 2 + other // 2, self.y, self.z, other % 2)


def greet(devices):
    barrier = pltpu.get_barrier_semaphore()
    for who in devices:
        pl.semaphore_signal(barrier, inc=1, device_id=who, device_id_type=MESH)
    pl.semaphore_wait(barrier, len(devices))


class Wires:
    def __init__(self, send_sem, recv_sem):
        self.send_sem, self.recv_sem = send_sem, recv_sem
        self.count = 0
        self.sent = []
        self.moved = []

    def send(self, src, dst, who):
        copy = pltpu.make_async_remote_copy(
            src_ref=src,
            dst_ref=dst,
            send_sem=self.send_sem.at[self.count],
            recv_sem=self.recv_sem.at[self.count],
            device_id=who,
            device_id_type=MESH,
        )
        self.count += 1
        copy.start()
        self.sent.append(copy)
        return copy

    def move(self, src, dst):
        copy = pltpu.make_async_copy(src, dst, self.send_sem.at[self.count])
        self.count += 1
        copy.start()
        return copy

    def done(self, copies):
        for copy in copies:
            self.sent = [other for other in self.sent if other is not copy]
            copy.wait_send()

    def close(self):
        self.done(list(self.sent))


def add_into(dst, *srcs, chunk=16):
    rows = dst.shape[-2]
    chunk = min(chunk, rows)

    def step(i, carry):
        span = pl.ds(pl.multiple_of(i * chunk, chunk), chunk)
        total = srcs[0][..., span, :].astype(F32)
        for src in srcs[1:]:
            total = total + src[..., span, :].astype(F32)
        dst[..., span, :] = total.astype(dst.dtype)
        return carry

    lax.fori_loop(0, rows // chunk, step, 0)


class RingGather:
    def __init__(self, wires, spot, axis, at):
        self.wires, self.at = wires, at
        self.me = spot.me(axis)
        self.next, self.prev = spot.along(axis, 1), spot.along(axis, -1)

    def start(self, own=None):
        own = own or (lambda half: self.at(self.me, half))
        send, at, me = self.wires.send, self.at, self.me
        self.right0 = send(own(0), at(me, 0), self.next)
        self.left1 = send(own(1), at(me, 1), self.prev)
        self.right1 = send(own(1), at(me, 1), self.next)
        self.left0 = send(own(0), at(me, 0), self.prev)

    def forward(self):
        send, at, me = self.wires.send, self.at, self.me
        self.right0.wait_recv()
        before = at(turn(me, -1), 0)
        self.pass0 = send(before, before, self.next)
        self.left1.wait_recv()
        after = at(turn(me, 1), 1)
        self.pass1 = send(after, after, self.prev)

    def near(self):
        self.right1.wait_recv()
        self.left0.wait_recv()

    def far(self):
        self.pass0.wait_recv()
        self.pass1.wait_recv()

    def close(self):
        near = [self.right0, self.left1, self.right1, self.left0]
        self.wires.done(near + [self.pass0, self.pass1])


class PairGather:
    def __init__(self, wires, spot, axis, out, own, start, size):
        self.wires, self.spot, self.out, self.own = wires, spot, out, own
        self.rows = pl.ds(start, size)
        cut = size // 2

        def half_rows(half):
            return pl.ds(start + half * cut, cut)

        self.half_rows = half_rows
        self.ring = RingGather(
            wires, spot, axis, lambda pos, half: out.at[spot.c, pos, half_rows(half)]
        )
        self.me = spot.me(axis)

    def share(self, pos):
        block = self.out.at[self.spot.c, pos, self.rows]
        return self.wires.send(block, block, self.spot.sibling)

    def start(self):
        self.ring.start(lambda half: self.own.at[self.half_rows(half)])
        mine = self.own.at[self.rows]
        place_of = self.out.at[self.spot.c, self.me, self.rows]
        self.shared = [self.wires.send(mine, place_of, self.spot.sibling)]
        self.kept = self.wires.move(mine, place_of)

    def forward(self):
        self.ring.forward()
        self.ring.near()
        self.shared.append(self.share(turn(self.me, -1)))
        self.shared.append(self.share(turn(self.me, 1)))

    def far(self):
        self.ring.far()
        self.shared.append(self.share(turn(self.me, 2)))

    def finish(self):
        for copy in self.shared:
            copy.wait_recv()
        self.kept.wait()

    def close(self):
        self.ring.close()
        self.wires.done(self.shared)


class PairScatter:
    def __init__(self, wires, spot, axis, part, got, passed, near, start, size):
        self.wires, self.spot = wires, spot
        self.me = spot.me(axis)
        self.next, self.prev = spot.along(axis, 1), spot.along(axis, -1)
        self.part, self.got, self.passed, self.near = part, got, passed, near
        self.start_row, self.size, self.cut = start, size, size // 2
        self.shared = {}

    def rows(self, half=None):
        if half is None:
            return pl.ds(self.start_row, self.size)
        return pl.ds(self.start_row + half * self.cut, self.cut)

    def share(self, by):
        pos = turn(self.me, by)
        self.shared[by] = self.wires.send(
            self.part.at[1 - self.spot.c, pos, self.rows()],
            self.got.at[pos, self.rows()],
            self.spot.sibling,
        )

    def first(self):
        self.shared[2].wait_recv()
        pos = turn(self.me, 2)
        mine = self.got.at[pos, self.rows()]
        add_into(mine, self.part.at[self.spot.c, pos, self.rows()], mine)
        self.pass0 = self.wires.send(
            self.got.at[pos, self.rows(0)], self.passed.at[0, self.rows(0)], self.next
        )
        self.pass1 = self.wires.send(
            self.got.at[pos, self.rows(1)], self.passed.at[1, self.rows(1)], self.prev
        )

    def second(self):
        self.arriving = []
        after, before = turn(self.me, 1), turn(self.me, -1)
        for by, half, who, side in ((1, 1, self.next, 0), (-1, 0, self.prev, 1)):
            pos = turn(self.me, by)
            self.shared[by].wait_recv()
            mine = self.got.at[pos, self.rows(half)]
            add_into(mine, self.part.at[self.spot.c, pos, self.rows(half)], mine)
            self.arriving.append(self.wires.send(mine, self.near.at[side, self.rows(half)], who))
        for pos, half, who, side, arrived in (
            (after, 0, self.next, 0, self.pass0),
            (before, 1, self.prev, 1, self.pass1),
        ):
            arrived.wait_recv()
            mine = self.got.at[pos, self.rows(half)]
            add_into(
                mine,
                self.part.at[self.spot.c, pos, self.rows(half)],
                mine,
                self.passed.at[side, self.rows(half)],
            )
            self.arriving.append(self.wires.send(mine, self.near.at[side, self.rows(half)], who))

    def arrive(self):
        self.shared[0].wait_recv()
        for copy in self.arriving:
            copy.wait_recv()

    def close(self):
        self.wires.done(list(self.shared.values()) + [self.pass0, self.pass1] + self.arriving)

    def total(self, span):
        return (
            self.part[self.spot.c, self.me, span].astype(F32)
            + self.got[self.me, span].astype(F32)
            + self.near[0, span].astype(F32)
            + self.near[1, span].astype(F32)
        )


class LineScatter:
    def __init__(self, wires, spot, at, work, passed, near, cut):
        self.wires, self.spot, self.at = wires, spot, at
        self.me = spot.z
        self.next, self.prev = spot.along("z", 1), spot.along("z", -1)
        self.work, self.passed, self.near = work, passed, near
        rows = work.shape[-2]
        self.spans = (pl.ds(0, cut), pl.ds(cut, rows - cut))

    def half(self, ref, half):
        return ref.at[:, self.spans[half]]

    def first(self):
        far = self.at(turn(self.me, 2))
        self.pass0 = self.wires.send(self.half(far, 0), self.half(self.passed.at[0], 0), self.next)
        self.pass1 = self.wires.send(self.half(far, 1), self.half(self.passed.at[1], 1), self.prev)
        after, before = self.at(turn(self.me, 1)), self.at(turn(self.me, -1))
        self.arriving = [
            self.wires.send(self.half(after, 1), self.half(self.near.at[0], 1), self.next),
            self.wires.send(self.half(before, 0), self.half(self.near.at[1], 0), self.prev),
        ]

    def second(self):
        after, before = self.at(turn(self.me, 1)), self.at(turn(self.me, -1))
        for src, half, who, side, arrived in (
            (after, 0, self.next, 0, self.pass0),
            (before, 1, self.prev, 1, self.pass1),
        ):
            arrived.wait_recv()
            mine = self.half(self.work.at[side], half)
            add_into(mine, self.half(src, half), self.half(self.passed.at[side], half))
            self.arriving.append(self.wires.send(mine, self.half(self.near.at[side], half), who))

    def finish(self, out):
        for copy in self.arriving:
            copy.wait_recv()
        add_into(out, self.at(self.me), self.near.at[0], self.near.at[1])


def line_scratch(lines, rows, columns):
    shape = (2, lines, rows, columns)
    return [pltpu.VMEM(shape, BF16)] * 3 + [pltpu.VMEM((lines, rows, columns), BF16)]


def norm_scale(values):
    return lax.rsqrt(jnp.mean(values * values, axis=-1, keepdims=True) + EPSILON)


def norm_back(upstream, values, inverse, gain):
    scaled = upstream * gain
    inner = jnp.sum(scaled * values, axis=-1, keepdims=True)
    return scaled * inverse - values * inner * (inverse * inverse * inverse) / values.shape[-1]


def over_rows(start, size, step, chunk=16):
    def body(i, carry):
        step(pl.ds(pl.multiple_of(start + i * chunk, chunk), chunk))
        return carry

    lax.fori_loop(0, size // chunk, body, 0)


def fold(total, values):
    part = values[0:8]
    for first in range(8, values.shape[0], 8):
        part = part + values[first : first + 8]
    total[...] += part


SUBS = ((0, 96), (96, 96))


def dot(left, right, a, b):
    return lax.dot_general(left, right, (((a,), (b,)), ((), ())), preferred_element_type=F32)


def repeat(count, step):
    def body(i, carry):
        step(i)
        return carry

    lax.fori_loop(0, count, body, 0)


def whole(i, size):
    return pl.ds(pl.multiple_of(i * size, size), size)


def grid_of(rows, columns):
    return (
        lax.broadcasted_iota(jnp.int32, (rows, columns), 0),
        lax.broadcasted_iota(jnp.int32, (rows, columns), 1),
    )


def picks(rows, columns, chosen):
    return jnp.where(chosen(*grid_of(rows, columns)), 1.0, 0.0).astype(BF16)


def quad_order(unit):
    return (((unit >> 5) & 3) << 7) + ((unit >> 7) << 5) + (unit & 31)


def swap_halves(values):
    lane = lax.broadcasted_iota(jnp.int32, values.shape, 1)
    up = pltpu.roll(values, 80, 1)
    down = pltpu.roll(values, 48, 1)
    return jnp.where(lane < 48, up, down)


def scatter_scratch():
    return [
        pltpu.VMEM((4, OWN, D), BF16),
        pltpu.VMEM((2, OWN, D), BF16),
        pltpu.VMEM((2, OWN, D), BF16),
    ]


def around(spot, axes):
    return [spot.along(a, by) for a in axes for by in (1, -1)] + [spot.sibling]


def forward_kernel(
    tokens, gain_attn, gain_mlp, cot, w_query, w_key, w_value, w_out, w_gate, w_up, w_down, marks,
    normed_out, grad_out, mlp_out, wq, wo, q, kv, prob, mix, cosine, sine,
    d_gu, d_dn, back_out, middle_out, gain_out,
    normed, cots, second, part, got, passed, near, att_two, own_out, aq, ao, gu, gu_own, dn,
    own, grad_hidden, hidden, acts, total, places,
    send_sem, recv_sem,
):
    spot = Spot()
    wires = Wires(send_sem, recv_sem)
    x, y, z, c = spot.x, spot.y, spot.z, spot.c
    greet(
        around(spot, "xyz")
        + [spot.along(a, 2) for a in "xyz"]
        + [spot.partner]
        + [spot.in_quad(by)[1] for by in (1, 2, 3)]
    )

    def three(first):
        return lambda r, k: r + first == k

    columns = (
        dot(w_query[...], picks(192, 384, three(0)), 1, 0)
        + dot(w_key[...], picks(96, 384, three(192)), 1, 0)
        + dot(w_value[...], picks(96, 384, three(288)), 1, 0)
    )
    att_two[0] = columns.astype(BF16)
    own_out[0] = jnp.zeros((16, D), BF16)
    own_out[0, 0:12] = w_out[...]
    swaps = [
        wires.send(att_two.at[0], att_two.at[1], spot.partner),
        wires.send(own_out.at[0], own_out.at[1], spot.partner),
    ]
    dn_here = dn.at[whole(y * 4 + z, 32)]
    dn_kept = wires.move(w_down, dn_here)
    dn_side = [wires.send(w_down, dn_here, spot.along("z", by)) for by in (1, -1, 2)]
    marks_kept = wires.move(marks, places.at[c])
    marks_got = wires.send(marks, places.at[c], spot.sibling)

    def normalise(span):
        rows = tokens[span, :].astype(F32)
        own[span, :] = (rows * norm_scale(rows) * gain_attn[...]).astype(BF16)

    over_rows(0, OWN, normalise)
    rows_y = [PairGather(wires, spot, "y", normed, own, s, n) for s, n in SUBS]
    for g in rows_y:
        g.start()

    order = picks(512, 512, lambda r, k: quad_order(r) == k)
    for shard, first in ((w_gate, 0), (w_up, 128)):
        moved = dot(shard[...], order, 1, 0).astype(BF16)
        for i in range(4):
            gu_own[i, :, first : first + 128] = moved[:, i * 128 : i * 128 + 128]
    gu_lanes = whole(y, 256)
    gu_here = gu.at[whole(z * 4 + spot.quad, 96), gu_lanes]
    gu_kept = wires.move(gu_own.at[spot.quad], gu_here)
    gu_swap = []
    for by in (1, 2, 3):
        other, who = spot.in_quad(by)
        gu_swap.append(wires.send(gu_own.at[other], gu_here, who))

    for copy in swaps:
        copy.wait_recv()
    slot = spot.low * 2 + spot.high
    pick = jnp.where(spot.high == c, 0, 1)
    aq_here, ao_here = aq.at[z, slot], ao.at[z, slot]
    att_kept = [wires.move(att_two.at[pick], aq_here), wires.move(own_out.at[pick], ao_here)]
    att_side = []
    for by in (1, -1, 2):
        who = spot.along("z", by)
        att_side.append(wires.send(att_two.at[pick], aq_here, who))
        att_side.append(wires.send(own_out.at[pick], ao_here, who))

    def trig(core):
        def step(i):
            span = whole(i, 128)
            lane = grid_of(128, 128)[1]
            turns = jnp.where(lane < 48, lane, lane - 48).astype(F32) * (2.0 / HD)
            angle = places[core, span, :].astype(F32) * jnp.exp(-math.log(ROPE_BASE) * turns)
            inside = lane < HD
            cosine[core, span, :] = jnp.where(inside, jnp.cos(angle), 0.0)
            wave = jnp.sin(angle)
            sine[core, span, :] = jnp.where(inside, jnp.where(lane < 48, -wave, wave), 0.0)

        repeat(6, step)

    marks_kept.wait()
    trig(c)
    for copy in att_kept:
        copy.wait()
    for copy in att_side:
        copy.wait_recv()

    def slot_of(pos):
        return (pos % 2) * 2 + pos // 2

    att_line = [
        RingGather(wires, spot, "x", lambda pos, h: aq.at[pl.ds(2 * h, 2), slot_of(pos)]),
        RingGather(wires, spot, "x", lambda pos, h: ao.at[pl.ds(2 * h, 2), slot_of(pos)]),
    ]
    for line in att_line:
        line.start()
    for g in rows_y:
        g.forward()
    marks_got.wait_recv()
    trig(1 - c)
    for line in att_line:
        line.forward()
    cot_x = [PairGather(wires, spot, "x", cots, cot, s, n) for s, n in SUBS]
    for g in cot_x:
        g.start()
    gu_kept.wait()
    for copy in gu_swap:
        copy.wait_recv()
    gu_block = gu.at[whole(z, 384), gu_lanes]
    gu_side = [wires.send(gu_block, gu_block, spot.along("y", by)) for by in (1, -1, 2)]
    dn_kept.wait()
    for copy in dn_side:
        copy.wait_recv()
    dn_line = RingGather(wires, spot, "y", lambda pos, h: dn.at[whole(pos * 2 + h, 64)])
    dn_line.start()
    for g in rows_y:
        g.far()
    for line in att_line:
        line.near()
        line.far()

    widen = picks(384, 512, lambda r, k: r + ((r * 683) >> 16) * 32 == k)

    def widen_rows(i):
        wq[whole(i, 96), :] = dot(aq[i // 4, i % 4], widen, 1, 0).astype(BF16)

    repeat(16, widen_rows)

    def out_row(r, k):
        unit = jnp.where(r < 128, r, r - 32)
        real = (r < 96) | ((r >= 128) & (r < 224))
        return real & (unit + ((unit * 5462) >> 16) * 4 == k)

    wo[...] = dot(picks(256, 256, out_row), ao[...].reshape(256, D), 1, 0).astype(BF16)

    for g in rows_y:
        g.finish()
    normed_kept = wires.move(normed, normed_out)

    def project(i):
        core, pos = i // 4, i % 4
        both = dot(normed[core, pos], wq[...], 1, 0)
        span = whole(pos, OWN)
        cos, sin = cosine[core, span, :], sine[core, span, :]

        def turned(first):
            values = both[:, first : first + 128]
            return (values * cos + swap_halves(values) * sin).astype(BF16)

        q[core, span, 0:128] = turned(0)
        q[core, span, 128:256] = turned(128)
        after = pl.ds(pl.multiple_of(WIN + pos * OWN, 64), OWN)
        kv[core, after, 0:128] = turned(256)
        kv[core, after, 128:256] = both[:, 384:512].astype(BF16)

    repeat(8, project)
    kv_got = wires.send(kv.at[:, pl.ds(768, WIN)], kv.at[:, pl.ds(0, WIN)], spot.along("x", 2))

    for copy in gu_side:
        copy.wait_recv()
    gu_line = RingGather(
        wires, spot, "z", lambda pos, h: gu.at[whole(pos, 384), pl.ds(h * 512, 512)]
    )
    gu_line.start()

    scale = HD ** (-0.5)

    def attend(core, run, head):
        span = whole(run, WIN)
        lanes = whole(head, 128)
        window = pl.ds(pl.multiple_of(run * WIN, WIN), SEQ)
        scores = dot(q[core, span, lanes], kv[core, window, 0:128], 1, 1) * scale
        row, column = grid_of(WIN, SEQ)
        spot_of = spot.high * HALF + run * WIN + row[:, 0:1]
        begin = jnp.maximum((spot_of >> 9) << 9, spot_of - places[core, span, 0:1])
        begin = begin - (spot.high * HALF + run * WIN) + WIN
        allowed = (column >= begin) & (column <= row + WIN)
        scores = jnp.where(allowed, scores, MASKED)
        weights = jnp.exp(scores - jnp.max(scores, axis=-1, keepdims=True))
        share = weights / jnp.sum(weights, axis=-1, keepdims=True)
        low = share.astype(BF16)
        prob[core, run, head] = low
        values = dot(low, kv[core, window, 128:256], 1, 0)
        mix[core, span, lanes] = values.astype(BF16)

    repeat(8, lambda i: attend(i // 4, 1 + (i // 2) % 2, i % 2))
    for g in cot_x:
        g.forward()
    dn_line.forward()
    kv_got.wait_recv()
    repeat(4, lambda i: attend(i // 2, 0, i % 2))

    def project_out(core):
        def step(pos):
            rows = mix[core, whole(pos, OWN), :]
            part[core, pos] = dot(rows, wo[...], 1, 0).astype(BF16)

        repeat(4, step)

    sums_y = [PairScatter(wires, spot, "y", part, got, passed, near, s, n) for s, n in SUBS]
    project_out(1 - c)
    for by in (2, 1, -1, 0):
        for s in sums_y:
            s.share(by)
    project_out(c)
    for s in sums_y:
        s.first()
    gu_line.forward()
    for g in cot_x:
        g.far()
    for s in sums_y:
        s.second()
    dn_line.near()
    dn_line.far()
    for g in cot_x:
        g.finish()

    def back_hidden(i):
        rows = cots[i // 2, pl.ds((i % 2) * 2, 2)].reshape(384, D)
        grad_hidden[i // 2, pl.ds((i % 2) * 2, 2)] = dot(rows, dn[...], 1, 1).reshape(2, OWN, 512)

    repeat(4, back_hidden)
    rows_x = [PairGather(wires, spot, "x", second, own, s, n) for s, n in SUBS]
    for g in rows_y:
        g.close()

    def middle_rows(s):
        def use(span):
            middle = tokens[span, :].astype(F32) + s.total(span)
            middle_out[span, :] = middle
            own[span, :] = (middle * norm_scale(middle) * gain_mlp[...]).astype(BF16)

        return use

    for s, g in zip(sums_y, rows_x):
        s.arrive()
        over_rows(s.start_row, s.size, middle_rows(s))
        g.start()
        g.forward()
    gu_line.near()
    gu_line.far()
    for s in sums_y:
        s.close()
    rows_x[0].far()
    rows_x[0].finish()

    def feed(core, s):
        span = s.rows()
        size = 4 * s.size

        rows = second[core, :, span].reshape(size, D)
        both = dot(rows, gu[...], 1, 0)
        upstream = grad_hidden[core, :, span].reshape(size, 512)
        for i in range(4):
            gate = both[:, i * 256 : i * 256 + 128]
            upward = both[:, i * 256 + 128 : i * 256 + 256]
            sent = upstream[:, i * 128 : i * 128 + 128]
            sigmoid = jax.nn.sigmoid(gate)
            silu = gate * sigmoid
            slope = sigmoid * (1.0 + gate * (1.0 - sigmoid))
            low = (silu * upward).astype(BF16)
            hidden[core, :, span, i * 128 : i * 128 + 128] = low.reshape(4, s.size, 128)
            low = (sent * upward * slope).astype(BF16)
            acts[core, :, span, i * 256 : i * 256 + 128] = low.reshape(4, s.size, 128)
            low = (sent * silu).astype(BF16)
            acts[core, :, span, i * 256 + 128 : i * 256 + 256] = low.reshape(4, s.size, 128)
        back = dot(acts[core, :, span].reshape(size, 1024), gu[...], 1, 1)
        part[core, :, span] = back.astype(BF16).reshape(4, s.size, D)

    sums_x = [PairScatter(wires, spot, "x", part, got, passed, near, s, n) for s, n in SUBS]
    feed(1 - c, sums_x[0])
    for by in (2, 1, -1, 0):
        sums_x[0].share(by)
    rows_x[1].far()
    feed(c, sums_x[0])
    sums_x[0].first()
    rows_x[1].finish()
    feed(1 - c, sums_x[1])
    for by in (2, 1, -1, 0):
        sums_x[1].share(by)
    sums_x[0].second()
    feed(c, sums_x[1])
    sums_x[1].first()

    def grad_gate_up(i):
        lanes = whole(i, 256)
        rows = second[:, :, :, lanes].reshape(8 * OWN, 256)
        d_gu[lanes, :] = dot(rows, acts[...].reshape(8 * OWN, 1024), 0, 0).astype(BF16)

    def grad_down(i):
        lanes = whole(i, 256)
        rows = hidden[:, :, :, lanes].reshape(8 * OWN, 256)
        d_dn[lanes, :] = dot(rows, cots[...].reshape(8 * OWN, D), 0, 0).astype(BF16)

    def down(i):
        rows = hidden[i // 2, pl.ds((i % 2) * 2, 2)].reshape(384, 512)
        normed[i // 2, pl.ds((i % 2) * 2, 2)] = (
            dot(rows, dn[...], 1, 0).astype(BF16).reshape(2, OWN, D)
        )

    total[...] = jnp.zeros_like(total)
    grads_y = [PairGather(wires, spot, "y", grad_out, own, s, n) for s, n in SUBS]

    def back_rows(s):
        def use(span):
            grad = s.total(span)
            rows = middle_out[span, :]
            inverse = norm_scale(rows)
            back = cot[span, :].astype(F32) + norm_back(grad, rows, inverse, gain_mlp[...])
            back_out[span, :] = back
            own[span, :] = back.astype(BF16)
            fold(total, grad * rows * inverse)

        return use

    for g in rows_x:
        g.close()
    repeat(2, grad_gate_up)
    sums_x[1].second()
    sums_x[0].arrive()
    over_rows(sums_x[0].start_row, sums_x[0].size, back_rows(sums_x[0]))
    grads_y[0].start()
    repeat(2, lambda i: grad_gate_up(2 + i))
    grads_y[0].forward()
    sums_x[1].arrive()
    over_rows(sums_x[1].start_row, sums_x[1].size, back_rows(sums_x[1]))
    grads_y[1].start()
    repeat(2, lambda i: grad_gate_up(4 + i))
    grads_y[1].forward()
    grads_y[0].far()
    repeat(2, grad_down)
    normed_kept.wait()
    grads_y[1].far()
    repeat(4, down)
    mlp_kept = wires.move(normed, mlp_out)
    gain_out[...] = jnp.sum(total[...], axis=0, keepdims=True)
    for g in grads_y:
        g.finish()
    mlp_kept.wait()
    wires.close()


def forward_call(
    tokens, gain_attn, gain_mlp, cot, w_query, w_key, w_value, w_out, w_gate, w_up, w_down, marks
):
    sems = 192
    shape = jax.ShapeDtypeStruct
    outs = (
        (shape((2, 4, OWN, D), BF16), ANY),
        (shape((2, 4, OWN, D), BF16), ANY),
        (shape((2, 4, OWN, D), BF16), ANY),
        (shape((D, 512), BF16), VMEM),
        (shape((256, D), BF16), VMEM),
        (shape((2, HALF, 256), BF16), VMEM),
        (shape((2, HALF + WIN, 256), BF16), VMEM),
        (shape((2, 3, 2, WIN, SEQ), BF16), VMEM),
        (shape((2, HALF, 256), BF16), VMEM),
        (shape((2, HALF, 128), F32), VMEM),
        (shape((2, HALF, 128), F32), VMEM),
        (shape((D, 1024), BF16), VMEM),
        (shape((512, D), BF16), VMEM),
        (shape((OWN, D), F32), VMEM),
        (shape((OWN, D), F32), VMEM),
        (shape((1, D), F32), VMEM),
    )
    return pl.pallas_call(
        forward_kernel,
        out_shape=tuple(o[0] for o in outs),
        in_specs=[VMEM] * 12,
        out_specs=[o[1] for o in outs],
        scratch_shapes=[
            pltpu.VMEM((2, 4, OWN, D), BF16),
            pltpu.VMEM((2, 4, OWN, D), BF16),
            pltpu.VMEM((2, 4, OWN, D), BF16),
            pltpu.VMEM((2, 4, OWN, D), BF16),
        ]
        + scatter_scratch()
        + [
            pltpu.VMEM((2, 96, 384), BF16),
            pltpu.VMEM((2, 16, D), BF16),
            pltpu.VMEM((4, 4, 96, 384), BF16),
            pltpu.VMEM((4, 4, 16, D), BF16),
            pltpu.VMEM((D, 1024), BF16),
            pltpu.VMEM((4, 96, 256), BF16),
            pltpu.VMEM((512, D), BF16),
            pltpu.VMEM((OWN, D), BF16),
            pltpu.VMEM((2, 4, OWN, 512), F32),
            pltpu.VMEM((2, 4, OWN, 512), BF16),
            pltpu.VMEM((2, 4, OWN, 1024), BF16),
            pltpu.VMEM((8, D), F32),
            pltpu.VMEM((2, HALF, 128), jnp.int32),
            pltpu.SemaphoreType.DMA((sems,)),
            pltpu.SemaphoreType.DMA((sems,)),
        ],
        compiler_params=pltpu.CompilerParams(
            collective_id=1, has_side_effects=True, vmem_limit_bytes=64 << 20
        ),
        name="forward_layer",
    )(tokens, gain_attn, gain_mlp, cot, w_query, w_key, w_value, w_out, w_gate, w_up, w_down, marks)


def final_kernel(
    normed_part, mlp_part, tokens, gain, back, middle, gain_two, d_att, d_gu, d_dn,
    result_out, token_out, gains_out, att_out, gu_out, dn_out,
    got_y, passed_y, near_y, got_x, passed_x, near_x,
    att_work, att_passed, att_near, att_line,
    gu_work, gu_passed, gu_near, gu_line,
    dn_work, dn_passed, dn_near, dn_line,
    att_in, gu_in, dn_in, att_two, gu_two, gain_c, gain_y, gain_x, gain_z, total,
    send_sem, recv_sem,
):
    spot = Spot()
    wires = Wires(send_sem, recv_sem)
    x, y, z, c = spot.x, spot.y, spot.z, spot.c
    greet(
        around(spot, "xyz")
        + [spot.along(a, 2) for a in "xyz"]
        + [spot.partner]
        + [spot.in_quad(by)[1] for by in (1, 2, 3)]
    )
    rows_y = [
        PairScatter(wires, spot, "y", normed_part, got_y, passed_y, near_y, s, n) for s, n in SUBS
    ]
    rows_x = [
        PairScatter(wires, spot, "x", mlp_part, got_x, passed_x, near_x, s, n) for s, n in SUBS
    ]
    lines = [
        LineScatter(wires, spot, lambda p: d_gu.at[:, p], gu_work, gu_passed, gu_near, 192),
        LineScatter(wires, spot, lambda p: d_dn.at[:, p], dn_work, dn_passed, dn_near, 16),
        LineScatter(wires, spot, lambda p: d_att.at[p], att_work, att_passed, att_near, 80),
    ]
    for line in lines:
        line.first()
    for by in (2, 1, -1, 0):
        for s in rows_y + rows_x:
            s.share(by)
    for s in rows_y + rows_x:
        s.first()
    for s in rows_y + rows_x:
        s.second()
    for line in lines:
        line.second()
    total[...] = jnp.zeros_like(total)

    def token_rows(s):
        def use(span):
            grad = s.total(span)
            rows = tokens[span, :].astype(F32)
            inverse = norm_scale(rows)
            out = back[span, :] + norm_back(grad, rows, inverse, gain[...])
            token_out[span, :] = out.astype(BF16)
            fold(total, grad * rows * inverse)

        return use

    def result_rows(s):
        def use(span):
            result_out[span, :] = (middle[span, :] + s.total(span)).astype(BF16)

        return use

    for s in rows_y:
        s.arrive()
        over_rows(s.start_row, s.size, token_rows(s))
    gain_c[c, 0:1] = jnp.sum(total[...], axis=0, keepdims=True)
    gain_c[c, 1:2] = gain_two[...]
    gain_got = [wires.send(gain_c.at[c], gain_c.at[c], spot.sibling)]
    for s in rows_x:
        s.arrive()
        over_rows(s.start_row, s.size, result_rows(s))

    held = gain_c
    for axis, into in (("y", gain_y), ("x", gain_x), ("z", gain_z), (None, None)):
        for copy in gain_got:
            copy.wait_recv()
        summed = held[0]
        for i in range(1, held.shape[0]):
            summed = summed + held[i]
        if into is None:
            gains_out[...] = summed
            break
        me = spot.me(axis)
        into[me] = summed
        gain_got = [
            wires.send(into.at[me], into.at[me], spot.along(axis, by)) for by in (1, -1, 2)
        ]
        held = into

    lines[0].finish(gu_line)
    gu_got = []
    for by in (1, -1, 2):
        gu_got.append(
            wires.send(gu_line.at[turn(y, by)], gu_in.at[y], spot.along("y", by))
        )
    lines[1].finish(dn_line)
    dn_got = []
    for by in (1, -1, 2):
        dn_got.append(
            wires.send(dn_line.at[turn(y, by)], dn_in.at[y], spot.along("y", by))
        )
    lines[2].finish(att_line)
    att_got = []
    for by in (1, -1, 2):
        far = turn(x, by)
        att_got.append(
            wires.send(
                att_line.at[(far % 2) * 2 + far // 2], att_in.at[x], spot.along("x", by)
            )
        )
    for copy in gu_got:
        copy.wait_recv()
    add_into(gu_line.at[y], gu_line.at[y], *[gu_in.at[turn(y, by)] for by in (1, -1, 2)])
    gu_done = []
    for by in (1, 2, 3):
        other, who = spot.in_quad(by)
        gu_done.append(
            wires.send(
                gu_line.at[y, pl.ds(pl.multiple_of(other * 96, 96), 96)],
                gu_two.at[spot.quad],
                who,
            )
        )
    for copy in att_got:
        copy.wait_recv()
    slot = spot.low * 2 + spot.high
    add_into(att_two.at[0], att_line.at[slot], *[att_in.at[turn(x, by)] for by in (1, -1, 2)])
    att_done = wires.send(att_two.at[0], att_two.at[1], spot.partner)
    for copy in dn_got:
        copy.wait_recv()
    add_into(dn_out, dn_line.at[y], *[dn_in.at[turn(y, by)] for by in (1, -1, 2)])
    own_rows = gu_line.at[y, pl.ds(pl.multiple_of(spot.quad * 96, 96), 96)]
    add_into(gu_out.at[spot.quad], own_rows)
    for copy in gu_done:
        copy.wait_recv()
    for by in (1, 2, 3):
        other = turn(spot.quad, by)
        add_into(gu_out.at[other], gu_two.at[other])
    att_done.wait_recv()
    add_into(att_out, att_two.at[jnp.where(spot.high == c, 0, 1)])
    wires.close()


def final_exchange(normed_part, mlp_part, tokens, gain, back, middle, gain_two, d_att, d_gu, d_dn):
    sems = 128
    return pl.pallas_call(
        final_kernel,
        out_shape=(
            jax.ShapeDtypeStruct((OWN, D), BF16),
            jax.ShapeDtypeStruct((OWN, D), BF16),
            jax.ShapeDtypeStruct((2, D), F32),
            jax.ShapeDtypeStruct((144, 384), F32),
            jax.ShapeDtypeStruct((4, 96, 256), F32),
            jax.ShapeDtypeStruct((32, D), F32),
        ),
        in_specs=[VMEM] * 10,
        out_specs=[VMEM] * 6,
        scratch_shapes=scatter_scratch()
        + scatter_scratch()
        + line_scratch(4, 144, 384)
        + line_scratch(4, 384, 256)
        + line_scratch(4, 32, D)
        + [
            pltpu.VMEM((4, 144, 384), BF16),
            pltpu.VMEM((4, 384, 256), BF16),
            pltpu.VMEM((4, 32, D), BF16),
            pltpu.VMEM((2, 144, 384), BF16),
            pltpu.VMEM((4, 96, 256), BF16),
            pltpu.VMEM((2, 2, D), F32),
            pltpu.VMEM((4, 2, D), F32),
            pltpu.VMEM((4, 2, D), F32),
            pltpu.VMEM((4, 2, D), F32),
            pltpu.VMEM((8, D), F32),
            pltpu.SemaphoreType.DMA((sems,)),
            pltpu.SemaphoreType.DMA((sems,)),
        ],
        compiler_params=pltpu.CompilerParams(
            collective_id=4, has_side_effects=True, vmem_limit_bytes=60 << 20
        ),
        name="final_exchange",
    )(normed_part, mlp_part, tokens, gain, back, middle, gain_two, d_att, d_gu, d_dn)


def rotary_tables(places):
    half_size = HD // 2
    exponent = jnp.arange(half_size, dtype=F32) * (2.0 / HD)
    frequency = jnp.exp(-math.log(ROPE_BASE) * exponent)
    angles = places.astype(F32)[:, None] * frequency[None, :]
    return (jnp.cos(angles)[:, None, :], jnp.sin(angles)[:, None, :])


def rotate(values, cosine, sine):
    half_size = values.shape[-1] // 2
    front = values[..., :half_size]
    behind = values[..., half_size:]
    return jnp.concatenate(
        [front * cosine - behind * sine, behind * cosine + front * sine], axis=-1
    )


def inner_rows(left, right):
    return lax.dot_general(left, right, (((0,), (0,)), ((), ())), preferred_element_type=F32)


def outer_cols(left, right):
    return lax.dot_general(left, right, (((1,), (1,)), ((), ())), preferred_element_type=F32)


def windows(blocks):
    return jnp.stack([blocks[:, i * WIN : i * WIN + SEQ] for i in range(3)], axis=1)


def unwindow(grads):
    none = jnp.zeros_like(grads[:, 0, :WIN])
    low = jnp.concatenate([grads[:, i, :WIN] for i in range(3)] + [none], axis=1)
    high = jnp.concatenate([none] + [grads[:, i, WIN:] for i in range(3)], axis=1)
    return low + high


def shards(
    tokens,
    gain_attn,
    gain_mlp,
    w_query,
    w_key,
    w_value,
    w_out,
    w_gate,
    w_up,
    w_down,
    segments,
    positions,
    cotangent,
):
    scale = HD ** (-0.5)
    rows = 8 * OWN
    half_way = [(t, (t + 4) % 8) for t in range(8)]
    high = lax.axis_index("tensor") // 4

    marks = lax.dynamic_slice_in_dim(positions, high * HALF, HALF)
    marks = jnp.broadcast_to(marks[:, None], (HALF, 128))
    (
        normed, grad_attn, mlp_part, wq, wo, query, key_value, prob_low, mix, cosine, sine,
        d_gu, d_dn, back, middle, gain_two,
    ) = forward_call(
        tokens, gain_attn[None], gain_mlp[None], cotangent,
        w_query, w_key, w_value, w_out, w_gate, w_up, w_down, marks,
    )
    normed = normed.reshape(rows, D)
    grad_attn = grad_attn.reshape(rows, D)
    keys = windows(key_value[..., :128])
    values = windows(key_value[..., 128:])
    queries = query.reshape(2, 3, WIN, 2, 128)
    prob = prob_low.astype(F32)
    cosine = cosine.reshape(rows, 1, 128)[..., :48]
    sine = sine.reshape(rows, 1, 128)[..., 48:96]
    mix = mix.reshape(rows, 256)

    d_out = inner_rows(mix, grad_attn).astype(BF16)
    d_out = d_out.reshape(2, 128, D)[:, :HD].reshape(192, D)
    grad_mixed = outer_cols(grad_attn, wo).astype(BF16).reshape(2, 3, WIN, 2, 128)
    grad_prob = jnp.einsum("btird,btjd->btrij", grad_mixed, values, preferred_element_type=F32)
    row_inner = jnp.sum(prob * grad_prob, axis=-1, keepdims=True)
    grad_scores = (prob * (grad_prob - row_inner)).astype(BF16)
    grad_query = (
        jnp.einsum("btrij,btjd->btird", grad_scores, keys, preferred_element_type=F32) * scale
    )
    grad_keys = (
        jnp.einsum("btrij,btird->btjd", grad_scores, queries, preferred_element_type=F32) * scale
    )
    grad_values = jnp.einsum("btrij,btird->btjd", prob_low, grad_mixed, preferred_element_type=F32)
    grad_kv = unwindow(jnp.concatenate([grad_keys, grad_values], axis=-1))
    far_back = lax.ppermute(grad_kv[:, :WIN].astype(BF16), "tensor", half_way).astype(F32)
    grad_kv = jnp.concatenate(
        [grad_kv[:, WIN : WIN + SEQ], grad_kv[:, WIN + SEQ :] + far_back], axis=1
    ).reshape(rows, 256)
    grad_query_act = rotate(grad_query.reshape(rows, 2, 128)[..., :HD], cosine, -sine)
    grad_key_act = rotate(grad_kv[:, :HD].reshape(rows, 1, HD), cosine, -sine)
    acts = jnp.concatenate(
        [
            grad_query_act.reshape(rows, 192),
            grad_key_act.reshape(rows, HD),
            grad_kv[:, 128 : 128 + HD],
        ],
        axis=-1,
    ).astype(BF16)
    d_qkv = inner_rows(normed, acts).astype(BF16)
    qkv_w = wq.reshape(D, 4, 128)[..., :HD].reshape(D, 384)
    grad_normed = outer_cols(acts, qkv_w).astype(BF16)

    d_att = jnp.concatenate([d_qkv.reshape(4, 4, 96, 384), d_out.reshape(4, 4, 48, 384)], axis=2)
    result, token_grad, gains, g_att, g_gu, g_dn = final_exchange(
        grad_normed.reshape(2, 4, OWN, D),
        mlp_part,
        tokens,
        gain_attn[None],
        back,
        middle,
        gain_two,
        d_att,
        d_gu.reshape(4, 384, 4, 256).transpose(2, 0, 1, 3),
        d_dn.reshape(4, 4, 32, D),
    )

    def from_quad(g):
        return g.reshape(4, 96, 4, 32).transpose(1, 2, 0, 3).reshape(96, 512)

    return (
        result,
        token_grad,
        gains[0],
        gains[1],
        g_att[:96, :192],
        g_att[:96, 192:288],
        g_att[:96, 288:],
        g_att[96:].reshape(12, D),
        from_quad(g_gu[..., :128]),
        from_quad(g_gu[..., 128:]),
        g_dn,
    )


def solution(mesh):
    placed = (
        P(("dp", "tensor"), None),
        P(),
        P(),
        P("dp", "tensor"),
        P("dp", "tensor"),
        P("dp", "tensor"),
        P(("tensor", "dp"), None),
        P("dp", "tensor"),
        P("dp", "tensor"),
        P(("tensor", "dp"), None),
        P("dp"),
        P("dp"),
        P(("dp", "tensor"), None),
    )
    return jax.shard_map(
        shards,
        mesh=mesh,
        in_specs=placed,
        out_specs=(
            P(("dp", "tensor"), None),
            P(("dp", "tensor"), None),
            P(),
            P(),
            P("dp", "tensor"),
            P("dp", "tensor"),
            P("dp", "tensor"),
            P(("tensor", "dp"), None),
            P("dp", "tensor"),
            P("dp", "tensor"),
            P(("tensor", "dp"), None),
        ),
        check_vma=False,
    )
```

```python
import functools
import math

import jax
import jax.numpy as jnp
from jax import lax
from jax.experimental import pallas as pl
from jax.experimental.pallas import tpu as pltpu
from jax.sharding import PartitionSpec as P

HD = 96
SEQ = 512
D = 1536
OWN = 192
HALF = 768
WIN = 256

EPSILON = 1e-05
ROPE_BASE = 100000.0
MASKED = -1e30
MESH = pl.DeviceIdType.MESH
ANY = pl.BlockSpec(memory_space=pl.ANY)
VMEM = pl.BlockSpec(memory_space=pltpu.VMEM)
BF16 = jnp.bfloat16
F32 = jnp.float32


def place():
    dp = lax.axis_index("dp")
    tensor = lax.axis_index("tensor")
    return (tensor // 4) * 2 + (dp // 2) % 2, tensor % 4, dp // 4, dp % 2


def device(x, y, z, c):
    return (z * 4 + (x % 2) * 2 + c, (x // 2) * 4 + y)


def turn(pos, by):
    return (pos + by + 4) % 4


class Spot:
    def __init__(self):
        x, y, z, c = place()
        self.x, self.y, self.z, self.c = x, y, z, c
        self.high, self.low = x // 2, x % 2
        self.quad = self.low * 2 + c
        self.sibling = device(x, y, z, 1 - c)
        self.partner = device(turn(x, 2), y, z, 1 - c)

    def along(self, axis, by):
        x, y, z, c = self.x, self.y, self.z, self.c
        if axis == "x":
            return device(turn(x, by), y, z, c)
        if axis == "y":
            return device(x, turn(y, by), z, c)
        return device(x, y, turn(z, by), c)

    def me(self, axis):
        return {"x": self.x, "y": self.y, "z": self.z}[axis]

    def in_quad(self, by):
        other = turn(self.quad, by)
        return other, device(self.high * 2 + other // 2, self.y, self.z, other % 2)


def greet(devices):
    barrier = pltpu.get_barrier_semaphore()
    for who in devices:
        pl.semaphore_signal(barrier, inc=1, device_id=who, device_id_type=MESH)
    pl.semaphore_wait(barrier, len(devices))


class Wires:
    def __init__(self, send_sem, recv_sem):
        self.send_sem, self.recv_sem = send_sem, recv_sem
        self.count = 0
        self.sent = []
        self.moved = []

    def send(self, src, dst, who):
        copy = pltpu.make_async_remote_copy(
            src_ref=src,
            dst_ref=dst,
            send_sem=self.send_sem.at[self.count],
            recv_sem=self.recv_sem.at[self.count],
            device_id=who,
            device_id_type=MESH,
        )
        self.count += 1
        copy.start()
        self.sent.append(copy)
        return copy

    def move(self, src, dst):
        copy = pltpu.make_async_copy(src, dst, self.send_sem.at[self.count])
        self.count += 1
        copy.start()
        return copy

    def done(self, copies):
        for copy in copies:
            if any(other is copy for other in self.sent):
                self.sent = [other for other in self.sent if other is not copy]
                copy.wait_send()

    def close(self):
        self.done(list(self.sent))


def add_into(dst, *srcs, chunk=16):
    rows = dst.shape[-2]
    chunk = min(chunk, rows)

    def step(i, carry):
        span = pl.ds(pl.multiple_of(i * chunk, chunk), chunk)
        total = srcs[0][..., span, :].astype(F32)
        for src in srcs[1:]:
            total = total + src[..., span, :].astype(F32)
        dst[..., span, :] = total.astype(dst.dtype)
        return carry

    lax.fori_loop(0, rows // chunk, step, 0)


class RingGather:
    def __init__(self, wires, spot, axis, at):
        self.wires, self.at = wires, at
        self.me = spot.me(axis)
        self.next, self.prev = spot.along(axis, 1), spot.along(axis, -1)

    def start(self, own=None):
        own = own or (lambda half: self.at(self.me, half))
        send, at, me = self.wires.send, self.at, self.me
        self.right0 = send(own(0), at(me, 0), self.next)
        self.left1 = send(own(1), at(me, 1), self.prev)
        self.right1 = send(own(1), at(me, 1), self.next)
        self.left0 = send(own(0), at(me, 0), self.prev)

    def forward(self):
        send, at, me = self.wires.send, self.at, self.me
        self.right0.wait_recv()
        before = at(turn(me, -1), 0)
        self.pass0 = send(before, before, self.next)
        self.left1.wait_recv()
        after = at(turn(me, 1), 1)
        self.pass1 = send(after, after, self.prev)

    def near(self):
        self.right1.wait_recv()
        self.left0.wait_recv()

    def far(self):
        self.pass0.wait_recv()
        self.pass1.wait_recv()

    def close(self):
        near = [self.right0, self.left1, self.right1, self.left0]
        self.wires.done(near + [self.pass0, self.pass1])


class PairGather:
    def __init__(self, wires, spot, axis, out, own, start, size):
        self.wires, self.spot, self.out, self.own = wires, spot, out, own
        self.rows = pl.ds(start, size)
        cut = size // 2

        def half_rows(half):
            return pl.ds(start + half * cut, cut)

        self.half_rows = half_rows
        self.ring = RingGather(
            wires, spot, axis, lambda pos, half: out.at[spot.c, pos, half_rows(half)]
        )
        self.me = spot.me(axis)

    def share(self, pos):
        block = self.out.at[self.spot.c, pos, self.rows]
        return self.wires.send(block, block, self.spot.sibling)

    def start(self):
        self.ring.start(lambda half: self.own.at[self.half_rows(half)])
        mine = self.own.at[self.rows]
        place_of = self.out.at[self.spot.c, self.me, self.rows]
        self.shared = [self.wires.send(mine, place_of, self.spot.sibling)]
        self.kept = self.wires.move(mine, place_of)

    def forward(self):
        self.ring.forward()
        self.ring.near()
        self.shared.append(self.share(turn(self.me, -1)))
        self.shared.append(self.share(turn(self.me, 1)))

    def far(self):
        self.ring.far()
        self.shared.append(self.share(turn(self.me, 2)))

    def finish(self):
        for copy in self.shared:
            copy.wait_recv()
        self.kept.wait()

    def close(self):
        self.ring.close()
        self.wires.done(self.shared)


class PairScatter:
    def __init__(self, wires, spot, axis, part, got, passed, near, start, size):
        self.wires, self.spot = wires, spot
        self.me = spot.me(axis)
        self.next, self.prev = spot.along(axis, 1), spot.along(axis, -1)
        self.part, self.got, self.passed, self.near = part, got, passed, near
        self.start_row, self.size, self.cut = start, size, size // 2
        self.shared = {}

    def rows(self, half=None):
        if half is None:
            return pl.ds(self.start_row, self.size)
        return pl.ds(self.start_row + half * self.cut, self.cut)

    def share(self, by):
        pos = turn(self.me, by)
        self.shared[by] = self.wires.send(
            self.part.at[1 - self.spot.c, pos, self.rows()],
            self.got.at[pos, self.rows()],
            self.spot.sibling,
        )

    def first(self):
        self.shared[2].wait_recv()
        pos = turn(self.me, 2)
        mine = self.got.at[pos, self.rows()]
        add_into(mine, self.part.at[self.spot.c, pos, self.rows()], mine)
        self.pass0 = self.wires.send(
            self.got.at[pos, self.rows(0)], self.passed.at[self.rows(0)], self.next
        )
        self.pass1 = self.wires.send(
            self.got.at[pos, self.rows(1)], self.passed.at[self.rows(1)], self.prev
        )

    def second(self):
        self.arriving = []
        after, before = turn(self.me, 1), turn(self.me, -1)
        for by, half, who, side in ((1, 1, self.next, 0), (-1, 0, self.prev, 1)):
            pos = turn(self.me, by)
            self.shared[by].wait_recv()
            mine = self.got.at[pos, self.rows(half)]
            add_into(mine, self.part.at[self.spot.c, pos, self.rows(half)], mine)
            self.arriving.append(self.wires.send(mine, self.near.at[side, self.rows(half)], who))
        for pos, half, who, side, arrived in (
            (after, 0, self.next, 0, self.pass0),
            (before, 1, self.prev, 1, self.pass1),
        ):
            arrived.wait_recv()
            mine = self.got.at[pos, self.rows(half)]
            add_into(
                mine,
                self.part.at[self.spot.c, pos, self.rows(half)],
                mine,
                self.passed.at[self.rows(half)],
            )
            self.arriving.append(self.wires.send(mine, self.near.at[side, self.rows(half)], who))

    def arrive(self):
        self.shared[0].wait_recv()
        for copy in self.arriving:
            copy.wait_recv()

    def close(self):
        self.wires.done(list(self.shared.values()) + [self.pass0, self.pass1] + self.arriving)

    def total(self, span):
        return (
            self.part[self.spot.c, self.me, span].astype(F32)
            + self.got[self.me, span].astype(F32)
            + self.near[0, span].astype(F32)
            + self.near[1, span].astype(F32)
        )


class LineScatter:
    def __init__(self, wires, spot, axis, at, passed, work, near):
        self.wires, self.at = wires, at
        self.me = spot.me(axis)
        self.next, self.prev = spot.along(axis, 1), spot.along(axis, -1)
        self.passed, self.work, self.near = passed, work, near

    def first(self):
        send, me = self.wires.send, self.me
        far, after, before = turn(me, 2), turn(me, 1), turn(me, -1)
        self.pass0 = send(self.at(far, 0), self.passed(0), self.next)
        self.pass1 = send(self.at(far, 1), self.passed(1), self.prev)
        self.arriving = [
            send(self.at(after, 1), self.near(0, 1), self.next),
            send(self.at(before, 0), self.near(1, 0), self.prev),
        ]

    def second(self):
        for by, half, who, side, arrived in (
            (1, 0, self.next, 0, self.pass0),
            (-1, 1, self.prev, 1, self.pass1),
        ):
            arrived.wait_recv()
            add_into(self.work(half), self.at(turn(self.me, by), half), self.passed(half))
            self.arriving.append(self.wires.send(self.work(half), self.near(side, half), who))

    def finish(self):
        for copy in self.arriving:
            copy.wait_recv()
        for half in (0, 1):
            mine = self.at(self.me, half)
            add_into(mine, mine, self.near(0, half), self.near(1, half))


def norm_scale(values):
    return lax.rsqrt(jnp.mean(values * values, axis=-1, keepdims=True) + EPSILON)


def norm_back(upstream, values, inverse, gain):
    scaled = upstream * gain
    inner = jnp.sum(scaled * values, axis=-1, keepdims=True)
    return scaled * inverse - values * inner * (inverse * inverse * inverse) / values.shape[-1]


def over_rows(start, size, step, chunk=16):
    def body(i, carry):
        step(pl.ds(pl.multiple_of(start + i * chunk, chunk), chunk))
        return carry

    lax.fori_loop(0, size // chunk, body, 0)


def fold(total, values):
    part = values[0:8]
    for first in range(8, values.shape[0], 8):
        part = part + values[first : first + 8]
    total[...] += part


SUBS = ((0, 96), (96, 96))


def dot(left, right, a, b):
    return lax.dot_general(left, right, (((a,), (b,)), ((), ())), preferred_element_type=F32)


def repeat(count, step):
    def body(i, carry):
        step(i)
        return carry

    lax.fori_loop(0, count, body, 0)


def whole(i, size):
    return pl.ds(pl.multiple_of(i * size, size), size)


def grid_of(rows, columns):
    return (
        lax.broadcasted_iota(jnp.int32, (rows, columns), 0),
        lax.broadcasted_iota(jnp.int32, (rows, columns), 1),
    )


def picks(rows, columns, chosen):
    return jnp.where(chosen(*grid_of(rows, columns)), 1.0, 0.0).astype(BF16)


def quad_order(unit):
    return (((unit >> 5) & 3) << 7) + ((unit >> 7) << 5) + (unit & 31)


def swap_halves(values):
    lane = lax.broadcasted_iota(jnp.int32, values.shape, 1)
    up = pltpu.roll(values, 80, 1)
    down = pltpu.roll(values, 48, 1)
    return jnp.where(lane < 48, up, down)


def around(spot, axes):
    return [spot.along(a, by) for a in axes for by in (1, -1)] + [spot.sibling]


def layer_kernel(
    tokens, gain_attn, gain_mlp, cot, w_query, w_key, w_value, w_out, w_gate, w_up, w_down, marks,
    normed_out, result_out, token_out, gains_out, att_out, out_out, gu_out, dn_out,
    normed, cots, second, part, got, passed, near, work, att_two, own_out, aq, ao, wq, wo,
    gu, gu_own, dn, d_gu, d_dn, own, grad_hidden, q, kv, prob, mix, cosine, sine,
    marks_two, gains, middle_all, back_all, total, grad_mix, grad_kv, far_kv,
    gu_in, dn_in, att_in, out_in, gain_c, gain_y, gain_x, gain_z,
    ready, send_sem, recv_sem,
):
    spot = Spot()
    wires = Wires(send_sem, recv_sem)
    x, y, z, c = spot.x, spot.y, spot.z, spot.c
    greet(
        around(spot, "xyz")
        + [spot.along(a, 2) for a in "xyz"]
        + [spot.partner]
        + [spot.in_quad(by)[1] for by in (1, 2, 3)]
    )

    def tell(which, devices):
        for who in devices:
            pl.semaphore_signal(ready.at[which], inc=1, device_id=who, device_id_type=MESH)

    def hear(which, count):
        pl.semaphore_wait(ready.at[which], count)

    def three(first):
        return lambda r, k: r + first == k

    columns = (
        dot(w_query[...], picks(192, 384, three(0)), 1, 0)
        + dot(w_key[...], picks(96, 384, three(192)), 1, 0)
        + dot(w_value[...], picks(96, 384, three(288)), 1, 0)
    )
    att_two[0] = columns.astype(BF16)
    own_out[0] = jnp.zeros((16, D), BF16)
    own_out[0, 0:12] = w_out[...]
    swaps = [
        wires.send(att_two.at[0], att_two.at[1], spot.partner),
        wires.send(own_out.at[0], own_out.at[1], spot.partner),
    ]
    dn_here = dn.at[whole(y * 4 + z, 32)]
    dn_kept = wires.move(w_down, dn_here)
    dn_side = [wires.send(w_down, dn_here, spot.along("z", by)) for by in (1, -1, 2)]
    marks_kept = wires.move(marks, marks_two.at[c])
    marks_got = wires.send(marks, marks_two.at[c], spot.sibling)
    for i, gain in enumerate((gain_attn, gain_mlp)):
        gains[i : i + 1, :] = jnp.concatenate([gain[j : j + 1, :] for j in range(12)], axis=1)

    def normalise(span):
        rows = tokens[span, :].astype(F32)
        own[span, :] = (rows * norm_scale(rows) * gains[0:1, :]).astype(BF16)

    over_rows(0, OWN, normalise)
    rows_y = [PairGather(wires, spot, "y", normed, own, s, n) for s, n in SUBS]
    for g in rows_y:
        g.start()

    order = picks(512, 512, lambda r, k: quad_order(r) == k)
    for shard, first in ((w_gate, 0), (w_up, 128)):
        moved = dot(shard[...], order, 1, 0).astype(BF16)
        for i in range(4):
            gu_own[i, :, first : first + 128] = moved[:, i * 128 : i * 128 + 128]
    gu_lanes = whole(y, 256)
    gu_here = gu.at[whole(z * 4 + spot.quad, 96), gu_lanes]
    gu_kept = wires.move(gu_own.at[spot.quad], gu_here)
    gu_swap = []
    for by in (1, 2, 3):
        other, who = spot.in_quad(by)
        gu_swap.append(wires.send(gu_own.at[other], gu_here, who))

    for copy in swaps:
        copy.wait_recv()
    slot = spot.low * 2 + spot.high
    pick = jnp.where(spot.high == c, 0, 1)
    aq_here, ao_here = aq.at[z, slot], ao.at[z, slot]
    att_kept = [wires.move(att_two.at[pick], aq_here), wires.move(own_out.at[pick], ao_here)]
    att_side = []
    for by in (1, -1, 2):
        who = spot.along("z", by)
        att_side.append(wires.send(att_two.at[pick], aq_here, who))
        att_side.append(wires.send(own_out.at[pick], ao_here, who))

    def trig(core):
        def step(i):
            span = whole(i, 128)
            row, lane = grid_of(128, 128)
            number = marks_two[core, pl.ds(spot.high * 6 + i, 1), :]
            ones = jnp.ones((128, 128), BF16)
            where = jnp.zeros((128, 128), F32)
            for digit, factor in ((number >> 5, 32.0), (number & 31, 1.0)):
                spread = jnp.where(row == lane, digit.astype(F32), 0.0).astype(BF16)
                where = where + factor * dot(spread, ones, 1, 0)
            grad_kv[core, span, 0:128] = where
            turns = jnp.where(lane < 48, lane, lane - 48).astype(F32) * (2.0 / HD)
            angle = where * jnp.exp(-math.log(ROPE_BASE) * turns)
            inside = lane < HD
            cosine[core, span, :] = jnp.where(inside, jnp.cos(angle), 0.0)
            wave = jnp.sin(angle)
            sine[core, span, :] = jnp.where(inside, jnp.where(lane < 48, -wave, wave), 0.0)

        repeat(6, step)

    marks_kept.wait()
    trig(c)
    for copy in att_kept:
        copy.wait()
    for copy in att_side:
        copy.wait_recv()

    def slot_of(pos):
        return (pos % 2) * 2 + pos // 2

    att_line = [
        RingGather(wires, spot, "x", lambda pos, h: aq.at[pl.ds(2 * h, 2), slot_of(pos)]),
        RingGather(wires, spot, "x", lambda pos, h: ao.at[pl.ds(2 * h, 2), slot_of(pos)]),
    ]
    for line in att_line:
        line.start()
    for g in rows_y:
        g.forward()
    marks_got.wait_recv()
    trig(1 - c)
    for line in att_line:
        line.forward()
    cot_x = [PairGather(wires, spot, "x", cots, cot, s, n) for s, n in SUBS]
    for g in cot_x:
        g.start()
    gu_kept.wait()
    for copy in gu_swap:
        copy.wait_recv()
    gu_block = gu.at[whole(z, 384), gu_lanes]
    gu_side = [wires.send(gu_block, gu_block, spot.along("y", by)) for by in (1, -1, 2)]
    dn_kept.wait()
    for copy in dn_side:
        copy.wait_recv()
    dn_line = RingGather(wires, spot, "y", lambda pos, h: dn.at[whole(pos * 2 + h, 64)])
    dn_line.start()
    for g in rows_y:
        g.far()
    for line in att_line:
        line.near()
        line.far()

    widen = picks(384, 512, lambda r, k: r + ((r * 683) >> 16) * 32 == k)

    def widen_rows(i):
        wq[i // 4, i % 4] = dot(aq[i // 4, i % 4], widen, 1, 0).astype(BF16)

    repeat(16, widen_rows)

    def out_row(r, k):
        unit = jnp.where(r < 128, r, r - 32)
        real = (r < 96) | ((r >= 128) & (r < 224))
        return real & (unit + ((unit * 5462) >> 16) * 4 == k)

    out_rows = picks(256, 256, out_row)
    wo[...] = dot(out_rows, ao[...].reshape(256, D), 1, 0).astype(BF16).reshape(4, 4, 16, D)

    for g in rows_y:
        g.finish()
    normed_kept = wires.move(normed, normed_out)

    def project(i):
        core, pos = i // 4, i % 4
        both = dot(normed[core, pos], wq[...].reshape(D, 512), 1, 0)
        span = whole(pos, OWN)
        cos, sin = cosine[core, span, :], sine[core, span, :]

        def turned(first):
            values = both[:, first : first + 128]
            return (values * cos + swap_halves(values) * sin).astype(BF16)

        q[core, span, 0:128] = turned(0)
        q[core, span, 128:256] = turned(128)
        after = pl.ds(pl.multiple_of(WIN + pos * OWN, 64), OWN)
        kv[core, after, 0:128] = turned(256)
        kv[core, after, 128:256] = both[:, 384:512].astype(BF16)

    repeat(8, project)
    kv_got = wires.send(kv.at[:, pl.ds(768, WIN)], kv.at[:, pl.ds(0, WIN)], spot.along("x", 2))

    for copy in gu_side:
        copy.wait_recv()
    gu_line = RingGather(
        wires, spot, "z", lambda pos, h: gu.at[whole(pos, 384), pl.ds(h * 512, 512)]
    )
    gu_line.start()

    scale = HD ** (-0.5)

    def attend(core, run, head):
        span = whole(run, WIN)
        lanes = whole(head, 128)
        window = pl.ds(pl.multiple_of(run * WIN, WIN), SEQ)
        scores = dot(q[core, span, lanes], kv[core, window, 0:128], 1, 1) * scale
        row, column = grid_of(WIN, SEQ)
        spot_of = spot.high * HALF + run * WIN + row[:, 0:1]
        begin = jnp.maximum((spot_of >> 9) << 9, spot_of - grad_kv[core, span, 0:1].astype(jnp.int32))
        begin = begin - (spot.high * HALF + run * WIN) + WIN
        allowed = (column >= begin) & (column <= row + WIN)
        scores = jnp.where(allowed, scores, MASKED)
        weights = jnp.exp(scores - jnp.max(scores, axis=-1, keepdims=True))
        share = weights / jnp.sum(weights, axis=-1, keepdims=True)
        low = share.astype(BF16)
        prob[core, run, head] = low
        values = dot(low, kv[core, window, 128:256], 1, 0)
        mix[core, span, lanes] = values.astype(BF16)

    repeat(8, lambda i: attend(i // 4, 1 + (i // 2) % 2, i % 2))
    for g in cot_x:
        g.forward()
    dn_line.forward()
    kv_got.wait_recv()
    repeat(4, lambda i: attend(i // 2, 0, i % 2))

    def project_out(core):
        def step(pos):
            rows = mix[core, whole(pos, OWN), :]
            part[core, pos] = dot(rows, wo[...].reshape(256, D), 1, 0).astype(BF16)

        repeat(4, step)

    sums_y = [PairScatter(wires, spot, "y", part, got, passed, near, s, n) for s, n in SUBS]
    project_out(1 - c)
    for by in (2, 1, -1, 0):
        for s in sums_y:
            s.share(by)
    project_out(c)
    for g in rows_y:
        g.close()
    normed_kept.wait()
    for s in sums_y:
        s.first()
    gu_line.forward()
    for g in cot_x:
        g.far()
    for s in sums_y:
        s.second()
    dn_line.near()
    dn_line.far()
    for g in cot_x:
        g.finish()

    def back_hidden(i):
        rows = cots[i // 2, pl.ds((i % 2) * 2, 2)].reshape(384, D)
        back = dot(rows, dn[...], 1, 1).astype(BF16)
        grad_hidden[i // 2, pl.ds((i % 2) * 2, 2)] = back.reshape(2, OWN, 512)

    repeat(4, back_hidden)
    rows_x = [PairGather(wires, spot, "x", second, own, s, n) for s, n in SUBS]

    def middle_rows(s):
        def use(span):
            middle = tokens[span, :].astype(F32) + s.total(span)
            middle_all[span, :] = middle
            own[span, :] = (middle * norm_scale(middle) * gains[1:2, :]).astype(BF16)

        return use

    for s, g in zip(sums_y, rows_x):
        s.arrive()
        over_rows(s.start_row, s.size, middle_rows(s))
        s.close()
        g.start()
        g.forward()
    gu_line.near()
    gu_line.far()
    rows_x[0].far()
    rows_x[0].finish()

    def feed(core, s):
        span = s.rows()
        size = 4 * s.size

        rows = second[core, :, span].reshape(size, D)
        both = dot(rows, gu[...], 1, 0)
        upstream = grad_hidden[core, :, span].reshape(size, 512).astype(F32)
        for i in range(4):
            gate = both[:, i * 256 : i * 256 + 128]
            upward = both[:, i * 256 + 128 : i * 256 + 256]
            sent = upstream[:, i * 128 : i * 128 + 128]
            sigmoid = jax.nn.sigmoid(gate)
            silu = gate * sigmoid
            slope = sigmoid * (1.0 + gate * (1.0 - sigmoid))
            low = (silu * upward).astype(BF16)
            work[core, :, span, 1024 + i * 128 : 1152 + i * 128] = low.reshape(4, s.size, 128)
            low = (sent * upward * slope).astype(BF16)
            work[core, :, span, i * 256 : i * 256 + 128] = low.reshape(4, s.size, 128)
            low = (sent * silu).astype(BF16)
            work[core, :, span, i * 256 + 128 : i * 256 + 256] = low.reshape(4, s.size, 128)
        back = dot(work[core, :, span, 0:1024].reshape(size, 1024), gu[...], 1, 1)
        part[core, :, span] = back.astype(BF16).reshape(4, s.size, D)

    early = list(wires.sent)
    sums_x = [PairScatter(wires, spot, "x", part, got, passed, near, s, n) for s, n in SUBS]
    feed(1 - c, sums_x[0])
    for by in (2, 1, -1, 0):
        sums_x[0].share(by)
    rows_x[1].far()
    feed(c, sums_x[0])
    sums_x[0].first()
    rows_x[1].finish()
    feed(1 - c, sums_x[1])
    for by in (2, 1, -1, 0):
        sums_x[1].share(by)
    sums_x[0].second()
    feed(c, sums_x[1])
    sums_x[1].first()

    def grad_gate_up(i):
        lanes = whole(i, 256)
        rows = second[:, :, :, lanes].reshape(8 * OWN, 256)
        d_gu[lanes, :] = dot(rows, work[:, :, :, 0:1024].reshape(8 * OWN, 1024), 0, 0).astype(BF16)

    def grad_down(i):
        lanes = pl.ds(pl.multiple_of(1024 + i * 256, 256), 256)
        rows = work[:, :, :, lanes].reshape(8 * OWN, 256)
        d_dn[whole(i, 256), :] = dot(rows, cots[...].reshape(8 * OWN, D), 0, 0).astype(BF16)

    def down(i):
        rows = work[i // 2, pl.ds((i % 2) * 2, 2), :, 1024:D].reshape(384, 512)
        second[i // 2, pl.ds((i % 2) * 2, 2)] = (
            dot(rows, dn[...], 1, 0).astype(BF16).reshape(2, OWN, D)
        )

    total[...] = jnp.zeros_like(total)
    grads_y = [PairGather(wires, spot, "y", normed, own, s, n) for s, n in SUBS]

    def back_rows(s):
        def use(span):
            grad = s.total(span)
            rows = middle_all[span, :]
            inverse = norm_scale(rows)
            back = cot[span, :].astype(F32) + norm_back(grad, rows, inverse, gains[1:2, :])
            back_all[span, :] = back
            own[span, :] = back.astype(BF16)
            fold(total, grad * rows * inverse)

        return use

    wires.done(early)
    for g in rows_x:
        g.close()
    tell(0, [spot.along("z", 1), spot.along("z", -1)])
    repeat(2, grad_gate_up)
    sums_x[1].second()
    sums_x[0].arrive()
    over_rows(sums_x[0].start_row, sums_x[0].size, back_rows(sums_x[0]))
    sums_x[0].close()
    grads_y[0].start()
    repeat(2, lambda i: grad_gate_up(2 + i))
    grads_y[0].forward()
    sums_x[1].arrive()
    over_rows(sums_x[1].start_row, sums_x[1].size, back_rows(sums_x[1]))
    sums_x[1].close()
    grads_y[1].start()
    repeat(2, lambda i: grad_gate_up(4 + i))
    hear(0, 2)
    gu_sum = LineScatter(
        wires, spot, "z",
        lambda pos, h: d_gu.at[whole(pos * 2 + h, 192)],
        lambda h: gu.at[pl.ds(h * 192, 192)],
        lambda h: gu.at[pl.ds(384 + h * 192, 192)],
        lambda side, h: gu.at[pl.ds(768 + side * 384 + h * 192, 192)],
    )
    gu_sum.first()
    grads_y[1].forward()
    grads_y[0].far()
    repeat(2, grad_down)
    grads_y[1].far()
    repeat(4, down)
    tell(1, around(spot, "xy"))
    gain_c[c, 1:2] = jnp.sum(total[...], axis=0, keepdims=True)
    total[...] = jnp.zeros_like(total)
    again = wires.move(normed_out, cots)
    for g in grads_y:
        g.finish()

    def mix_back(i):
        span = whole(i % 4, OWN)
        rows = dot(normed[i // 4, i % 4], wo[...].reshape(256, D), 1, 1)
        grad_mix[i // 4, span, :] = rows.astype(BF16)

    repeat(8, mix_back)
    hear(1, 5)
    sums_m = [
        PairScatter(
            wires, spot, "x", second, work.at[0], work.at[1, 0], work.at[1, pl.ds(1, 2)], s, n
        )
        for s, n in SUBS
    ]
    for by in (2, 1, -1, 0):
        for s in sums_m:
            s.share(by)
    dn_sum = LineScatter(
        wires, spot, "y",
        lambda pos, h: d_dn.at[whole(pos * 2 + h, 64)],
        lambda h: dn.at[pl.ds(h * 64, 64)],
        lambda h: dn.at[pl.ds(128 + h * 64, 64)],
        lambda side, h: dn.at[pl.ds(256 + side * 128 + h * 64, 64)],
    )
    dn_sum.first()
    grad_kv[...] = jnp.zeros_like(grad_kv)

    def attend_back(core, run, head):
        span = whole(run, WIN)
        lanes = whole(head, 128)
        window = pl.ds(pl.multiple_of(run * WIN, WIN), SEQ)
        low = prob[core, run, head]
        share = low.astype(F32)
        mixed = grad_mix[core, span, lanes]
        asked = q[core, span, lanes]
        grad = dot(mixed, kv[core, window, 128:256], 1, 1)
        inner = jnp.sum(share * grad, axis=-1, keepdims=True)
        scored = (share * (grad - inner)).astype(BF16)
        grad_kv[core, window, 0:128] += dot(scored, asked, 0, 0) * scale
        grad_kv[core, window, 128:256] += dot(low, mixed, 0, 0)
        grad_q = dot(scored, kv[core, window, 0:128], 1, 0) * scale
        cos, sin = cosine[core, span, :], sine[core, span, :]
        q[core, span, lanes] = (grad_q * cos - swap_halves(grad_q) * sin).astype(BF16)

    repeat(4, lambda i: attend_back(i // 2, 0, i % 2))
    own_far = att_far = grad_mix.at[:, pl.ds(0, WIN)]
    for core in (0, 1):
        own_far[core] = grad_kv[core, 0:WIN, :].astype(BF16)
    far_got = wires.send(att_far, far_kv, spot.along("x", 2))
    repeat(4, lambda i: attend_back(i // 2, 1, i % 2))
    for s in sums_m:
        s.first()
    gu_sum.second()
    dn_sum.second()
    repeat(4, lambda i: attend_back(i // 2, 2, i % 2))
    for s in sums_m:
        s.second()
    far_got.wait_recv()
    for core in (0, 1):
        grad_kv[core, 768:1024, :] += far_kv[core].astype(F32)

    def turn_back(i):
        core, pos = i // 4, i % 4
        after = pl.ds(pl.multiple_of(WIN + pos * OWN, 64), OWN)
        span = whole(pos, OWN)
        grad = grad_kv[core, after, 0:128]
        cos, sin = cosine[core, span, :], sine[core, span, :]
        kv[core, after, 0:128] = (grad * cos - swap_halves(grad) * sin).astype(BF16)
        kv[core, after, 128:256] = grad_kv[core, after, 128:256].astype(BF16)

    repeat(8, turn_back)


    def normed_back(core):
        def step(pos):
            span = whole(pos, OWN)
            after = pl.ds(pl.multiple_of(WIN + pos * OWN, 64), OWN)
            rows = jnp.concatenate([q[core, span, :], kv[core, after, :]], axis=1)
            part[core, pos] = dot(rows, wq[...].reshape(D, 512), 1, 1).astype(BF16)

        repeat(4, step)

    sums_n = [PairScatter(wires, spot, "y", part, got, passed, near, s, n) for s, n in SUBS]
    normed_back(1 - c)
    for by in (2, 1, -1, 0):
        for s in sums_n:
            s.share(by)
    normed_back(c)
    for s in sums_n:
        s.first()

    def out_rows_back(r, k):
        unit = jnp.where(k < 128, k, k - 32)
        real = (k < 96) | ((k >= 128) & (k < 224))
        return real & (unit + ((unit * 5462) >> 16) * 4 == r)

    grad_out = dot(mix[...].reshape(8 * OWN, 256), normed[...].reshape(8 * OWN, D), 0, 0)
    grad_out = dot(picks(256, 256, out_rows_back), grad_out.astype(BF16), 1, 0)
    wo[...] = grad_out.astype(BF16).reshape(4, 4, 16, D)
    again.wait()
    narrow = picks(512, 384, lambda r, k: k + ((k * 683) >> 16) * 32 == r)

    def grad_columns(i):
        rows = cots[:, :, :, whole(i, 384)].reshape(8 * OWN, 384)
        grad = dot(rows, q[...].reshape(8 * OWN, 256), 0, 0).astype(BF16)
        grad = dot(grad, narrow[0:256], 1, 0)
        keyed = kv[:, pl.ds(WIN, HALF), :].reshape(8 * OWN, 256)
        other = dot(rows, keyed, 0, 0).astype(BF16)
        grad = (grad + dot(other, narrow[256:512], 1, 0)).astype(BF16)
        wq[i, :, :, 0:384] = grad.reshape(4, 96, 384)

    repeat(4, grad_columns)
    att_sum = [
        LineScatter(
            wires, spot, "x",
            lambda pos, h: wq.at[pl.ds(2 * h, 2), slot_of(pos), :, pl.ds(0, 384)],
            lambda h: aq.at[0, pl.ds(2 * h, 2)],
            lambda h: aq.at[1, pl.ds(2 * h, 2)],
            lambda side, h: aq.at[2 + side, pl.ds(2 * h, 2)],
        ),
        LineScatter(
            wires, spot, "x",
            lambda pos, h: wo.at[pl.ds(2 * h, 2), slot_of(pos)],
            lambda h: ao.at[0, pl.ds(2 * h, 2)],
            lambda h: ao.at[1, pl.ds(2 * h, 2)],
            lambda side, h: ao.at[2 + side, pl.ds(2 * h, 2)],
        ),
    ]
    for line in att_sum:
        line.first()
    for s in sums_n:
        s.second()

    gu_sum.finish()
    gu_got = [
        wires.send(d_gu.at[whole(z, 384), whole(turn(y, by), 256)], gu_in.at[y], spot.along("y", by))
        for by in (1, -1, 2)
    ]
    dn_sum.finish()
    dn_got = [
        wires.send(d_dn.at[whole(y * 4 + turn(z, by), 32)], dn_in.at[z], spot.along("z", by))
        for by in (1, -1, 2)
    ]

    def result_rows(s):
        def use(span):
            second[c, x, span] = (middle_all[span, :] + s.total(span)).astype(BF16)

        return use

    for s in sums_m:
        s.arrive()
        over_rows(s.start_row, s.size, result_rows(s))
    result_kept = wires.move(second.at[c, x], result_out)
    for line in att_sum:
        line.second()

    def token_rows(s):
        def use(span):
            grad = s.total(span)
            rows = tokens[span, :].astype(F32)
            inverse = norm_scale(rows)
            out = back_all[span, :] + norm_back(grad, rows, inverse, gains[0:1, :])
            part[c, y, span] = out.astype(BF16)
            fold(total, grad * rows * inverse)

        return use

    for s in sums_n:
        s.arrive()
        over_rows(s.start_row, s.size, token_rows(s))
    token_kept = wires.move(part.at[c, y], token_out)
    gain_c[c, 0:1] = jnp.sum(total[...], axis=0, keepdims=True)
    gain_got = [wires.send(gain_c.at[c], gain_c.at[c], spot.sibling)]

    for copy in gu_got:
        copy.wait_recv()
    mine = d_gu.at[whole(z, 384), whole(y, 256)]
    add_into(mine, mine, *[gu_in.at[turn(y, by)] for by in (1, -1, 2)])
    gu_done = []
    for by in (1, 2, 3):
        other, who = spot.in_quad(by)
        gu_done.append(
            wires.send(
                d_gu.at[whole(z * 4 + other, 96), whole(y, 256)], gu_own.at[spot.quad], who
            )
        )
    for line in att_sum:
        line.finish()
    slot_me = slot_of(x)
    att_got = []
    for by in (1, -1, 2):
        far = turn(z, by)
        who = spot.along("z", by)
        att_got.append(
            wires.send(wq.at[far, slot_me, :, pl.ds(0, 384)], att_in.at[z], who)
        )
        att_got.append(wires.send(wo.at[far, slot_me], out_in.at[z], who))

    held = gain_c
    for axis, into in (("y", gain_y), ("x", gain_x), ("z", gain_z), (None, None)):
        for copy in gain_got:
            copy.wait_recv()
        summed = held[0]
        for i in range(1, held.shape[0]):
            summed = summed + held[i]
        if into is None:
            gains_out[...] = summed
            break
        me = spot.me(axis)
        into[me] = summed
        gain_got = [
            wires.send(into.at[me], into.at[me], spot.along(axis, by)) for by in (1, -1, 2)
        ]
        held = into
        if axis == "y":
            for copy in dn_got:
                copy.wait_recv()
            add_into(
                dn_out,
                d_dn.at[whole(y * 4 + z, 32)],
                *[dn_in.at[turn(z, by)] for by in (1, -1, 2)],
            )
        if axis == "x":
            for copy in att_got:
                copy.wait_recv()
            others = [turn(z, by) for by in (1, -1, 2)]
            add_into(
                att_two.at[0],
                wq.at[z, slot_me, :, pl.ds(0, 384)],
                *[att_in.at[far] for far in others],
            )
            add_into(own_out.at[0], wo.at[z, slot_me], *[out_in.at[far] for far in others])
            swaps = [
                wires.send(att_two.at[0], att_two.at[1], spot.partner),
                wires.send(own_out.at[0], own_out.at[1], spot.partner),
            ]
    kept_rows = d_gu.at[whole(z * 4 + spot.quad, 96), whole(y, 256)]
    gu_out[spot.quad] = kept_rows[...]
    for copy in gu_done:
        copy.wait_recv()
    for by in (1, 2, 3):
        other = turn(spot.quad, by)
        gu_out[other] = gu_own[other]
    for copy in swaps:
        copy.wait_recv()
    att_out[...] = att_two[pick]
    out_out[...] = own_out[pick]
    result_kept.wait()
    token_kept.wait()
    wires.close()


def finish_kernel(
    result, token, gains, att, out, gu, dn,
    result_out, token_out, attn_out, mlp_out, query_out, key_out, value_out, out_out,
    gate_out, up_out, dn_out,
):
    result_out[...] = result[...]
    token_out[...] = token[...]
    for i, into in enumerate((attn_out, mlp_out)):
        for j in range(12):
            into[j : j + 1, :] = gains[i : i + 1, j * 128 : j * 128 + 128]
    rows = att[...]

    def three(first):
        return lambda r, k: r == k + first

    query_out[...] = dot(rows, picks(384, 192, three(0)), 1, 0)
    key_out[...] = dot(rows, picks(384, 96, three(192)), 1, 0)
    value_out[...] = dot(rows, picks(384, 96, three(288)), 1, 0)
    out_out[...] = out[0:12, :].astype(F32)
    order = picks(512, 512, lambda r, k: quad_order(k) == r)
    for first, into in ((0, gate_out), (128, up_out)):
        moved = jnp.concatenate([gu[i, :, first : first + 128] for i in range(4)], axis=1)
        into[...] = dot(moved, order, 1, 0)
    dn_out[...] = dn[...]


def layer_call(
    tokens, gain_attn, gain_mlp, cot, w_query, w_key, w_value, w_out, w_gate, w_up, w_down, marks
):
    sems = 288
    shape = jax.ShapeDtypeStruct
    outs = (
        (shape((2, 4, OWN, D), BF16), ANY),
        (shape((OWN, D), BF16), ANY),
        (shape((OWN, D), BF16), ANY),
        (shape((2, D), F32), VMEM),
        (shape((96, 384), BF16), VMEM),
        (shape((16, D), BF16), VMEM),
        (shape((4, 96, 256), BF16), VMEM),
        (shape((32, D), F32), VMEM),
    )
    scratch = [
        ((2, 4, OWN, D), BF16),
        ((2, 4, OWN, D), BF16),
        ((2, 4, OWN, D), BF16),
        ((2, 4, OWN, D), BF16),
        ((4, OWN, D), BF16),
        ((OWN, D), BF16),
        ((2, OWN, D), BF16),
        ((2, 4, OWN, D), BF16),
        ((2, 96, 384), BF16),
        ((2, 16, D), BF16),
        ((4, 4, 96, 384), BF16),
        ((4, 4, 16, D), BF16),
        ((4, 4, 96, 512), BF16),
        ((4, 4, 16, D), BF16),
        ((D, 1024), BF16),
        ((4, 96, 256), BF16),
        ((512, D), BF16),
        ((D, 1024), BF16),
        ((512, D), BF16),
        ((OWN, D), BF16),
        ((2, 4, OWN, 512), BF16),
        ((2, HALF, 256), BF16),
        ((2, HALF + WIN, 256), BF16),
        ((2, 3, 2, WIN, SEQ), BF16),
        ((2, HALF, 256), BF16),
        ((2, HALF, 128), F32),
        ((2, HALF, 128), F32),
        ((2, 12, 128), jnp.int32),
        ((2, D), F32),
        ((OWN, D), F32),
        ((OWN, D), F32),
        ((8, D), F32),
        ((2, HALF, 256), BF16),
        ((2, HALF + WIN, 256), F32),
        ((2, WIN, 256), BF16),
        ((4, 384, 256), BF16),
        ((4, 32, D), BF16),
        ((4, 96, 384), BF16),
        ((4, 16, D), BF16),
        ((2, 2, D), F32),
        ((4, 2, D), F32),
        ((4, 2, D), F32),
        ((4, 2, D), F32),
    ]
    outs_raw = pl.pallas_call(
        layer_kernel,
        out_shape=tuple(o[0] for o in outs),
        in_specs=[VMEM] * 12,
        out_specs=[o[1] for o in outs],
        scratch_shapes=[pltpu.VMEM(*s) for s in scratch]
        + [
            pltpu.SemaphoreType.REGULAR((2,)),
            pltpu.SemaphoreType.DMA((sems,)),
            pltpu.SemaphoreType.DMA((sems,)),
        ],
        compiler_params=pltpu.CompilerParams(
            collective_id=1, has_side_effects=True, vmem_limit_bytes=64 << 20
        ),
        name="layer",
    )(tokens, gain_attn, gain_mlp, cot, w_query, w_key, w_value, w_out, w_gate, w_up, w_down, marks)
    finals = (
        shape((OWN, D), BF16),
        shape((OWN, D), BF16),
        shape((12, 128), F32),
        shape((12, 128), F32),
        shape((96, 192), F32),
        shape((96, 96), F32),
        shape((96, 96), F32),
        shape((12, D), F32),
        shape((96, 512), F32),
        shape((96, 512), F32),
        shape((32, D), F32),
    )
    return pl.pallas_call(
        finish_kernel,
        out_shape=finals,
        in_specs=[VMEM] * 7,
        out_specs=[VMEM] * 11,
        name="finish",
    )(*outs_raw[1:])


def shards(
    tokens,
    gain_attn,
    gain_mlp,
    w_query,
    w_key,
    w_value,
    w_out,
    w_gate,
    w_up,
    w_down,
    segments,
    positions,
    cotangent,
):
    del segments
    done = layer_call(
        tokens,
        gain_attn.reshape(12, 128),
        gain_mlp.reshape(12, 128),
        cotangent,
        w_query,
        w_key,
        w_value,
        w_out,
        w_gate,
        w_up,
        w_down,
        positions.reshape(12, 128),
    )
    return (*done[:2], done[2].reshape(D), done[3].reshape(D), *done[4:])


def solution(mesh):
    placed = (
        P(("dp", "tensor"), None),
        P(),
        P(),
        P("dp", "tensor"),
        P("dp", "tensor"),
        P("dp", "tensor"),
        P(("tensor", "dp"), None),
        P("dp", "tensor"),
        P("dp", "tensor"),
        P(("tensor", "dp"), None),
        P("dp"),
        P("dp"),
        P(("dp", "tensor"), None),
    )
    return jax.shard_map(
        shards,
        mesh=mesh,
        in_specs=placed,
        out_specs=(
            P(("dp", "tensor"), None),
            P(("dp", "tensor"), None),
            P(),
            P(),
            P("dp", "tensor"),
            P("dp", "tensor"),
            P("dp", "tensor"),
            P(("tensor", "dp"), None),
            P("dp", "tensor"),
            P("dp", "tensor"),
            P(("tensor", "dp"), None),
        ),
        check_vma=False,
    )
```

```python
import functools
import math

import jax
import jax.numpy as jnp
from jax import lax
from jax.experimental import pallas as pl
from jax.experimental.pallas import tpu as pltpu
from jax.sharding import PartitionSpec as P

HD = 96
SEQ = 512
D = 1536
OWN = 192
HALF = 768
WIN = 256

EPSILON = 1e-05
ROPE_BASE = 100000.0
MASKED = -1e30
MESH = pl.DeviceIdType.MESH
ANY = pl.BlockSpec(memory_space=pl.ANY)
VMEM = pl.BlockSpec(memory_space=pltpu.VMEM)
BF16 = jnp.bfloat16
F32 = jnp.float32


def place():
    dp = lax.axis_index("dp")
    tensor = lax.axis_index("tensor")
    return (tensor // 4) * 2 + (dp // 2) % 2, tensor % 4, dp // 4, dp % 2


def device(x, y, z, c):
    return (z * 4 + (x % 2) * 2 + c, (x // 2) * 4 + y)


def turn(pos, by):
    return (pos + by + 4) % 4


class Spot:
    def __init__(self):
        x, y, z, c = place()
        self.x, self.y, self.z, self.c = x, y, z, c
        self.high, self.low = x // 2, x % 2
        self.quad = self.low * 2 + c
        self.sibling = device(x, y, z, 1 - c)
        self.partner = device(turn(x, 2), y, z, 1 - c)

    def along(self, axis, by):
        x, y, z, c = self.x, self.y, self.z, self.c
        if axis == "x":
            return device(turn(x, by), y, z, c)
        if axis == "y":
            return device(x, turn(y, by), z, c)
        return device(x, y, turn(z, by), c)

    def me(self, axis):
        return {"x": self.x, "y": self.y, "z": self.z}[axis]

    def in_quad(self, by):
        other = turn(self.quad, by)
        return other, device(self.high * 2 + other // 2, self.y, self.z, other % 2)


def greet(devices):
    for who in devices:
        pl.semaphore_signal(
            pltpu.get_barrier_semaphore(), inc=1, device_id=who, device_id_type=MESH
        )


def greeted(devices):
    pl.semaphore_wait(pltpu.get_barrier_semaphore(), len(devices))


class Wires:
    def __init__(self, send_sem, recv_sem):
        self.send_sem, self.recv_sem = send_sem, recv_sem
        self.free = list(range(send_sem.shape[0]))
        self.count = 0
        self.sent = []

    def again(self):
        self.count = 0

    def take(self):
        held = min(self.free)
        self.free.remove(held)
        return held

    def send(self, src, dst, who):
        held = self.take()
        assert self.count < self.recv_sem.shape[0]
        copy = pltpu.make_async_remote_copy(
            src_ref=src,
            dst_ref=dst,
            send_sem=self.send_sem.at[held],
            recv_sem=self.recv_sem.at[self.count],
            device_id=who,
            device_id_type=MESH,
        )
        self.count += 1
        copy.start()
        self.sent.append((copy, held))
        return copy

    def move(self, src, dst):
        held = self.take()
        copy = pltpu.make_async_copy(src, dst, self.send_sem.at[held])
        copy.start()
        return Moved(self, copy, held)

    def done(self, copies):
        kept = []
        for copy, held in self.sent:
            if any(copy is other for other in copies):
                copy.wait_send()
                self.free.append(held)
            else:
                kept.append((copy, held))
        self.sent = kept

    def started(self):
        return [copy for copy, _ in self.sent]

    def close(self):
        self.done(self.started())


class Moved:
    def __init__(self, wires, copy, held):
        self.wires, self.copy, self.held = wires, copy, held

    def wait(self):
        self.copy.wait()
        self.wires.free.append(self.held)


def add_into(dst, *srcs, chunk=16):
    rows = dst.shape[-2]
    chunk = min(chunk, rows)

    def step(i, carry):
        span = pl.ds(pl.multiple_of(i * chunk, chunk), chunk)
        total = srcs[0][..., span, :].astype(F32)
        for src in srcs[1:]:
            total = total + src[..., span, :].astype(F32)
        dst[..., span, :] = total.astype(dst.dtype)
        return carry

    lax.fori_loop(0, rows // chunk, step, 0)


class RingGather:
    def __init__(self, wires, spot, axis, at):
        self.wires, self.at = wires, at
        self.me = spot.me(axis)
        self.next, self.prev = spot.along(axis, 1), spot.along(axis, -1)

    def start(self, own=None):
        own = own or (lambda half: self.at(self.me, half))
        send, at, me = self.wires.send, self.at, self.me
        self.right0 = send(own(0), at(me, 0), self.next)
        self.left1 = send(own(1), at(me, 1), self.prev)
        self.right1 = send(own(1), at(me, 1), self.next)
        self.left0 = send(own(0), at(me, 0), self.prev)

    def forward(self):
        send, at, me = self.wires.send, self.at, self.me
        self.right0.wait_recv()
        before = at(turn(me, -1), 0)
        self.pass0 = send(before, before, self.next)
        self.left1.wait_recv()
        after = at(turn(me, 1), 1)
        self.pass1 = send(after, after, self.prev)

    def near(self):
        self.right1.wait_recv()
        self.left0.wait_recv()

    def far(self):
        self.pass0.wait_recv()
        self.pass1.wait_recv()

    def close(self):
        near = [self.right0, self.left1, self.right1, self.left0]
        self.wires.done(near + [self.pass0, self.pass1])


class PairGather:
    def __init__(self, wires, spot, axis, out, own, start, size):
        self.wires, self.spot, self.out, self.own = wires, spot, out, own
        self.rows = pl.ds(start, size)
        cut = size // 2

        def half_rows(half):
            return pl.ds(start + half * cut, cut)

        self.half_rows = half_rows
        self.ring = RingGather(
            wires, spot, axis, lambda pos, half: out.at[spot.c, pos, half_rows(half)]
        )
        self.me = spot.me(axis)

    def share(self, pos):
        block = self.out.at[self.spot.c, pos, self.rows]
        return self.wires.send(block, block, self.spot.sibling)

    def start(self):
        self.ring.start(lambda half: self.own.at[self.half_rows(half)])
        mine = self.own.at[self.rows]
        place_of = self.out.at[self.spot.c, self.me, self.rows]
        self.shared = [self.wires.send(mine, place_of, self.spot.sibling)]
        self.kept = self.wires.move(mine, place_of)

    def forward(self):
        self.ring.forward()

    def near(self):
        self.ring.near()
        self.shared.append(self.share(turn(self.me, -1)))
        self.shared.append(self.share(turn(self.me, 1)))

    def far(self):
        self.ring.far()
        self.shared.append(self.share(turn(self.me, 2)))

    def finish(self):
        for copy in self.shared:
            copy.wait_recv()
        self.kept.wait()

    def close(self):
        self.ring.close()
        self.wires.done(self.shared)


class PairScatter:
    def __init__(self, wires, spot, axis, part, got, passed, near, start, size):
        self.wires, self.spot = wires, spot
        self.me = spot.me(axis)
        self.next, self.prev = spot.along(axis, 1), spot.along(axis, -1)
        self.part, self.got, self.passed, self.near = part, got, passed, near
        self.start_row, self.size, self.cut = start, size, size // 2

    def rows(self, half=None):
        if half is None:
            return pl.ds(self.start_row, self.size)
        return pl.ds(self.start_row + half * self.cut, self.cut)

    def share(self):
        self.shared = self.wires.send(
            self.part.at[1 - self.spot.c, :, self.rows()],
            self.got.at[:, self.rows()],
            self.spot.sibling,
        )

    def first(self):
        self.shared.wait_recv()
        pos = turn(self.me, 2)
        mine = self.got.at[pos, self.rows()]
        add_into(mine, self.part.at[self.spot.c, pos, self.rows()], mine)
        self.pass0 = self.wires.send(
            self.got.at[pos, self.rows(0)], self.passed.at[self.rows(0)], self.next
        )
        self.pass1 = self.wires.send(
            self.got.at[pos, self.rows(1)], self.passed.at[self.rows(1)], self.prev
        )

    def direct(self):
        self.arriving = []
        for by, half, who, side in ((1, 1, self.next, 0), (-1, 0, self.prev, 1)):
            pos = turn(self.me, by)
            mine = self.got.at[pos, self.rows(half)]
            add_into(mine, self.part.at[self.spot.c, pos, self.rows(half)], mine)
            self.arriving.append(self.wires.send(mine, self.near.at[side, self.rows(half)], who))

    def through(self):
        after, before = turn(self.me, 1), turn(self.me, -1)
        for pos, half, who, side, arrived in (
            (after, 0, self.next, 0, self.pass0),
            (before, 1, self.prev, 1, self.pass1),
        ):
            arrived.wait_recv()
            mine = self.got.at[pos, self.rows(half)]
            add_into(
                mine,
                self.part.at[self.spot.c, pos, self.rows(half)],
                mine,
                self.passed.at[self.rows(half)],
            )
            self.arriving.append(self.wires.send(mine, self.near.at[side, self.rows(half)], who))

    def arrive(self):
        for copy in self.arriving:
            copy.wait_recv()

    def close(self):
        self.wires.done([self.shared, self.pass0, self.pass1] + self.arriving)

    def total(self, span):
        return (
            self.part[self.spot.c, self.me, span].astype(F32)
            + self.got[self.me, span].astype(F32)
            + self.near[0, span].astype(F32)
            + self.near[1, span].astype(F32)
        )


class LineScatter:
    def __init__(self, wires, spot, axis, at, passed, work, near):
        self.wires, self.at = wires, at
        self.me = spot.me(axis)
        self.next, self.prev = spot.along(axis, 1), spot.along(axis, -1)
        self.passed, self.work, self.near = passed, work, near

    def first(self):
        send, me = self.wires.send, self.me
        far, after, before = turn(me, 2), turn(me, 1), turn(me, -1)
        self.pass0 = send(self.at(far, 0), self.passed(0), self.next)
        self.pass1 = send(self.at(far, 1), self.passed(1), self.prev)
        self.arriving = [
            send(self.at(after, 1), self.near(0, 1), self.next),
            send(self.at(before, 0), self.near(1, 0), self.prev),
        ]

    def second(self):
        for by, half, who, side, arrived in (
            (1, 0, self.next, 0, self.pass0),
            (-1, 1, self.prev, 1, self.pass1),
        ):
            arrived.wait_recv()
            add_into(self.work(half), self.at(turn(self.me, by), half), self.passed(half))
            self.arriving.append(self.wires.send(self.work(half), self.near(side, half), who))

    def finish(self):
        for copy in self.arriving:
            copy.wait_recv()
        for half in (0, 1):
            mine = self.at(self.me, half)
            add_into(mine, mine, self.near(0, half), self.near(1, half))


def norm_scale(values):
    return lax.rsqrt(jnp.mean(values * values, axis=-1, keepdims=True) + EPSILON)


def norm_back(upstream, values, inverse, gain):
    scaled = upstream * gain
    inner = jnp.sum(scaled * values, axis=-1, keepdims=True)
    return scaled * inverse - values * inner * (inverse * inverse * inverse) / values.shape[-1]


def over_rows(start, size, step, chunk=16):
    def body(i, carry):
        step(pl.ds(pl.multiple_of(start + i * chunk, chunk), chunk))
        return carry

    lax.fori_loop(0, size // chunk, body, 0)


def fold(total, values):
    part = values[0:8]
    for first in range(8, values.shape[0], 8):
        part = part + values[first : first + 8]
    total[...] += part


TWO = ((0, 96), (96, 96))
THREE = ((0, 64), (64, 64), (128, 64))


def dot(left, right, a, b):
    return lax.dot_general(left, right, (((a,), (b,)), ((), ())), preferred_element_type=F32)


def repeat(count, step):
    def body(i, carry):
        step(i)
        return carry

    lax.fori_loop(0, count, body, 0)


def whole(i, size):
    return pl.ds(pl.multiple_of(i * size, size), size)


def grid_of(rows, columns):
    return (
        lax.broadcasted_iota(jnp.int32, (rows, columns), 0),
        lax.broadcasted_iota(jnp.int32, (rows, columns), 1),
    )


def picks(rows, columns, chosen):
    return jnp.where(chosen(*grid_of(rows, columns)), 1.0, 0.0).astype(BF16)


def quad_order(unit):
    return (((unit >> 5) & 3) << 7) + ((unit >> 7) << 5) + (unit & 31)


def swap_halves(values):
    lane = lax.broadcasted_iota(jnp.int32, values.shape, 1)
    up = pltpu.roll(values, 80, 1)
    down = pltpu.roll(values, 48, 1)
    return jnp.where(lane < 48, up, down)


def around(spot, axes):
    return [spot.along(a, by) for a in axes for by in (1, -1)] + [spot.sibling]


def layer_kernel(
    tokens, gain_attn, gain_mlp, cot, w_query, w_key, w_value, w_out, w_gate, w_up, w_down, marks,
    normed_out, result_out, token_out, gains_out, att_out, out_out, gu_out, dn_out,
    normed, cots, second, part, got, passed, near, work, att_two, own_out, aq, ao, d_att, wo,
    gu, gu_own, dn, d_gu, d_dn, own, grad_hidden, q, kv, prob, mix, cosine, sine,
    marks_two, gains, middle_all, back_all, total, grad_mix, grad_kv, far_kv,
    gu_in, dn_in, att_in, out_in, gain_c, gain_y, gain_x, gain_z,
    ready, send_sem, recv_sem,
):
    spot = Spot()
    wires = Wires(send_sem, recv_sem)
    x, y, z, c = spot.x, spot.y, spot.z, spot.c
    neighbours = (
        around(spot, "xyz")
        + [spot.along(a, 2) for a in "xyz"]
        + [spot.partner]
        + [spot.in_quad(by)[1] for by in (1, 2, 3)]
    )
    greet(neighbours)

    def tell(which, devices):
        for who in devices:
            pl.semaphore_signal(ready.at[which], inc=1, device_id=who, device_id_type=MESH)

    def hear(which, count):
        pl.semaphore_wait(ready.at[which], count)

    for i, gain in enumerate((gain_attn, gain_mlp)):
        gains[i : i + 1, :] = jnp.concatenate([gain[j : j + 1, :] for j in range(12)], axis=1)

    def normalise(span):
        rows = tokens[span, :].astype(F32)
        own[span, :] = (rows * norm_scale(rows) * gains[0:1, :]).astype(BF16)

    over_rows(0, OWN, normalise)

    def three(first):
        return lambda r, k: r + first == k

    columns = (
        dot(w_query[...], picks(192, 384, three(0)), 1, 0)
        + dot(w_key[...], picks(96, 384, three(192)), 1, 0)
        + dot(w_value[...], picks(96, 384, three(288)), 1, 0)
    )
    att_two[0] = columns.astype(BF16)
    own_out[0] = jnp.zeros((16, D), BF16)
    own_out[0, 0:12] = w_out[...]
    greeted(neighbours)

    swaps = [
        wires.send(att_two.at[0], att_two.at[1], spot.partner),
        wires.send(own_out.at[0], own_out.at[1], spot.partner),
    ]
    rows_y = [PairGather(wires, spot, "y", normed, own, s, n) for s, n in TWO]
    for g in rows_y:
        g.start()
    marks_kept = wires.move(marks, marks_two.at[c])
    marks_got = wires.send(marks, marks_two.at[c], spot.sibling)

    order = picks(512, 512, lambda r, k: quad_order(r) == k)
    for shard, first in ((w_gate, 0), (w_up, 128)):
        moved = dot(shard[...], order, 1, 0).astype(BF16)
        for i in range(4):
            gu_own[i, :, first : first + 128] = moved[:, i * 128 : i * 128 + 128]
    gu_lanes = whole(y, 256)
    gu_here = gu.at[whole(z * 4 + spot.quad, 96), gu_lanes]
    gu_kept = wires.move(gu_own.at[spot.quad], gu_here)
    gu_swap = []
    for by in (1, 2, 3):
        other, who = spot.in_quad(by)
        gu_swap.append(wires.send(gu_own.at[other], gu_here, who))

    def trig(core):
        def step(i):
            span = whole(i, 128)
            row, lane = grid_of(128, 128)
            number = marks_two[core, pl.ds(spot.high * 6 + i, 1), :]
            ones = jnp.ones((128, 128), BF16)
            where = jnp.zeros((128, 128), F32)
            for digit, factor in ((number >> 5, 32.0), (number & 31, 1.0)):
                spread = jnp.where(row == lane, digit.astype(F32), 0.0).astype(BF16)
                where = where + factor * dot(spread, ones, 1, 0)
            grad_kv[core, span, 0:128] = where
            turns = jnp.where(lane < 48, lane, lane - 48).astype(F32) * (2.0 / HD)
            angle = where * jnp.exp(-math.log(ROPE_BASE) * turns)
            inside = lane < HD
            cosine[core, span, :] = jnp.where(inside, jnp.cos(angle), 0.0)
            wave = jnp.sin(angle)
            sine[core, span, :] = jnp.where(inside, jnp.where(lane < 48, -wave, wave), 0.0)

        repeat(6, step)

    marks_kept.wait()
    trig(c)
    for copy in swaps:
        copy.wait_recv()

    def slot_of(pos):
        return (pos % 2) * 2 + pos // 2

    slot = slot_of(x)
    pick = jnp.where(spot.high == c, 0, 1)
    low, high = pl.ds(0, 48), pl.ds(48, 48)
    att_kept = [
        wires.move(att_two.at[pick], aq.at[z, slot]),
        wires.move(own_out.at[pick], ao.at[z, slot]),
    ]
    att_side, out_side = [], []
    for by in (1, -1, 2):
        att_side.append(
            wires.send(att_two.at[pick, low], aq.at[z, slot, low], spot.along("z", by))
        )
        att_side.append(
            wires.send(att_two.at[pick, high], aq.at[z, slot, high], spot.along("x", by))
        )
    for by in (1, -1, 2):
        out_side.append(wires.send(own_out.at[pick], ao.at[z, slot], spot.along("x", by)))
    att_line = [
        RingGather(wires, spot, "x", lambda pos, h: aq.at[pl.ds(2 * h, 2), slot_of(pos), low]),
        RingGather(wires, spot, "z", lambda pos, h: aq.at[pos, pl.ds(2 * h, 2), high]),
    ]
    out_line = RingGather(wires, spot, "z", lambda pos, h: ao.at[pos, pl.ds(2 * h, 2)])
    cot_x = [PairGather(wires, spot, "x", cots, cot, s, n) for s, n in TWO]
    marks_got.wait_recv()
    trig(1 - c)
    for copy in att_kept:
        copy.wait()
    for copy in att_side:
        copy.wait_recv()
    for line in att_line:
        line.start()
    for g in rows_y:
        g.forward()
    rows_y[0].near()
    for line in att_line:
        line.forward()
    for copy in out_side:
        copy.wait_recv()
    out_line.start()
    dn_here = dn.at[y, z]
    dn_kept = wires.move(w_down, dn_here)
    dn_side = [wires.send(w_down, dn_here, spot.along("z", by)) for by in (1, -1, 2)]
    cot_x[0].start()
    rows_y[1].near()
    for line in att_line:
        line.near()
        line.far()

    def out_row(r, k):
        unit = jnp.where(r < 128, r, r - 32)
        real = (r < 96) | ((r >= 128) & (r < 224))
        return real & (unit + ((unit * 5462) >> 16) * 4 == k)

    def project(core, pos):
        both = dot(normed[core, pos], aq[...].reshape(D, 384), 1, 0)
        span = whole(pos, OWN)
        cos, sin = cosine[core, span, :], sine[core, span, :]
        tile = [both[:, 128 * i : 128 * i + 128] for i in range(3)]
        lane = lax.broadcasted_iota(jnp.int32, tile[0].shape, 1)

        def turned(values):
            return (values * cos + swap_halves(values) * sin).astype(BF16)

        q[core, span, 0:128] = turned(tile[0])
        q[core, span, 128:256] = turned(
            jnp.where(lane < 32, pltpu.roll(tile[0], 32, 1), pltpu.roll(tile[1], 32, 1))
        )
        after = pl.ds(pl.multiple_of(WIN + pos * OWN, 64), OWN)
        kv[core, after, 0:128] = turned(
            jnp.where(lane < 64, pltpu.roll(tile[1], 64, 1), pltpu.roll(tile[2], 64, 1))
        )
        kv[core, after, 128:256] = jnp.where(lane < HD, pltpu.roll(tile[2], 96, 1), 0.0).astype(
            BF16
        )

    for g in rows_y:
        g.kept.wait()
    repeat(3, lambda i: project(c, turn(y, i - 1)))
    for g in rows_y:
        for copy in g.shared[:3]:
            copy.wait_recv()
    repeat(3, lambda i: project(1 - c, turn(y, i - 1)))
    for g in rows_y:
        g.far()
    gu_kept.wait()
    for copy in gu_swap:
        copy.wait_recv()
    gu_side = RingGather(
        wires, spot, "y", lambda pos, h: gu.at[whole(z * 2 + h, 192), whole(pos, 256)]
    )
    gu_side.start()
    out_line.forward()
    project(c, turn(y, 2))
    for g in rows_y:
        g.shared[3].wait_recv()
    project(1 - c, turn(y, 2))
    kv_got = wires.send(kv.at[:, pl.ds(768, WIN)], kv.at[:, pl.ds(0, WIN)], spot.along("x", 2))
    normed_kept = wires.move(normed, normed_out)
    left = wires.started()
    cot_x[0].forward()
    cot_x[0].near()
    dn_kept.wait()
    for copy in dn_side:
        copy.wait_recv()
    dn_line = RingGather(wires, spot, "y", lambda pos, h: dn.at[pos, pl.ds(2 * h, 2)])
    gu_line = RingGather(
        wires, spot, "z", lambda pos, h: gu.at[whole(pos, 384), pl.ds(h * 512, 512)]
    )

    scale = HD ** (-0.5)

    def attend(core, run, head):
        span = whole(run, WIN)
        lanes = whole(head, 128)
        window = pl.ds(pl.multiple_of(run * WIN, WIN), SEQ)
        scores = dot(q[core, span, lanes], kv[core, window, 0:128], 1, 1) * scale
        row, column = grid_of(WIN, SEQ)
        spot_of = spot.high * HALF + run * WIN + row[:, 0:1]
        begin = jnp.maximum(
            (spot_of >> 9) << 9, spot_of - grad_kv[core, span, 0:1].astype(jnp.int32)
        )
        begin = begin - (spot.high * HALF + run * WIN) + WIN
        allowed = (column >= begin) & (column <= row + WIN)
        scores = jnp.where(allowed, scores, MASKED)
        weights = jnp.exp(scores - jnp.max(scores, axis=-1, keepdims=True))
        share = weights / jnp.sum(weights, axis=-1, keepdims=True)
        rounded = share.astype(BF16)
        prob[core, run, head] = rounded
        values = dot(rounded, kv[core, window, 128:256], 1, 0)
        mix[core, span, lanes] = values.astype(BF16)

    repeat(4, lambda i: attend(i // 2, 1, i % 2))
    gu_side.forward()
    dn_line.start()
    repeat(4, lambda i: attend(i // 2, 2, i % 2))
    gu_side.near()
    gu_side.far()
    gu_line.start()
    out_line.near()
    out_line.far()
    out_rows = picks(256, 256, out_row)
    wo[...] = dot(out_rows, ao[...].reshape(256, D), 1, 0).astype(BF16).reshape(4, 4, 16, D)

    def project_out(core, half):
        rows = mix[core, half * 384 : half * 384 + 384, :]
        out = dot(rows, wo[...].reshape(256, D), 1, 0).astype(BF16)
        part[core, half * 2 : half * 2 + 2] = out.reshape(2, OWN, D)

    def share_all(sums):
        for s in sums:
            s.share()

    def back_hidden(s):
        def step(core):
            rows = cots[core, :, pl.ds(s * 64, 64)].reshape(256, D)
            grad_hidden[core * 3 + s] = dot(rows, dn[...].reshape(512, D), 1, 1).astype(BF16)

        repeat(2, step)

    sums_y = [PairScatter(wires, spot, "y", part, got, passed, near, s, n) for s, n in THREE]
    rows_x = [PairGather(wires, spot, "x", second, own, s, n) for s, n in THREE]
    repeat(2, lambda i: project_out(i, 1))
    kv_got.wait_recv()
    cot_x[1].start()
    repeat(4, lambda i: attend(i // 2, 0, i % 2))
    cot_x[0].far()
    cot_x[0].finish()
    project_out(1 - c, 0)
    share_all(sums_y)
    project_out(c, 0)
    for g in rows_y:
        g.close()
    normed_kept.wait()
    sums_y[0].first()
    sums_y[1].first()
    sums_y[0].direct()
    dn_line.forward()
    cot_x[1].forward()
    sums_y[0].through()
    sums_y[2].first()
    sums_y[1].direct()
    gu_line.forward()
    sums_y[1].through()
    wires.done(left)
    cot_x[1].near()
    sums_y[2].direct()
    dn_line.near()
    dn_line.far()
    cot_x[1].far()
    cot_x[1].finish()

    def middle_rows(s):
        def use(span):
            middle = tokens[span, :].astype(F32) + s.total(span)
            middle_all[span, :] = middle
            own[span, :] = (middle * norm_scale(middle) * gains[1:2, :]).astype(BF16)

        return use

    def gather_next(i):
        s = sums_y[i]
        s.arrive()
        over_rows(s.start_row, s.size, middle_rows(s))
        s.close()
        rows_x[i].start()

    gather_next(0)
    back_hidden(0)
    sums_y[2].through()
    gather_next(1)
    back_hidden(1)
    rows_x[0].forward()
    back_hidden(2)
    rows_x[0].near()
    gather_next(2)
    rows_x[1].forward()
    rows_x[0].far()
    gu_line.near()
    gu_line.far()
    rows_x[0].finish()
    early = wires.started()

    def feed(core, i):
        span = pl.ds(*THREE[i])
        size = 4 * THREE[i][1]
        rows = second[core, :, span].reshape(size, D)
        both = dot(rows, gu[...], 1, 0)
        upstream = grad_hidden[core * 3 + i].astype(F32)
        for j in range(4):
            gate = both[:, j * 256 : j * 256 + 128]
            upward = both[:, j * 256 + 128 : j * 256 + 256]
            sent = upstream[:, j * 128 : j * 128 + 128]
            sigmoid = jax.nn.sigmoid(gate)
            silu = gate * sigmoid
            slope = sigmoid * (1.0 + gate * (1.0 - sigmoid))
            for first, values in (
                (1024 + j * 128, silu * upward),
                (j * 256, sent * upward * slope),
                (j * 256 + 128, sent * silu),
            ):
                rounded = values.astype(BF16).reshape(4, THREE[i][1], 128)
                work[core, :, span, first : first + 128] = rounded
        back = dot(work[core, :, span, 0:1024].reshape(size, 1024), gu[...], 1, 1)
        part[core, :, span] = back.astype(BF16).reshape(4, THREE[i][1], D)

    sums_x = [PairScatter(wires, spot, "x", part, got, passed, near, s, n) for s, n in THREE]
    grads_y = [PairGather(wires, spot, "y", normed, own, s, n) for s, n in THREE]

    def feed_share(i):
        feed(1 - c, i)
        sums_x[i].share()

    wires.again()
    feed_share(0)
    rows_x[1].near()
    feed(c, 0)
    sums_x[0].first()
    rows_x[2].forward()
    rows_x[1].far()
    rows_x[1].finish()
    feed_share(1)
    sums_x[0].direct()
    rows_x[2].near()
    feed(c, 1)
    sums_x[1].first()
    sums_x[0].through()
    rows_x[2].far()
    sums_x[1].direct()
    rows_x[2].finish()
    feed_share(2)
    sums_x[1].through()
    feed(c, 2)
    sums_x[2].first()
    sums_x[2].direct()
    wires.done(early)
    tell(0, [spot.along("z", 1), spot.along("z", -1)])

    def grad_gate_up(i):
        lanes = whole(i, 256)
        rows = second[:, :, :, lanes].reshape(8 * OWN, 256)
        sent = work[:, :, :, 0:1024].reshape(8 * OWN, 1024)
        d_gu[lanes, :] = dot(rows, sent, 0, 0).astype(BF16)

    def grad_down(i):
        lanes = pl.ds(pl.multiple_of(1024 + i * 256, 256), 256)
        rows = work[:, :, :, lanes].reshape(8 * OWN, 256)
        grad = dot(rows, cots[...].reshape(8 * OWN, D), 0, 0).astype(BF16)
        d_dn[pl.ds(i * 2, 2)] = grad.reshape(2, 4, 32, D)

    def down(i):
        rows = work[i // 2, pl.ds((i % 2) * 2, 2), :, 1024:D].reshape(384, 512)
        second[i // 2, pl.ds((i % 2) * 2, 2)] = (
            dot(rows, dn[...].reshape(512, D), 1, 0).astype(BF16).reshape(2, OWN, D)
        )

    def back_rows(s):
        def use(span):
            grad = s.total(span)
            rows = middle_all[span, :]
            inverse = norm_scale(rows)
            back = cot[span, :].astype(F32) + norm_back(grad, rows, inverse, gains[1:2, :])
            back_all[span, :] = back
            own[span, :] = back.astype(BF16)
            fold(total, grad * rows * inverse)

        return use

    def gather_back(i):
        s = sums_x[i]
        s.arrive()
        rows_x[i].close()
        over_rows(s.start_row, s.size, back_rows(s))
        s.close()
        grads_y[i].start()

    def mix_back(i):
        def step(core):
            span = pl.ds(*THREE[i])
            rows = normed[core, :, span].reshape(256, D)
            grad = dot(rows, wo[...].reshape(256, D), 1, 1).astype(BF16)
            for pos in range(4):
                start = pos * OWN + THREE[i][0]
                grad_mix[core, start : start + 64, :] = grad[pos * 64 : pos * 64 + 64]

        repeat(2, step)

    total[...] = jnp.zeros_like(total)
    repeat(2, grad_gate_up)
    gather_back(0)
    repeat(2, lambda i: grad_gate_up(2 + i))
    sums_x[2].through()
    grads_y[0].forward()
    repeat(2, lambda i: grad_gate_up(4 + i))
    hear(0, 2)
    gu_sum = [
        LineScatter(
            wires, spot, "z",
            lambda pos, h, lot=lot: d_gu.at[whole(pos * 4 + lot * 2 + h, 96)],
            lambda h, lot=lot: gu.at[pl.ds(lot * 192 + h * 96, 96)],
            lambda h, lot=lot: gu.at[pl.ds(384 + lot * 192 + h * 96, 96)],
            lambda side, h, lot=lot: gu.at[pl.ds(768 + side * 384 + lot * 192 + h * 96, 96)],
        )
        for lot in (0, 1)
    ]
    gu_got = []

    def gu_beside(lot):
        gu_sum[lot].finish()
        for by in (1, -1, 2):
            part_of = d_gu.at[whole(z * 2 + lot, 192), whole(turn(y, by), 256)]
            into = gu_in.at[y, pl.ds(lot * 192, 192)]
            gu_got.append(wires.send(part_of, into, spot.along("y", by)))

    gu_sum[0].first()
    gather_back(1)
    grads_y[0].near()
    repeat(2, grad_down)
    grads_y[1].forward()
    grads_y[0].far()
    gather_back(2)
    repeat(2, down)
    gu_sum[0].second()
    gu_sum[1].first()
    grads_y[1].near()
    grads_y[2].forward()
    repeat(2, lambda i: down(2 + i))
    tell(1, around(spot, "xy") + [spot.along("z", 1), spot.along("z", -1)])
    again = wires.move(normed_out, cots)
    gain_c[c, 1:2] = jnp.sum(total[...], axis=0, keepdims=True)
    grads_y[0].finish()
    mix_back(0)
    grads_y[1].far()
    grads_y[2].near()
    grads_y[1].finish()
    mix_back(1)
    hear(1, 7)
    sums_m = [
        PairScatter(
            wires, spot, "x", second, work.at[0], work.at[1, 0], work.at[1, pl.ds(1, 2)], s, n
        )
        for s, n in TWO
    ]
    share_all(sums_m)
    grad_kv[...] = jnp.zeros_like(grad_kv)
    grads_y[2].far()
    grads_y[2].finish()
    mix_back(2)
    left = wires.started()
    gu_beside(0)

    def attend_back(core, run, head):
        span = whole(run, WIN)
        lanes = whole(head, 128)
        window = pl.ds(pl.multiple_of(run * WIN, WIN), SEQ)
        rounded = prob[core, run, head]
        share = rounded.astype(F32)
        mixed = grad_mix[core, span, lanes]
        asked = q[core, span, lanes]
        grad = dot(mixed, kv[core, window, 128:256], 1, 1)
        inner = jnp.sum(share * grad, axis=-1, keepdims=True)
        scored = (share * (grad - inner)).astype(BF16)
        grad_kv[core, window, 0:128] += dot(scored, asked, 0, 0) * scale
        grad_kv[core, window, 128:256] += dot(rounded, mixed, 0, 0)
        grad_q = dot(scored, kv[core, window, 0:128], 1, 0) * scale
        cos, sin = cosine[core, span, :], sine[core, span, :]
        q[core, span, lanes] = (grad_q * cos - swap_halves(grad_q) * sin).astype(BF16)

    repeat(4, lambda i: attend_back(i // 2, 0, i % 2))
    far_from = grad_mix.at[:, pl.ds(0, WIN)]
    for core in (0, 1):
        far_from[core] = grad_kv[core, 0:WIN, :].astype(BF16)
    far_got = wires.send(far_from, far_kv, spot.along("x", 2))
    for s in sums_m:
        s.first()
    gu_sum[1].second()
    dn_sum = LineScatter(
        wires, spot, "z",
        lambda pos, h: d_dn.at[pl.ds(2 * h, 2), pos],
        lambda h: dn.at[0, pl.ds(2 * h, 2)],
        lambda h: dn.at[1, pl.ds(2 * h, 2)],
        lambda side, h: dn.at[2 + side, pl.ds(2 * h, 2)],
    )
    dn_sum.first()
    repeat(4, lambda i: attend_back(i // 2, 1, i % 2))
    for s in sums_m:
        s.direct()
    repeat(4, lambda i: attend_back(i // 2, 2, i % 2))
    gu_beside(1)

    def out_rows_back(r, k):
        unit = jnp.where(k < 128, k, k - 32)
        real = (k < 96) | ((k >= 128) & (k < 224))
        return real & (unit + ((unit * 5462) >> 16) * 4 == r)

    grad_out = dot(mix[...].reshape(8 * OWN, 256), normed[...].reshape(8 * OWN, D), 0, 0)
    grad_out = dot(picks(256, 256, out_rows_back), grad_out.astype(BF16), 1, 0)
    wo[...] = grad_out.astype(BF16).reshape(4, 4, 16, D)
    out_sum = LineScatter(
        wires, spot, "z",
        lambda pos, h: wo.at[pos, pl.ds(2 * h, 2)],
        lambda h: ao.at[0, pl.ds(2 * h, 2)],
        lambda h: ao.at[1, pl.ds(2 * h, 2)],
        lambda side, h: ao.at[2 + side, pl.ds(2 * h, 2)],
    )
    out_sum.first()
    far_got.wait_recv()
    for core in (0, 1):
        grad_kv[core, 768:1024, :] += far_kv[core].astype(F32)

    def turn_back(i):
        core, pos = i // 4, i % 4
        after = pl.ds(pl.multiple_of(WIN + pos * OWN, 64), OWN)
        span = whole(pos, OWN)
        cos, sin = cosine[core, span, :], sine[core, span, :]
        keyed = grad_kv[core, after, 0:128]
        keyed = pltpu.roll(keyed * cos - swap_halves(keyed) * sin, 64, 1)
        valued = pltpu.roll(grad_kv[core, after, 128:256], 32, 1)
        front = q[core, span, 0:128].astype(F32)
        behind = pltpu.roll(q[core, span, 128:256].astype(F32), 96, 1)
        lane = lax.broadcasted_iota(jnp.int32, front.shape, 1)
        q[core, span, 0:128] = jnp.where(lane < 96, front, behind).astype(BF16)
        q[core, span, 128:256] = jnp.where(lane < 64, behind, keyed).astype(BF16)
        kv[core, after, 0:128] = jnp.where(lane < 32, keyed, valued).astype(BF16)

    repeat(8, turn_back)

    def normed_back(core):
        def step(pos):
            after = pl.ds(pl.multiple_of(WIN + pos * 384, 128), 384)
            rows = jnp.concatenate([q[core, whole(pos, 384), :], kv[core, after, 0:128]], axis=1)
            grad = dot(rows, aq[...].reshape(D, 384), 1, 1).astype(BF16)
            part[core, pl.ds(pos * 2, 2)] = grad.reshape(2, OWN, D)

        repeat(2, step)

    sums_n = [PairScatter(wires, spot, "y", part, got, passed, near, s, n) for s, n in THREE]
    normed_back(1 - c)
    share_all(sums_n)
    normed_back(c)
    sums_n[0].first()
    sums_n[1].first()
    sums_n[0].direct()
    dn_sum.second()
    again.wait()

    def grad_columns(i):
        rows = cots[:, :, :, whole(i, 384)].reshape(8 * OWN, 384)
        asked = dot(rows, q[...].reshape(8 * OWN, 256), 0, 0)
        other = dot(rows, kv[:, pl.ds(WIN, HALF), 0:128].reshape(8 * OWN, 128), 0, 0)
        d_att[i, :, :, 0:256] = asked.astype(BF16).reshape(4, 96, 256)
        d_att[i, :, :, 256:384] = other.astype(BF16).reshape(4, 96, 128)
        held = aq[i].reshape(384, 384).astype(F32)
        folded = (
            held[:, 0:128] * asked[:, 0:128]
            + held[:, 128:256] * asked[:, 128:256]
            + held[:, 256:384] * other
        )
        gain_c[c, 0:1, whole(i, 384)] = jnp.sum(folded.T, axis=0, keepdims=True)

    repeat(2, grad_columns)
    sums_n[0].through()
    sums_n[2].first()
    sums_n[1].direct()
    for s in sums_m:
        s.through()
    repeat(2, lambda i: grad_columns(2 + i))
    gain_c[c, 0:1] = gain_c[c, 0:1] / gains[0:1, :]
    tell(2, [spot.along(a, by) for a in "xz" for by in (1, -1)])
    gain_got = [wires.send(gain_c.at[c], gain_c.at[c], spot.sibling)]
    sums_n[1].through()
    sums_n[2].direct()
    wires.done(left)
    hear(2, 4)
    att_sum = [
        LineScatter(
            wires, spot, "x",
            lambda pos, h: d_att.at[pl.ds(2 * h, 2), slot_of(pos), low],
            lambda h: aq.at[0, pl.ds(2 * h, 2), low],
            lambda h: aq.at[1, pl.ds(2 * h, 2), low],
            lambda side, h: aq.at[2 + side, pl.ds(2 * h, 2), low],
        ),
        LineScatter(
            wires, spot, "z",
            lambda pos, h: d_att.at[pos, pl.ds(2 * h, 2), high],
            lambda h: aq.at[0, pl.ds(2 * h, 2), high],
            lambda h: aq.at[1, pl.ds(2 * h, 2), high],
            lambda side, h: aq.at[2 + side, pl.ds(2 * h, 2), high],
        ),
    ]
    for line in att_sum:
        line.first()
    out_sum.second()

    def add_gains(held, axis, into):
        for copy in gain_got:
            copy.wait_recv()
        summed = held[0]
        for i in range(1, held.shape[0]):
            summed = summed + held[i]
        if into is None:
            gains_out[...] = summed
            return []
        me = spot.me(axis)
        into[me] = summed
        return [wires.send(into.at[me], into.at[me], spot.along(axis, by)) for by in (1, -1, 2)]

    gain_got = add_gains(gain_c, "x", gain_x)
    for line in att_sum:
        line.second()
    sums_n[2].through()
    dn_sum.finish()
    dn_got = [
        wires.send(d_dn.at[turn(y, by), z], dn_in.at[y], spot.along("y", by))
        for by in (1, -1, 2)
    ]
    gain_got = add_gains(gain_x, "z", gain_z)

    for copy in gu_got:
        copy.wait_recv()
    mine = d_gu.at[whole(z, 384), whole(y, 256)]
    add_into(mine, mine, *[gu_in.at[turn(y, by)] for by in (1, -1, 2)])
    gu_done = []
    for by in (1, 2, 3):
        other, who = spot.in_quad(by)
        rows = d_gu.at[whole(z * 4 + other, 96), whole(y, 256)]
        gu_done.append(wires.send(rows, gu_own.at[spot.quad], who))

    def token_rows(s):
        def use(span):
            grad = s.total(span)
            rows = tokens[span, :].astype(F32)
            inverse = norm_scale(rows)
            out = back_all[span, :] + norm_back(grad, rows, inverse, gains[0:1, :])
            part[c, y, span] = out.astype(BF16)

        return use

    def result_rows(s):
        def use(span):
            second[c, x, span] = (middle_all[span, :] + s.total(span)).astype(BF16)

        return use

    token_kept = []

    def token_part(i):
        s = sums_n[i]
        s.arrive()
        over_rows(s.start_row, s.size, token_rows(s))
        token_kept.append(wires.move(part.at[c, y, s.rows()], token_out.at[s.rows()]))

    def result_part(s):
        s.arrive()
        over_rows(s.start_row, s.size, result_rows(s))

    for s in sums_m:
        result_part(s)
    result_kept = wires.move(second.at[c, x], result_out)
    att_got = []
    for line in att_sum:
        line.finish()
    out_sum.finish()
    for by in (1, -1, 2):
        far, who = turn(z, by), spot.along("z", by)
        att_got.append(wires.send(d_att.at[far, slot, low], att_in.at[z, low], who))
        far, who = slot_of(turn(x, by)), spot.along("x", by)
        att_got.append(wires.send(d_att.at[z, far, high], att_in.at[x, high], who))
        att_got.append(wires.send(wo.at[z, far], out_in.at[x], who))
    token_part(0)
    gain_got = add_gains(gain_z, "y", gain_y)
    kept_rows = d_gu.at[whole(z * 4 + spot.quad, 96), whole(y, 256)]
    gu_out[spot.quad] = kept_rows[...]
    for copy in att_got:
        copy.wait_recv()
    for span, me in ((low, z), (high, x)):
        others = [att_in.at[turn(me, by), span] for by in (1, -1, 2)]
        add_into(att_two.at[0, span], d_att.at[z, slot, span], *others)
    others = [out_in.at[turn(x, by)] for by in (1, -1, 2)]
    add_into(own_out.at[0], wo.at[z, slot], *others)
    swaps = [
        wires.send(att_two.at[0], att_two.at[1], spot.partner),
        wires.send(own_out.at[0], own_out.at[1], spot.partner),
    ]
    token_part(1)
    for copy in gu_done:
        copy.wait_recv()
    for by in (1, 2, 3):
        other = turn(spot.quad, by)
        gu_out[other] = gu_own[other]
    for copy in dn_got:
        copy.wait_recv()
    add_into(
        dn_out, d_dn.at[y, z], *[dn_in.at[turn(y, by)] for by in (1, -1, 2)]
    )
    token_part(2)
    add_gains(gain_y, None, None)
    for copy in swaps:
        copy.wait_recv()
    att_out[...] = att_two[pick]
    out_out[...] = own_out[pick]
    result_kept.wait()
    for copy in token_kept:
        copy.wait()
    wires.close()


def finish_kernel(
    result, token, gains, att, out, gu, dn,
    result_out, token_out, attn_out, mlp_out, query_out, key_out, value_out, out_out,
    gate_out, up_out, dn_out,
):
    result_out[...] = result[...]
    token_out[...] = token[...]
    for i, into in enumerate((attn_out, mlp_out)):
        for j in range(12):
            into[j : j + 1, :] = gains[i : i + 1, j * 128 : j * 128 + 128]
    rows = att[...]

    def three(first):
        return lambda r, k: r == k + first

    query_out[...] = dot(rows, picks(384, 192, three(0)), 1, 0)
    key_out[...] = dot(rows, picks(384, 96, three(192)), 1, 0)
    value_out[...] = dot(rows, picks(384, 96, three(288)), 1, 0)
    out_out[...] = out[0:12, :].astype(F32)
    order = picks(512, 512, lambda r, k: quad_order(k) == r)
    for first, into in ((0, gate_out), (128, up_out)):
        moved = jnp.concatenate([gu[i, :, first : first + 128] for i in range(4)], axis=1)
        into[...] = dot(moved, order, 1, 0)
    dn_out[...] = dn[...]


def layer_call(
    tokens, gain_attn, gain_mlp, cot, w_query, w_key, w_value, w_out, w_gate, w_up, w_down, marks
):
    sends, receives = 120, 170
    shape = jax.ShapeDtypeStruct
    outs = (
        (shape((2, 4, OWN, D), BF16), ANY),
        (shape((OWN, D), BF16), ANY),
        (shape((OWN, D), BF16), ANY),
        (shape((2, D), F32), VMEM),
        (shape((96, 384), BF16), VMEM),
        (shape((16, D), BF16), VMEM),
        (shape((4, 96, 256), BF16), VMEM),
        (shape((32, D), F32), VMEM),
    )
    scratch = [
        ((2, 4, OWN, D), BF16),
        ((2, 4, OWN, D), BF16),
        ((2, 4, OWN, D), BF16),
        ((2, 4, OWN, D), BF16),
        ((4, OWN, D), BF16),
        ((OWN, D), BF16),
        ((2, OWN, D), BF16),
        ((2, 4, OWN, D), BF16),
        ((2, 96, 384), BF16),
        ((2, 16, D), BF16),
        ((4, 4, 96, 384), BF16),
        ((4, 4, 16, D), BF16),
        ((4, 4, 96, 384), BF16),
        ((4, 4, 16, D), BF16),
        ((D, 1024), BF16),
        ((4, 96, 256), BF16),
        ((4, 4, 32, D), BF16),
        ((D, 1024), BF16),
        ((4, 4, 32, D), BF16),
        ((OWN, D), BF16),
        ((6, 256, 512), BF16),
        ((2, HALF, 256), BF16),
        ((2, HALF + WIN, 256), BF16),
        ((2, 3, 2, WIN, SEQ), BF16),
        ((2, HALF, 256), BF16),
        ((2, HALF, 128), F32),
        ((2, HALF, 128), F32),
        ((2, 12, 128), jnp.int32),
        ((2, D), F32),
        ((OWN, D), F32),
        ((OWN, D), F32),
        ((8, D), F32),
        ((2, HALF, 256), BF16),
        ((2, HALF + WIN, 256), F32),
        ((2, WIN, 256), BF16),
        ((4, 384, 256), BF16),
        ((4, 32, D), BF16),
        ((4, 96, 384), BF16),
        ((4, 16, D), BF16),
        ((2, 2, D), F32),
        ((4, 2, D), F32),
        ((4, 2, D), F32),
        ((4, 2, D), F32),
    ]
    outs_raw = pl.pallas_call(
        layer_kernel,
        out_shape=tuple(o[0] for o in outs),
        in_specs=[VMEM] * 12,
        out_specs=[o[1] for o in outs],
        scratch_shapes=[pltpu.VMEM(*s) for s in scratch]
        + [
            pltpu.SemaphoreType.REGULAR((3,)),
            pltpu.SemaphoreType.DMA((sends,)),
            pltpu.SemaphoreType.DMA((receives,)),
        ],
        compiler_params=pltpu.CompilerParams(
            collective_id=1, has_side_effects=True, vmem_limit_bytes=64 << 20
        ),
        name="layer",
    )(tokens, gain_attn, gain_mlp, cot, w_query, w_key, w_value, w_out, w_gate, w_up, w_down, marks)
    finals = (
        shape((OWN, D), BF16),
        shape((OWN, D), BF16),
        shape((12, 128), F32),
        shape((12, 128), F32),
        shape((96, 192), F32),
        shape((96, 96), F32),
        shape((96, 96), F32),
        shape((12, D), F32),
        shape((96, 512), F32),
        shape((96, 512), F32),
        shape((32, D), F32),
    )
    return pl.pallas_call(
        finish_kernel,
        out_shape=finals,
        in_specs=[VMEM] * 7,
        out_specs=[VMEM] * 11,
        name="finish",
    )(*outs_raw[1:])


def shards(
    tokens,
    gain_attn,
    gain_mlp,
    w_query,
    w_key,
    w_value,
    w_out,
    w_gate,
    w_up,
    w_down,
    segments,
    positions,
    cotangent,
):
    del segments
    done = layer_call(
        tokens,
        gain_attn.reshape(12, 128),
        gain_mlp.reshape(12, 128),
        cotangent,
        w_query,
        w_key,
        w_value,
        w_out,
        w_gate,
        w_up,
        w_down,
        positions.reshape(12, 128),
    )
    return (*done[:2], done[2].reshape(D), done[3].reshape(D), *done[4:])


def solution(mesh):
    placed = (
        P(("dp", "tensor"), None),
        P(),
        P(),
        P("dp", "tensor"),
        P("dp", "tensor"),
        P("dp", "tensor"),
        P(("tensor", "dp"), None),
        P("dp", "tensor"),
        P("dp", "tensor"),
        P(("tensor", "dp"), None),
        P("dp"),
        P("dp"),
        P(("dp", "tensor"), None),
    )
    return jax.shard_map(
        shards,
        mesh=mesh,
        in_specs=placed,
        out_specs=(
            P(("dp", "tensor"), None),
            P(("dp", "tensor"), None),
            P(),
            P(),
            P("dp", "tensor"),
            P("dp", "tensor"),
            P("dp", "tensor"),
            P(("tensor", "dp"), None),
            P("dp", "tensor"),
            P("dp", "tensor"),
            P(("tensor", "dp"), None),
        ),
        check_vma=False,
    )
```

```python
import functools
import math

import jax
import jax.numpy as jnp
from jax import lax
from jax.experimental import pallas as pl
from jax.experimental.pallas import tpu as pltpu
from jax.sharding import PartitionSpec as P

HD = 96
SEQ = 512
D = 1536
OWN = 192
HALF = 768
WIN = 256

EPSILON = 1e-05
ROPE_BASE = 100000.0
MASKED = -1e30
MESH = pl.DeviceIdType.MESH
ANY = pl.BlockSpec(memory_space=pl.ANY)
VMEM = pl.BlockSpec(memory_space=pltpu.VMEM)
BF16 = jnp.bfloat16
F32 = jnp.float32


def place():
    dp = lax.axis_index("dp")
    tensor = lax.axis_index("tensor")
    return (tensor // 4) * 2 + (dp // 2) % 2, tensor % 4, dp // 4, dp % 2


def device(x, y, z, c):
    return (z * 4 + (x % 2) * 2 + c, (x // 2) * 4 + y)


def turn(pos, by):
    return (pos + by + 4) % 4


class Spot:
    def __init__(self):
        x, y, z, c = place()
        self.x, self.y, self.z, self.c = x, y, z, c
        self.high, self.low = x // 2, x % 2
        self.quad = self.low * 2 + c
        self.sibling = device(x, y, z, 1 - c)
        self.partner = device(turn(x, 2), y, z, 1 - c)

    def along(self, axis, by):
        x, y, z, c = self.x, self.y, self.z, self.c
        if axis == "x":
            return device(turn(x, by), y, z, c)
        if axis == "y":
            return device(x, turn(y, by), z, c)
        return device(x, y, turn(z, by), c)

    def me(self, axis):
        return {"x": self.x, "y": self.y, "z": self.z}[axis]

    def in_quad(self, by):
        other = turn(self.quad, by)
        return other, device(self.high * 2 + other // 2, self.y, self.z, other % 2)


def greet(devices):
    for who in devices:
        pl.semaphore_signal(
            pltpu.get_barrier_semaphore(), inc=1, device_id=who, device_id_type=MESH
        )


def greeted(devices):
    pl.semaphore_wait(pltpu.get_barrier_semaphore(), len(devices))


class Wires:
    def __init__(self, send_sem, recv_sem):
        self.send_sem, self.recv_sem = send_sem, recv_sem
        self.free = list(range(send_sem.shape[0]))
        self.count = 0
        self.sent = []

    def again(self):
        self.count = 0

    def take(self):
        held = min(self.free)
        self.free.remove(held)
        return held

    def send(self, src, dst, who):
        held = self.take()
        assert self.count < self.recv_sem.shape[0]
        copy = pltpu.make_async_remote_copy(
            src_ref=src,
            dst_ref=dst,
            send_sem=self.send_sem.at[held],
            recv_sem=self.recv_sem.at[self.count],
            device_id=who,
            device_id_type=MESH,
        )
        self.count += 1
        copy.start()
        self.sent.append((copy, held))
        return copy

    def move(self, src, dst):
        held = self.take()
        copy = pltpu.make_async_copy(src, dst, self.send_sem.at[held])
        copy.start()
        return Moved(self, copy, held)

    def done(self, copies):
        kept = []
        for copy, held in self.sent:
            if any(copy is other for other in copies):
                copy.wait_send()
                self.free.append(held)
            else:
                kept.append((copy, held))
        self.sent = kept

    def started(self):
        return [copy for copy, _ in self.sent]

    def close(self):
        self.done(self.started())


class Moved:
    def __init__(self, wires, copy, held):
        self.wires, self.copy, self.held = wires, copy, held

    def wait(self):
        self.copy.wait()
        self.wires.free.append(self.held)


def add_into(dst, *srcs, chunk=16):
    rows = dst.shape[-2]
    chunk = min(chunk, rows)

    def step(i, carry):
        span = pl.ds(pl.multiple_of(i * chunk, chunk), chunk)
        total = srcs[0][..., span, :].astype(F32)
        for src in srcs[1:]:
            total = total + src[..., span, :].astype(F32)
        dst[..., span, :] = total.astype(dst.dtype)
        return carry

    lax.fori_loop(0, rows // chunk, step, 0)


class RingGather:
    def __init__(self, wires, spot, axis, at):
        self.wires, self.at = wires, at
        self.me = spot.me(axis)
        self.next, self.prev = spot.along(axis, 1), spot.along(axis, -1)

    def start(self, own=None):
        self.own = own or (lambda half: self.at(self.me, half))
        send, at, me = self.wires.send, self.at, self.me
        self.right0 = send(self.own(0), at(me, 0), self.next)
        self.left1 = send(self.own(1), at(me, 1), self.prev)

    def rest(self):
        send, at, me = self.wires.send, self.at, self.me
        self.right1 = send(self.own(1), at(me, 1), self.next)
        self.left0 = send(self.own(0), at(me, 0), self.prev)

    def begin(self):
        self.start()
        self.rest()

    def forward(self):
        send, at, me = self.wires.send, self.at, self.me
        self.right0.wait_recv()
        before = at(turn(me, -1), 0)
        self.pass0 = send(before, before, self.next)
        self.left1.wait_recv()
        after = at(turn(me, 1), 1)
        self.pass1 = send(after, after, self.prev)

    def near(self):
        self.right1.wait_recv()
        self.left0.wait_recv()

    def far(self):
        self.pass0.wait_recv()
        self.pass1.wait_recv()

    def close(self):
        near = [self.right0, self.left1, self.right1, self.left0]
        self.wires.done(near + [self.pass0, self.pass1])


class PairGather:
    def __init__(self, wires, spot, axis, out, own, start, size):
        self.wires, self.spot, self.out, self.own = wires, spot, out, own
        self.rows = pl.ds(start, size)
        cut = size // 2

        def half_rows(half):
            return pl.ds(start + half * cut, cut)

        self.half_rows = half_rows
        self.ring = RingGather(
            wires, spot, axis, lambda pos, half: out.at[spot.c, pos, half_rows(half)]
        )
        self.me = spot.me(axis)

    def share(self, pos):
        block = self.out.at[self.spot.c, pos, self.rows]
        return self.wires.send(block, block, self.spot.sibling)

    def start(self):
        self.ring.start(lambda half: self.own.at[self.half_rows(half)])
        mine = self.own.at[self.rows]
        place_of = self.out.at[self.spot.c, self.me, self.rows]
        self.shared = [self.wires.send(mine, place_of, self.spot.sibling)]
        self.kept = self.wires.move(mine, place_of)

    def rest(self):
        self.ring.rest()

    def forward(self):
        self.ring.forward()

    def near(self):
        self.ring.near()
        self.shared.append(self.share(turn(self.me, -1)))
        self.shared.append(self.share(turn(self.me, 1)))

    def far(self):
        self.ring.far()
        self.shared.append(self.share(turn(self.me, 2)))

    def finish(self):
        for copy in self.shared:
            copy.wait_recv()
        self.kept.wait()

    def close(self):
        self.ring.close()
        self.wires.done(self.shared)


class PairScatter:
    def __init__(self, wires, spot, axis, part, got, passed, near, start, size):
        self.wires, self.spot = wires, spot
        self.me = spot.me(axis)
        self.next, self.prev = spot.along(axis, 1), spot.along(axis, -1)
        self.part, self.got, self.passed, self.near = part, got, passed, near
        self.start_row, self.size, self.cut = start, size, size // 2

    def rows(self, half=None):
        if half is None:
            return pl.ds(self.start_row, self.size)
        return pl.ds(self.start_row + half * self.cut, self.cut)

    def share(self):
        self.shared = self.wires.send(
            self.part.at[1 - self.spot.c, :, self.rows()],
            self.got.at[:, self.rows()],
            self.spot.sibling,
        )

    def first(self):
        self.shared.wait_recv()
        pos = turn(self.me, 2)
        mine = self.got.at[pos, self.rows()]
        add_into(mine, self.part.at[self.spot.c, pos, self.rows()], mine)
        self.pass0 = self.wires.send(
            self.got.at[pos, self.rows(0)], self.passed.at[self.rows(0)], self.next
        )
        self.pass1 = self.wires.send(
            self.got.at[pos, self.rows(1)], self.passed.at[self.rows(1)], self.prev
        )

    def left(self):
        self.wires.done([self.pass0, self.pass1])

    def gone(self):
        self.wires.done(self.arriving)

    def direct(self):
        self.arriving = []
        for by, half, who, side in ((1, 1, self.next, 0), (-1, 0, self.prev, 1)):
            pos = turn(self.me, by)
            mine = self.got.at[pos, self.rows(half)]
            add_into(mine, self.part.at[self.spot.c, pos, self.rows(half)], mine)
            self.arriving.append(self.wires.send(mine, self.near.at[side, self.rows(half)], who))

    def through(self):
        after, before = turn(self.me, 1), turn(self.me, -1)
        for pos, half, who, side, arrived in (
            (after, 0, self.next, 0, self.pass0),
            (before, 1, self.prev, 1, self.pass1),
        ):
            arrived.wait_recv()
            mine = self.got.at[pos, self.rows(half)]
            add_into(
                mine,
                self.part.at[self.spot.c, pos, self.rows(half)],
                mine,
                self.passed.at[self.rows(half)],
            )
            self.arriving.append(self.wires.send(mine, self.near.at[side, self.rows(half)], who))

    def arrive(self):
        for copy in self.arriving:
            copy.wait_recv()

    def close(self):
        self.wires.done([self.shared, self.pass0, self.pass1] + self.arriving)

    def total(self, span):
        return (
            self.part[self.spot.c, self.me, span].astype(F32)
            + self.got[self.me, span].astype(F32)
            + self.near[0, span].astype(F32)
            + self.near[1, span].astype(F32)
        )


class LineScatter:
    def __init__(self, wires, spot, axis, at, passed, work, near):
        self.wires, self.at = wires, at
        self.me = spot.me(axis)
        self.next, self.prev = spot.along(axis, 1), spot.along(axis, -1)
        self.passed, self.work, self.near = passed, work, near

    def first(self):
        send, me = self.wires.send, self.me
        far, after, before = turn(me, 2), turn(me, 1), turn(me, -1)
        self.pass0 = send(self.at(far, 0), self.passed(0), self.next)
        self.pass1 = send(self.at(far, 1), self.passed(1), self.prev)
        self.arriving = [
            send(self.at(after, 1), self.near(0, 1), self.next),
            send(self.at(before, 0), self.near(1, 0), self.prev),
        ]

    def second(self):
        for by, half, who, side, arrived in (
            (1, 0, self.next, 0, self.pass0),
            (-1, 1, self.prev, 1, self.pass1),
        ):
            arrived.wait_recv()
            add_into(self.work(half), self.at(turn(self.me, by), half), self.passed(half))
            self.arriving.append(self.wires.send(self.work(half), self.near(side, half), who))

    def finish(self):
        for copy in self.arriving:
            copy.wait_recv()
        for half in (0, 1):
            mine = self.at(self.me, half)
            add_into(mine, mine, self.near(0, half), self.near(1, half))


def norm_scale(values):
    return lax.rsqrt(jnp.mean(values * values, axis=-1, keepdims=True) + EPSILON)


def norm_back(upstream, values, inverse, gain):
    scaled = upstream * gain
    inner = jnp.sum(scaled * values, axis=-1, keepdims=True)
    return scaled * inverse - values * inner * (inverse * inverse * inverse) / values.shape[-1]


def over_rows(start, size, step, chunk=16):
    def body(i, carry):
        step(pl.ds(pl.multiple_of(start + i * chunk, chunk), chunk))
        return carry

    lax.fori_loop(0, size // chunk, body, 0)


def fold(total, values):
    part = values[0:8]
    for first in range(8, values.shape[0], 8):
        part = part + values[first : first + 8]
    total[...] += part


TWO = ((0, 96), (96, 96))
THREE = ((0, 64), (64, 64), (128, 64))


def dot(left, right, a, b):
    return lax.dot_general(left, right, (((a,), (b,)), ((), ())), preferred_element_type=F32)


def repeat(count, step):
    def body(i, carry):
        step(i)
        return carry

    lax.fori_loop(0, count, body, 0)


def whole(i, size):
    return pl.ds(pl.multiple_of(i * size, size), size)


def grid_of(rows, columns):
    return (
        lax.broadcasted_iota(jnp.int32, (rows, columns), 0),
        lax.broadcasted_iota(jnp.int32, (rows, columns), 1),
    )


def picks(rows, columns, chosen):
    return jnp.where(chosen(*grid_of(rows, columns)), 1.0, 0.0).astype(BF16)


def quad_order(unit):
    return (((unit >> 5) & 3) << 7) + ((unit >> 7) << 5) + (unit & 31)


def swap_halves(values):
    lane = lax.broadcasted_iota(jnp.int32, values.shape, 1)
    up = pltpu.roll(values, 80, 1)
    down = pltpu.roll(values, 48, 1)
    return jnp.where(lane < 48, up, down)


def around(spot, axes):
    return [spot.along(a, by) for a in axes for by in (1, -1)] + [spot.sibling]


def layer_kernel(
    tokens, gain_attn, gain_mlp, cot, w_query, w_key, w_value, w_out, w_gate, w_up, w_down, marks,
    normed_out, result_out, token_out, gains_out, att_out, out_out, gate_out, up_out, dn_out,
    normed, cots, second, part, got, passed, near, work, att_two, own_out, aq, ao, d_att, wo,
    gu, gu_own, dn, d_gu, d_dn, own, grad_hidden, q, kv, prob, mix, cosine, sine,
    marks_two, gains, middle_all, back_all, total, grad_mix, grad_kv, far_kv,
    gu_in, dn_in, att_in, out_in, gain_c, gain_y, gain_x, gain_z,
    ready, send_sem, recv_sem,
):
    spot = Spot()
    wires = Wires(send_sem, recv_sem)
    x, y, z, c = spot.x, spot.y, spot.z, spot.c
    neighbours = (
        around(spot, "xyz")
        + [spot.along(a, 2) for a in "xyz"]
        + [spot.partner]
        + [spot.in_quad(by)[1] for by in (1, 2, 3)]
    )
    greet(neighbours)

    def tell(which, devices):
        for who in devices:
            pl.semaphore_signal(ready.at[which], inc=1, device_id=who, device_id_type=MESH)

    def hear(which, count):
        pl.semaphore_wait(ready.at[which], count)

    for i, gain in enumerate((gain_attn, gain_mlp)):
        gains[i : i + 1, :] = jnp.concatenate([gain[j : j + 1, :] for j in range(12)], axis=1)

    def normalise(span):
        rows = tokens[span, :].astype(F32)
        own[span, :] = (rows * norm_scale(rows) * gains[0:1, :]).astype(BF16)

    over_rows(0, OWN, normalise)

    def three(first):
        return lambda r, k: r + first == k

    columns = (
        dot(w_query[...], picks(192, 384, three(0)), 1, 0)
        + dot(w_key[...], picks(96, 384, three(192)), 1, 0)
        + dot(w_value[...], picks(96, 384, three(288)), 1, 0)
    )
    att_two[0] = columns.astype(BF16)
    own_out[0] = jnp.zeros((16, D), BF16)
    own_out[0, 0:12] = w_out[...]
    greeted(neighbours)

    swaps = [
        wires.send(att_two.at[0], att_two.at[1], spot.partner),
        wires.send(own_out.at[0], own_out.at[1], spot.partner),
    ]
    rows_y = [PairGather(wires, spot, "y", normed, own, s, n) for s, n in TWO]
    for g in rows_y:
        g.start()
    marks_kept = wires.move(marks, marks_two.at[c])
    marks_got = wires.send(marks, marks_two.at[c], spot.sibling)

    order = picks(512, 512, lambda r, k: quad_order(r) == k)
    for shard, first in ((w_gate, 0), (w_up, 128)):
        moved = dot(shard[...], order, 1, 0).astype(BF16)
        for i in range(4):
            gu_own[i, :, first : first + 128] = moved[:, i * 128 : i * 128 + 128]
    gu_lanes = whole(y, 256)
    gu_here = gu.at[whole(z * 4 + spot.quad, 96), gu_lanes]
    gu_kept = wires.move(gu_own.at[spot.quad], gu_here)
    gu_swap = []
    for by in (1, 2, 3):
        other, who = spot.in_quad(by)
        gu_swap.append(wires.send(gu_own.at[other], gu_here, who))

    def trig(core):
        def step(i):
            span = whole(i, 128)
            row, lane = grid_of(128, 128)
            number = marks_two[core, pl.ds(spot.high * 6 + i, 1), :]
            ones = jnp.ones((128, 128), BF16)
            where = jnp.zeros((128, 128), F32)
            for digit, factor in ((number >> 5, 32.0), (number & 31, 1.0)):
                spread = jnp.where(row == lane, digit.astype(F32), 0.0).astype(BF16)
                where = where + factor * dot(spread, ones, 1, 0)
            grad_kv[core, span, 0:128] = where
            turns = jnp.where(lane < 48, lane, lane - 48).astype(F32) * (2.0 / HD)
            angle = where * jnp.exp(-math.log(ROPE_BASE) * turns)
            inside = lane < HD
            cosine[core, span, :] = jnp.where(inside, jnp.cos(angle), 0.0)
            wave = jnp.sin(angle)
            sine[core, span, :] = jnp.where(inside, jnp.where(lane < 48, -wave, wave), 0.0)

        repeat(6, step)

    marks_kept.wait()
    trig(c)
    for copy in swaps:
        copy.wait_recv()

    def slot_of(pos):
        return (pos % 2) * 2 + pos // 2

    slot = slot_of(x)
    pick = jnp.where(spot.high == c, 0, 1)
    low, high = pl.ds(0, 48), pl.ds(48, 48)
    att_kept = [
        wires.move(att_two.at[pick], aq.at[z, slot]),
        wires.move(own_out.at[pick], ao.at[z, slot]),
    ]
    att_side, out_side = [], []
    for by in (1, -1, 2):
        att_side.append(
            wires.send(att_two.at[pick, low], aq.at[z, slot, low], spot.along("z", by))
        )
        att_side.append(
            wires.send(att_two.at[pick, high], aq.at[z, slot, high], spot.along("x", by))
        )
    for by in (1, -1, 2):
        out_side.append(wires.send(own_out.at[pick], ao.at[z, slot], spot.along("x", by)))
    for g in rows_y:
        g.rest()
    att_line = [
        RingGather(wires, spot, "x", lambda pos, h: aq.at[pl.ds(2 * h, 2), slot_of(pos), low]),
        RingGather(wires, spot, "z", lambda pos, h: aq.at[pos, pl.ds(2 * h, 2), high]),
    ]
    out_line = RingGather(wires, spot, "z", lambda pos, h: ao.at[pos, pl.ds(2 * h, 2)])
    cot_x = [PairGather(wires, spot, "x", cots, cot, s, n) for s, n in TWO]
    marks_got.wait_recv()
    trig(1 - c)
    for copy in att_kept:
        copy.wait()
    for copy in att_side:
        copy.wait_recv()
    for line in att_line:
        line.begin()
    for g in rows_y:
        g.forward()
    rows_y[0].near()
    for line in att_line:
        line.forward()
    for copy in out_side:
        copy.wait_recv()
    out_line.begin()
    dn_here = dn.at[y, z]
    dn_kept = wires.move(w_down, dn_here)
    first_rows, last_rows = pl.ds(0, 16), pl.ds(16, 16)
    dn_side = []
    for by in (1, -1, 2):
        for axis, rows in (("z", first_rows), ("y", last_rows)):
            dn_side.append(
                wires.send(w_down.at[rows], dn.at[y, z, rows], spot.along(axis, by))
            )
    cot_x[0].start()
    cot_x[0].rest()
    rows_y[1].near()
    for line in att_line:
        line.near()
        line.far()

    def out_row(r, k):
        unit = jnp.where(r < 128, r, r - 32)
        real = (r < 96) | ((r >= 128) & (r < 224))
        return real & (unit + ((unit * 5462) >> 16) * 4 == k)

    def project(core, pos):
        both = dot(normed[core, pos], aq[...].reshape(D, 384), 1, 0)
        span = whole(pos, OWN)
        cos, sin = cosine[core, span, :], sine[core, span, :]
        tile = [both[:, 128 * i : 128 * i + 128] for i in range(3)]
        lane = lax.broadcasted_iota(jnp.int32, tile[0].shape, 1)

        def turned(values):
            return (values * cos + swap_halves(values) * sin).astype(BF16)

        q[core, span, 0:128] = turned(tile[0])
        q[core, span, 128:256] = turned(
            jnp.where(lane < 32, pltpu.roll(tile[0], 32, 1), pltpu.roll(tile[1], 32, 1))
        )
        after = pl.ds(pl.multiple_of(WIN + pos * OWN, 64), OWN)
        kv[core, after, 0:128] = turned(
            jnp.where(lane < 64, pltpu.roll(tile[1], 64, 1), pltpu.roll(tile[2], 64, 1))
        )
        kv[core, after, 128:256] = jnp.where(lane < HD, pltpu.roll(tile[2], 96, 1), 0.0).astype(
            BF16
        )

    for g in rows_y:
        g.kept.wait()
    repeat(3, lambda i: project(c, turn(y, i - 1)))
    for g in rows_y:
        for copy in g.shared[:3]:
            copy.wait_recv()
    repeat(3, lambda i: project(1 - c, turn(y, i - 1)))
    for g in rows_y:
        g.far()
    gu_kept.wait()
    for copy in gu_swap:
        copy.wait_recv()
    gu_side = RingGather(
        wires, spot, "y", lambda pos, h: gu.at[whole(z * 2 + h, 192), whole(pos, 256)]
    )
    gu_side.begin()
    out_line.forward()
    project(c, turn(y, 2))
    for g in rows_y:
        g.shared[3].wait_recv()
    project(1 - c, turn(y, 2))
    kv_got = wires.send(kv.at[:, pl.ds(768, WIN)], kv.at[:, pl.ds(0, WIN)], spot.along("x", 2))
    normed_kept = wires.move(normed, normed_out)
    left = wires.started()
    cot_x[0].forward()
    cot_x[0].near()
    gu_line = RingGather(
        wires, spot, "z", lambda pos, h: gu.at[whole(pos, 384), pl.ds(h * 512, 512)]
    )

    scale = HD ** (-0.5)

    def attend(core, run, head):
        span = whole(run, WIN)
        lanes = whole(head, 128)
        window = pl.ds(pl.multiple_of(run * WIN, WIN), SEQ)
        scores = dot(q[core, span, lanes], kv[core, window, 0:128], 1, 1) * scale
        row, column = grid_of(WIN, SEQ)
        spot_of = spot.high * HALF + run * WIN + row[:, 0:1]
        begin = jnp.maximum(
            (spot_of >> 9) << 9, spot_of - grad_kv[core, span, 0:1].astype(jnp.int32)
        )
        begin = begin - (spot.high * HALF + run * WIN) + WIN
        allowed = (column >= begin) & (column <= row + WIN)
        scores = jnp.where(allowed, scores, MASKED)
        weights = jnp.exp(scores - jnp.max(scores, axis=-1, keepdims=True))
        share = weights / jnp.sum(weights, axis=-1, keepdims=True)
        rounded = share.astype(BF16)
        prob[core, run, head] = rounded
        values = dot(rounded, kv[core, window, 128:256], 1, 0)
        mix[core, span, lanes] = values.astype(BF16)

    repeat(4, lambda i: attend(i // 2, 1, i % 2))
    gu_side.forward()
    dn_kept.wait()
    for copy in dn_side:
        copy.wait_recv()
    dn_line = [
        RingGather(wires, spot, "y", lambda pos, h: dn.at[pos, pl.ds(2 * h, 2), first_rows]),
        RingGather(wires, spot, "z", lambda pos, h: dn.at[pl.ds(2 * h, 2), pos, last_rows]),
    ]
    for line in dn_line:
        line.begin()
    repeat(4, lambda i: attend(i // 2, 2, i % 2))
    out_line.near()
    out_line.far()
    out_rows = picks(256, 256, out_row)
    wo[...] = dot(out_rows, ao[...].reshape(256, D), 1, 0).astype(BF16).reshape(4, 4, 16, D)

    def project_out(core, half):
        rows = mix[core, half * 384 : half * 384 + 384, :]
        out = dot(rows, wo[...].reshape(256, D), 1, 0).astype(BF16)
        part[core, half * 2 : half * 2 + 2] = out.reshape(2, OWN, D)

    def share_all(sums):
        for s in sums:
            s.share()

    def back_hidden(s):
        def step(core):
            rows = cots[core, :, pl.ds(s * 64, 64)].reshape(256, D)
            grad_hidden[core * 3 + s] = dot(rows, dn[...].reshape(512, D), 1, 1).astype(BF16)

        repeat(2, step)

    sums_y = [PairScatter(wires, spot, "y", part, got, passed, near, s, n) for s, n in THREE]
    rows_x = [PairGather(wires, spot, "x", second, own, s, n) for s, n in THREE]
    repeat(2, lambda i: project_out(i, 1))
    gu_side.near()
    gu_side.far()
    gu_line.start()
    kv_got.wait_recv()
    cot_x[1].start()
    repeat(4, lambda i: attend(i // 2, 0, i % 2))
    cot_x[1].rest()
    for line in dn_line:
        line.forward()
    project_out(1 - c, 0)
    sums_y[0].share()
    project_out(c, 0)
    for g in rows_y:
        g.close()
    normed_kept.wait()
    sums_y[0].first()
    cot_x[1].forward()
    gu_line.rest()
    cot_x[0].far()
    cot_x[0].finish()
    sums_y[0].left()
    sums_y[0].direct()
    sums_y[1].share()
    cot_x[1].near()
    sums_y[0].through()
    gu_line.forward()
    cot_x[1].far()
    sums_y[0].gone()
    sums_y[1].first()
    sums_y[2].share()
    for line in dn_line:
        line.near()
        line.far()
    cot_x[1].finish()

    def middle_rows(s):
        def use(span):
            middle = tokens[span, :].astype(F32) + s.total(span)
            middle_all[span, :] = middle
            own[span, :] = (middle * norm_scale(middle) * gains[1:2, :]).astype(BF16)

        return use

    def gather_next(i):
        s = sums_y[i]
        s.arrive()
        over_rows(s.start_row, s.size, middle_rows(s))
        s.close()
        rows_x[i].start()

    gather_next(0)
    sums_y[1].direct()
    back_hidden(0)
    sums_y[1].through()
    rows_x[0].rest()
    grad_kv[...] = jnp.zeros_like(grad_kv)
    wires.done(left)
    rows_x[0].forward()
    sums_y[1].gone()
    sums_y[2].first()
    back_hidden(1)
    gather_next(1)
    sums_y[2].direct()
    rows_x[0].near()
    back_hidden(2)
    sums_y[2].through()
    rows_x[1].rest()
    rows_x[0].far()
    rows_x[1].forward()
    gu_line.near()
    gu_line.far()
    rows_x[0].finish()

    def feed(core, i):
        span = pl.ds(*THREE[i])
        size = 4 * THREE[i][1]
        rows = second[core, :, span].reshape(size, D)
        both = dot(rows, gu[...], 1, 0)
        upstream = grad_hidden[core * 3 + i].astype(F32)
        for j in range(4):
            gate = both[:, j * 256 : j * 256 + 128]
            upward = both[:, j * 256 + 128 : j * 256 + 256]
            sent = upstream[:, j * 128 : j * 128 + 128]
            sigmoid = jax.nn.sigmoid(gate)
            silu = gate * sigmoid
            slope = sigmoid * (1.0 + gate * (1.0 - sigmoid))
            for first, values in (
                (1024 + j * 128, silu * upward),
                (j * 256, sent * upward * slope),
                (j * 256 + 128, sent * silu),
            ):
                rounded = values.astype(BF16).reshape(4, THREE[i][1], 128)
                work[core, :, span, first : first + 128] = rounded
        back = dot(work[core, :, span, 0:1024].reshape(size, 1024), gu[...], 1, 1)
        part[core, :, span] = back.astype(BF16).reshape(4, THREE[i][1], D)

    sums_x = [PairScatter(wires, spot, "x", part, got, passed, near, s, n) for s, n in THREE]
    grads_y = [PairGather(wires, spot, "y", normed, own, s, n) for s, n in THREE]

    def feed_share(i):
        feed(1 - c, i)
        sums_x[i].share()

    gather_next(2)
    early = wires.started()
    wires.again()
    feed_share(0)
    rows_x[2].rest()
    rows_x[1].near()
    feed(c, 0)
    rows_x[2].forward()
    sums_x[0].first()
    rows_x[1].far()
    sums_x[0].direct()
    rows_x[1].finish()
    rows_x[2].near()
    feed_share(1)
    rows_x[2].far()
    feed(c, 1)
    sums_x[1].first()
    sums_x[0].through()
    rows_x[2].finish()
    sums_x[1].direct()
    feed_share(2)
    feed(c, 2)
    sums_x[2].first()
    sums_x[1].through()
    wires.done(early)
    tell(0, [spot.along("z", 1), spot.along("z", -1)])

    def grad_gate_up(i):
        lanes = whole(i, 256)
        rows = second[:, :, :, lanes].reshape(8 * OWN, 256)
        sent = work[:, :, :, 0:1024].reshape(8 * OWN, 1024)
        d_gu[lanes, :] = dot(rows, sent, 0, 0).astype(BF16)

    def grad_down(i):
        lanes = pl.ds(pl.multiple_of(1024 + i * 256, 256), 256)
        rows = work[:, :, :, lanes].reshape(8 * OWN, 256)
        grad = dot(rows, cots[...].reshape(8 * OWN, D), 0, 0).astype(BF16)
        d_dn[pl.ds(i * 2, 2)] = grad.reshape(2, 4, 32, D)

    def down(i):
        rows = work[i // 2, pl.ds((i % 2) * 2, 2), :, 1024:D].reshape(384, 512)
        second[i // 2, pl.ds((i % 2) * 2, 2)] = (
            dot(rows, dn[...].reshape(512, D), 1, 0).astype(BF16).reshape(2, OWN, D)
        )

    def back_rows(s):
        def use(span):
            grad = s.total(span)
            rows = middle_all[span, :]
            inverse = norm_scale(rows)
            back = cot[span, :].astype(F32) + norm_back(grad, rows, inverse, gains[1:2, :])
            back_all[span, :] = back
            own[span, :] = back.astype(BF16)
            fold(total, grad * rows * inverse)

        return use

    def gather_back(i):
        s = sums_x[i]
        s.arrive()
        rows_x[i].close()
        over_rows(s.start_row, s.size, back_rows(s))
        s.close()
        grads_y[i].start()

    def mix_back(i):
        def step(core):
            span = pl.ds(*THREE[i])
            rows = normed[core, :, span].reshape(256, D)
            grad = dot(rows, wo[...].reshape(256, D), 1, 1).astype(BF16)
            for pos in range(4):
                start = pos * OWN + THREE[i][0]
                grad_mix[core, start : start + 64, :] = grad[pos * 64 : pos * 64 + 64]

        repeat(2, step)

    total[...] = jnp.zeros_like(total)
    gather_back(0)
    sums_x[2].direct()
    repeat(2, grad_gate_up)
    grads_y[0].rest()
    repeat(2, lambda i: grad_gate_up(2 + i))
    gather_back(1)
    grads_y[0].forward()
    sums_x[2].through()
    grads_y[1].rest()
    repeat(2, lambda i: grad_gate_up(4 + i))
    hear(0, 2)
    gu_sum = [
        LineScatter(
            wires, spot, "z",
            lambda pos, h, lot=lot: d_gu.at[whole(pos * 4 + lot * 2 + h, 96)],
            lambda h, lot=lot: gu.at[pl.ds(lot * 192 + h * 96, 96)],
            lambda h, lot=lot: gu.at[pl.ds(384 + lot * 192 + h * 96, 96)],
            lambda side, h, lot=lot: gu.at[pl.ds(768 + side * 384 + lot * 192 + h * 96, 96)],
        )
        for lot in (0, 1)
    ]
    gu_got = []

    def gu_beside(lot):
        gu_sum[lot].finish()
        for by in (1, -1, 2):
            part_of = d_gu.at[whole(z * 2 + lot, 192), whole(turn(y, by), 256)]
            into = gu_in.at[y, pl.ds(lot * 192, 192)]
            gu_got.append(wires.send(part_of, into, spot.along("y", by)))

    gu_sum[0].first()
    grads_y[0].near()
    grads_y[1].forward()
    gather_back(2)
    grads_y[0].far()
    grad_down(0)
    grads_y[2].rest()
    grads_y[1].near()
    repeat(2, down)
    grads_y[2].forward()
    grads_y[0].finish()
    mix_back(0)
    gu_sum[0].second()
    gu_sum[1].first()
    grads_y[1].far()
    grad_down(1)
    grads_y[2].near()
    grads_y[1].finish()
    mix_back(1)
    grads_y[2].far()
    repeat(2, lambda i: down(2 + i))
    tell(1, around(spot, "xy") + [spot.along("z", 1), spot.along("z", -1)])
    again = wires.move(normed_out, cots)
    gain_c[c, 1:2] = jnp.sum(total[...], axis=0, keepdims=True)
    grads_y[2].finish()
    mix_back(2)
    left = wires.started()

    def attend_back(core, run, head):
        span = whole(run, WIN)
        lanes = whole(head, 128)
        window = pl.ds(pl.multiple_of(run * WIN, WIN), SEQ)
        rounded = prob[core, run, head]
        share = rounded.astype(F32)
        mixed = grad_mix[core, span, lanes]
        asked = q[core, span, lanes]
        grad = dot(mixed, kv[core, window, 128:256], 1, 1)
        inner = jnp.sum(share * grad, axis=-1, keepdims=True)
        scored = (share * (grad - inner)).astype(BF16)
        grad_kv[core, window, 0:128] += dot(scored, asked, 0, 0) * scale
        grad_kv[core, window, 128:256] += dot(rounded, mixed, 0, 0)
        grad_q = dot(scored, kv[core, window, 0:128], 1, 0) * scale
        cos, sin = cosine[core, span, :], sine[core, span, :]
        q[core, span, lanes] = (grad_q * cos - swap_halves(grad_q) * sin).astype(BF16)

    repeat(4, lambda i: attend_back(i // 2, 0, i % 2))
    far_from = grad_mix.at[:, pl.ds(0, WIN)]
    for core in (0, 1):
        far_from[core] = grad_kv[core, 0:WIN, :].astype(BF16)
    far_got = wires.send(far_from, far_kv, spot.along("x", 2))
    gu_sum[1].second()
    gu_beside(0)
    hear(1, 7)
    sums_m = [
        PairScatter(
            wires, spot, "x", second, work.at[0], work.at[1, 0], work.at[1, pl.ds(1, 2)], s, n
        )
        for s, n in TWO
    ]
    share_all(sums_m)
    repeat(4, lambda i: attend_back(i // 2, 1, i % 2))
    sums_m[0].first()
    sums_m[0].direct()
    repeat(4, lambda i: attend_back(i // 2, 2, i % 2))
    sums_m[1].first()
    sums_m[1].direct()
    dn_sum = LineScatter(
        wires, spot, "z",
        lambda pos, h: d_dn.at[pl.ds(2 * h, 2), pos],
        lambda h: dn.at[0, pl.ds(2 * h, 2)],
        lambda h: dn.at[1, pl.ds(2 * h, 2)],
        lambda side, h: dn.at[2 + side, pl.ds(2 * h, 2)],
    )
    dn_sum.first()
    far_got.wait_recv()
    for core in (0, 1):
        grad_kv[core, 768:1024, :] += far_kv[core].astype(F32)

    def turn_back(i):
        core, pos = i // 4, i % 4
        after = pl.ds(pl.multiple_of(WIN + pos * OWN, 64), OWN)
        span = whole(pos, OWN)
        cos, sin = cosine[core, span, :], sine[core, span, :]
        keyed = grad_kv[core, after, 0:128]
        keyed = pltpu.roll(keyed * cos - swap_halves(keyed) * sin, 64, 1)
        valued = pltpu.roll(grad_kv[core, after, 128:256], 32, 1)
        front = q[core, span, 0:128].astype(F32)
        behind = pltpu.roll(q[core, span, 128:256].astype(F32), 96, 1)
        lane = lax.broadcasted_iota(jnp.int32, front.shape, 1)
        q[core, span, 0:128] = jnp.where(lane < 96, front, behind).astype(BF16)
        q[core, span, 128:256] = jnp.where(lane < 64, behind, keyed).astype(BF16)
        kv[core, after, 0:128] = jnp.where(lane < 32, keyed, valued).astype(BF16)

    repeat(8, turn_back)
    gu_beside(1)

    def normed_back(core):
        def step(pos):
            after = pl.ds(pl.multiple_of(WIN + pos * 384, 128), 384)
            rows = jnp.concatenate([q[core, whole(pos, 384), :], kv[core, after, 0:128]], axis=1)
            grad = dot(rows, aq[...].reshape(D, 384), 1, 1).astype(BF16)
            part[core, pl.ds(pos * 2, 2)] = grad.reshape(2, OWN, D)

        repeat(2, step)

    sums_n = [PairScatter(wires, spot, "y", part, got, passed, near, s, n) for s, n in THREE]
    normed_back(1 - c)
    share_all(sums_n)
    normed_back(c)
    sums_n[0].first()
    dn_sum.second()
    again.wait()

    def grad_columns(i):
        rows = cots[:, :, :, whole(i, 384)].reshape(8 * OWN, 384)
        asked = dot(rows, q[...].reshape(8 * OWN, 256), 0, 0)
        other = dot(rows, kv[:, pl.ds(WIN, HALF), 0:128].reshape(8 * OWN, 128), 0, 0)
        d_att[i, :, :, 0:256] = asked.astype(BF16).reshape(4, 96, 256)
        d_att[i, :, :, 256:384] = other.astype(BF16).reshape(4, 96, 128)
        held = aq[i].reshape(384, 384).astype(F32)
        folded = (
            held[:, 0:128] * asked[:, 0:128]
            + held[:, 128:256] * asked[:, 128:256]
            + held[:, 256:384] * other
        )
        gain_c[c, 0:1, whole(i, 384)] = jnp.sum(folded.T, axis=0, keepdims=True)

    repeat(2, grad_columns)
    sums_n[1].first()
    sums_n[2].first()
    repeat(2, lambda i: grad_columns(2 + i))
    gain_c[c, 0:1] = gain_c[c, 0:1] / gains[0:1, :]
    tell(2, [spot.along(a, by) for a in "xz" for by in (1, -1)])
    gain_got = [wires.send(gain_c.at[c], gain_c.at[c], spot.sibling)]
    for s in sums_n:
        s.direct()
    for s in sums_m:
        s.through()

    hear(2, 4)
    att_sum = [
        LineScatter(
            wires, spot, "x",
            lambda pos, h: d_att.at[pl.ds(2 * h, 2), slot_of(pos), low],
            lambda h: aq.at[0, pl.ds(2 * h, 2), low],
            lambda h: aq.at[1, pl.ds(2 * h, 2), low],
            lambda side, h: aq.at[2 + side, pl.ds(2 * h, 2), low],
        ),
        LineScatter(
            wires, spot, "z",
            lambda pos, h: d_att.at[pos, pl.ds(2 * h, 2), high],
            lambda h: aq.at[0, pl.ds(2 * h, 2), high],
            lambda h: aq.at[1, pl.ds(2 * h, 2), high],
            lambda side, h: aq.at[2 + side, pl.ds(2 * h, 2), high],
        ),
    ]
    for line in att_sum:
        line.first()

    def out_rows_back(r, k):
        unit = jnp.where(k < 128, k, k - 32)
        real = (k < 96) | ((k >= 128) & (k < 224))
        return real & (unit + ((unit * 5462) >> 16) * 4 == r)

    grad_out = dot(mix[...].reshape(8 * OWN, 256), normed[...].reshape(8 * OWN, D), 0, 0)
    grad_out = dot(picks(256, 256, out_rows_back), grad_out.astype(BF16), 1, 0)
    wo[...] = grad_out.astype(BF16).reshape(4, 4, 16, D)
    out_sum = LineScatter(
        wires, spot, "z",
        lambda pos, h: wo.at[pos, pl.ds(2 * h, 2)],
        lambda h: ao.at[0, pl.ds(2 * h, 2)],
        lambda h: ao.at[1, pl.ds(2 * h, 2)],
        lambda side, h: ao.at[2 + side, pl.ds(2 * h, 2)],
    )
    out_sum.first()
    for s in sums_n:
        s.through()

    def add_gains(held, axis, into):
        for copy in gain_got:
            copy.wait_recv()
        summed = held[0]
        for i in range(1, held.shape[0]):
            summed = summed + held[i]
        if into is None:
            gains_out[...] = summed
            return []
        me = spot.me(axis)
        into[me] = summed
        return [wires.send(into.at[me], into.at[me], spot.along(axis, by)) for by in (1, -1, 2)]

    gain_got = add_gains(gain_c, "x", gain_x)
    wires.done(left)
    for line in att_sum:
        line.second()

    for copy in gu_got:
        copy.wait_recv()
    mine = d_gu.at[whole(z, 384), whole(y, 256)]
    add_into(mine, mine, *[gu_in.at[turn(y, by)] for by in (1, -1, 2)])
    gu_done = []
    for by in (1, 2, 3):
        other, who = spot.in_quad(by)
        rows = d_gu.at[whole(z * 4 + other, 96), whole(y, 256)]
        gu_done.append(wires.send(rows, gu_own.at[spot.quad], who))
    gain_got = add_gains(gain_x, "z", gain_z)
    out_sum.second()

    def token_rows(s):
        def use(span):
            grad = s.total(span)
            rows = tokens[span, :].astype(F32)
            inverse = norm_scale(rows)
            out = back_all[span, :] + norm_back(grad, rows, inverse, gains[0:1, :])
            part[c, y, span] = out.astype(BF16)

        return use

    def result_rows(s):
        def use(span):
            second[c, x, span] = (middle_all[span, :] + s.total(span)).astype(BF16)

        return use

    token_kept = []

    def token_part(i):
        s = sums_n[i]
        s.arrive()
        over_rows(s.start_row, s.size, token_rows(s))
        token_kept.append(wires.move(part.at[c, y, s.rows()], token_out.at[s.rows()]))

    def result_part(s):
        s.arrive()
        over_rows(s.start_row, s.size, result_rows(s))

    att_got, out_got = [], []
    for line in att_sum:
        line.finish()
    for by in (1, -1, 2):
        far, who = turn(z, by), spot.along("z", by)
        att_got.append(wires.send(d_att.at[far, slot, low], att_in.at[z, low], who))
        far, who = slot_of(turn(x, by)), spot.along("x", by)
        att_got.append(wires.send(d_att.at[z, far, high], att_in.at[x, high], who))
    dn_sum.finish()
    dn_got = [
        wires.send(d_dn.at[turn(y, by), z], dn_in.at[y], spot.along("y", by)) for by in (1, -1, 2)
    ]
    token_part(0)
    out_sum.finish()
    for by in (1, -1, 2):
        far, who = slot_of(turn(x, by)), spot.along("x", by)
        out_got.append(wires.send(wo.at[z, far], out_in.at[x], who))
    for s in sums_m:
        result_part(s)
    result_kept = wires.move(second.at[c, x], result_out)
    gain_got = add_gains(gain_z, "y", gain_y)
    kept_rows = d_gu.at[whole(z * 4 + spot.quad, 96), whole(y, 256)]
    gu_own[spot.quad] = kept_rows[...]
    for copy in att_got:
        copy.wait_recv()
    for span, me in ((low, z), (high, x)):
        others = [att_in.at[turn(me, by), span] for by in (1, -1, 2)]
        add_into(att_two.at[0, span], d_att.at[z, slot, span], *others)
    swaps = [wires.send(att_two.at[0], att_two.at[1], spot.partner)]
    for copy in out_got:
        copy.wait_recv()
    others = [out_in.at[turn(x, by)] for by in (1, -1, 2)]
    add_into(own_out.at[0], wo.at[z, slot], *others)
    swaps.append(wires.send(own_out.at[0], own_out.at[1], spot.partner))
    token_part(1)
    for copy in gu_done:
        copy.wait_recv()
    order = picks(512, 512, lambda r, k: quad_order(k) == r)
    for into, first in ((gate_out, 0), (up_out, 128)):
        moved = jnp.concatenate([gu_own[i, :, first : first + 128] for i in range(4)], axis=1)
        into[...] = dot(moved, order, 1, 0)
    for copy in dn_got:
        copy.wait_recv()
    add_into(
        dn_out, d_dn.at[y, z], *[dn_in.at[turn(y, by)] for by in (1, -1, 2)]
    )
    token_part(2)
    add_gains(gain_y, None, None)
    for copy in swaps:
        copy.wait_recv()
    att_out[...] = att_two[pick]
    out_out[...] = own_out[pick]
    result_kept.wait()
    for copy in token_kept:
        copy.wait()
    wires.close()


def finish_kernel(
    result, token, gains, att, out, gate, up, dn,
    result_out, token_out, attn_out, mlp_out, query_out, key_out, value_out, out_out,
    gate_out, up_out, dn_out,
):
    for src, dst in (
        (result, result_out), (token, token_out), (gate, gate_out), (up, up_out), (dn, dn_out)
    ):
        dst[...] = src[...]
    for i, into in enumerate((attn_out, mlp_out)):
        for j in range(12):
            into[j : j + 1, :] = gains[i : i + 1, j * 128 : j * 128 + 128]
    rows = att[...]

    def three(first):
        return lambda r, k: r == k + first

    query_out[...] = dot(rows, picks(384, 192, three(0)), 1, 0)
    key_out[...] = dot(rows, picks(384, 96, three(192)), 1, 0)
    value_out[...] = dot(rows, picks(384, 96, three(288)), 1, 0)
    out_out[...] = out[0:12, :].astype(F32)


def layer_call(
    tokens, gain_attn, gain_mlp, cot, w_query, w_key, w_value, w_out, w_gate, w_up, w_down, marks
):
    sends, receives = 120, 170
    shape = jax.ShapeDtypeStruct
    outs = (
        (shape((2, 4, OWN, D), BF16), ANY),
        (shape((OWN, D), BF16), ANY),
        (shape((OWN, D), BF16), ANY),
        (shape((2, D), F32), VMEM),
        (shape((96, 384), BF16), VMEM),
        (shape((16, D), BF16), VMEM),
        (shape((96, 512), F32), VMEM),
        (shape((96, 512), F32), VMEM),
        (shape((32, D), F32), VMEM),
    )
    scratch = [
        ((2, 4, OWN, D), BF16),
        ((2, 4, OWN, D), BF16),
        ((2, 4, OWN, D), BF16),
        ((2, 4, OWN, D), BF16),
        ((4, OWN, D), BF16),
        ((OWN, D), BF16),
        ((2, OWN, D), BF16),
        ((2, 4, OWN, D), BF16),
        ((2, 96, 384), BF16),
        ((2, 16, D), BF16),
        ((4, 4, 96, 384), BF16),
        ((4, 4, 16, D), BF16),
        ((4, 4, 96, 384), BF16),
        ((4, 4, 16, D), BF16),
        ((D, 1024), BF16),
        ((4, 96, 256), BF16),
        ((4, 4, 32, D), BF16),
        ((D, 1024), BF16),
        ((4, 4, 32, D), BF16),
        ((OWN, D), BF16),
        ((6, 256, 512), BF16),
        ((2, HALF, 256), BF16),
        ((2, HALF + WIN, 256), BF16),
        ((2, 3, 2, WIN, SEQ), BF16),
        ((2, HALF, 256), BF16),
        ((2, HALF, 128), F32),
        ((2, HALF, 128), F32),
        ((2, 12, 128), jnp.int32),
        ((2, D), F32),
        ((OWN, D), F32),
        ((OWN, D), F32),
        ((8, D), F32),
        ((2, HALF, 256), BF16),
        ((2, HALF + WIN, 256), F32),
        ((2, WIN, 256), BF16),
        ((4, 384, 256), BF16),
        ((4, 32, D), BF16),
        ((4, 96, 384), BF16),
        ((4, 16, D), BF16),
        ((2, 2, D), F32),
        ((4, 2, D), F32),
        ((4, 2, D), F32),
        ((4, 2, D), F32),
    ]
    outs_raw = pl.pallas_call(
        layer_kernel,
        out_shape=tuple(o[0] for o in outs),
        in_specs=[VMEM] * 12,
        out_specs=[o[1] for o in outs],
        scratch_shapes=[pltpu.VMEM(*s) for s in scratch]
        + [
            pltpu.SemaphoreType.REGULAR((3,)),
            pltpu.SemaphoreType.DMA((sends,)),
            pltpu.SemaphoreType.DMA((receives,)),
        ],
        compiler_params=pltpu.CompilerParams(
            collective_id=1, has_side_effects=True, vmem_limit_bytes=64 << 20
        ),
        name="layer",
    )(tokens, gain_attn, gain_mlp, cot, w_query, w_key, w_value, w_out, w_gate, w_up, w_down, marks)
    finals = (
        shape((OWN, D), BF16),
        shape((OWN, D), BF16),
        shape((12, 128), F32),
        shape((12, 128), F32),
        shape((96, 192), F32),
        shape((96, 96), F32),
        shape((96, 96), F32),
        shape((12, D), F32),
        shape((96, 512), F32),
        shape((96, 512), F32),
        shape((32, D), F32),
    )
    return pl.pallas_call(
        finish_kernel,
        out_shape=finals,
        in_specs=[VMEM] * 8,
        out_specs=[VMEM] * 11,
        name="finish",
    )(*outs_raw[1:])


def shards(
    tokens,
    gain_attn,
    gain_mlp,
    w_query,
    w_key,
    w_value,
    w_out,
    w_gate,
    w_up,
    w_down,
    segments,
    positions,
    cotangent,
):
    del segments
    done = layer_call(
        tokens,
        gain_attn.reshape(12, 128),
        gain_mlp.reshape(12, 128),
        cotangent,
        w_query,
        w_key,
        w_value,
        w_out,
        w_gate,
        w_up,
        w_down,
        positions.reshape(12, 128),
    )
    return (*done[:2], done[2].reshape(D), done[3].reshape(D), *done[4:])


def solution(mesh):
    placed = (
        P(("dp", "tensor"), None),
        P(),
        P(),
        P("dp", "tensor"),
        P("dp", "tensor"),
        P("dp", "tensor"),
        P(("tensor", "dp"), None),
        P("dp", "tensor"),
        P("dp", "tensor"),
        P(("tensor", "dp"), None),
        P("dp"),
        P("dp"),
        P(("dp", "tensor"), None),
    )
    return jax.shard_map(
        shards,
        mesh=mesh,
        in_specs=placed,
        out_specs=(
            P(("dp", "tensor"), None),
            P(("dp", "tensor"), None),
            P(),
            P(),
            P("dp", "tensor"),
            P("dp", "tensor"),
            P("dp", "tensor"),
            P(("tensor", "dp"), None),
            P("dp", "tensor"),
            P("dp", "tensor"),
            P(("tensor", "dp"), None),
        ),
        check_vma=False,
    )
```

```python
import functools
import math

import jax
import jax.numpy as jnp
from jax import lax
from jax.experimental import pallas as pl
from jax.experimental.pallas import tpu as pltpu
from jax.sharding import PartitionSpec as P

HD = 96
SEQ = 512
D = 1536
OWN = 192
HALF = 768
WIN = 256

EPSILON = 1e-05
ROPE_BASE = 100000.0
MASKED = -1e30
MESH = pl.DeviceIdType.MESH
ANY = pl.BlockSpec(memory_space=pl.ANY)
VMEM = pl.BlockSpec(memory_space=pltpu.VMEM)
BF16 = jnp.bfloat16
F32 = jnp.float32


def place():
    dp = lax.axis_index("dp")
    tensor = lax.axis_index("tensor")
    return (tensor // 4) * 2 + (dp // 2) % 2, tensor % 4, dp // 4, dp % 2


def device(x, y, z, c):
    return (z * 4 + (x % 2) * 2 + c, (x // 2) * 4 + y)


def turn(pos, by):
    return (pos + by + 4) % 4


class Spot:
    def __init__(self):
        x, y, z, c = place()
        self.x, self.y, self.z, self.c = x, y, z, c
        self.high, self.low, self.other = x // 2, x % 2, 1 - c
        self.quad = self.low * 2 + c
        self.sibling = device(x, y, z, 1 - c)
        self.partner = device(turn(x, 2), y, z, 1 - c)

    def along(self, axis, by):
        x, y, z, c = self.x, self.y, self.z, self.c
        if axis == "x":
            return device(turn(x, by), y, z, c)
        if axis == "y":
            return device(x, turn(y, by), z, c)
        return device(x, y, turn(z, by), c)

    def me(self, axis):
        return {"x": self.x, "y": self.y, "z": self.z}[axis]

    def in_quad(self, by):
        other = turn(self.quad, by)
        return other, device(self.high * 2 + other // 2, self.y, self.z, other % 2)


def greet(devices):
    for who in devices:
        pl.semaphore_signal(
            pltpu.get_barrier_semaphore(), inc=1, device_id=who, device_id_type=MESH
        )


def greeted(devices):
    pl.semaphore_wait(pltpu.get_barrier_semaphore(), len(devices))


class Wires:
    def __init__(self, send_sem, recv_sem):
        self.send_sem, self.recv_sem = send_sem, recv_sem
        self.free = list(range(send_sem.shape[0]))
        self.count = 0
        self.sent = []

    def again(self):
        self.count = 0

    def take(self):
        held = min(self.free)
        self.free.remove(held)
        return held

    def forget(self, copy):
        self.free += [held for other, held in self.sent if other is copy]
        self.sent = [pair for pair in self.sent if pair[0] is not copy]

    def send(self, src, dst, who, start=True):
        held = self.take()
        assert self.count < self.recv_sem.shape[0]
        copy = pltpu.make_async_remote_copy(
            src_ref=src,
            dst_ref=dst,
            send_sem=self.send_sem.at[held],
            recv_sem=self.recv_sem.at[self.count],
            device_id=who,
            device_id_type=MESH,
        )
        self.count += 1
        if start:
            copy.start()
        self.sent.append((copy, held))
        return copy

    def move(self, src, dst):
        held = self.take()
        copy = pltpu.make_async_copy(src, dst, self.send_sem.at[held])
        copy.start()
        return Moved(self, copy, held)

    def done(self, copies):
        kept = []
        for copy, held in self.sent:
            if any(copy is other for other in copies):
                copy.wait_send()
                self.free.append(held)
            else:
                kept.append((copy, held))
        self.sent = kept

    def started(self):
        return [copy for copy, _ in self.sent]

    def close(self):
        self.done(self.started())


class Placed:
    def __init__(self, wires, stays, pieces):
        self.wires, self.stays = wires, stays
        self.others = [wires.send(*piece) for piece in pieces[1:]]
        self.own = wires.send(*pieces[0], start=False)
        held = wires.sent[-1][1]

        @pl.when(jnp.logical_not(stays))
        def _():
            self.own.start()

        @pl.when(stays)
        def _():
            kept = pltpu.make_async_copy(pieces[0][0], pieces[0][1], wires.send_sem.at[held])
            kept.start()
            kept.wait()

    def wait(self):
        for copy in self.others:
            copy.wait_recv()

        @pl.when(jnp.logical_not(self.stays))
        def _():
            self.own.wait_recv()

    def close(self):
        self.wires.done(self.others)

        @pl.when(jnp.logical_not(self.stays))
        def _():
            self.own.wait_send()

        self.wires.forget(self.own)


class Moved:
    def __init__(self, wires, copy, held):
        self.wires, self.copy, self.held = wires, copy, held

    def wait(self):
        self.copy.wait()
        self.wires.free.append(self.held)


def add_into(dst, *srcs, chunk=16):
    rows = dst.shape[-2]
    chunk = min(chunk, rows)

    def step(i, carry):
        span = pl.ds(pl.multiple_of(i * chunk, chunk), chunk)
        total = srcs[0][..., span, :].astype(F32)
        for src in srcs[1:]:
            total = total + src[..., span, :].astype(F32)
        dst[..., span, :] = total.astype(dst.dtype)
        return carry

    lax.fori_loop(0, rows // chunk, step, 0)


class RingGather:
    def __init__(self, wires, spot, axis, at):
        self.wires, self.at = wires, at
        self.me = spot.me(axis)
        self.next, self.prev = spot.along(axis, 1), spot.along(axis, -1)

    def start(self, own=None):
        self.own = own or (lambda half: self.at(self.me, half))
        send, at, me = self.wires.send, self.at, self.me
        self.right0 = send(self.own(0), at(me, 0), self.next)
        self.left1 = send(self.own(1), at(me, 1), self.prev)

    def rest(self):
        send, at, me = self.wires.send, self.at, self.me
        self.right1 = send(self.own(1), at(me, 1), self.next)
        self.left0 = send(self.own(0), at(me, 0), self.prev)

    def begin(self):
        self.start()
        self.rest()

    def forward(self):
        send, at, me = self.wires.send, self.at, self.me
        self.right0.wait_recv()
        before = at(turn(me, -1), 0)
        self.pass0 = send(before, before, self.next)
        self.left1.wait_recv()
        after = at(turn(me, 1), 1)
        self.pass1 = send(after, after, self.prev)

    def near(self):
        self.right1.wait_recv()
        self.left0.wait_recv()

    def far(self):
        self.pass0.wait_recv()
        self.pass1.wait_recv()

    def close(self):
        near = [self.right0, self.left1, self.right1, self.left0]
        self.wires.done(near + [self.pass0, self.pass1])


class PairGather:
    def __init__(self, wires, spot, axis, out, own, start, size):
        self.wires, self.spot, self.out, self.own = wires, spot, out, own
        self.rows = pl.ds(start, size)
        cut = size // 2

        def half_rows(half):
            return pl.ds(start + half * cut, cut)

        self.half_rows = half_rows
        self.ring = RingGather(
            wires, spot, axis, lambda pos, half: out.at[spot.c, pos, half_rows(half)]
        )
        self.me = spot.me(axis)

    def share(self, pos):
        block = self.out.at[self.spot.c, pos, self.rows]
        return self.wires.send(block, block, self.spot.sibling)

    def start(self):
        self.ring.start(lambda half: self.own.at[self.half_rows(half)])
        mine = self.own.at[self.rows]
        place_of = self.out.at[self.spot.c, self.me, self.rows]
        self.shared = [self.wires.send(mine, place_of, self.spot.sibling)]
        self.kept = self.wires.move(mine, place_of)

    def rest(self):
        self.ring.rest()

    def forward(self):
        self.ring.forward()

    def near(self):
        self.ring.near()
        self.shared.append(self.share(turn(self.me, -1)))
        self.shared.append(self.share(turn(self.me, 1)))

    def far(self):
        self.ring.far()
        self.shared.append(self.share(turn(self.me, 2)))

    def finish(self):
        for copy in self.shared:
            copy.wait_recv()
        self.kept.wait()

    def close(self):
        self.ring.close()
        self.wires.done(self.shared)


class PairScatter:
    def __init__(self, wires, spot, axis, part, got, passed, near, start, size):
        self.wires, self.spot = wires, spot
        self.me = spot.me(axis)
        self.next, self.prev = spot.along(axis, 1), spot.along(axis, -1)
        self.part, self.got, self.passed, self.near = part, got, passed, near
        self.start_row, self.size, self.cut = start, size, size // 2

    def rows(self, half=None):
        if half is None:
            return pl.ds(self.start_row, self.size)
        return pl.ds(self.start_row + half * self.cut, self.cut)

    def share(self, start=True):
        self.shared = self.wires.send(
            self.part.at[self.spot.other, :, self.rows()],
            self.got.at[:, self.rows()],
            self.spot.sibling,
            start,
        )

    def first(self):
        self.shared.wait_recv()
        pos = turn(self.me, 2)
        mine = self.got.at[pos, self.rows()]
        add_into(mine, self.part.at[self.spot.c, pos, self.rows()], mine)
        self.pass0 = self.wires.send(
            self.got.at[pos, self.rows(0)], self.passed.at[self.rows(0)], self.next
        )
        self.pass1 = self.wires.send(
            self.got.at[pos, self.rows(1)], self.passed.at[self.rows(1)], self.prev
        )

    def left(self):
        self.wires.done([self.pass0, self.pass1])

    def gone(self):
        self.wires.done(self.arriving)

    def direct(self):
        self.arriving = []
        for by, half, who, side in ((1, 1, self.next, 0), (-1, 0, self.prev, 1)):
            pos = turn(self.me, by)
            mine = self.got.at[pos, self.rows(half)]
            add_into(mine, self.part.at[self.spot.c, pos, self.rows(half)], mine)
            self.arriving.append(self.wires.send(mine, self.near.at[side, self.rows(half)], who))

    def through(self):
        after, before = turn(self.me, 1), turn(self.me, -1)
        for pos, half, who, side, arrived in (
            (after, 0, self.next, 0, self.pass0),
            (before, 1, self.prev, 1, self.pass1),
        ):
            arrived.wait_recv()
            mine = self.got.at[pos, self.rows(half)]
            add_into(
                mine,
                self.part.at[self.spot.c, pos, self.rows(half)],
                mine,
                self.passed.at[self.rows(half)],
            )
            self.arriving.append(self.wires.send(mine, self.near.at[side, self.rows(half)], who))

    def arrive(self):
        for copy in self.arriving:
            copy.wait_recv()

    def close(self):
        self.wires.done([self.shared, self.pass0, self.pass1] + self.arriving)

    def total(self, span):
        return (
            self.part[self.spot.c, self.me, span].astype(F32)
            + self.got[self.me, span].astype(F32)
            + self.near[0, span].astype(F32)
            + self.near[1, span].astype(F32)
        )


class LineScatter:
    def __init__(self, wires, spot, axis, at, passed, work, near):
        self.wires, self.at = wires, at
        self.me = spot.me(axis)
        self.next, self.prev = spot.along(axis, 1), spot.along(axis, -1)
        self.passed, self.work, self.near = passed, work, near

    def first(self, paced=False):
        send, me = self.wires.send, self.me
        far = turn(me, 2)
        self.pass0 = send(self.at(far, 0), self.passed(0), self.next)
        self.pass1 = send(self.at(far, 1), self.passed(1), self.prev)
        if not paced:
            self.direct()

    def direct(self):
        send, me = self.wires.send, self.me
        after, before = turn(me, 1), turn(me, -1)
        self.arriving = [
            send(self.at(after, 1), self.near(0, 1), self.next),
            send(self.at(before, 0), self.near(1, 0), self.prev),
        ]

    def second(self):
        for by, half, who, side, arrived in (
            (1, 0, self.next, 0, self.pass0),
            (-1, 1, self.prev, 1, self.pass1),
        ):
            arrived.wait_recv()
            add_into(self.work(half), self.at(turn(self.me, by), half), self.passed(half))
            self.arriving.append(self.wires.send(self.work(half), self.near(side, half), who))

    def finish(self):
        for copy in self.arriving:
            copy.wait_recv()
        for half in (0, 1):
            mine = self.at(self.me, half)
            add_into(mine, mine, self.near(0, half), self.near(1, half))


def norm_scale(values):
    return lax.rsqrt(jnp.mean(values * values, axis=-1, keepdims=True) + EPSILON)


def norm_back(upstream, values, inverse, gain):
    scaled = upstream * gain
    inner = jnp.sum(scaled * values, axis=-1, keepdims=True)
    return scaled * inverse - values * inner * (inverse * inverse * inverse) / values.shape[-1]


def over_rows(start, size, step, chunk=16):
    def body(i, carry):
        step(pl.ds(pl.multiple_of(start + i * chunk, chunk), chunk))
        return carry

    lax.fori_loop(0, size // chunk, body, 0)


def fold(total, values):
    part = values[0:8]
    for first in range(8, values.shape[0], 8):
        part = part + values[first : first + 8]
    total[...] += part


TWO = ((0, 96), (96, 96))
THREE = ((0, 64), (64, 64), (128, 64))


def dot(left, right, a, b):
    return lax.dot_general(left, right, (((a,), (b,)), ((), ())), preferred_element_type=F32)


def repeat(count, step):
    def body(i, carry):
        step(i)
        return carry

    lax.fori_loop(0, count, body, 0)


def whole(i, size):
    return pl.ds(pl.multiple_of(i * size, size), size)


def grid_of(rows, columns):
    return (
        lax.broadcasted_iota(jnp.int32, (rows, columns), 0),
        lax.broadcasted_iota(jnp.int32, (rows, columns), 1),
    )


def picks(rows, columns, chosen):
    return jnp.where(chosen(*grid_of(rows, columns)), 1.0, 0.0).astype(BF16)


def quad_order(unit):
    return (((unit >> 5) & 3) << 7) + ((unit >> 7) << 5) + (unit & 31)


def swap_halves(values):
    lane = lax.broadcasted_iota(jnp.int32, values.shape, 1)
    up = pltpu.roll(values, 80, 1)
    down = pltpu.roll(values, 48, 1)
    return jnp.where(lane < 48, up, down)


def around(spot, axes):
    return [spot.along(a, by) for a in axes for by in (1, -1)] + [spot.sibling]


def layer_kernel(
    tokens, gain_attn, gain_mlp, cot, w_query, w_key, w_value, w_out, w_gate, w_up, w_down, marks,
    normed_out, result_out, token_out, gains_out, att_out, out_out, gate_out, up_out, dn_out,
    normed, cots, second, part, got, passed, near, work, att_two, own_out, aq, ao, d_att, wo,
    gu, gu_own, dn, d_gu, d_dn, own, grad_hidden, q, kv, prob, mix, cosine, sine,
    marks_two, gains, middle_all, back_all, total, grad_mix, grad_kv, far_kv,
    gu_in, dn_in, att_in, out_in, gain_c, gain_y, gain_x, gain_z,
    ready, send_sem, recv_sem,
):
    spot = Spot()
    wires = Wires(send_sem, recv_sem)
    x, y, z, c = spot.x, spot.y, spot.z, spot.c
    neighbours = (
        around(spot, "xyz")
        + [spot.along(a, 2) for a in "xyz"]
        + [spot.partner]
        + [spot.in_quad(by)[1] for by in (1, 2, 3)]
        + [device(turn(x, by), y, z, 1 - c) for by in (1, -1)]
        + [device(turn(x, 2), y, turn(z, by), 1 - c) for by in (1, -1, 2)]
    )
    greet(neighbours)

    def tell(which, devices):
        for who in devices:
            pl.semaphore_signal(ready.at[which], inc=1, device_id=who, device_id_type=MESH)

    def hear(which, count):
        pl.semaphore_wait(ready.at[which], count)

    for i, gain in enumerate((gain_attn, gain_mlp)):
        gains[i : i + 1, :] = jnp.concatenate([gain[j : j + 1, :] for j in range(12)], axis=1)

    def normalise(span):
        rows = tokens[span, :].astype(F32)
        own[span, :] = (rows * norm_scale(rows) * gains[0:1, :]).astype(BF16)

    over_rows(0, OWN, normalise)

    def three(first):
        return lambda r, k: r + first == k

    columns = (
        dot(w_query[...], picks(192, 384, three(0)), 1, 0)
        + dot(w_key[...], picks(96, 384, three(192)), 1, 0)
        + dot(w_value[...], picks(96, 384, three(288)), 1, 0)
    )
    att_two[0] = columns.astype(BF16)
    own_out[0] = jnp.zeros((16, D), BF16)
    own_out[0, 0:12] = w_out[...]
    greeted(neighbours)

    def slot_of(pos):
        return (pos % 2) * 2 + pos // 2

    slot = slot_of(x)
    low, high = pl.ds(0, 48), pl.ds(48, 48)
    stays = spot.high == c
    there_x, there_c = jnp.where(stays, x, turn(x, 2)), jnp.where(stays, c, 1 - c)
    there = slot_of(there_x)
    line_z = [device(there_x, y, turn(z, by), there_c) for by in (0, 1, -1, 2)]
    line_x = [device(turn(there_x, by), y, z, there_c) for by in (0, 1, -1, 2)]
    att_side = [
        Placed(
            wires, stays, [(att_two.at[0, low], aq.at[z, there, low], who) for who in line_z]
        ),
        Placed(
            wires, stays, [(att_two.at[0, high], aq.at[z, there, high], who) for who in line_x]
        ),
    ]
    rows_y = [PairGather(wires, spot, "y", normed, own, s, n) for s, n in TWO]
    for g in rows_y:
        g.start()
    out_side = Placed(wires, stays, [(own_out.at[0], ao.at[z, there], who) for who in line_x])
    marks_kept = wires.move(marks, marks_two.at[c])
    marks_got = wires.send(marks, marks_two.at[c], spot.sibling)

    order = picks(512, 512, lambda r, k: quad_order(r) == k)
    for shard, first in ((w_gate, 0), (w_up, 128)):
        moved = dot(shard[...], order, 1, 0).astype(BF16)
        for i in range(4):
            gu_own[i, :, first : first + 128] = moved[:, i * 128 : i * 128 + 128]
    gu_lanes = whole(y, 256)
    gu_here = gu.at[whole(z * 4 + spot.quad, 96), gu_lanes]
    gu_kept = wires.move(gu_own.at[spot.quad], gu_here)
    gu_swap = []
    for by in (1, 2, 3):
        other, who = spot.in_quad(by)
        gu_swap.append(wires.send(gu_own.at[other], gu_here, who))

    def trig(core):
        def step(i):
            span = whole(i, 128)
            row, lane = grid_of(128, 128)
            number = marks_two[core, pl.ds(spot.high * 6 + i, 1), :]
            ones = jnp.ones((128, 128), BF16)
            where = jnp.zeros((128, 128), F32)
            for digit, factor in ((number >> 5, 32.0), (number & 31, 1.0)):
                spread = jnp.where(row == lane, digit.astype(F32), 0.0).astype(BF16)
                where = where + factor * dot(spread, ones, 1, 0)
            grad_kv[core, span, 0:128] = where
            turns = jnp.where(lane < 48, lane, lane - 48).astype(F32) * (2.0 / HD)
            angle = where * jnp.exp(-math.log(ROPE_BASE) * turns)
            inside = lane < HD
            cosine[core, span, :] = jnp.where(inside, jnp.cos(angle), 0.0)
            wave = jnp.sin(angle)
            sine[core, span, :] = jnp.where(inside, jnp.where(lane < 48, -wave, wave), 0.0)

        repeat(6, step)

    marks_kept.wait()
    trig(c)
    for g in rows_y:
        g.rest()
    att_line = [
        RingGather(wires, spot, "x", lambda pos, h: aq.at[pl.ds(2 * h, 2), slot_of(pos), low]),
        RingGather(wires, spot, "z", lambda pos, h: aq.at[pos, pl.ds(2 * h, 2), high]),
    ]
    out_line = RingGather(wires, spot, "z", lambda pos, h: ao.at[pos, pl.ds(2 * h, 2)])
    cot_x = [PairGather(wires, spot, "x", cots, cot, s, n) for s, n in TWO]
    for piece in att_side:
        piece.wait()
    for line in att_line:
        line.begin()
    marks_got.wait_recv()
    trig(1 - c)
    for g in rows_y:
        g.forward()
    rows_y[0].near()
    for line in att_line:
        line.forward()
    out_side.wait()
    out_line.begin()
    dn_here = dn.at[y, z]
    dn_kept = wires.move(w_down, dn_here)
    first_rows, last_rows = pl.ds(0, 16), pl.ds(16, 16)
    dn_side = []
    for by in (1, -1, 2):
        for axis, rows in (("z", first_rows), ("y", last_rows)):
            dn_side.append(
                wires.send(w_down.at[rows], dn.at[y, z, rows], spot.along(axis, by))
            )
    cot_x[0].start()
    cot_x[0].rest()
    rows_y[1].near()
    for line in att_line:
        line.near()
        line.far()

    def out_row(r, k):
        unit = jnp.where(r < 128, r, r - 32)
        real = (r < 96) | ((r >= 128) & (r < 224))
        return real & (unit + ((unit * 5462) >> 16) * 4 == k)

    scale = HD ** (-0.5)

    def project(core, pos):
        both = dot(normed[core, pos], aq[...].reshape(D, 384), 1, 0)
        span = whole(pos, OWN)
        cos, sin = cosine[core, span, :], sine[core, span, :]
        tile = [both[:, 128 * i : 128 * i + 128] for i in range(3)]
        lane = lax.broadcasted_iota(jnp.int32, tile[0].shape, 1)

        def turned(values, factor=None):
            values = values * cos + swap_halves(values) * sin
            return (values if factor is None else values * factor).astype(BF16)

        q[core, span, 0:128] = turned(tile[0], scale)
        q[core, span, 128:256] = turned(
            jnp.where(lane < 32, pltpu.roll(tile[0], 32, 1), pltpu.roll(tile[1], 32, 1)), scale
        )
        after = pl.ds(pl.multiple_of(WIN + pos * OWN, 64), OWN)
        kv[core, after, 0:128] = turned(
            jnp.where(lane < 64, pltpu.roll(tile[1], 64, 1), pltpu.roll(tile[2], 64, 1))
        )
        kv[core, after, 128:256] = jnp.where(lane < HD, pltpu.roll(tile[2], 96, 1), 0.0).astype(
            BF16
        )

    for g in rows_y:
        g.kept.wait()
    repeat(3, lambda i: project(c, turn(y, i - 1)))
    for g in rows_y:
        for copy in g.shared[:3]:
            copy.wait_recv()
    repeat(3, lambda i: project(1 - c, turn(y, i - 1)))
    for g in rows_y:
        g.far()
    gu_kept.wait()
    for copy in gu_swap:
        copy.wait_recv()
    gu_side = RingGather(
        wires, spot, "y", lambda pos, h: gu.at[whole(z * 2 + h, 192), whole(pos, 256)]
    )
    gu_side.begin()
    out_line.forward()
    project(c, turn(y, 2))

    def send_kv(core):
        last, first = kv.at[core, pl.ds(768, WIN)], kv.at[core, pl.ds(0, WIN)]
        return wires.send(last, first, spot.along("x", 2))

    kv_got = [send_kv(c)]
    dn_kept.wait()
    for copy in dn_side:
        copy.wait_recv()
    dn_line = [
        RingGather(wires, spot, "y", lambda pos, h: dn.at[pos, pl.ds(2 * h, 2), first_rows]),
        RingGather(wires, spot, "z", lambda pos, h: dn.at[pl.ds(2 * h, 2), pos, last_rows]),
    ]
    dn_line[1].begin()
    for g in rows_y:
        g.shared[3].wait_recv()
    project(1 - c, turn(y, 2))
    kv_got.append(send_kv(1 - c))
    normed_kept = wires.move(normed, normed_out)
    for piece in att_side + [out_side]:
        piece.close()
    left = wires.started()
    cot_x[0].forward()
    cot_x[0].near()
    gu_line = RingGather(
        wires, spot, "z", lambda pos, h: gu.at[whole(pos, 384), pl.ds(h * 512, 512)]
    )

    def both_heads(ref, core, span):
        return jnp.concatenate([ref[core, span, 0:128], ref[core, span, 128:256]], axis=0)

    def attend(core, run):
        span = pl.ds(run * WIN, WIN)
        window = pl.ds(run * WIN, SEQ)
        scores = dot(both_heads(q, core, span), kv[core, window, 0:128], 1, 1)
        row, column = grid_of(2 * WIN, SEQ)
        row = row & (WIN - 1)
        spot_of = spot.high * HALF + run * WIN + row[0:WIN, 0:1]
        begin = jnp.maximum(
            (spot_of >> 9) << 9, spot_of - grad_kv[core, span, 0:1].astype(jnp.int32)
        )
        begin = begin - (spot.high * HALF + run * WIN) + WIN
        begin = jnp.concatenate([begin, begin], axis=0)
        allowed = (column >= begin) & (column <= row + WIN)
        scores = jnp.where(allowed, scores, MASKED)
        weights = jnp.exp(scores - jnp.max(scores, axis=-1, keepdims=True))
        share = weights * (1.0 / jnp.sum(weights, axis=-1, keepdims=True))
        rounded = share.astype(BF16)
        prob[core, run] = rounded
        values = dot(rounded, kv[core, window, 128:256], 1, 0).astype(BF16)
        mix[core, span, 0:128] = values[0:WIN]
        mix[core, span, 128:256] = values[WIN : 2 * WIN]

    repeat(2, lambda i: attend(i, 1))
    gu_side.forward()
    dn_line[0].begin()
    repeat(2, lambda i: attend(i, 2))
    dn_line[1].forward()
    out_line.near()
    out_line.far()
    out_rows = picks(256, 256, out_row)
    wo[...] = dot(out_rows, ao[...].reshape(256, D), 1, 0).astype(BF16).reshape(4, 4, 16, D)

    def project_out(core, half):
        rows = mix[core, half * 384 : half * 384 + 384, :]
        out = dot(rows, wo[...].reshape(256, D), 1, 0).astype(BF16)
        part[core, half * 2 : half * 2 + 2] = out.reshape(2, OWN, D)

    def share_all(sums):
        for s in sums:
            s.share()

    def back_hidden(i):
        start, size = THREE[i]

        def step(core):
            rows = cots[core, :, pl.ds(start, size)].reshape(4 * size, D)
            grad = dot(rows, dn[...].reshape(512, D), 1, 1).astype(BF16)
            grad_hidden[core, pl.ds(4 * start, 4 * size)] = grad

        repeat(2, step)

    sums_y = [PairScatter(wires, spot, "y", part, got, passed, near, s, n) for s, n in THREE]
    rows_x = [PairGather(wires, spot, "x", second, own, s, n) for s, n in THREE]
    repeat(2, lambda i: project_out(i, 1))
    for copy in kv_got:
        copy.wait_recv()
    cot_x[1].start()
    gu_side.near()
    gu_side.far()
    gu_line.start()
    repeat(2, lambda i: attend(i, 0))
    cot_x[1].rest()
    dn_line[0].forward()
    project_out(1 - c, 0)
    sums_y[0].share()
    project_out(c, 0)
    for g in rows_y:
        g.close()
    normed_kept.wait()
    sums_y[0].first()
    cot_x[1].forward()
    gu_line.rest()
    cot_x[0].far()
    cot_x[0].finish()
    sums_y[0].left()
    sums_y[0].direct()
    sums_y[1].share()
    cot_x[1].near()
    sums_y[0].through()
    gu_line.forward()
    cot_x[1].far()
    sums_y[0].gone()
    sums_y[1].first()
    sums_y[2].share()
    for line in dn_line:
        line.near()
        line.far()
    cot_x[1].finish()

    def middle_rows(s):
        def use(span):
            middle = tokens[span, :].astype(F32) + s.total(span)
            middle_all[span, :] = middle
            own[span, :] = (middle * norm_scale(middle) * gains[1:2, :]).astype(BF16)

        return use

    def gather_next(i):
        s = sums_y[i]
        s.arrive()
        over_rows(s.start_row, s.size, middle_rows(s))
        s.close()
        rows_x[i].start()

    gather_next(0)
    sums_y[1].direct()
    back_hidden(0)
    sums_y[1].through()
    rows_x[0].rest()
    grad_kv[...] = jnp.zeros_like(grad_kv)
    wires.done(left)
    rows_x[0].forward()
    sums_y[1].gone()
    sums_y[2].first()
    back_hidden(1)
    gather_next(1)
    sums_y[2].direct()
    rows_x[0].near()
    back_hidden(2)
    sums_y[2].through()
    rows_x[1].rest()
    rows_x[0].far()
    rows_x[1].forward()
    gu_line.near()
    gu_line.far()
    rows_x[0].finish()

    def feed(core, i):
        start, part_size = THREE[i]
        span, size = pl.ds(start, part_size), 4 * part_size
        rows = second[core, :, span].reshape(size, D)
        both = dot(rows, gu[...], 1, 0)
        upstream = grad_hidden[core, pl.ds(4 * start, size)].astype(F32)
        for j in range(4):
            gate = both[:, j * 256 : j * 256 + 128]
            upward = both[:, j * 256 + 128 : j * 256 + 256]
            sent = upstream[:, j * 128 : j * 128 + 128]
            sigmoid = jax.nn.sigmoid(gate)
            silu = gate * sigmoid
            slope = sigmoid * (1.0 + gate * (1.0 - sigmoid))
            for first, values in (
                (1024 + j * 128, silu * upward),
                (j * 256, sent * upward * slope),
                (j * 256 + 128, sent * silu),
            ):
                rounded = values.astype(BF16).reshape(4, part_size, 128)
                work[core, :, span, first : first + 128] = rounded
        back = dot(work[core, :, span, 0:1024].reshape(size, 1024), gu[...], 1, 1)
        part[core, :, span] = back.astype(BF16).reshape(4, part_size, D)

    sums_x = [PairScatter(wires, spot, "x", part, got, passed, near, s, n) for s, n in THREE]
    grads_y = [PairGather(wires, spot, "y", normed, own, s, n) for s, n in THREE]

    def feed_both(i):
        sums_x[i].share(start=False)

        def step(k):
            feed(jnp.where(k == 0, spot.other, c), i)

            @pl.when(k == 0)
            def _():
                sums_x[i].shared.start()

        repeat(2, step)

    gather_next(2)
    early = wires.started()
    wires.again()

    def grad_gate_up(i):
        lanes = whole(i, 256)
        rows = second[:, :, :, lanes].reshape(8 * OWN, 256)
        sent = work[:, :, :, 0:1024].reshape(8 * OWN, 1024)
        d_gu[lanes, :] = dot(rows, sent, 0, 0).astype(BF16)

    def grad_down(i):
        lanes = pl.ds(pl.multiple_of(1024 + i * 256, 256), 256)
        rows = work[:, :, :, lanes].reshape(8 * OWN, 256)
        grad = dot(rows, cots[...].reshape(8 * OWN, D), 0, 0).astype(BF16)
        d_dn[pl.ds(i * 2, 2)] = grad.reshape(2, 4, 32, D)

    def down(i):
        rows = work[i // 2, pl.ds((i % 2) * 2, 2), :, 1024:D].reshape(384, 512)
        second[i // 2, pl.ds((i % 2) * 2, 2)] = (
            dot(rows, dn[...].reshape(512, D), 1, 0).astype(BF16).reshape(2, OWN, D)
        )

    def back_rows(s):
        def use(span):
            grad = s.total(span)
            rows = middle_all[span, :]
            inverse = norm_scale(rows)
            back = cot[span, :].astype(F32) + norm_back(grad, rows, inverse, gains[1:2, :])
            back_all[span, :] = back
            own[span, :] = back.astype(BF16)
            fold(total, grad * rows * inverse)

        return use

    def gather_back(i):
        s = sums_x[i]
        s.arrive()
        rows_x[i].close()
        over_rows(s.start_row, s.size, back_rows(s))
        s.close()
        grads_y[i].start()

    def mix_back(i):
        first, size = THREE[i]

        def step(core):
            rows = normed[core, :, pl.ds(first, size)].reshape(4 * size, D)
            grad = dot(rows, wo[...].reshape(256, D), 1, 1).astype(BF16)
            for pos in range(4):
                start = pos * OWN + first
                grad_mix[core, start : start + size, :] = grad[pos * size : pos * size + size]

        repeat(2, step)

    total[...] = jnp.zeros_like(total)

    feed_both(0)
    rows_x[2].rest()
    rows_x[2].forward()
    rows_x[1].near()
    rows_x[1].far()
    sums_x[0].first()
    rows_x[1].finish()
    feed_both(1)
    rows_x[2].near()
    sums_x[0].direct()
    rows_x[2].far()
    sums_x[0].through()
    sums_x[1].first()
    rows_x[2].finish()
    sums_x[1].direct()
    feed_both(2)
    sums_x[2].first()
    gather_back(0)
    sums_x[1].through()
    sums_x[2].direct()
    wires.done(early)
    tell(0, [spot.along("z", 1), spot.along("z", -1)])

    grads_y[0].rest()
    repeat(2, grad_gate_up)
    grads_y[0].forward()
    repeat(2, lambda i: grad_gate_up(2 + i))
    sums_x[2].through()
    gather_back(1)
    grads_y[0].near()
    repeat(2, lambda i: grad_gate_up(4 + i))
    grads_y[1].rest()
    hear(0, 2)
    gu_sum = [
        LineScatter(
            wires, spot, "z",
            lambda pos, h, lot=lot: d_gu.at[whole(pos * 4 + lot * 2 + h, 96)],
            lambda h, lot=lot: gu.at[pl.ds(lot * 192 + h * 96, 96)],
            lambda h, lot=lot: gu.at[pl.ds(384 + lot * 192 + h * 96, 96)],
            lambda side, h, lot=lot: gu.at[pl.ds(768 + side * 384 + lot * 192 + h * 96, 96)],
        )
        for lot in (0, 1)
    ]
    gu_got = []

    def gu_beside(lot):
        gu_sum[lot].finish()
        for by in (1, -1, 2):
            part_of = d_gu.at[whole(z * 2 + lot, 192), whole(turn(y, by), 256)]
            into = gu_in.at[y, pl.ds(lot * 192, 192)]
            gu_got.append(wires.send(part_of, into, spot.along("y", by)))

    gu_sum[0].first()
    grads_y[0].far()
    gather_back(2)
    grads_y[1].forward()
    grad_down(0)
    grads_y[2].rest()
    grads_y[0].finish()
    mix_back(0)
    grads_y[1].near()
    grads_y[2].forward()
    gu_sum[0].second()
    gu_sum[1].first()
    grad_down(1)
    grads_y[1].far()
    grads_y[2].near()
    repeat(2, down)
    grads_y[2].far()
    grads_y[1].finish()
    mix_back(1)
    repeat(2, lambda i: down(2 + i))
    tell(1, around(spot, "xy") + [spot.along("z", 1), spot.along("z", -1)])
    again = wires.move(normed_out, cots)
    gain_c[c, 1:2] = jnp.sum(total[...], axis=0, keepdims=True)
    grads_y[2].finish()
    mix_back(2)
    left = wires.started()

    def attend_back(core, run):
        span = pl.ds(run * WIN, WIN)
        window = pl.ds(run * WIN, SEQ)
        rounded = prob[core, run]
        mixed = both_heads(grad_mix, core, span)
        inner = mixed.astype(F32) * both_heads(mix, core, span).astype(F32)
        inner = jnp.sum(inner, axis=-1, keepdims=True)
        grad = dot(mixed, kv[core, window, 128:256], 1, 1)
        scored = (rounded.astype(F32) * (grad - inner)).astype(BF16)
        grad_kv[core, window, 0:128] += dot(scored, both_heads(q, core, span), 0, 0)
        grad_kv[core, window, 128:256] += dot(rounded, mixed, 0, 0)
        grad_q = dot(scored, kv[core, window, 0:128], 1, 0) * scale
        cos, sin = cosine[core, span, :], sine[core, span, :]
        for head in (0, 1):
            grad = grad_q[head * WIN : head * WIN + WIN]
            grad = (grad * cos - swap_halves(grad) * sin).astype(BF16)
            q[core, span, head * 128 : head * 128 + 128] = grad

    def send_far(core):
        far_from = grad_mix.at[core, pl.ds(0, WIN)]
        far_from[...] = grad_kv[core, 0:WIN, :].astype(BF16)
        return wires.send(far_from, far_kv.at[core], spot.along("x", 2))

    far_got = []
    for core in (0, 1):
        attend_back(core, 0)
        far_got.append(send_far(core))
    gu_beside(0)
    hear(1, 7)
    sums_m = [
        PairScatter(
            wires, spot, "x", second, work.at[0], work.at[1, 0], work.at[1, pl.ds(1, 2)], s, n
        )
        for s, n in TWO
    ]
    sums_m[0].share()
    gu_sum[1].second()
    repeat(2, lambda i: attend_back(i, 1))
    sums_m[0].first()
    sums_m[0].direct()
    sums_m[1].share()
    repeat(2, lambda i: attend_back(i, 2))
    sums_m[1].first()
    sums_m[1].direct()
    dn_sum = LineScatter(
        wires, spot, "z",
        lambda pos, h: d_dn.at[pl.ds(2 * h, 2), pos],
        lambda h: dn.at[0, pl.ds(2 * h, 2)],
        lambda h: dn.at[1, pl.ds(2 * h, 2)],
        lambda side, h: dn.at[2 + side, pl.ds(2 * h, 2)],
    )
    dn_sum.first()

    def turn_back(core, pos):
        after = pl.ds(pl.multiple_of(WIN + pos * OWN, 64), OWN)
        span = whole(pos, OWN)
        cos, sin = cosine[core, span, :], sine[core, span, :]
        keyed = grad_kv[core, after, 0:128]
        keyed = pltpu.roll(keyed * cos - swap_halves(keyed) * sin, 64, 1)
        valued = pltpu.roll(grad_kv[core, after, 128:256], 32, 1)
        front = q[core, span, 0:128].astype(F32)
        behind = pltpu.roll(q[core, span, 128:256].astype(F32), 96, 1)
        lane = lax.broadcasted_iota(jnp.int32, front.shape, 1)
        q[core, span, 0:128] = jnp.where(lane < 96, front, behind).astype(BF16)
        q[core, span, 128:256] = jnp.where(lane < 64, behind, keyed).astype(BF16)
        kv[core, after, 0:128] = jnp.where(lane < 32, keyed, valued).astype(BF16)


    def normed_back(core, half):
        after = pl.ds(WIN + half * 384, 384)
        span = pl.ds(half * 384, 384)
        rows = jnp.concatenate([q[core, span, :], kv[core, after, 0:128]], axis=1)
        grad = dot(rows, aq[...].reshape(D, 384), 1, 1).astype(BF16)
        part[core, half * 2 : half * 2 + 2] = grad.reshape(2, OWN, D)

    sums_n = [PairScatter(wires, spot, "y", part, got, passed, near, s, n) for s, n in THREE]
    gu_beside(1)
    repeat(4, lambda i: turn_back(i // 2, i % 2))
    repeat(2, lambda i: normed_back(i, 0))
    for copy in far_got:
        copy.wait_recv()
    for core in (0, 1):
        grad_kv[core, 768:1024, :] += far_kv[core].astype(F32)
    repeat(4, lambda i: turn_back(i // 2, 2 + i % 2))
    normed_back(1 - c, 1)
    share_all(sums_n)
    normed_back(c, 1)
    sums_n[0].first()
    sums_n[1].first()
    sums_n[2].first()
    dn_sum.second()
    again.wait()

    def grad_columns(i):
        rows = cots[:, :, :, whole(i, 384)].reshape(8 * OWN, 384)
        asked = dot(rows, q[...].reshape(8 * OWN, 256), 0, 0)
        other = dot(rows, kv[:, pl.ds(WIN, HALF), 0:128].reshape(8 * OWN, 128), 0, 0)
        d_att[i, :, :, 0:256] = asked.astype(BF16).reshape(4, 96, 256)
        d_att[i, :, :, 256:384] = other.astype(BF16).reshape(4, 96, 128)
        held = aq[i].reshape(384, 384).astype(F32)
        folded = (
            held[:, 0:128] * asked[:, 0:128]
            + held[:, 128:256] * asked[:, 128:256]
            + held[:, 256:384] * other
        )
        gain_c[c, 0:1, whole(i, 384)] = jnp.sum(folded.T, axis=0, keepdims=True)

    repeat(4, grad_columns)
    gain_c[c, 0:1] = gain_c[c, 0:1] / gains[0:1, :]
    tell(2, [spot.along(a, by) for a in "xz" for by in (1, -1)])
    gain_got = [wires.send(gain_c.at[c], gain_c.at[c], spot.sibling)]
    for s in sums_n:
        s.direct()
    for s in sums_m:
        s.through()

    def out_rows_back(r, k):
        unit = jnp.where(k < 128, k, k - 32)
        real = (k < 96) | ((k >= 128) & (k < 224))
        return real & (unit + ((unit * 5462) >> 16) * 4 == r)

    grad_out = dot(mix[...].reshape(8 * OWN, 256), normed[...].reshape(8 * OWN, D), 0, 0)
    grad_out = dot(picks(256, 256, out_rows_back), grad_out.astype(BF16), 1, 0)
    wo[...] = grad_out.astype(BF16).reshape(4, 4, 16, D)
    out_sum = LineScatter(
        wires, spot, "z",
        lambda pos, h: wo.at[pos, pl.ds(2 * h, 2)],
        lambda h: ao.at[0, pl.ds(2 * h, 2)],
        lambda h: ao.at[1, pl.ds(2 * h, 2)],
        lambda side, h: ao.at[2 + side, pl.ds(2 * h, 2)],
    )
    hear(2, 4)
    att_sum = [
        LineScatter(
            wires, spot, "x",
            lambda pos, h: d_att.at[pl.ds(2 * h, 2), slot_of(pos), low],
            lambda h: aq.at[0, pl.ds(2 * h, 2), low],
            lambda h: aq.at[1, pl.ds(2 * h, 2), low],
            lambda side, h: aq.at[2 + side, pl.ds(2 * h, 2), low],
        ),
        LineScatter(
            wires, spot, "z",
            lambda pos, h: d_att.at[pos, pl.ds(2 * h, 2), high],
            lambda h: aq.at[0, pl.ds(2 * h, 2), high],
            lambda h: aq.at[1, pl.ds(2 * h, 2), high],
            lambda side, h: aq.at[2 + side, pl.ds(2 * h, 2), high],
        ),
    ]
    for line in att_sum + [out_sum]:
        line.first(paced=True)

    for s in sums_n:
        s.through()

    def add_gains(held, axis, into):
        for copy in gain_got:
            copy.wait_recv()
        summed = held[0]
        for i in range(1, held.shape[0]):
            summed = summed + held[i]
        if into is None:
            gains_out[...] = summed
            return []
        me = spot.me(axis)
        into[me] = summed
        return [wires.send(into.at[me], into.at[me], spot.along(axis, by)) for by in (1, -1, 2)]

    gain_got = add_gains(gain_c, "x", gain_x)
    for line in att_sum + [out_sum]:
        line.direct()
    wires.done(left)

    for line in att_sum + [out_sum]:
        line.second()
    for copy in gu_got:
        copy.wait_recv()
    mine = d_gu.at[whole(z, 384), whole(y, 256)]
    add_into(mine, mine, *[gu_in.at[turn(y, by)] for by in (1, -1, 2)])
    gu_done = []
    for by in (1, 2, 3):
        other, who = spot.in_quad(by)
        rows = d_gu.at[whole(z * 4 + other, 96), whole(y, 256)]
        gu_done.append(wires.send(rows, gu_own.at[spot.quad], who))
    gain_got = add_gains(gain_x, "z", gain_z)

    def token_rows(s):
        def use(span):
            grad = s.total(span)
            rows = tokens[span, :].astype(F32)
            inverse = norm_scale(rows)
            out = back_all[span, :] + norm_back(grad, rows, inverse, gains[0:1, :])
            part[c, y, span] = out.astype(BF16)

        return use

    def result_rows(s):
        def use(span):
            second[c, x, span] = (middle_all[span, :] + s.total(span)).astype(BF16)

        return use

    token_kept = []

    def token_part(i):
        s = sums_n[i]
        s.arrive()
        over_rows(s.start_row, s.size, token_rows(s))
        token_kept.append(wires.move(part.at[c, y, s.rows()], token_out.at[s.rows()]))

    def result_part(s):
        s.arrive()
        over_rows(s.start_row, s.size, result_rows(s))

    dn_sum.finish()
    dn_got = [
        wires.send(d_dn.at[turn(y, by), z], dn_in.at[y], spot.along("y", by)) for by in (1, -1, 2)
    ]
    for s in sums_m:
        result_part(s)
    result_kept = wires.move(second.at[c, x], result_out)
    for line in att_sum:
        line.finish()

    def home(pos):
        stay = pos // 2 == c
        return device(jnp.where(stay, pos, turn(pos, 2)), y, z, jnp.where(stay, c, 1 - c))

    places_z = [(turn(z, by), who) for by, who in zip((0, 1, -1, 2), line_z)]
    places_x = [turn(x, by) for by in (0, 1, -1, 2)]
    att_got = [
        Placed(
            wires, stays, [(d_att.at[to, slot, low], att_in.at[z, low], w) for to, w in places_z]
        ),
        Placed(
            wires, stays,
            [(d_att.at[z, slot_of(to), high], att_in.at[x, high], home(to)) for to in places_x],
        ),
    ]
    out_sum.finish()
    out_got = Placed(
        wires, stays, [(wo.at[z, slot_of(to)], out_in.at[x], home(to)) for to in places_x]
    )
    gain_got = add_gains(gain_z, "y", gain_y)
    kept_rows = d_gu.at[whole(z * 4 + spot.quad, 96), whole(y, 256)]
    gu_own[spot.quad] = kept_rows[...]
    token_part(0)
    token_part(1)
    token_part(2)
    for copy in gu_done:
        copy.wait_recv()
    order = picks(512, 512, lambda r, k: quad_order(k) == r)
    for into, first in ((gate_out, 0), (up_out, 128)):
        moved = jnp.concatenate([gu_own[i, :, first : first + 128] for i in range(4)], axis=1)
        into[...] = dot(moved, order, 1, 0)
    for copy in dn_got:
        copy.wait_recv()
    add_into(
        dn_out, d_dn.at[y, z], *[dn_in.at[turn(y, by)] for by in (1, -1, 2)]
    )
    for piece in att_got:
        piece.wait()
    add_into(att_out, *[att_in.at[i] for i in range(4)])
    out_got.wait()
    add_into(out_out, *[out_in.at[i] for i in range(4)])
    add_gains(gain_y, None, None)
    result_kept.wait()
    for copy in token_kept:
        copy.wait()
    for piece in att_got + [out_got]:
        piece.close()
    wires.close()


def finish_kernel(
    result, token, gains, att, out, gate, up, dn,
    result_out, token_out, attn_out, mlp_out, query_out, key_out, value_out, out_out,
    gate_out, up_out, dn_out,
):
    for src, dst in (
        (result, result_out), (token, token_out), (gate, gate_out), (up, up_out), (dn, dn_out)
    ):
        dst[...] = src[...]
    for i, into in enumerate((attn_out, mlp_out)):
        for j in range(12):
            into[j : j + 1, :] = gains[i : i + 1, j * 128 : j * 128 + 128]
    rows = att[...]

    def three(first):
        return lambda r, k: r == k + first

    query_out[...] = dot(rows, picks(384, 192, three(0)), 1, 0)
    key_out[...] = dot(rows, picks(384, 96, three(192)), 1, 0)
    value_out[...] = dot(rows, picks(384, 96, three(288)), 1, 0)
    out_out[...] = out[0:12, :].astype(F32)


def layer_call(
    tokens, gain_attn, gain_mlp, cot, w_query, w_key, w_value, w_out, w_gate, w_up, w_down, marks
):
    sends, receives = 120, 170
    shape = jax.ShapeDtypeStruct
    outs = (
        (shape((2, 4, OWN, D), BF16), ANY),
        (shape((OWN, D), BF16), ANY),
        (shape((OWN, D), BF16), ANY),
        (shape((2, D), F32), VMEM),
        (shape((96, 384), BF16), VMEM),
        (shape((16, D), BF16), VMEM),
        (shape((96, 512), F32), VMEM),
        (shape((96, 512), F32), VMEM),
        (shape((32, D), F32), VMEM),
    )
    scratch = [
        ((2, 4, OWN, D), BF16),
        ((2, 4, OWN, D), BF16),
        ((2, 4, OWN, D), BF16),
        ((2, 4, OWN, D), BF16),
        ((4, OWN, D), BF16),
        ((OWN, D), BF16),
        ((2, OWN, D), BF16),
        ((2, 4, OWN, D), BF16),
        ((1, 96, 384), BF16),
        ((1, 16, D), BF16),
        ((4, 4, 96, 384), BF16),
        ((4, 4, 16, D), BF16),
        ((4, 4, 96, 384), BF16),
        ((4, 4, 16, D), BF16),
        ((D, 1024), BF16),
        ((4, 96, 256), BF16),
        ((4, 4, 32, D), BF16),
        ((D, 1024), BF16),
        ((4, 4, 32, D), BF16),
        ((OWN, D), BF16),
        ((2, 4 * OWN, 512), BF16),
        ((2, HALF, 256), BF16),
        ((2, HALF + WIN, 256), BF16),
        ((2, 3, 2 * WIN, SEQ), BF16),
        ((2, HALF, 256), BF16),
        ((2, HALF, 128), F32),
        ((2, HALF, 128), F32),
        ((2, 12, 128), jnp.int32),
        ((2, D), F32),
        ((OWN, D), F32),
        ((OWN, D), F32),
        ((8, D), F32),
        ((2, HALF, 256), BF16),
        ((2, HALF + WIN, 256), F32),
        ((2, WIN, 256), BF16),
        ((4, 384, 256), BF16),
        ((4, 32, D), BF16),
        ((4, 96, 384), BF16),
        ((4, 16, D), BF16),
        ((2, 2, D), F32),
        ((4, 2, D), F32),
        ((4, 2, D), F32),
        ((4, 2, D), F32),
    ]
    outs_raw = pl.pallas_call(
        layer_kernel,
        out_shape=tuple(o[0] for o in outs),
        in_specs=[VMEM] * 12,
        out_specs=[o[1] for o in outs],
        scratch_shapes=[pltpu.VMEM(*s) for s in scratch]
        + [
            pltpu.SemaphoreType.REGULAR((3,)),
            pltpu.SemaphoreType.DMA((sends,)),
            pltpu.SemaphoreType.DMA((receives,)),
        ],
        compiler_params=pltpu.CompilerParams(
            collective_id=1, has_side_effects=True, vmem_limit_bytes=64 << 20
        ),
        name="layer",
    )(tokens, gain_attn, gain_mlp, cot, w_query, w_key, w_value, w_out, w_gate, w_up, w_down, marks)
    finals = (
        shape((OWN, D), BF16),
        shape((OWN, D), BF16),
        shape((12, 128), F32),
        shape((12, 128), F32),
        shape((96, 192), F32),
        shape((96, 96), F32),
        shape((96, 96), F32),
        shape((12, D), F32),
        shape((96, 512), F32),
        shape((96, 512), F32),
        shape((32, D), F32),
    )
    return pl.pallas_call(
        finish_kernel,
        out_shape=finals,
        in_specs=[VMEM] * 8,
        out_specs=[VMEM] * 11,
        name="finish",
    )(*outs_raw[1:])


def shards(
    tokens,
    gain_attn,
    gain_mlp,
    w_query,
    w_key,
    w_value,
    w_out,
    w_gate,
    w_up,
    w_down,
    segments,
    positions,
    cotangent,
):
    del segments
    done = layer_call(
        tokens,
        gain_attn.reshape(12, 128),
        gain_mlp.reshape(12, 128),
        cotangent,
        w_query,
        w_key,
        w_value,
        w_out,
        w_gate,
        w_up,
        w_down,
        positions.reshape(12, 128),
    )
    return (*done[:2], done[2].reshape(D), done[3].reshape(D), *done[4:])


def solution(mesh):
    placed = (
        P(("dp", "tensor"), None),
        P(),
        P(),
        P("dp", "tensor"),
        P("dp", "tensor"),
        P("dp", "tensor"),
        P(("tensor", "dp"), None),
        P("dp", "tensor"),
        P("dp", "tensor"),
        P(("tensor", "dp"), None),
        P("dp"),
        P("dp"),
        P(("dp", "tensor"), None),
    )
    return jax.shard_map(
        shards,
        mesh=mesh,
        in_specs=placed,
        out_specs=(
            P(("dp", "tensor"), None),
            P(("dp", "tensor"), None),
            P(),
            P(),
            P("dp", "tensor"),
            P("dp", "tensor"),
            P("dp", "tensor"),
            P(("tensor", "dp"), None),
            P("dp", "tensor"),
            P("dp", "tensor"),
            P(("tensor", "dp"), None),
        ),
        check_vma=False,
    )
```

```python
import functools
import math

import jax
import jax.numpy as jnp
from jax import lax
from jax.experimental import pallas as pl
from jax.experimental.pallas import tpu as pltpu
from jax.sharding import PartitionSpec as P

HD = 96
SEQ = 512
D = 1536
OWN = 192
HALF = 768
WIN = 256

EPSILON = 1e-05
ROPE_BASE = 100000.0
MASKED = -1e30
MESH = pl.DeviceIdType.MESH
ANY = pl.BlockSpec(memory_space=pl.ANY)
VMEM = pl.BlockSpec(memory_space=pltpu.VMEM)
BF16 = jnp.bfloat16
F32 = jnp.float32


def place():
    dp = lax.axis_index("dp")
    tensor = lax.axis_index("tensor")
    return (tensor // 4) * 2 + (dp // 2) % 2, tensor % 4, dp // 4, dp % 2


def device(x, y, z, c):
    return (z * 4 + (x % 2) * 2 + c, (x // 2) * 4 + y)


def turn(pos, by):
    return (pos + by + 4) % 4


class Spot:
    def __init__(self):
        x, y, z, c = place()
        self.x, self.y, self.z, self.c = x, y, z, c
        self.high, self.low, self.other = x // 2, x % 2, 1 - c
        self.quad = self.low * 2 + c
        self.sibling = device(x, y, z, 1 - c)
        self.partner = device(turn(x, 2), y, z, 1 - c)

    def along(self, axis, by):
        x, y, z, c = self.x, self.y, self.z, self.c
        if axis == "x":
            return device(turn(x, by), y, z, c)
        if axis == "y":
            return device(x, turn(y, by), z, c)
        return device(x, y, turn(z, by), c)

    def me(self, axis):
        return {"x": self.x, "y": self.y, "z": self.z}[axis]

    def in_quad(self, by):
        other = turn(self.quad, by)
        return other, device(self.high * 2 + other // 2, self.y, self.z, other % 2)


def greet(devices):
    for who in devices:
        pl.semaphore_signal(
            pltpu.get_barrier_semaphore(), inc=1, device_id=who, device_id_type=MESH
        )


def greeted(devices):
    pl.semaphore_wait(pltpu.get_barrier_semaphore(), len(devices))


class Wires:
    def __init__(self, send_sem, recv_sem):
        self.send_sem, self.recv_sem = send_sem, recv_sem
        self.free = list(range(send_sem.shape[0]))
        self.count = 0
        self.sent = []

    def again(self):
        self.count = 0

    def take(self):
        held = min(self.free)
        self.free.remove(held)
        return held

    def forget(self, copy):
        self.free += [held for other, held in self.sent if other is copy]
        self.sent = [pair for pair in self.sent if pair[0] is not copy]

    def send(self, src, dst, who, start=True):
        held = self.take()
        assert self.count < self.recv_sem.shape[0]
        copy = pltpu.make_async_remote_copy(
            src_ref=src,
            dst_ref=dst,
            send_sem=self.send_sem.at[held],
            recv_sem=self.recv_sem.at[self.count],
            device_id=who,
            device_id_type=MESH,
        )
        self.count += 1
        if start:
            copy.start()
        self.sent.append((copy, held))
        return copy

    def move(self, src, dst):
        held = self.take()
        copy = pltpu.make_async_copy(src, dst, self.send_sem.at[held])
        copy.start()
        return Moved(self, copy, held)

    def done(self, copies):
        kept = []
        for copy, held in self.sent:
            if any(copy is other for other in copies):
                copy.wait_send()
                self.free.append(held)
            else:
                kept.append((copy, held))
        self.sent = kept

    def started(self):
        return [copy for copy, _ in self.sent]

    def close(self):
        self.done(self.started())


class Placed:
    def __init__(self, wires, stays, pieces):
        self.wires, self.stays = wires, stays
        self.others = [wires.send(*piece) for piece in pieces[1:]]
        self.own = wires.send(*pieces[0], start=False)
        held = wires.sent[-1][1]

        @pl.when(jnp.logical_not(stays))
        def _():
            self.own.start()

        @pl.when(stays)
        def _():
            kept = pltpu.make_async_copy(pieces[0][0], pieces[0][1], wires.send_sem.at[held])
            kept.start()
            kept.wait()

    def wait(self):
        for copy in self.others:
            copy.wait_recv()

        @pl.when(jnp.logical_not(self.stays))
        def _():
            self.own.wait_recv()

    def close(self):
        self.wires.done(self.others)

        @pl.when(jnp.logical_not(self.stays))
        def _():
            self.own.wait_send()

        self.wires.forget(self.own)


class Moved:
    def __init__(self, wires, copy, held):
        self.wires, self.copy, self.held = wires, copy, held

    def wait(self):
        self.copy.wait()
        self.wires.free.append(self.held)


def add_into(dst, *srcs, chunk=16):
    rows = dst.shape[-2]
    chunk = min(chunk, rows)

    def step(i, carry):
        span = pl.ds(pl.multiple_of(i * chunk, chunk), chunk)
        total = srcs[0][..., span, :].astype(F32)
        for src in srcs[1:]:
            total = total + src[..., span, :].astype(F32)
        dst[..., span, :] = total.astype(dst.dtype)
        return carry

    lax.fori_loop(0, rows // chunk, step, 0)


class RingGather:
    def __init__(self, wires, spot, axis, at):
        self.wires, self.at = wires, at
        self.me = spot.me(axis)
        self.next, self.prev = spot.along(axis, 1), spot.along(axis, -1)

    def start(self, own=None):
        self.own = own or (lambda half: self.at(self.me, half))
        send, at, me = self.wires.send, self.at, self.me
        self.right0 = send(self.own(0), at(me, 0), self.next)
        self.left1 = send(self.own(1), at(me, 1), self.prev)

    def rest(self):
        send, at, me = self.wires.send, self.at, self.me
        self.right1 = send(self.own(1), at(me, 1), self.next)
        self.left0 = send(self.own(0), at(me, 0), self.prev)

    def begin(self):
        self.start()
        self.rest()

    def forward(self):
        send, at, me = self.wires.send, self.at, self.me
        self.right0.wait_recv()
        before = at(turn(me, -1), 0)
        self.pass0 = send(before, before, self.next)
        self.left1.wait_recv()
        after = at(turn(me, 1), 1)
        self.pass1 = send(after, after, self.prev)

    def near(self):
        self.right1.wait_recv()
        self.left0.wait_recv()

    def far(self):
        self.pass0.wait_recv()
        self.pass1.wait_recv()

    def close(self):
        near = [self.right0, self.left1, self.right1, self.left0]
        self.wires.done(near + [self.pass0, self.pass1])


class PairGather:
    def __init__(self, wires, spot, axis, out, own, start, size):
        self.wires, self.spot, self.out, self.own = wires, spot, out, own
        self.rows = pl.ds(start, size)
        cut = size // 2

        def half_rows(half):
            return pl.ds(start + half * cut, cut)

        self.half_rows = half_rows
        self.ring = RingGather(
            wires, spot, axis, lambda pos, half: out.at[spot.c, pos, half_rows(half)]
        )
        self.me = spot.me(axis)

    def share(self, pos):
        block = self.out.at[self.spot.c, pos, self.rows]
        return self.wires.send(block, block, self.spot.sibling)

    def start(self):
        self.ring.start(lambda half: self.own.at[self.half_rows(half)])
        mine = self.own.at[self.rows]
        place_of = self.out.at[self.spot.c, self.me, self.rows]
        self.shared = [self.wires.send(mine, place_of, self.spot.sibling)]
        self.kept = self.wires.move(mine, place_of)

    def rest(self):
        self.ring.rest()

    def forward(self):
        self.ring.forward()

    def near(self):
        self.ring.near()
        self.shared.append(self.share(turn(self.me, -1)))
        self.shared.append(self.share(turn(self.me, 1)))

    def far(self):
        self.ring.far()
        self.shared.append(self.share(turn(self.me, 2)))

    def finish(self):
        for copy in self.shared:
            copy.wait_recv()
        self.kept.wait()

    def close(self):
        self.ring.close()
        self.wires.done(self.shared)


class PairScatter:
    def __init__(self, wires, spot, axis, part, got, passed, near, start, size):
        self.wires, self.spot = wires, spot
        self.me = spot.me(axis)
        self.next, self.prev = spot.along(axis, 1), spot.along(axis, -1)
        self.part, self.got, self.passed, self.near = part, got, passed, near
        self.start_row, self.size, self.cut = start, size, size // 2
        self.shared = []

    def rows(self, half=None):
        if half is None:
            return pl.ds(self.start_row, self.size)
        return pl.ds(self.start_row + half * self.cut, self.cut)

    def share(self, half=None, start=True):
        places = slice(None) if half is None else pl.ds(half * 2, 2)
        copy = self.wires.send(
            self.part.at[self.spot.other, places, self.rows()],
            self.got.at[places, self.rows()],
            self.spot.sibling,
            start,
        )
        self.shared = (self.shared if half is not None else []) + [copy]

    def first(self):
        for copy in self.shared:
            copy.wait_recv()
        pos = turn(self.me, 2)
        mine = self.got.at[pos, self.rows()]
        add_into(mine, self.part.at[self.spot.c, pos, self.rows()], mine)
        self.pass0 = self.wires.send(
            self.got.at[pos, self.rows(0)], self.passed.at[self.rows(0)], self.next
        )
        self.pass1 = self.wires.send(
            self.got.at[pos, self.rows(1)], self.passed.at[self.rows(1)], self.prev
        )

    def left(self):
        self.wires.done([self.pass0, self.pass1])

    def gone(self):
        self.wires.done(self.arriving)

    def direct(self):
        self.arriving = []
        for by, half, who, side in ((1, 1, self.next, 0), (-1, 0, self.prev, 1)):
            pos = turn(self.me, by)
            mine = self.got.at[pos, self.rows(half)]
            add_into(mine, self.part.at[self.spot.c, pos, self.rows(half)], mine)
            self.arriving.append(self.wires.send(mine, self.near.at[side, self.rows(half)], who))

    def through(self):
        after, before = turn(self.me, 1), turn(self.me, -1)
        for pos, half, who, side, arrived in (
            (after, 0, self.next, 0, self.pass0),
            (before, 1, self.prev, 1, self.pass1),
        ):
            arrived.wait_recv()
            mine = self.got.at[pos, self.rows(half)]
            add_into(
                mine,
                self.part.at[self.spot.c, pos, self.rows(half)],
                mine,
                self.passed.at[self.rows(half)],
            )
            self.arriving.append(self.wires.send(mine, self.near.at[side, self.rows(half)], who))

    def arrive(self):
        for copy in self.arriving:
            copy.wait_recv()

    def close(self):
        self.wires.done(self.shared + [self.pass0, self.pass1] + self.arriving)

    def total(self, span):
        return (
            self.part[self.spot.c, self.me, span].astype(F32)
            + self.got[self.me, span].astype(F32)
            + self.near[0, span].astype(F32)
            + self.near[1, span].astype(F32)
        )


class LineScatter:
    def __init__(self, wires, spot, axis, at, passed, work, near):
        self.wires, self.at = wires, at
        self.me = spot.me(axis)
        self.next, self.prev = spot.along(axis, 1), spot.along(axis, -1)
        self.passed, self.work, self.near = passed, work, near

    def first(self, paced=False):
        send, me = self.wires.send, self.me
        far = turn(me, 2)
        self.pass0 = send(self.at(far, 0), self.passed(0), self.next)
        self.pass1 = send(self.at(far, 1), self.passed(1), self.prev)
        if not paced:
            self.direct()

    def direct(self):
        send, me = self.wires.send, self.me
        after, before = turn(me, 1), turn(me, -1)
        self.arriving = [
            send(self.at(after, 1), self.near(0, 1), self.next),
            send(self.at(before, 0), self.near(1, 0), self.prev),
        ]

    def second(self):
        for by, half, who, side, arrived in (
            (1, 0, self.next, 0, self.pass0),
            (-1, 1, self.prev, 1, self.pass1),
        ):
            arrived.wait_recv()
            add_into(self.work(half), self.at(turn(self.me, by), half), self.passed(half))
            self.arriving.append(self.wires.send(self.work(half), self.near(side, half), who))

    def finish(self):
        for copy in self.arriving:
            copy.wait_recv()
        for half in (0, 1):
            mine = self.at(self.me, half)
            add_into(mine, mine, self.near(0, half), self.near(1, half))


def norm_scale(values):
    return lax.rsqrt(jnp.mean(values * values, axis=-1, keepdims=True) + EPSILON)


def norm_back(upstream, values, inverse, gain):
    scaled = upstream * gain
    inner = jnp.sum(scaled * values, axis=-1, keepdims=True)
    return scaled * inverse - values * inner * (inverse * inverse * inverse) / values.shape[-1]


def over_rows(start, size, step, chunk=16):
    def body(i, carry):
        step(pl.ds(pl.multiple_of(start + i * chunk, chunk), chunk))
        return carry

    lax.fori_loop(0, size // chunk, body, 0)


def fold(total, values):
    part = values[0:8]
    for first in range(8, values.shape[0], 8):
        part = part + values[first : first + 8]
    total[...] += part


TWO = ((0, 96), (96, 96))
THREE = ((0, 64), (64, 64), (128, 64))


def dot(left, right, a, b):
    return lax.dot_general(left, right, (((a,), (b,)), ((), ())), preferred_element_type=F32)


def repeat(count, step):
    def body(i, carry):
        step(i)
        return carry

    lax.fori_loop(0, count, body, 0)


def whole(i, size):
    return pl.ds(pl.multiple_of(i * size, size), size)


def grid_of(rows, columns):
    return (
        lax.broadcasted_iota(jnp.int32, (rows, columns), 0),
        lax.broadcasted_iota(jnp.int32, (rows, columns), 1),
    )


def picks(rows, columns, chosen):
    return jnp.where(chosen(*grid_of(rows, columns)), 1.0, 0.0).astype(BF16)


def quad_order(unit):
    return (((unit >> 5) & 3) << 7) + ((unit >> 7) << 5) + (unit & 31)


def swap_halves(values):
    lane = lax.broadcasted_iota(jnp.int32, values.shape, 1)
    up = pltpu.roll(values, 80, 1)
    down = pltpu.roll(values, 48, 1)
    return jnp.where(lane < 48, up, down)


def around(spot, axes):
    return [spot.along(a, by) for a in axes for by in (1, -1)] + [spot.sibling]


def layer_kernel(
    tokens, gain_attn, gain_mlp, cot, w_query, w_key, w_value, w_out, w_gate, w_up, w_down, marks,
    normed_out, result_out, token_out, gains_out, att_out, out_out, gate_out, up_out, dn_out,
    normed, cots, second, part, got, passed, near, work, att_two, own_out, aq, ao, d_att, wo,
    gu, gu_own, dn, d_gu, d_dn, own, grad_hidden, q, kv, prob, mix, cosine, sine,
    marks_two, gains, middle_all, back_all, total, grad_mix, grad_kv, far_kv,
    gu_in, dn_in, att_in, out_in, gain_c, gain_y, gain_x, gain_z,
    ready, send_sem, recv_sem,
):
    spot = Spot()
    wires = Wires(send_sem, recv_sem)
    x, y, z, c = spot.x, spot.y, spot.z, spot.c
    neighbours = (
        around(spot, "xyz")
        + [spot.along(a, 2) for a in "xyz"]
        + [spot.partner]
        + [spot.in_quad(by)[1] for by in (1, 2, 3)]
        + [device(turn(x, by), y, z, 1 - c) for by in (1, -1)]
        + [device(turn(x, 2), y, turn(z, by), 1 - c) for by in (1, -1, 2)]
    )
    greet(neighbours)

    def tell(which, devices):
        for who in devices:
            pl.semaphore_signal(ready.at[which], inc=1, device_id=who, device_id_type=MESH)

    def hear(which, count):
        pl.semaphore_wait(ready.at[which], count)

    for i, gain in enumerate((gain_attn, gain_mlp)):
        gains[i : i + 1, :] = jnp.concatenate([gain[j : j + 1, :] for j in range(12)], axis=1)

    def normalise(span):
        rows = tokens[span, :].astype(F32)
        own[span, :] = (rows * norm_scale(rows) * gains[0:1, :]).astype(BF16)

    over_rows(0, OWN, normalise)

    def three(first):
        return lambda r, k: r + first == k

    columns = (
        dot(w_query[...], picks(192, 384, three(0)), 1, 0)
        + dot(w_key[...], picks(96, 384, three(192)), 1, 0)
        + dot(w_value[...], picks(96, 384, three(288)), 1, 0)
    )
    att_two[0] = columns.astype(BF16)
    own_out[0] = jnp.zeros((16, D), BF16)
    own_out[0, 0:12] = w_out[...]
    greeted(neighbours)

    def slot_of(pos):
        return (pos % 2) * 2 + pos // 2

    slot = slot_of(x)
    low, high = pl.ds(0, 48), pl.ds(48, 48)
    stays = spot.high == c
    there_x, there_c = jnp.where(stays, x, turn(x, 2)), jnp.where(stays, c, 1 - c)
    there = slot_of(there_x)
    line_z = [device(there_x, y, turn(z, by), there_c) for by in (0, 1, -1, 2)]
    line_x = [device(turn(there_x, by), y, z, there_c) for by in (0, 1, -1, 2)]
    att_side = [
        Placed(
            wires, stays, [(att_two.at[0, low], aq.at[z, there, low], who) for who in line_z]
        ),
        Placed(
            wires, stays, [(att_two.at[0, high], aq.at[z, there, high], who) for who in line_x]
        ),
    ]
    rows_y = [PairGather(wires, spot, "y", normed, own, s, n) for s, n in TWO]
    for g in rows_y:
        g.start()
    out_side = Placed(wires, stays, [(own_out.at[0], ao.at[z, there], who) for who in line_x])
    marks_kept = wires.move(marks, marks_two.at[c])
    marks_got = wires.send(marks, marks_two.at[c], spot.sibling)

    order = picks(512, 512, lambda r, k: quad_order(r) == k)
    for shard, first in ((w_gate, 0), (w_up, 128)):
        moved = dot(shard[...], order, 1, 0).astype(BF16)
        for i in range(4):
            gu_own[i, :, first : first + 128] = moved[:, i * 128 : i * 128 + 128]
    gu_lanes = whole(y, 256)
    gu_here = gu.at[whole(z * 4 + spot.quad, 96), gu_lanes]
    gu_kept = wires.move(gu_own.at[spot.quad], gu_here)
    gu_swap = []
    for by in (1, 2, 3):
        other, who = spot.in_quad(by)
        gu_swap.append(wires.send(gu_own.at[other], gu_here, who))

    def trig(core):
        def step(i):
            span = whole(i, 128)
            row, lane = grid_of(128, 128)
            number = marks_two[core, pl.ds(spot.high * 6 + i, 1), :]
            ones = jnp.ones((128, 128), BF16)
            where = jnp.zeros((128, 128), F32)
            for digit, factor in ((number >> 5, 32.0), (number & 31, 1.0)):
                spread = jnp.where(row == lane, digit.astype(F32), 0.0).astype(BF16)
                where = where + factor * dot(spread, ones, 1, 0)
            grad_kv[core, span, 0:128] = where
            turns = jnp.where(lane < 48, lane, lane - 48).astype(F32) * (2.0 / HD)
            angle = where * jnp.exp(-math.log(ROPE_BASE) * turns)
            inside = lane < HD
            cosine[core, span, :] = jnp.where(inside, jnp.cos(angle), 0.0)
            wave = jnp.sin(angle)
            sine[core, span, :] = jnp.where(inside, jnp.where(lane < 48, -wave, wave), 0.0)

        repeat(6, step)

    marks_kept.wait()
    trig(c)
    for g in rows_y:
        g.rest()
    att_line = [
        RingGather(wires, spot, "x", lambda pos, h: aq.at[pl.ds(2 * h, 2), slot_of(pos), low]),
        RingGather(wires, spot, "z", lambda pos, h: aq.at[pos, pl.ds(2 * h, 2), high]),
    ]
    out_line = RingGather(wires, spot, "z", lambda pos, h: ao.at[pos, pl.ds(2 * h, 2)])
    cot_x = [PairGather(wires, spot, "x", cots, cot, s, n) for s, n in TWO]
    for piece in att_side:
        piece.wait()
    for line in att_line:
        line.begin()
    marks_got.wait_recv()
    trig(1 - c)
    for g in rows_y:
        g.forward()
    rows_y[0].near()
    for line in att_line:
        line.forward()
    out_side.wait()
    out_line.begin()
    dn_here = dn.at[y, z]
    dn_kept = wires.move(w_down, dn_here)
    first_rows, last_rows = pl.ds(0, 16), pl.ds(16, 16)
    dn_side = []
    for by in (1, -1, 2):
        for axis, rows in (("z", first_rows), ("y", last_rows)):
            dn_side.append(
                wires.send(w_down.at[rows], dn.at[y, z, rows], spot.along(axis, by))
            )
    cot_x[0].start()
    cot_x[0].rest()
    rows_y[1].near()
    for line in att_line:
        line.near()
        line.far()

    def out_row(r, k):
        unit = jnp.where(r < 128, r, r - 32)
        real = (r < 96) | ((r >= 128) & (r < 224))
        return real & (unit + ((unit * 5462) >> 16) * 4 == k)

    scale = HD ** (-0.5)

    def project(core, pos):
        both = dot(normed[core, pos], aq[...].reshape(D, 384), 1, 0)
        span = whole(pos, OWN)
        cos, sin = cosine[core, span, :], sine[core, span, :]
        tile = [both[:, 128 * i : 128 * i + 128] for i in range(3)]
        lane = lax.broadcasted_iota(jnp.int32, tile[0].shape, 1)

        def turned(values, factor=None):
            values = values * cos + swap_halves(values) * sin
            return (values if factor is None else values * factor).astype(BF16)

        q[core, span, 0:128] = turned(tile[0], scale)
        q[core, span, 128:256] = turned(
            jnp.where(lane < 32, pltpu.roll(tile[0], 32, 1), pltpu.roll(tile[1], 32, 1)), scale
        )
        after = pl.ds(pl.multiple_of(WIN + pos * OWN, 64), OWN)
        kv[core, after, 0:128] = turned(
            jnp.where(lane < 64, pltpu.roll(tile[1], 64, 1), pltpu.roll(tile[2], 64, 1))
        )
        kv[core, after, 128:256] = jnp.where(lane < HD, pltpu.roll(tile[2], 96, 1), 0.0).astype(
            BF16
        )

    for g in rows_y:
        g.kept.wait()
    repeat(3, lambda i: project(c, turn(y, i - 1)))
    for g in rows_y:
        for copy in g.shared[:3]:
            copy.wait_recv()
    repeat(3, lambda i: project(1 - c, turn(y, i - 1)))
    for g in rows_y:
        g.far()
    gu_kept.wait()
    for copy in gu_swap:
        copy.wait_recv()
    gu_side = RingGather(
        wires, spot, "y", lambda pos, h: gu.at[whole(z * 2 + h, 192), whole(pos, 256)]
    )
    gu_side.begin()
    out_line.forward()
    project(c, turn(y, 2))

    def send_kv(core):
        last, first = kv.at[core, pl.ds(768, WIN)], kv.at[core, pl.ds(0, WIN)]
        return wires.send(last, first, spot.along("x", 2))

    kv_got = [send_kv(c)]
    dn_kept.wait()
    for copy in dn_side:
        copy.wait_recv()
    dn_line = [
        RingGather(wires, spot, "y", lambda pos, h: dn.at[pos, pl.ds(2 * h, 2), first_rows]),
        RingGather(wires, spot, "z", lambda pos, h: dn.at[pl.ds(2 * h, 2), pos, last_rows]),
    ]
    dn_line[1].begin()
    for g in rows_y:
        g.shared[3].wait_recv()
    project(1 - c, turn(y, 2))
    kv_got.append(send_kv(1 - c))
    normed_kept = wires.move(normed, normed_out)
    for piece in att_side + [out_side]:
        piece.close()
    left = wires.started()
    cot_x[0].forward()
    cot_x[0].near()
    gu_line = RingGather(
        wires, spot, "z", lambda pos, h: gu.at[whole(pos, 384), pl.ds(h * 512, 512)]
    )

    def both_heads(ref, core, span):
        return jnp.concatenate([ref[core, span, 0:128], ref[core, span, 128:256]], axis=0)

    def attend(core, run):
        span = pl.ds(run * WIN, WIN)
        window = pl.ds(run * WIN, SEQ)
        scores = dot(both_heads(q, core, span), kv[core, window, 0:128], 1, 1)
        row, column = grid_of(2 * WIN, SEQ)
        row = row & (WIN - 1)
        spot_of = spot.high * HALF + run * WIN + row[0:WIN, 0:1]
        begin = jnp.maximum(
            (spot_of >> 9) << 9, spot_of - grad_kv[core, span, 0:1].astype(jnp.int32)
        )
        begin = begin - (spot.high * HALF + run * WIN) + WIN
        begin = jnp.concatenate([begin, begin], axis=0)
        allowed = (column >= begin) & (column <= row + WIN)
        scores = jnp.where(allowed, scores, MASKED)
        weights = jnp.exp(scores - jnp.max(scores, axis=-1, keepdims=True))
        share = weights * (1.0 / jnp.sum(weights, axis=-1, keepdims=True))
        rounded = share.astype(BF16)
        prob[core, run] = rounded
        values = dot(rounded, kv[core, window, 128:256], 1, 0).astype(BF16)
        mix[core, span, 0:128] = values[0:WIN]
        mix[core, span, 128:256] = values[WIN : 2 * WIN]

    repeat(2, lambda i: attend(i, 1))
    gu_side.forward()
    dn_line[0].begin()
    repeat(2, lambda i: attend(i, 2))
    dn_line[1].forward()
    out_line.near()
    out_line.far()
    out_rows = picks(256, 256, out_row)
    wo[...] = dot(out_rows, ao[...].reshape(256, D), 1, 0).astype(BF16).reshape(4, 4, 16, D)

    def project_out(core, half):
        rows = mix[core, half * 384 : half * 384 + 384, :]
        out = dot(rows, wo[...].reshape(256, D), 1, 0).astype(BF16)
        part[core, half * 2 : half * 2 + 2] = out.reshape(2, OWN, D)

    def share_all(sums):
        for s in sums:
            s.share()

    def back_hidden(i):
        start, size = THREE[i]

        def step(core):
            rows = cots[core, :, pl.ds(start, size)].reshape(4 * size, D)
            grad = dot(rows, dn[...].reshape(512, D), 1, 1).astype(BF16)
            grad_hidden[core, pl.ds(4 * start, 4 * size)] = grad

        repeat(2, step)

    rows_x = [PairGather(wires, spot, "x", second, own, s, n) for s, n in THREE]
    sums_y = [PairScatter(wires, spot, "y", part, got, passed, near, s, n) for s, n in THREE]
    repeat(2, lambda i: project_out(i, 1))
    sums_y[0].share(1)
    for copy in kv_got:
        copy.wait_recv()
    cot_x[1].start()
    gu_side.near()
    gu_side.far()
    gu_line.start()
    repeat(2, lambda i: attend(i, 0))
    cot_x[1].rest()
    dn_line[0].forward()
    project_out(1 - c, 0)
    sums_y[0].share(0)
    project_out(c, 0)
    for g in rows_y:
        g.close()
    normed_kept.wait()
    sums_y[0].first()
    cot_x[1].forward()
    gu_line.rest()
    cot_x[0].far()
    cot_x[0].finish()
    sums_y[0].left()
    sums_y[0].direct()
    sums_y[1].share()
    cot_x[1].near()
    sums_y[0].through()
    gu_line.forward()
    cot_x[1].far()
    sums_y[0].gone()
    sums_y[1].first()
    sums_y[2].share()
    for line in dn_line:
        line.near()
        line.far()
    cot_x[1].finish()

    def middle_rows(s):
        def use(span):
            middle = tokens[span, :].astype(F32) + s.total(span)
            middle_all[span, :] = middle
            own[span, :] = (middle * norm_scale(middle) * gains[1:2, :]).astype(BF16)

        return use

    def gather_next(i):
        s = sums_y[i]
        s.arrive()
        over_rows(s.start_row, s.size, middle_rows(s))
        s.close()
        rows_x[i].start()

    gather_next(0)
    sums_y[1].direct()
    back_hidden(0)
    sums_y[1].through()
    rows_x[0].rest()
    grad_kv[...] = jnp.zeros_like(grad_kv)
    wires.done(left)
    rows_x[0].forward()
    sums_y[1].gone()
    sums_y[2].first()
    back_hidden(1)
    gather_next(1)
    sums_y[2].direct()
    rows_x[0].near()
    back_hidden(2)
    sums_y[2].through()
    rows_x[1].rest()
    rows_x[0].far()
    rows_x[1].forward()
    gu_line.near()
    gu_line.far()
    rows_x[0].finish()

    def feed(core, i):
        start, part_size = THREE[i]
        span, size = pl.ds(start, part_size), 4 * part_size
        rows = second[core, :, span].reshape(size, D)
        both = dot(rows, gu[...], 1, 0)
        upstream = grad_hidden[core, pl.ds(4 * start, size)].astype(F32)
        for j in range(4):
            gate = both[:, j * 256 : j * 256 + 128]
            upward = both[:, j * 256 + 128 : j * 256 + 256]
            sent = upstream[:, j * 128 : j * 128 + 128]
            sigmoid = jax.nn.sigmoid(gate)
            silu = gate * sigmoid
            slope = sigmoid * (1.0 + gate * (1.0 - sigmoid))
            for first, values in (
                (1024 + j * 128, silu * upward),
                (j * 256, sent * upward * slope),
                (j * 256 + 128, sent * silu),
            ):
                rounded = values.astype(BF16).reshape(4, part_size, 128)
                work[core, :, span, first : first + 128] = rounded
        back = dot(work[core, :, span, 0:1024].reshape(size, 1024), gu[...], 1, 1)
        part[core, :, span] = back.astype(BF16).reshape(4, part_size, D)

    sums_x = [PairScatter(wires, spot, "x", part, got, passed, near, s, n) for s, n in THREE]
    grads_y = [PairGather(wires, spot, "y", normed, own, s, n) for s, n in THREE]

    def feed_both(i):
        sums_x[i].share(start=False)

        def step(k):
            feed(jnp.where(k == 0, spot.other, c), i)

            @pl.when(k == 0)
            def _():
                sums_x[i].shared[0].start()

        repeat(2, step)

    gather_next(2)
    early = wires.started()
    wires.again()

    def grad_gate_up(i):
        lanes = whole(i, 256)
        rows = second[:, :, :, lanes].reshape(8 * OWN, 256)
        sent = work[:, :, :, 0:1024].reshape(8 * OWN, 1024)
        d_gu[lanes, :] = dot(rows, sent, 0, 0).astype(BF16)

    def grad_down(i):
        lanes = pl.ds(pl.multiple_of(1024 + i * 256, 256), 256)
        rows = work[:, :, :, lanes].reshape(8 * OWN, 256)
        grad = dot(rows, cots[...].reshape(8 * OWN, D), 0, 0).astype(BF16)
        d_dn[pl.ds(i * 2, 2)] = grad.reshape(2, 4, 32, D)

    def down(i):
        rows = work[i // 2, pl.ds((i % 2) * 2, 2), :, 1024:D].reshape(384, 512)
        second[i // 2, pl.ds((i % 2) * 2, 2)] = (
            dot(rows, dn[...].reshape(512, D), 1, 0).astype(BF16).reshape(2, OWN, D)
        )

    def back_rows(s):
        def use(span):
            grad = s.total(span)
            rows = middle_all[span, :]
            inverse = norm_scale(rows)
            back = cot[span, :].astype(F32) + norm_back(grad, rows, inverse, gains[1:2, :])
            back_all[span, :] = back
            own[span, :] = back.astype(BF16)
            fold(total, grad * rows * inverse)

        return use

    def gather_back(i):
        s = sums_x[i]
        s.arrive()
        rows_x[i].close()
        over_rows(s.start_row, s.size, back_rows(s))
        s.close()
        grads_y[i].start()

    def mix_back(i):
        first, size = THREE[i]

        def step(core):
            rows = normed[core, :, pl.ds(first, size)].reshape(4 * size, D)
            grad = dot(rows, wo[...].reshape(256, D), 1, 1).astype(BF16)
            for pos in range(4):
                start = pos * OWN + first
                grad_mix[core, start : start + size, :] = grad[pos * size : pos * size + size]

        repeat(2, step)

    total[...] = jnp.zeros_like(total)

    feed_both(0)
    rows_x[2].rest()
    rows_x[2].forward()
    rows_x[1].near()
    rows_x[1].far()
    sums_x[0].first()
    rows_x[1].finish()
    feed_both(1)
    rows_x[2].near()
    sums_x[0].direct()
    rows_x[2].far()
    sums_x[0].through()
    sums_x[1].first()
    rows_x[2].finish()
    sums_x[1].direct()
    feed_both(2)
    sums_x[2].first()
    gather_back(0)
    sums_x[1].through()
    sums_x[2].direct()
    wires.done(early)
    tell(0, [spot.along("z", 1), spot.along("z", -1)])

    grads_y[0].rest()
    repeat(2, grad_gate_up)
    grads_y[0].forward()
    repeat(2, lambda i: grad_gate_up(2 + i))
    sums_x[2].through()
    gather_back(1)
    grads_y[0].near()
    repeat(2, lambda i: grad_gate_up(4 + i))
    grads_y[1].rest()
    hear(0, 2)
    gu_sum = [
        LineScatter(
            wires, spot, "z",
            lambda pos, h, lot=lot: d_gu.at[whole(pos * 4 + lot * 2 + h, 96)],
            lambda h, lot=lot: gu.at[pl.ds(lot * 192 + h * 96, 96)],
            lambda h, lot=lot: gu.at[pl.ds(384 + lot * 192 + h * 96, 96)],
            lambda side, h, lot=lot: gu.at[pl.ds(768 + side * 384 + lot * 192 + h * 96, 96)],
        )
        for lot in (0, 1)
    ]
    gu_got = []

    def gu_beside(lot):
        gu_sum[lot].finish()
        for by in (1, -1, 2):
            part_of = d_gu.at[whole(z * 2 + lot, 192), whole(turn(y, by), 256)]
            into = gu_in.at[y, pl.ds(lot * 192, 192)]
            gu_got.append(wires.send(part_of, into, spot.along("y", by)))

    gu_sum[0].first()
    grads_y[0].far()
    gather_back(2)
    grads_y[1].forward()
    grads_y[2].rest()
    repeat(2, grad_down)
    grads_y[0].finish()
    mix_back(0)
    grads_y[1].near()
    grads_y[2].forward()
    gu_sum[0].second()
    gu_sum[1].first()
    grads_y[1].far()
    repeat(4, down)
    grads_y[2].near()
    grads_y[1].finish()
    mix_back(1)
    grads_y[2].far()
    tell(1, around(spot, "xy") + [spot.along("z", 1), spot.along("z", -1)])
    again = wires.move(normed_out, cots)
    gain_c[c, 1:2] = jnp.sum(total[...], axis=0, keepdims=True)
    grads_y[2].finish()
    mix_back(2)
    left = wires.started()

    def attend_back(core, run):
        span = pl.ds(run * WIN, WIN)
        window = pl.ds(run * WIN, SEQ)
        rounded = prob[core, run]
        mixed = both_heads(grad_mix, core, span)
        inner = mixed.astype(F32) * both_heads(mix, core, span).astype(F32)
        inner = jnp.sum(inner, axis=-1, keepdims=True)
        grad = dot(mixed, kv[core, window, 128:256], 1, 1)
        scored = (rounded.astype(F32) * (grad - inner)).astype(BF16)
        grad_kv[core, window, 0:128] += dot(scored, both_heads(q, core, span), 0, 0)
        grad_kv[core, window, 128:256] += dot(rounded, mixed, 0, 0)
        grad_q = dot(scored, kv[core, window, 0:128], 1, 0) * scale
        cos, sin = cosine[core, span, :], sine[core, span, :]
        for head in (0, 1):
            grad = grad_q[head * WIN : head * WIN + WIN]
            grad = (grad * cos - swap_halves(grad) * sin).astype(BF16)
            q[core, span, head * 128 : head * 128 + 128] = grad

    def send_far(core):
        far_from = grad_mix.at[core, pl.ds(0, WIN)]
        far_from[...] = grad_kv[core, 0:WIN, :].astype(BF16)
        return wires.send(far_from, far_kv.at[core], spot.along("x", 2))

    far_got = []
    for core in (0, 1):
        attend_back(core, 0)
        far_got.append(send_far(core))
    gu_beside(0)
    hear(1, 7)
    sums_m = [
        PairScatter(
            wires, spot, "x", second, work.at[0], work.at[1, 0], work.at[1, pl.ds(1, 2)], s, n
        )
        for s, n in TWO
    ]
    sums_m[0].share()
    repeat(2, lambda i: attend_back(i, 1))
    gu_sum[1].second()
    sums_m[0].first()
    sums_m[0].direct()
    sums_m[1].share()
    repeat(2, lambda i: attend_back(i, 2))
    sums_m[1].first()
    sums_m[1].direct()
    dn_sum = LineScatter(
        wires, spot, "z",
        lambda pos, h: d_dn.at[pl.ds(2 * h, 2), pos],
        lambda h: dn.at[0, pl.ds(2 * h, 2)],
        lambda h: dn.at[1, pl.ds(2 * h, 2)],
        lambda side, h: dn.at[2 + side, pl.ds(2 * h, 2)],
    )
    dn_sum.first()

    def turn_back(core, pos):
        after = pl.ds(pl.multiple_of(WIN + pos * OWN, 64), OWN)
        span = whole(pos, OWN)
        cos, sin = cosine[core, span, :], sine[core, span, :]
        keyed = grad_kv[core, after, 0:128]
        keyed = pltpu.roll(keyed * cos - swap_halves(keyed) * sin, 64, 1)
        valued = pltpu.roll(grad_kv[core, after, 128:256], 32, 1)
        front = q[core, span, 0:128].astype(F32)
        behind = pltpu.roll(q[core, span, 128:256].astype(F32), 96, 1)
        lane = lax.broadcasted_iota(jnp.int32, front.shape, 1)
        q[core, span, 0:128] = jnp.where(lane < 96, front, behind).astype(BF16)
        q[core, span, 128:256] = jnp.where(lane < 64, behind, keyed).astype(BF16)
        kv[core, after, 0:128] = jnp.where(lane < 32, keyed, valued).astype(BF16)


    def normed_back(core, half):
        after = pl.ds(WIN + half * 384, 384)
        span = pl.ds(half * 384, 384)
        rows = jnp.concatenate([q[core, span, :], kv[core, after, 0:128]], axis=1)
        grad = dot(rows, aq[...].reshape(D, 384), 1, 1).astype(BF16)
        part[core, half * 2 : half * 2 + 2] = grad.reshape(2, OWN, D)

    sums_n = [PairScatter(wires, spot, "y", part, got, passed, near, s, n) for s, n in THREE]
    repeat(4, lambda i: turn_back(i // 2, i % 2))
    repeat(2, lambda i: normed_back(i, 0))
    for s in sums_n:
        s.share(0)
    gu_beside(1)
    for copy in far_got:
        copy.wait_recv()
    for core in (0, 1):
        grad_kv[core, 768:1024, :] += far_kv[core].astype(F32)
    repeat(4, lambda i: turn_back(i // 2, 2 + i % 2))
    normed_back(1 - c, 1)
    for s in sums_n:
        s.share(1)
    normed_back(c, 1)
    sums_n[0].first()
    sums_n[1].first()
    sums_n[2].first()
    sums_m[0].through()
    dn_sum.second()

    def out_rows_back(r, k):
        unit = jnp.where(k < 128, k, k - 32)
        real = (k < 96) | ((k >= 128) & (k < 224))
        return real & (unit + ((unit * 5462) >> 16) * 4 == r)

    grad_out = dot(mix[...].reshape(8 * OWN, 256), normed[...].reshape(8 * OWN, D), 0, 0)
    grad_out = dot(picks(256, 256, out_rows_back), grad_out.astype(BF16), 1, 0)
    wo[...] = grad_out.astype(BF16).reshape(4, 4, 16, D)
    out_sum = LineScatter(
        wires, spot, "z",
        lambda pos, h: wo.at[pos, pl.ds(2 * h, 2)],
        lambda h: ao.at[0, pl.ds(2 * h, 2)],
        lambda h: ao.at[1, pl.ds(2 * h, 2)],
        lambda side, h: ao.at[2 + side, pl.ds(2 * h, 2)],
    )
    out_sum.first(paced=True)
    again.wait()

    def grad_columns(i):
        rows = cots[:, :, :, whole(i, 384)].reshape(8 * OWN, 384)
        asked = dot(rows, q[...].reshape(8 * OWN, 256), 0, 0)
        other = dot(rows, kv[:, pl.ds(WIN, HALF), 0:128].reshape(8 * OWN, 128), 0, 0)
        d_att[i, :, :, 0:256] = asked.astype(BF16).reshape(4, 96, 256)
        d_att[i, :, :, 256:384] = other.astype(BF16).reshape(4, 96, 128)
        held = aq[i].reshape(384, 384).astype(F32)
        folded = (
            held[:, 0:128] * asked[:, 0:128]
            + held[:, 128:256] * asked[:, 128:256]
            + held[:, 256:384] * other
        )
        gain_c[c, 0:1, whole(i, 384)] = jnp.sum(folded.T, axis=0, keepdims=True)

    repeat(4, grad_columns)
    gain_c[c, 0:1] = gain_c[c, 0:1] / gains[0:1, :]
    tell(2, [spot.along(a, by) for a in "xz" for by in (1, -1)])
    gain_got = [wires.send(gain_c.at[c], gain_c.at[c], spot.sibling)]
    for s in sums_n:
        s.direct()
    sums_m[1].through()
    out_sum.direct()
    wires.done(left)
    hear(2, 4)
    att_sum = [
        LineScatter(
            wires, spot, "x",
            lambda pos, h: d_att.at[pl.ds(2 * h, 2), slot_of(pos), low],
            lambda h: aq.at[0, pl.ds(2 * h, 2), low],
            lambda h: aq.at[1, pl.ds(2 * h, 2), low],
            lambda side, h: aq.at[2 + side, pl.ds(2 * h, 2), low],
        ),
        LineScatter(
            wires, spot, "z",
            lambda pos, h: d_att.at[pos, pl.ds(2 * h, 2), high],
            lambda h: aq.at[0, pl.ds(2 * h, 2), high],
            lambda h: aq.at[1, pl.ds(2 * h, 2), high],
            lambda side, h: aq.at[2 + side, pl.ds(2 * h, 2), high],
        ),
    ]
    for line in att_sum:
        line.first(paced=True)

    def add_gains(held, axis, into):
        for copy in gain_got:
            copy.wait_recv()
        summed = held[0]
        for i in range(1, held.shape[0]):
            summed = summed + held[i]
        if into is None:
            gains_out[...] = summed
            return []
        me = spot.me(axis)
        into[me] = summed
        return [wires.send(into.at[me], into.at[me], spot.along(axis, by)) for by in (1, -1, 2)]

    gain_got = add_gains(gain_c, "x", gain_x)
    for line in att_sum:
        line.direct()
    out_sum.second()
    for s in sums_n:
        s.through()
    for line in (att_sum[1], att_sum[0]):
        line.second()
    for copy in gu_got:
        copy.wait_recv()
    mine = d_gu.at[whole(z, 384), whole(y, 256)]
    add_into(mine, mine, *[gu_in.at[turn(y, by)] for by in (1, -1, 2)])
    gu_done = []
    for by in (1, 2, 3):
        other, who = spot.in_quad(by)
        rows = d_gu.at[whole(z * 4 + other, 96), whole(y, 256)]
        gu_done.append(wires.send(rows, gu_own.at[spot.quad], who))
    gain_got = add_gains(gain_x, "z", gain_z)

    def token_rows(s):
        def use(span):
            grad = s.total(span)
            rows = tokens[span, :].astype(F32)
            inverse = norm_scale(rows)
            out = back_all[span, :] + norm_back(grad, rows, inverse, gains[0:1, :])
            part[c, y, span] = out.astype(BF16)

        return use

    def result_rows(s):
        def use(span):
            second[c, x, span] = (middle_all[span, :] + s.total(span)).astype(BF16)

        return use

    token_kept = []

    def token_part(i):
        s = sums_n[i]
        s.arrive()
        over_rows(s.start_row, s.size, token_rows(s))
        token_kept.append(wires.move(part.at[c, y, s.rows()], token_out.at[s.rows()]))

    def result_part(s):
        s.arrive()
        over_rows(s.start_row, s.size, result_rows(s))

    dn_sum.finish()
    dn_got = [
        wires.send(d_dn.at[turn(y, by), z], dn_in.at[y], spot.along("y", by)) for by in (1, -1, 2)
    ]
    for s in sums_m:
        result_part(s)
    result_kept = wires.move(second.at[c, x], result_out)
    for line in att_sum:
        line.finish()

    def home(pos):
        stay = pos // 2 == c
        return device(jnp.where(stay, pos, turn(pos, 2)), y, z, jnp.where(stay, c, 1 - c))

    places_z = [(turn(z, by), who) for by, who in zip((0, 1, -1, 2), line_z)]
    places_x = [turn(x, by) for by in (0, 1, -1, 2)]
    att_got = [
        Placed(
            wires, stays, [(d_att.at[to, slot, low], att_in.at[z, low], w) for to, w in places_z]
        ),
        Placed(
            wires, stays,
            [(d_att.at[z, slot_of(to), high], att_in.at[x, high], home(to)) for to in places_x],
        ),
    ]
    out_sum.finish()
    out_got = Placed(
        wires, stays, [(wo.at[z, slot_of(to)], out_in.at[x], home(to)) for to in places_x]
    )
    gain_got = add_gains(gain_z, "y", gain_y)
    kept_rows = d_gu.at[whole(z * 4 + spot.quad, 96), whole(y, 256)]
    gu_own[spot.quad] = kept_rows[...]
    token_part(0)
    token_part(1)
    token_part(2)
    for copy in gu_done:
        copy.wait_recv()
    order = picks(512, 512, lambda r, k: quad_order(k) == r)
    for into, first in ((gate_out, 0), (up_out, 128)):
        moved = jnp.concatenate([gu_own[i, :, first : first + 128] for i in range(4)], axis=1)
        into[...] = dot(moved, order, 1, 0)
    for copy in dn_got:
        copy.wait_recv()
    add_into(
        dn_out, d_dn.at[y, z], *[dn_in.at[turn(y, by)] for by in (1, -1, 2)]
    )
    for piece in att_got:
        piece.wait()
    add_into(att_out, *[att_in.at[i] for i in range(4)])
    out_got.wait()
    add_into(out_out, *[out_in.at[i] for i in range(4)])
    add_gains(gain_y, None, None)
    result_kept.wait()
    for copy in token_kept:
        copy.wait()
    for piece in att_got + [out_got]:
        piece.close()
    wires.close()


def finish_kernel(
    result, token, gains, att, out, gate, up, dn,
    result_out, token_out, attn_out, mlp_out, query_out, key_out, value_out, out_out,
    gate_out, up_out, dn_out,
):
    for src, dst in (
        (result, result_out), (token, token_out), (gate, gate_out), (up, up_out), (dn, dn_out)
    ):
        dst[...] = src[...]
    for i, into in enumerate((attn_out, mlp_out)):
        for j in range(12):
            into[j : j + 1, :] = gains[i : i + 1, j * 128 : j * 128 + 128]
    rows = att[...]

    def three(first):
        return lambda r, k: r == k + first

    query_out[...] = dot(rows, picks(384, 192, three(0)), 1, 0)
    key_out[...] = dot(rows, picks(384, 96, three(192)), 1, 0)
    value_out[...] = dot(rows, picks(384, 96, three(288)), 1, 0)
    out_out[...] = out[0:12, :].astype(F32)


def layer_call(
    tokens, gain_attn, gain_mlp, cot, w_query, w_key, w_value, w_out, w_gate, w_up, w_down, marks
):
    sends, receives = 110, 174
    shape = jax.ShapeDtypeStruct
    outs = (
        (shape((2, 4, OWN, D), BF16), ANY),
        (shape((OWN, D), BF16), ANY),
        (shape((OWN, D), BF16), ANY),
        (shape((2, D), F32), VMEM),
        (shape((96, 384), BF16), VMEM),
        (shape((16, D), BF16), VMEM),
        (shape((96, 512), F32), VMEM),
        (shape((96, 512), F32), VMEM),
        (shape((32, D), F32), VMEM),
    )
    scratch = [
        ((2, 4, OWN, D), BF16),
        ((2, 4, OWN, D), BF16),
        ((2, 4, OWN, D), BF16),
        ((2, 4, OWN, D), BF16),
        ((4, OWN, D), BF16),
        ((OWN, D), BF16),
        ((2, OWN, D), BF16),
        ((2, 4, OWN, D), BF16),
        ((1, 96, 384), BF16),
        ((1, 16, D), BF16),
        ((4, 4, 96, 384), BF16),
        ((4, 4, 16, D), BF16),
        ((4, 4, 96, 384), BF16),
        ((4, 4, 16, D), BF16),
        ((D, 1024), BF16),
        ((4, 96, 256), BF16),
        ((4, 4, 32, D), BF16),
        ((D, 1024), BF16),
        ((4, 4, 32, D), BF16),
        ((OWN, D), BF16),
        ((2, 4 * OWN, 512), BF16),
        ((2, HALF, 256), BF16),
        ((2, HALF + WIN, 256), BF16),
        ((2, 3, 2 * WIN, SEQ), BF16),
        ((2, HALF, 256), BF16),
        ((2, HALF, 128), F32),
        ((2, HALF, 128), F32),
        ((2, 12, 128), jnp.int32),
        ((2, D), F32),
        ((OWN, D), F32),
        ((OWN, D), F32),
        ((8, D), F32),
        ((2, HALF, 256), BF16),
        ((2, HALF + WIN, 256), F32),
        ((2, WIN, 256), BF16),
        ((4, 384, 256), BF16),
        ((4, 32, D), BF16),
        ((4, 96, 384), BF16),
        ((4, 16, D), BF16),
        ((2, 2, D), F32),
        ((4, 2, D), F32),
        ((4, 2, D), F32),
        ((4, 2, D), F32),
    ]
    outs_raw = pl.pallas_call(
        layer_kernel,
        out_shape=tuple(o[0] for o in outs),
        in_specs=[VMEM] * 12,
        out_specs=[o[1] for o in outs],
        scratch_shapes=[pltpu.VMEM(*s) for s in scratch]
        + [
            pltpu.SemaphoreType.REGULAR((3,)),
            pltpu.SemaphoreType.DMA((sends,)),
            pltpu.SemaphoreType.DMA((receives,)),
        ],
        compiler_params=pltpu.CompilerParams(
            collective_id=1, has_side_effects=True, vmem_limit_bytes=64 << 20
        ),
        name="layer",
    )(tokens, gain_attn, gain_mlp, cot, w_query, w_key, w_value, w_out, w_gate, w_up, w_down, marks)
    finals = (
        shape((OWN, D), BF16),
        shape((OWN, D), BF16),
        shape((12, 128), F32),
        shape((12, 128), F32),
        shape((96, 192), F32),
        shape((96, 96), F32),
        shape((96, 96), F32),
        shape((12, D), F32),
        shape((96, 512), F32),
        shape((96, 512), F32),
        shape((32, D), F32),
    )
    return pl.pallas_call(
        finish_kernel,
        out_shape=finals,
        in_specs=[VMEM] * 8,
        out_specs=[VMEM] * 11,
        name="finish",
    )(*outs_raw[1:])


def shards(
    tokens,
    gain_attn,
    gain_mlp,
    w_query,
    w_key,
    w_value,
    w_out,
    w_gate,
    w_up,
    w_down,
    segments,
    positions,
    cotangent,
):
    del segments
    done = layer_call(
        tokens,
        gain_attn.reshape(12, 128),
        gain_mlp.reshape(12, 128),
        cotangent,
        w_query,
        w_key,
        w_value,
        w_out,
        w_gate,
        w_up,
        w_down,
        positions.reshape(12, 128),
    )
    return (*done[:2], done[2].reshape(D), done[3].reshape(D), *done[4:])


def solution(mesh):
    placed = (
        P(("dp", "tensor"), None),
        P(),
        P(),
        P("dp", "tensor"),
        P("dp", "tensor"),
        P("dp", "tensor"),
        P(("tensor", "dp"), None),
        P("dp", "tensor"),
        P("dp", "tensor"),
        P(("tensor", "dp"), None),
        P("dp"),
        P("dp"),
        P(("dp", "tensor"), None),
    )
    return jax.shard_map(
        shards,
        mesh=mesh,
        in_specs=placed,
        out_specs=(
            P(("dp", "tensor"), None),
            P(("dp", "tensor"), None),
            P(),
            P(),
            P("dp", "tensor"),
            P("dp", "tensor"),
            P("dp", "tensor"),
            P(("tensor", "dp"), None),
            P("dp", "tensor"),
            P("dp", "tensor"),
            P(("tensor", "dp"), None),
        ),
        check_vma=False,
    )
```

```python
import functools
import math

import jax
import jax.numpy as jnp
from jax import lax
from jax.experimental import pallas as pl
from jax.experimental.pallas import tpu as pltpu
from jax.sharding import PartitionSpec as P

HD = 96
SEQ = 512
D = 1536
OWN = 192
HALF = 768
WIN = 256

EPSILON = 1e-05
ROPE_BASE = 100000.0
MASKED = -1e30
MESH = pl.DeviceIdType.MESH
ANY = pl.BlockSpec(memory_space=pl.ANY)
VMEM = pl.BlockSpec(memory_space=pltpu.VMEM)
BF16 = jnp.bfloat16
F32 = jnp.float32


def place():
    dp = lax.axis_index("dp")
    tensor = lax.axis_index("tensor")
    return (tensor // 4) * 2 + (dp // 2) % 2, tensor % 4, dp // 4, dp % 2


def device(x, y, z, c):
    return (z * 4 + (x % 2) * 2 + c, (x // 2) * 4 + y)


def turn(pos, by):
    return (pos + by + 4) % 4


class Spot:
    def __init__(self):
        x, y, z, c = place()
        self.x, self.y, self.z, self.c = x, y, z, c
        self.high, self.low, self.other = x // 2, x % 2, 1 - c
        self.quad = self.low * 2 + c
        self.sibling = device(x, y, z, 1 - c)
        self.partner = device(turn(x, 2), y, z, 1 - c)

    def along(self, axis, by):
        x, y, z, c = self.x, self.y, self.z, self.c
        if axis == "x":
            return device(turn(x, by), y, z, c)
        if axis == "y":
            return device(x, turn(y, by), z, c)
        return device(x, y, turn(z, by), c)

    def me(self, axis):
        return {"x": self.x, "y": self.y, "z": self.z}[axis]

    def in_quad(self, by):
        other = turn(self.quad, by)
        return other, device(self.high * 2 + other // 2, self.y, self.z, other % 2)


def greet(devices):
    for who in devices:
        pl.semaphore_signal(
            pltpu.get_barrier_semaphore(), inc=1, device_id=who, device_id_type=MESH
        )


def greeted(devices):
    pl.semaphore_wait(pltpu.get_barrier_semaphore(), len(devices))


class Wires:
    def __init__(self, send_sem, recv_sem):
        self.send_sem, self.recv_sem = send_sem, recv_sem
        self.free = list(range(send_sem.shape[0]))
        self.count = 0
        self.sent = []

    def again(self):
        self.count = 0

    def take(self):
        held = min(self.free)
        self.free.remove(held)
        return held

    def forget(self, copy):
        self.free += [held for other, held in self.sent if other is copy]
        self.sent = [pair for pair in self.sent if pair[0] is not copy]

    def send(self, src, dst, who, start=True):
        held = self.take()
        assert self.count < self.recv_sem.shape[0]
        copy = pltpu.make_async_remote_copy(
            src_ref=src,
            dst_ref=dst,
            send_sem=self.send_sem.at[held],
            recv_sem=self.recv_sem.at[self.count],
            device_id=who,
            device_id_type=MESH,
        )
        self.count += 1
        if start:
            copy.start()
        self.sent.append((copy, held))
        return copy

    def move(self, src, dst):
        held = self.take()
        copy = pltpu.make_async_copy(src, dst, self.send_sem.at[held])
        copy.start()
        return Moved(self, copy, held)

    def done(self, copies):
        kept = []
        for copy, held in self.sent:
            if any(copy is other for other in copies):
                copy.wait_send()
                self.free.append(held)
            else:
                kept.append((copy, held))
        self.sent = kept

    def started(self):
        return [copy for copy, _ in self.sent]

    def close(self):
        self.done(self.started())


class Placed:
    def __init__(self, wires, stays, pieces):
        self.wires, self.stays = wires, stays
        self.others = [wires.send(*piece) for piece in pieces[1:]]
        self.own = wires.send(*pieces[0], start=False)
        held = wires.sent[-1][1]

        @pl.when(jnp.logical_not(stays))
        def _():
            self.own.start()

        @pl.when(stays)
        def _():
            kept = pltpu.make_async_copy(pieces[0][0], pieces[0][1], wires.send_sem.at[held])
            kept.start()
            kept.wait()

    def wait(self):
        for copy in self.others:
            copy.wait_recv()

        @pl.when(jnp.logical_not(self.stays))
        def _():
            self.own.wait_recv()

    def close(self):
        self.wires.done(self.others)

        @pl.when(jnp.logical_not(self.stays))
        def _():
            self.own.wait_send()

        self.wires.forget(self.own)


class Moved:
    def __init__(self, wires, copy, held):
        self.wires, self.copy, self.held = wires, copy, held

    def wait(self):
        self.copy.wait()
        self.wires.free.append(self.held)


def add_into(dst, *srcs, chunk=16):
    rows = dst.shape[-2]
    chunk = min(chunk, rows)

    def step(i, carry):
        span = pl.ds(pl.multiple_of(i * chunk, chunk), chunk)
        total = srcs[0][..., span, :].astype(F32)
        for src in srcs[1:]:
            total = total + src[..., span, :].astype(F32)
        dst[..., span, :] = total.astype(dst.dtype)
        return carry

    lax.fori_loop(0, rows // chunk, step, 0)


class RingGather:
    def __init__(self, wires, spot, axis, at):
        self.wires, self.at = wires, at
        self.me = spot.me(axis)
        self.next, self.prev = spot.along(axis, 1), spot.along(axis, -1)

    def start(self, own=None):
        self.own = own or (lambda half: self.at(self.me, half))
        send, at, me = self.wires.send, self.at, self.me
        self.right0 = send(self.own(0), at(me, 0), self.next)
        self.left1 = send(self.own(1), at(me, 1), self.prev)

    def rest(self):
        send, at, me = self.wires.send, self.at, self.me
        self.right1 = send(self.own(1), at(me, 1), self.next)
        self.left0 = send(self.own(0), at(me, 0), self.prev)

    def begin(self):
        self.start()
        self.rest()

    def forward(self):
        send, at, me = self.wires.send, self.at, self.me
        self.right0.wait_recv()
        before = at(turn(me, -1), 0)
        self.pass0 = send(before, before, self.next)
        self.left1.wait_recv()
        after = at(turn(me, 1), 1)
        self.pass1 = send(after, after, self.prev)

    def near(self):
        self.right1.wait_recv()
        self.left0.wait_recv()

    def far(self):
        self.pass0.wait_recv()
        self.pass1.wait_recv()

    def close(self):
        near = [self.right0, self.left1, self.right1, self.left0]
        self.wires.done(near + [self.pass0, self.pass1])


class PairGather:
    def __init__(self, wires, spot, axis, out, own, start, size):
        self.wires, self.spot, self.out, self.own = wires, spot, out, own
        self.rows = pl.ds(start, size)
        cut = size // 2

        def half_rows(half):
            return pl.ds(start + half * cut, cut)

        self.half_rows = half_rows
        self.ring = RingGather(
            wires, spot, axis, lambda pos, half: out.at[spot.c, pos, half_rows(half)]
        )
        self.me = spot.me(axis)

    def share(self, pos):
        block = self.out.at[self.spot.c, pos, self.rows]
        return self.wires.send(block, block, self.spot.sibling)

    def start(self):
        self.ring.start(lambda half: self.own.at[self.half_rows(half)])
        mine = self.own.at[self.rows]
        place_of = self.out.at[self.spot.c, self.me, self.rows]
        self.shared = [self.wires.send(mine, place_of, self.spot.sibling)]
        self.kept = self.wires.move(mine, place_of)

    def rest(self):
        self.ring.rest()

    def forward(self):
        self.ring.forward()

    def near(self):
        self.ring.near()
        self.shared.append(self.share(turn(self.me, -1)))
        self.shared.append(self.share(turn(self.me, 1)))

    def far(self):
        self.ring.far()
        self.shared.append(self.share(turn(self.me, 2)))

    def finish(self):
        for copy in self.shared:
            copy.wait_recv()
        self.kept.wait()

    def close(self):
        self.ring.close()
        self.wires.done(self.shared)


class PairScatter:
    def __init__(self, wires, spot, axis, part, got, passed, near, start, size):
        self.wires, self.spot = wires, spot
        self.me = spot.me(axis)
        self.next, self.prev = spot.along(axis, 1), spot.along(axis, -1)
        self.part, self.got, self.passed, self.near = part, got, passed, near
        self.start_row, self.size, self.cut = start, size, size // 2
        self.shared = []

    def rows(self, half=None):
        if half is None:
            return pl.ds(self.start_row, self.size)
        return pl.ds(self.start_row + half * self.cut, self.cut)

    def share(self, half=None, start=True):
        places = slice(None) if half is None else pl.ds(half * 2, 2)
        copy = self.wires.send(
            self.part.at[self.spot.other, places, self.rows()],
            self.got.at[places, self.rows()],
            self.spot.sibling,
            start,
        )
        self.shared = (self.shared if half is not None else []) + [copy]

    def first(self):
        for copy in self.shared:
            copy.wait_recv()
        pos = turn(self.me, 2)
        mine = self.got.at[pos, self.rows()]
        add_into(mine, self.part.at[self.spot.c, pos, self.rows()], mine)
        self.pass0 = self.wires.send(
            self.got.at[pos, self.rows(0)], self.passed.at[self.rows(0)], self.next
        )
        self.pass1 = self.wires.send(
            self.got.at[pos, self.rows(1)], self.passed.at[self.rows(1)], self.prev
        )

    def left(self):
        self.wires.done([self.pass0, self.pass1])

    def gone(self):
        self.wires.done(self.arriving)

    def direct(self):
        self.arriving = []
        for by, half, who, side in ((1, 1, self.next, 0), (-1, 0, self.prev, 1)):
            pos = turn(self.me, by)
            mine = self.got.at[pos, self.rows(half)]
            add_into(mine, self.part.at[self.spot.c, pos, self.rows(half)], mine)
            self.arriving.append(self.wires.send(mine, self.near.at[side, self.rows(half)], who))

    def through(self):
        after, before = turn(self.me, 1), turn(self.me, -1)
        for pos, half, who, side, arrived in (
            (after, 0, self.next, 0, self.pass0),
            (before, 1, self.prev, 1, self.pass1),
        ):
            arrived.wait_recv()
            mine = self.got.at[pos, self.rows(half)]
            add_into(
                mine,
                self.part.at[self.spot.c, pos, self.rows(half)],
                mine,
                self.passed.at[self.rows(half)],
            )
            self.arriving.append(self.wires.send(mine, self.near.at[side, self.rows(half)], who))

    def arrive(self):
        for copy in self.arriving:
            copy.wait_recv()

    def close(self):
        self.wires.done(self.shared + [self.pass0, self.pass1] + self.arriving)

    def total(self, span):
        return (
            self.part[self.spot.c, self.me, span].astype(F32)
            + self.got[self.me, span].astype(F32)
            + self.near[0, span].astype(F32)
            + self.near[1, span].astype(F32)
        )


class LineScatter:
    def __init__(self, wires, spot, axis, at, passed, work, near):
        self.wires, self.at = wires, at
        self.me = spot.me(axis)
        self.next, self.prev = spot.along(axis, 1), spot.along(axis, -1)
        self.passed, self.work, self.near = passed, work, near

    def first(self, paced=False):
        send, me = self.wires.send, self.me
        far = turn(me, 2)
        self.pass0 = send(self.at(far, 0), self.passed(0), self.next)
        self.pass1 = send(self.at(far, 1), self.passed(1), self.prev)
        if not paced:
            self.direct()

    def direct(self):
        send, me = self.wires.send, self.me
        after, before = turn(me, 1), turn(me, -1)
        self.arriving = [
            send(self.at(after, 1), self.near(0, 1), self.next),
            send(self.at(before, 0), self.near(1, 0), self.prev),
        ]

    def second(self):
        for by, half, who, side, arrived in (
            (1, 0, self.next, 0, self.pass0),
            (-1, 1, self.prev, 1, self.pass1),
        ):
            arrived.wait_recv()
            add_into(self.work(half), self.at(turn(self.me, by), half), self.passed(half))
            self.arriving.append(self.wires.send(self.work(half), self.near(side, half), who))

    def finish(self):
        for copy in self.arriving:
            copy.wait_recv()
        for half in (0, 1):
            mine = self.at(self.me, half)
            add_into(mine, mine, self.near(0, half), self.near(1, half))


def norm_scale(values):
    return lax.rsqrt(jnp.mean(values * values, axis=-1, keepdims=True) + EPSILON)


def norm_back(upstream, values, inverse, gain):
    scaled = upstream * gain
    inner = jnp.sum(scaled * values, axis=-1, keepdims=True)
    return scaled * inverse - values * inner * (inverse * inverse * inverse) / values.shape[-1]


def over_rows(start, size, step, chunk=16):
    def body(i, carry):
        step(pl.ds(pl.multiple_of(start + i * chunk, chunk), chunk))
        return carry

    lax.fori_loop(0, size // chunk, body, 0)


def fold(total, values):
    part = values[0:8]
    for first in range(8, values.shape[0], 8):
        part = part + values[first : first + 8]
    total[...] += part


TWO = ((0, 96), (96, 96))
THREE = ((0, 64), (64, 64), (128, 64))
LOTS = ((0, 128), (128, 256))


def dot(left, right, a, b):
    return lax.dot_general(left, right, (((a,), (b,)), ((), ())), preferred_element_type=F32)


def repeat(count, step):
    def body(i, carry):
        step(i)
        return carry

    lax.fori_loop(0, count, body, 0)


def whole(i, size):
    return pl.ds(pl.multiple_of(i * size, size), size)


def grid_of(rows, columns):
    return (
        lax.broadcasted_iota(jnp.int32, (rows, columns), 0),
        lax.broadcasted_iota(jnp.int32, (rows, columns), 1),
    )


def picks(rows, columns, chosen):
    return jnp.where(chosen(*grid_of(rows, columns)), 1.0, 0.0).astype(BF16)


def quad_order(unit):
    return (((unit >> 5) & 3) << 7) + ((unit >> 7) << 5) + (unit & 31)


def swap_halves(values):
    lane = lax.broadcasted_iota(jnp.int32, values.shape, 1)
    up = pltpu.roll(values, 80, 1)
    down = pltpu.roll(values, 48, 1)
    return jnp.where(lane < 48, up, down)


def around(spot, axes):
    return [spot.along(a, by) for a in axes for by in (1, -1)] + [spot.sibling]


def layer_kernel(
    tokens, gain_attn, gain_mlp, cot, w_query, w_key, w_value, w_out, w_gate, w_up, w_down, marks,
    normed_out, result_out, token_out, gains_out, att_out, out_out, gate_out, up_out, dn_out,
    normed, cots, second, part, got, passed, near, work, att_two, own_out, aq, ao, d_att, wo,
    gu, gu_own, dn, d_gu, d_dn, own, grad_hidden, q, kv, prob, mix, cosine, sine,
    marks_two, gains, middle_all, back_all, total, grad_mix, grad_kv, far_kv,
    gu_in, dn_in, att_in, out_in, gain_c, gain_y, gain_x, gain_z,
    ready, send_sem, recv_sem,
):
    spot = Spot()
    wires = Wires(send_sem, recv_sem)
    x, y, z, c = spot.x, spot.y, spot.z, spot.c
    neighbours = (
        around(spot, "xyz")
        + [spot.along(a, 2) for a in "xyz"]
        + [spot.partner]
        + [spot.in_quad(by)[1] for by in (1, 2, 3)]
        + [device(turn(x, by), y, z, 1 - c) for by in (1, -1)]
        + [device(turn(x, 2), y, turn(z, by), 1 - c) for by in (1, -1, 2)]
    )
    greet(neighbours)

    def tell(which, devices):
        for who in devices:
            pl.semaphore_signal(ready.at[which], inc=1, device_id=who, device_id_type=MESH)

    def hear(which, count):
        pl.semaphore_wait(ready.at[which], count)

    for i, gain in enumerate((gain_attn, gain_mlp)):
        gains[i : i + 1, :] = jnp.concatenate([gain[j : j + 1, :] for j in range(12)], axis=1)

    def normalise(span):
        rows = tokens[span, :].astype(F32)
        own[span, :] = (rows * norm_scale(rows) * gains[0:1, :]).astype(BF16)

    over_rows(0, OWN, normalise)

    def three(first):
        return lambda r, k: r + first == k

    columns = (
        dot(w_query[...], picks(192, 384, three(0)), 1, 0)
        + dot(w_key[...], picks(96, 384, three(192)), 1, 0)
        + dot(w_value[...], picks(96, 384, three(288)), 1, 0)
    )
    att_two[0] = columns.astype(BF16)
    own_out[0] = jnp.zeros((16, D), BF16)
    own_out[0, 0:12] = w_out[...]
    greeted(neighbours)

    def slot_of(pos):
        return (pos % 2) * 2 + pos // 2

    slot = slot_of(x)
    low, high = pl.ds(0, 48), pl.ds(48, 48)
    stays = spot.high == c
    there_x, there_c = jnp.where(stays, x, turn(x, 2)), jnp.where(stays, c, 1 - c)
    there = slot_of(there_x)
    line_z = [device(there_x, y, turn(z, by), there_c) for by in (0, 1, -1, 2)]
    line_x = [device(turn(there_x, by), y, z, there_c) for by in (0, 1, -1, 2)]
    att_side = [
        Placed(
            wires, stays, [(att_two.at[0, low], aq.at[z, there, low], who) for who in line_z]
        ),
        Placed(
            wires, stays, [(att_two.at[0, high], aq.at[z, there, high], who) for who in line_x]
        ),
    ]
    rows_y = [PairGather(wires, spot, "y", normed, own, s, n) for s, n in TWO]
    for g in rows_y:
        g.start()
    out_side = Placed(wires, stays, [(own_out.at[0], ao.at[z, there], who) for who in line_x])
    marks_kept = wires.move(marks, marks_two.at[c])
    marks_got = wires.send(marks, marks_two.at[c], spot.sibling)

    order = picks(512, 512, lambda r, k: quad_order(r) == k)
    for shard, first in ((w_gate, 0), (w_up, 128)):
        moved = dot(shard[...], order, 1, 0).astype(BF16)
        for i in range(4):
            gu_own[i, :, first : first + 128] = moved[:, i * 128 : i * 128 + 128]
    gu_lanes = whole(y, 256)
    gu_here = gu.at[whole(z * 4 + spot.quad, 96), gu_lanes]
    gu_kept = wires.move(gu_own.at[spot.quad], gu_here)
    gu_swap = []
    for by in (1, 2, 3):
        other, who = spot.in_quad(by)
        gu_swap.append(wires.send(gu_own.at[other], gu_here, who))

    def trig(core):
        def step(i):
            span = whole(i, 128)
            row, lane = grid_of(128, 128)
            number = marks_two[core, pl.ds(spot.high * 6 + i, 1), :]
            ones = jnp.ones((128, 128), BF16)
            where = jnp.zeros((128, 128), F32)
            for digit, factor in ((number >> 5, 32.0), (number & 31, 1.0)):
                spread = jnp.where(row == lane, digit.astype(F32), 0.0).astype(BF16)
                where = where + factor * dot(spread, ones, 1, 0)
            grad_kv[core, span, 0:128] = where
            turns = jnp.where(lane < 48, lane, lane - 48).astype(F32) * (2.0 / HD)
            angle = where * jnp.exp(-math.log(ROPE_BASE) * turns)
            inside = lane < HD
            cosine[core, span, :] = jnp.where(inside, jnp.cos(angle), 0.0)
            wave = jnp.sin(angle)
            sine[core, span, :] = jnp.where(inside, jnp.where(lane < 48, -wave, wave), 0.0)

        repeat(6, step)

    marks_kept.wait()
    trig(c)
    for g in rows_y:
        g.rest()
    att_line = [
        RingGather(wires, spot, "x", lambda pos, h: aq.at[pl.ds(2 * h, 2), slot_of(pos), low]),
        RingGather(wires, spot, "z", lambda pos, h: aq.at[pos, pl.ds(2 * h, 2), high]),
    ]
    out_line = RingGather(wires, spot, "z", lambda pos, h: ao.at[pos, pl.ds(2 * h, 2)])
    cot_x = [PairGather(wires, spot, "x", cots, cot, s, n) for s, n in TWO]
    for piece in att_side:
        piece.wait()
    for line in att_line:
        line.begin()
    marks_got.wait_recv()
    trig(1 - c)
    for g in rows_y:
        g.forward()
    rows_y[0].near()
    for line in att_line:
        line.forward()
    out_side.wait()
    out_line.begin()
    dn_here = dn.at[y, z]
    dn_kept = wires.move(w_down, dn_here)
    first_rows, last_rows = pl.ds(0, 16), pl.ds(16, 16)
    dn_side = []
    for by in (1, -1, 2):
        for axis, rows in (("z", first_rows), ("y", last_rows)):
            dn_side.append(
                wires.send(w_down.at[rows], dn.at[y, z, rows], spot.along(axis, by))
            )
    cot_x[0].start()
    cot_x[0].rest()
    rows_y[1].near()
    for line in att_line:
        line.near()
        line.far()

    def out_row(r, k):
        unit = jnp.where(r < 128, r, r - 32)
        real = (r < 96) | ((r >= 128) & (r < 224))
        return real & (unit + ((unit * 5462) >> 16) * 4 == k)

    scale = HD ** (-0.5)

    def project(core, pos):
        both = dot(normed[core, pos], aq[...].reshape(D, 384), 1, 0)
        span = whole(pos, OWN)
        cos, sin = cosine[core, span, :], sine[core, span, :]
        tile = [both[:, 128 * i : 128 * i + 128] for i in range(3)]
        lane = lax.broadcasted_iota(jnp.int32, tile[0].shape, 1)

        def turned(values, factor=None):
            values = values * cos + swap_halves(values) * sin
            return (values if factor is None else values * factor).astype(BF16)

        q[core, span, 0:128] = turned(tile[0], scale)
        q[core, span, 128:256] = turned(
            jnp.where(lane < 32, pltpu.roll(tile[0], 32, 1), pltpu.roll(tile[1], 32, 1)), scale
        )
        after = pl.ds(pl.multiple_of(WIN + pos * OWN, 64), OWN)
        kv[core, after, 0:128] = turned(
            jnp.where(lane < 64, pltpu.roll(tile[1], 64, 1), pltpu.roll(tile[2], 64, 1))
        )
        kv[core, after, 128:256] = jnp.where(lane < HD, pltpu.roll(tile[2], 96, 1), 0.0).astype(
            BF16
        )

    for g in rows_y:
        g.kept.wait()
    repeat(3, lambda i: project(c, turn(y, i - 1)))
    for g in rows_y:
        for copy in g.shared[:3]:
            copy.wait_recv()
    repeat(3, lambda i: project(1 - c, turn(y, i - 1)))
    for g in rows_y:
        g.far()
    gu_kept.wait()
    for copy in gu_swap:
        copy.wait_recv()
    gu_side = RingGather(
        wires, spot, "y", lambda pos, h: gu.at[whole(z * 2 + h, 192), whole(pos, 256)]
    )
    gu_side.begin()
    out_line.forward()
    project(c, turn(y, 2))

    def send_kv(core):
        last, first = kv.at[core, pl.ds(768, WIN)], kv.at[core, pl.ds(0, WIN)]
        return wires.send(last, first, spot.along("x", 2))

    kv_got = [send_kv(c)]
    for g in rows_y:
        g.shared[3].wait_recv()
    project(1 - c, turn(y, 2))
    kv_got.append(send_kv(1 - c))
    dn_kept.wait()
    for copy in dn_side:
        copy.wait_recv()
    dn_line = [
        RingGather(wires, spot, "y", lambda pos, h: dn.at[pos, pl.ds(2 * h, 2), first_rows]),
        RingGather(wires, spot, "z", lambda pos, h: dn.at[pl.ds(2 * h, 2), pos, last_rows]),
    ]
    dn_line[1].begin()
    normed_kept = wires.move(normed, normed_out)
    for piece in att_side + [out_side]:
        piece.close()
    left = wires.started()
    cot_x[0].forward()
    cot_x[0].near()
    gu_line = RingGather(
        wires, spot, "z", lambda pos, h: gu.at[whole(pos, 384), pl.ds(h * 512, 512)]
    )

    def both_heads(ref, core, span):
        return jnp.concatenate([ref[core, span, 0:128], ref[core, span, 128:256]], axis=0)

    def attend(core, run):
        span = pl.ds(run * WIN, WIN)
        window = pl.ds(run * WIN, SEQ)
        scores = dot(both_heads(q, core, span), kv[core, window, 0:128], 1, 1)
        row, column = grid_of(2 * WIN, SEQ)
        row = row & (WIN - 1)
        spot_of = spot.high * HALF + run * WIN + row[0:WIN, 0:1]
        begin = jnp.maximum(
            (spot_of >> 9) << 9, spot_of - grad_kv[core, span, 0:1].astype(jnp.int32)
        )
        begin = begin - (spot.high * HALF + run * WIN) + WIN
        begin = jnp.concatenate([begin, begin], axis=0)
        allowed = (column >= begin) & (column <= row + WIN)
        scores = jnp.where(allowed, scores, MASKED)
        weights = jnp.exp(scores - jnp.max(scores, axis=-1, keepdims=True))
        share = weights * (1.0 / jnp.sum(weights, axis=-1, keepdims=True))
        rounded = share.astype(BF16)
        prob[core, run] = rounded
        values = dot(rounded, kv[core, window, 128:256], 1, 0).astype(BF16)
        mix[core, span, 0:128] = values[0:WIN]
        mix[core, span, 128:256] = values[WIN : 2 * WIN]

    repeat(2, lambda i: attend(i, 1))
    gu_side.forward()
    dn_line[0].begin()
    repeat(2, lambda i: attend(i, 2))
    dn_line[1].forward()
    out_line.near()
    out_line.far()
    out_rows = picks(256, 256, out_row)
    wo[...] = dot(out_rows, ao[...].reshape(256, D), 1, 0).astype(BF16).reshape(4, 4, 16, D)

    def project_out(core, half):
        rows = mix[core, half * 384 : half * 384 + 384, :]
        out = dot(rows, wo[...].reshape(256, D), 1, 0).astype(BF16)
        part[core, half * 2 : half * 2 + 2] = out.reshape(2, OWN, D)

    def share_all(sums):
        for s in sums:
            s.share()

    def back_hidden(i):
        start, size = THREE[i]

        def step(core):
            rows = cots[core, :, pl.ds(start, size)].reshape(4 * size, D)
            grad = dot(rows, dn[...].reshape(512, D), 1, 1).astype(BF16)
            grad_hidden[core, pl.ds(4 * start, 4 * size)] = grad

        repeat(2, step)

    rows_x = [PairGather(wires, spot, "x", second, own, s, n) for s, n in THREE]
    sums_y = [PairScatter(wires, spot, "y", part, got, passed, near, s, n) for s, n in THREE]
    repeat(2, lambda i: project_out(i, 1))
    sums_y[0].share(1)
    for copy in kv_got:
        copy.wait_recv()
    cot_x[1].start()
    gu_side.near()
    gu_side.far()
    gu_line.start()
    repeat(2, lambda i: attend(i, 0))
    cot_x[1].rest()
    dn_line[0].forward()
    project_out(1 - c, 0)
    sums_y[0].share(0)
    project_out(c, 0)
    for g in rows_y:
        g.close()
    normed_kept.wait()
    sums_y[0].first()
    sums_y[0].left()
    sums_y[0].direct()
    cot_x[1].forward()
    gu_line.rest()
    sums_y[1].share()
    sums_y[0].through()
    cot_x[0].far()
    cot_x[1].near()
    sums_y[0].gone()
    sums_y[1].first()
    gu_line.forward()
    cot_x[1].far()
    sums_y[2].share()
    for line in dn_line:
        line.near()
        line.far()

    def middle_rows(s):
        def use(span):
            middle = tokens[span, :].astype(F32) + s.total(span)
            middle_all[span, :] = middle
            own[span, :] = (middle * norm_scale(middle) * gains[1:2, :]).astype(BF16)

        return use

    def gather_next(i):
        s = sums_y[i]
        s.arrive()
        over_rows(s.start_row, s.size, middle_rows(s))
        s.close()
        rows_x[i].start()

    gather_next(0)
    sums_y[1].direct()
    sums_y[1].through()
    rows_x[0].rest()
    cot_x[0].finish()
    cot_x[1].finish()
    back_hidden(0)
    rows_x[0].forward()
    sums_y[1].gone()
    sums_y[2].first()
    grad_kv[...] = jnp.zeros_like(grad_kv)
    wires.done(left)
    back_hidden(1)
    gather_next(1)
    sums_y[2].direct()
    rows_x[0].near()
    sums_y[2].through()
    rows_x[1].rest()
    back_hidden(2)
    rows_x[0].far()
    rows_x[1].forward()

    def feed(core, i):
        start, part_size = THREE[i]
        span, size = pl.ds(start, part_size), 4 * part_size
        rows = second[core, :, span].reshape(size, D)
        both = dot(rows, gu[...], 1, 0)
        upstream = grad_hidden[core, pl.ds(4 * start, size)].astype(F32)
        for j in range(4):
            gate = both[:, j * 256 : j * 256 + 128]
            upward = both[:, j * 256 + 128 : j * 256 + 256]
            sent = upstream[:, j * 128 : j * 128 + 128]
            sigmoid = jax.nn.sigmoid(gate)
            silu = gate * sigmoid
            slope = sigmoid * (1.0 + gate * (1.0 - sigmoid))
            for first, values in (
                (1024 + j * 128, silu * upward),
                (j * 256, sent * upward * slope),
                (j * 256 + 128, sent * silu),
            ):
                rounded = values.astype(BF16).reshape(4, part_size, 128)
                work[core, :, span, first : first + 128] = rounded
        back = dot(work[core, :, span, 0:1024].reshape(size, 1024), gu[...], 1, 1)
        part[core, :, span] = back.astype(BF16).reshape(4, part_size, D)

    sums_x = [PairScatter(wires, spot, "x", part, got, passed, near, s, n) for s, n in THREE]
    grads_y = [PairGather(wires, spot, "y", normed, own, s, n) for s, n in THREE]

    def feed_both(i):
        sums_x[i].share(start=False)

        def step(k):
            feed(jnp.where(k == 0, spot.other, c), i)

            @pl.when(k == 0)
            def _():
                sums_x[i].shared[0].start()

        repeat(2, step)

    gather_next(2)
    gu_line.near()
    gu_line.far()
    rows_x[0].finish()
    early = wires.started()
    wires.again()

    def grad_gate_up(i, lot):
        first, size = LOTS[lot]
        lanes = pl.ds(pl.multiple_of(i * 384 + first, 128), size)
        rows = second[:, :, :, lanes].reshape(8 * OWN, size)
        sent = work[:, :, :, 0:1024].reshape(8 * OWN, 1024)
        d_gu[lanes, :] = dot(rows, sent, 0, 0).astype(BF16)

    def grad_down(i):
        lanes = pl.ds(pl.multiple_of(1024 + i * 256, 256), 256)
        rows = work[:, :, :, lanes].reshape(8 * OWN, 256)
        grad = dot(rows, cots[...].reshape(8 * OWN, D), 0, 0).astype(BF16)
        d_dn[pl.ds(i * 2, 2)] = grad.reshape(2, 4, 32, D)

    def down(i):
        rows = work[i // 2, pl.ds((i % 2) * 2, 2), :, 1024:D].reshape(384, 512)
        second[i // 2, pl.ds((i % 2) * 2, 2)] = (
            dot(rows, dn[...].reshape(512, D), 1, 0).astype(BF16).reshape(2, OWN, D)
        )

    def back_rows(s):
        def use(span):
            grad = s.total(span)
            rows = middle_all[span, :]
            inverse = norm_scale(rows)
            back = cot[span, :].astype(F32) + norm_back(grad, rows, inverse, gains[1:2, :])
            back_all[span, :] = back
            own[span, :] = back.astype(BF16)
            fold(total, grad * rows * inverse)

        return use

    def gather_back(i):
        s = sums_x[i]
        s.arrive()
        rows_x[i].close()
        over_rows(s.start_row, s.size, back_rows(s))
        s.close()
        grads_y[i].start()

    def mix_back(i):
        first, size = THREE[i]

        def step(core):
            rows = normed[core, :, pl.ds(first, size)].reshape(4 * size, D)
            grad = dot(rows, wo[...].reshape(256, D), 1, 1).astype(BF16)
            for pos in range(4):
                start = pos * OWN + first
                grad_mix[core, start : start + size, :] = grad[pos * size : pos * size + size]

        repeat(2, step)

    total[...] = jnp.zeros_like(total)

    feed_both(0)
    rows_x[2].rest()
    rows_x[2].forward()
    rows_x[1].near()
    rows_x[1].far()
    sums_x[0].first()
    rows_x[1].finish()
    feed_both(1)
    rows_x[2].near()
    sums_x[0].direct()
    rows_x[2].far()
    sums_x[0].through()
    sums_x[1].first()
    rows_x[2].finish()
    sums_x[1].direct()
    feed_both(2)
    sums_x[2].first()
    gather_back(0)
    sums_x[1].through()
    sums_x[2].direct()
    wires.done(early)
    tell(0, [spot.along("z", 1), spot.along("z", -1)])

    grads_y[0].rest()
    repeat(4, lambda i: grad_gate_up(i, 0))
    hear(0, 2)
    def lot_rows(base, lot, half=None):
        first, size = LOTS[lot]
        if half is None:
            return pl.ds(pl.multiple_of(base + first, 64), size)
        return pl.ds(pl.multiple_of(base + first + half * (size // 2), 64), size // 2)

    gu_sum = [
        LineScatter(
            wires, spot, "z",
            lambda pos, h, lot=lot: d_gu.at[lot_rows(pos * 384, lot, h)],
            lambda h, lot=lot: gu.at[lot_rows(0, lot, h)],
            lambda h, lot=lot: gu.at[lot_rows(384, lot, h)],
            lambda side, h, lot=lot: gu.at[lot_rows(768 + side * 384, lot, h)],
        )
        for lot in (0, 1)
    ]
    gu_got = []

    def gu_beside(lot):
        gu_sum[lot].finish()
        for by in (1, -1, 2):
            part_of = d_gu.at[lot_rows(z * 384, lot), whole(turn(y, by), 256)]
            into = gu_in.at[y, pl.ds(*LOTS[lot])]
            gu_got.append(wires.send(part_of, into, spot.along("y", by)))

    gu_sum[0].first()
    grads_y[0].forward()
    sums_x[2].through()
    repeat(2, lambda i: grad_gate_up(i, 1))
    gather_back(1)
    grads_y[0].near()
    repeat(2, lambda i: grad_gate_up(2 + i, 1))
    grads_y[1].rest()
    gu_sum[0].second()
    gu_sum[1].first()
    grads_y[0].far()
    gather_back(2)
    grads_y[1].forward()
    grads_y[2].rest()
    repeat(2, grad_down)
    grads_y[0].finish()
    mix_back(0)
    grads_y[1].near()
    grads_y[2].forward()
    grads_y[1].far()
    repeat(4, down)
    gu_sum[1].second()
    grads_y[2].near()
    grads_y[1].finish()
    mix_back(1)
    gu_beside(0)
    grads_y[2].far()
    tell(1, around(spot, "xy") + [spot.along("z", 1), spot.along("z", -1)])
    again = wires.move(normed_out, cots)
    gain_c[c, 1:2] = jnp.sum(total[...], axis=0, keepdims=True)
    grads_y[2].finish()
    mix_back(2)
    left = wires.started()

    def attend_back(core, run):
        span = pl.ds(run * WIN, WIN)
        window = pl.ds(run * WIN, SEQ)
        rounded = prob[core, run]
        mixed = both_heads(grad_mix, core, span)
        inner = mixed.astype(F32) * both_heads(mix, core, span).astype(F32)
        inner = jnp.sum(inner, axis=-1, keepdims=True)
        grad = dot(mixed, kv[core, window, 128:256], 1, 1)
        scored = (rounded.astype(F32) * (grad - inner)).astype(BF16)
        grad_kv[core, window, 0:128] += dot(scored, both_heads(q, core, span), 0, 0)
        grad_kv[core, window, 128:256] += dot(rounded, mixed, 0, 0)
        grad_q = dot(scored, kv[core, window, 0:128], 1, 0) * scale
        cos, sin = cosine[core, span, :], sine[core, span, :]
        for head in (0, 1):
            grad = grad_q[head * WIN : head * WIN + WIN]
            grad = (grad * cos - swap_halves(grad) * sin).astype(BF16)
            q[core, span, head * 128 : head * 128 + 128] = grad

    def send_far(core):
        far_from = grad_mix.at[core, pl.ds(0, WIN)]
        far_from[...] = grad_kv[core, 0:WIN, :].astype(BF16)
        return wires.send(far_from, far_kv.at[core], spot.along("x", 2))

    far_got = []
    for core in (0, 1):
        attend_back(core, 0)
        far_got.append(send_far(core))
    hear(1, 7)
    sums_m = [
        PairScatter(
            wires, spot, "x", second, work.at[0], work.at[1, 0], work.at[1, pl.ds(1, 2)], s, n
        )
        for s, n in TWO
    ]
    sums_m[0].share()
    repeat(2, lambda i: attend_back(i, 1))
    sums_m[0].first()
    sums_m[0].direct()
    sums_m[1].share()
    repeat(2, lambda i: attend_back(i, 2))
    sums_m[1].first()
    sums_m[1].direct()
    dn_sum = LineScatter(
        wires, spot, "z",
        lambda pos, h: d_dn.at[pl.ds(2 * h, 2), pos],
        lambda h: dn.at[0, pl.ds(2 * h, 2)],
        lambda h: dn.at[1, pl.ds(2 * h, 2)],
        lambda side, h: dn.at[2 + side, pl.ds(2 * h, 2)],
    )
    dn_sum.first()

    def turn_back(core, pos):
        after = pl.ds(pl.multiple_of(WIN + pos * OWN, 64), OWN)
        span = whole(pos, OWN)
        cos, sin = cosine[core, span, :], sine[core, span, :]
        keyed = grad_kv[core, after, 0:128]
        keyed = pltpu.roll(keyed * cos - swap_halves(keyed) * sin, 64, 1)
        valued = pltpu.roll(grad_kv[core, after, 128:256], 32, 1)
        front = q[core, span, 0:128].astype(F32)
        behind = pltpu.roll(q[core, span, 128:256].astype(F32), 96, 1)
        lane = lax.broadcasted_iota(jnp.int32, front.shape, 1)
        q[core, span, 0:128] = jnp.where(lane < 96, front, behind).astype(BF16)
        q[core, span, 128:256] = jnp.where(lane < 64, behind, keyed).astype(BF16)
        kv[core, after, 0:128] = jnp.where(lane < 32, keyed, valued).astype(BF16)


    def normed_back(core, half):
        after = pl.ds(WIN + half * 384, 384)
        span = pl.ds(half * 384, 384)
        rows = jnp.concatenate([q[core, span, :], kv[core, after, 0:128]], axis=1)
        grad = dot(rows, aq[...].reshape(D, 384), 1, 1).astype(BF16)
        part[core, half * 2 : half * 2 + 2] = grad.reshape(2, OWN, D)

    sums_n = [PairScatter(wires, spot, "y", part, got, passed, near, s, n) for s, n in THREE]
    gu_beside(1)
    repeat(4, lambda i: turn_back(i // 2, i % 2))
    repeat(2, lambda i: normed_back(i, 0))
    for s in sums_n:
        s.share(0)
    for copy in far_got:
        copy.wait_recv()
    for core in (0, 1):
        grad_kv[core, 768:1024, :] += far_kv[core].astype(F32)
    repeat(4, lambda i: turn_back(i // 2, 2 + i % 2))
    normed_back(1 - c, 1)
    for s in sums_n:
        s.share(1)
    normed_back(c, 1)
    sums_n[0].first()
    sums_n[1].first()
    sums_n[2].first()
    sums_m[0].through()
    dn_sum.second()

    def out_rows_back(r, k):
        unit = jnp.where(k < 128, k, k - 32)
        real = (k < 96) | ((k >= 128) & (k < 224))
        return real & (unit + ((unit * 5462) >> 16) * 4 == r)

    grad_out = dot(mix[...].reshape(8 * OWN, 256), normed[...].reshape(8 * OWN, D), 0, 0)
    grad_out = dot(picks(256, 256, out_rows_back), grad_out.astype(BF16), 1, 0)
    wo[...] = grad_out.astype(BF16).reshape(4, 4, 16, D)
    out_sum = LineScatter(
        wires, spot, "z",
        lambda pos, h: wo.at[pos, pl.ds(2 * h, 2)],
        lambda h: ao.at[0, pl.ds(2 * h, 2)],
        lambda h: ao.at[1, pl.ds(2 * h, 2)],
        lambda side, h: ao.at[2 + side, pl.ds(2 * h, 2)],
    )
    out_sum.first(paced=True)
    again.wait()

    def grad_columns(i):
        rows = cots[:, :, :, whole(i, 384)].reshape(8 * OWN, 384)
        asked = dot(rows, q[...].reshape(8 * OWN, 256), 0, 0)
        other = dot(rows, kv[:, pl.ds(WIN, HALF), 0:128].reshape(8 * OWN, 128), 0, 0)
        d_att[i, :, :, 0:256] = asked.astype(BF16).reshape(4, 96, 256)
        d_att[i, :, :, 256:384] = other.astype(BF16).reshape(4, 96, 128)
        held = aq[i].reshape(384, 384).astype(F32)
        folded = (
            held[:, 0:128] * asked[:, 0:128]
            + held[:, 128:256] * asked[:, 128:256]
            + held[:, 256:384] * other
        )
        gain_c[c, 0:1, whole(i, 384)] = jnp.sum(folded.T, axis=0, keepdims=True)

    repeat(4, grad_columns)
    gain_c[c, 0:1] = gain_c[c, 0:1] / gains[0:1, :]
    tell(2, [spot.along(a, by) for a in "xz" for by in (1, -1)])
    gain_got = [wires.send(gain_c.at[c], gain_c.at[c], spot.sibling)]
    for s in sums_n:
        s.direct()
    sums_m[1].through()
    out_sum.direct()
    wires.done(left)
    hear(2, 4)
    att_sum = [
        LineScatter(
            wires, spot, "x",
            lambda pos, h: d_att.at[pl.ds(2 * h, 2), slot_of(pos), low],
            lambda h: aq.at[0, pl.ds(2 * h, 2), low],
            lambda h: aq.at[1, pl.ds(2 * h, 2), low],
            lambda side, h: aq.at[2 + side, pl.ds(2 * h, 2), low],
        ),
        LineScatter(
            wires, spot, "z",
            lambda pos, h: d_att.at[pos, pl.ds(2 * h, 2), high],
            lambda h: aq.at[0, pl.ds(2 * h, 2), high],
            lambda h: aq.at[1, pl.ds(2 * h, 2), high],
            lambda side, h: aq.at[2 + side, pl.ds(2 * h, 2), high],
        ),
    ]
    for line in att_sum:
        line.first(paced=True)

    def add_gains(held, axis, into):
        for copy in gain_got:
            copy.wait_recv()
        summed = held[0]
        for i in range(1, held.shape[0]):
            summed = summed + held[i]
        if into is None:
            gains_out[...] = summed
            return []
        me = spot.me(axis)
        into[me] = summed
        return [wires.send(into.at[me], into.at[me], spot.along(axis, by)) for by in (1, -1, 2)]

    gain_got = add_gains(gain_c, "x", gain_x)
    for line in att_sum:
        line.direct()
    out_sum.second()
    for s in sums_n:
        s.through()
    for line in (att_sum[1], att_sum[0]):
        line.second()
    for copy in gu_got:
        copy.wait_recv()
    mine = d_gu.at[whole(z, 384), whole(y, 256)]
    add_into(mine, mine, *[gu_in.at[turn(y, by)] for by in (1, -1, 2)])
    gu_done = []
    for by in (1, 2, 3):
        other, who = spot.in_quad(by)
        rows = d_gu.at[whole(z * 4 + other, 96), whole(y, 256)]
        gu_done.append(wires.send(rows, gu_own.at[spot.quad], who))
    gain_got = add_gains(gain_x, "z", gain_z)

    def token_rows(s):
        def use(span):
            grad = s.total(span)
            rows = tokens[span, :].astype(F32)
            inverse = norm_scale(rows)
            out = back_all[span, :] + norm_back(grad, rows, inverse, gains[0:1, :])
            part[c, y, span] = out.astype(BF16)

        return use

    def result_rows(s):
        def use(span):
            second[c, x, span] = (middle_all[span, :] + s.total(span)).astype(BF16)

        return use

    token_kept = []

    def token_part(i):
        s = sums_n[i]
        s.arrive()
        over_rows(s.start_row, s.size, token_rows(s))
        token_kept.append(wires.move(part.at[c, y, s.rows()], token_out.at[s.rows()]))

    def result_part(s):
        s.arrive()
        over_rows(s.start_row, s.size, result_rows(s))

    dn_sum.finish()
    dn_got = [
        wires.send(d_dn.at[turn(y, by), z], dn_in.at[y], spot.along("y", by)) for by in (1, -1, 2)
    ]
    for s in sums_m:
        result_part(s)
    result_kept = wires.move(second.at[c, x], result_out)
    for line in att_sum:
        line.finish()

    def home(pos):
        stay = pos // 2 == c
        return device(jnp.where(stay, pos, turn(pos, 2)), y, z, jnp.where(stay, c, 1 - c))

    places_z = [(turn(z, by), who) for by, who in zip((0, 1, -1, 2), line_z)]
    places_x = [turn(x, by) for by in (0, 1, -1, 2)]
    att_got = [
        Placed(
            wires, stays, [(d_att.at[to, slot, low], att_in.at[z, low], w) for to, w in places_z]
        ),
        Placed(
            wires, stays,
            [(d_att.at[z, slot_of(to), high], att_in.at[x, high], home(to)) for to in places_x],
        ),
    ]
    out_sum.finish()
    out_got = Placed(
        wires, stays, [(wo.at[z, slot_of(to)], out_in.at[x], home(to)) for to in places_x]
    )
    gain_got = add_gains(gain_z, "y", gain_y)
    kept_rows = d_gu.at[whole(z * 4 + spot.quad, 96), whole(y, 256)]
    gu_own[spot.quad] = kept_rows[...]
    token_part(0)
    token_part(1)
    token_part(2)
    for copy in gu_done:
        copy.wait_recv()
    order = picks(512, 512, lambda r, k: quad_order(k) == r)
    for into, first in ((gate_out, 0), (up_out, 128)):
        moved = jnp.concatenate([gu_own[i, :, first : first + 128] for i in range(4)], axis=1)
        into[...] = dot(moved, order, 1, 0)
    for copy in dn_got:
        copy.wait_recv()
    add_into(
        dn_out, d_dn.at[y, z], *[dn_in.at[turn(y, by)] for by in (1, -1, 2)]
    )
    for piece in att_got:
        piece.wait()
    add_into(att_out, *[att_in.at[i] for i in range(4)])
    out_got.wait()
    add_into(out_out, *[out_in.at[i] for i in range(4)])
    add_gains(gain_y, None, None)
    result_kept.wait()
    for copy in token_kept:
        copy.wait()
    for piece in att_got + [out_got]:
        piece.close()
    wires.close()


def finish_kernel(
    result, token, gains, att, out, gate, up, dn,
    result_out, token_out, attn_out, mlp_out, query_out, key_out, value_out, out_out,
    gate_out, up_out, dn_out,
):
    for src, dst in (
        (result, result_out), (token, token_out), (gate, gate_out), (up, up_out), (dn, dn_out)
    ):
        dst[...] = src[...]
    for i, into in enumerate((attn_out, mlp_out)):
        for j in range(12):
            into[j : j + 1, :] = gains[i : i + 1, j * 128 : j * 128 + 128]
    rows = att[...]

    def three(first):
        return lambda r, k: r == k + first

    query_out[...] = dot(rows, picks(384, 192, three(0)), 1, 0)
    key_out[...] = dot(rows, picks(384, 96, three(192)), 1, 0)
    value_out[...] = dot(rows, picks(384, 96, three(288)), 1, 0)
    out_out[...] = out[0:12, :].astype(F32)


def layer_call(
    tokens, gain_attn, gain_mlp, cot, w_query, w_key, w_value, w_out, w_gate, w_up, w_down, marks
):
    sends, receives = 110, 174
    shape = jax.ShapeDtypeStruct
    outs = (
        (shape((2, 4, OWN, D), BF16), ANY),
        (shape((OWN, D), BF16), ANY),
        (shape((OWN, D), BF16), ANY),
        (shape((2, D), F32), VMEM),
        (shape((96, 384), BF16), VMEM),
        (shape((16, D), BF16), VMEM),
        (shape((96, 512), F32), VMEM),
        (shape((96, 512), F32), VMEM),
        (shape((32, D), F32), VMEM),
    )
    scratch = [
        ((2, 4, OWN, D), BF16),
        ((2, 4, OWN, D), BF16),
        ((2, 4, OWN, D), BF16),
        ((2, 4, OWN, D), BF16),
        ((4, OWN, D), BF16),
        ((OWN, D), BF16),
        ((2, OWN, D), BF16),
        ((2, 4, OWN, D), BF16),
        ((1, 96, 384), BF16),
        ((1, 16, D), BF16),
        ((4, 4, 96, 384), BF16),
        ((4, 4, 16, D), BF16),
        ((4, 4, 96, 384), BF16),
        ((4, 4, 16, D), BF16),
        ((D, 1024), BF16),
        ((4, 96, 256), BF16),
        ((4, 4, 32, D), BF16),
        ((D, 1024), BF16),
        ((4, 4, 32, D), BF16),
        ((OWN, D), BF16),
        ((2, 4 * OWN, 512), BF16),
        ((2, HALF, 256), BF16),
        ((2, HALF + WIN, 256), BF16),
        ((2, 3, 2 * WIN, SEQ), BF16),
        ((2, HALF, 256), BF16),
        ((2, HALF, 128), F32),
        ((2, HALF, 128), F32),
        ((2, 12, 128), jnp.int32),
        ((2, D), F32),
        ((OWN, D), F32),
        ((OWN, D), F32),
        ((8, D), F32),
        ((2, HALF, 256), BF16),
        ((2, HALF + WIN, 256), F32),
        ((2, WIN, 256), BF16),
        ((4, 384, 256), BF16),
        ((4, 32, D), BF16),
        ((4, 96, 384), BF16),
        ((4, 16, D), BF16),
        ((2, 2, D), F32),
        ((4, 2, D), F32),
        ((4, 2, D), F32),
        ((4, 2, D), F32),
    ]
    outs_raw = pl.pallas_call(
        layer_kernel,
        out_shape=tuple(o[0] for o in outs),
        in_specs=[VMEM] * 12,
        out_specs=[o[1] for o in outs],
        scratch_shapes=[pltpu.VMEM(*s) for s in scratch]
        + [
            pltpu.SemaphoreType.REGULAR((3,)),
            pltpu.SemaphoreType.DMA((sends,)),
            pltpu.SemaphoreType.DMA((receives,)),
        ],
        compiler_params=pltpu.CompilerParams(
            collective_id=1, has_side_effects=True, vmem_limit_bytes=64 << 20
        ),
        name="layer",
    )(tokens, gain_attn, gain_mlp, cot, w_query, w_key, w_value, w_out, w_gate, w_up, w_down, marks)
    finals = (
        shape((OWN, D), BF16),
        shape((OWN, D), BF16),
        shape((12, 128), F32),
        shape((12, 128), F32),
        shape((96, 192), F32),
        shape((96, 96), F32),
        shape((96, 96), F32),
        shape((12, D), F32),
        shape((96, 512), F32),
        shape((96, 512), F32),
        shape((32, D), F32),
    )
    return pl.pallas_call(
        finish_kernel,
        out_shape=finals,
        in_specs=[VMEM] * 8,
        out_specs=[VMEM] * 11,
        name="finish",
    )(*outs_raw[1:])


def shards(
    tokens,
    gain_attn,
    gain_mlp,
    w_query,
    w_key,
    w_value,
    w_out,
    w_gate,
    w_up,
    w_down,
    segments,
    positions,
    cotangent,
):
    del segments
    done = layer_call(
        tokens,
        gain_attn.reshape(12, 128),
        gain_mlp.reshape(12, 128),
        cotangent,
        w_query,
        w_key,
        w_value,
        w_out,
        w_gate,
        w_up,
        w_down,
        positions.reshape(12, 128),
    )
    return (*done[:2], done[2].reshape(D), done[3].reshape(D), *done[4:])


def solution(mesh):
    placed = (
        P(("dp", "tensor"), None),
        P(),
        P(),
        P("dp", "tensor"),
        P("dp", "tensor"),
        P("dp", "tensor"),
        P(("tensor", "dp"), None),
        P("dp", "tensor"),
        P("dp", "tensor"),
        P(("tensor", "dp"), None),
        P("dp"),
        P("dp"),
        P(("dp", "tensor"), None),
    )
    return jax.shard_map(
        shards,
        mesh=mesh,
        in_specs=placed,
        out_specs=(
            P(("dp", "tensor"), None),
            P(("dp", "tensor"), None),
            P(),
            P(),
            P("dp", "tensor"),
            P("dp", "tensor"),
            P("dp", "tensor"),
            P(("tensor", "dp"), None),
            P("dp", "tensor"),
            P("dp", "tensor"),
            P(("tensor", "dp"), None),
        ),
        check_vma=False,
    )
```

```python
import functools
import math

import jax
import jax.numpy as jnp
from jax import lax
from jax.experimental import pallas as pl
from jax.experimental.pallas import tpu as pltpu
from jax.sharding import PartitionSpec as P

HD = 96
SEQ = 512
D = 1536
OWN = 192
HALF = 768
WIN = 256

EPSILON = 1e-05
ROPE_BASE = 100000.0
MASKED = -1e30
MESH = pl.DeviceIdType.MESH
ANY = pl.BlockSpec(memory_space=pl.ANY)
VMEM = pl.BlockSpec(memory_space=pltpu.VMEM)
BF16 = jnp.bfloat16
F32 = jnp.float32


def place():
    dp = lax.axis_index("dp")
    tensor = lax.axis_index("tensor")
    return (tensor // 4) * 2 + (dp // 2) % 2, tensor % 4, dp // 4, dp % 2


def device(x, y, z, c):
    return (z * 4 + (x % 2) * 2 + c, (x // 2) * 4 + y)


def turn(pos, by):
    return (pos + by + 4) % 4


class Spot:
    def __init__(self):
        x, y, z, c = place()
        self.x, self.y, self.z, self.c = x, y, z, c
        self.high, self.low, self.other = x // 2, x % 2, 1 - c
        self.quad = self.low * 2 + c
        self.sibling = device(x, y, z, 1 - c)
        self.partner = device(turn(x, 2), y, z, 1 - c)

    def along(self, axis, by):
        x, y, z, c = self.x, self.y, self.z, self.c
        if axis == "x":
            return device(turn(x, by), y, z, c)
        if axis == "y":
            return device(x, turn(y, by), z, c)
        return device(x, y, turn(z, by), c)

    def me(self, axis):
        return {"x": self.x, "y": self.y, "z": self.z}[axis]

    def in_quad(self, by):
        other = turn(self.quad, by)
        return other, device(self.high * 2 + other // 2, self.y, self.z, other % 2)


def greet(devices):
    for who in devices:
        pl.semaphore_signal(
            pltpu.get_barrier_semaphore(), inc=1, device_id=who, device_id_type=MESH
        )


def greeted(devices):
    pl.semaphore_wait(pltpu.get_barrier_semaphore(), len(devices))


class Wires:
    def __init__(self, send_sem, recv_sem):
        self.send_sem, self.recv_sem = send_sem, recv_sem
        self.free = list(range(send_sem.shape[0]))
        self.count = 0
        self.sent = []

    def again(self):
        self.count = 0

    def take(self):
        held = min(self.free)
        self.free.remove(held)
        return held

    def forget(self, copy):
        self.free += [held for other, held in self.sent if other is copy]
        self.sent = [pair for pair in self.sent if pair[0] is not copy]

    def send(self, src, dst, who, start=True):
        held = self.take()
        assert self.count < self.recv_sem.shape[0]
        copy = pltpu.make_async_remote_copy(
            src_ref=src,
            dst_ref=dst,
            send_sem=self.send_sem.at[held],
            recv_sem=self.recv_sem.at[self.count],
            device_id=who,
            device_id_type=MESH,
        )
        self.count += 1
        if start:
            copy.start()
        self.sent.append((copy, held))
        return copy

    def move(self, src, dst):
        held = self.take()
        copy = pltpu.make_async_copy(src, dst, self.send_sem.at[held])
        copy.start()
        return Moved(self, copy, held)

    def done(self, copies):
        kept = []
        for copy, held in self.sent:
            if any(copy is other for other in copies):
                copy.wait_send()
                self.free.append(held)
            else:
                kept.append((copy, held))
        self.sent = kept

    def started(self):
        return [copy for copy, _ in self.sent]

    def close(self):
        self.done(self.started())


class Placed:
    def __init__(self, wires, stays, pieces):
        self.wires, self.stays = wires, stays
        self.others = [wires.send(*piece) for piece in pieces[1:]]
        self.own = wires.send(*pieces[0], start=False)
        held = wires.sent[-1][1]

        @pl.when(jnp.logical_not(stays))
        def _():
            self.own.start()

        @pl.when(stays)
        def _():
            kept = pltpu.make_async_copy(pieces[0][0], pieces[0][1], wires.send_sem.at[held])
            kept.start()
            kept.wait()

    def wait(self):
        for copy in self.others:
            copy.wait_recv()

        @pl.when(jnp.logical_not(self.stays))
        def _():
            self.own.wait_recv()

    def close(self):
        self.wires.done(self.others)

        @pl.when(jnp.logical_not(self.stays))
        def _():
            self.own.wait_send()

        self.wires.forget(self.own)


class Moved:
    def __init__(self, wires, copy, held):
        self.wires, self.copy, self.held = wires, copy, held

    def wait(self):
        self.copy.wait()
        self.wires.free.append(self.held)


def add_into(dst, *srcs, chunk=16):
    rows = dst.shape[-2]
    chunk = min(chunk, rows)

    def step(i, carry):
        span = pl.ds(pl.multiple_of(i * chunk, chunk), chunk)
        total = srcs[0][..., span, :].astype(F32)
        for src in srcs[1:]:
            total = total + src[..., span, :].astype(F32)
        dst[..., span, :] = total.astype(dst.dtype)
        return carry

    lax.fori_loop(0, rows // chunk, step, 0)


class RingGather:
    def __init__(self, wires, spot, axis, at):
        self.wires, self.at = wires, at
        self.me = spot.me(axis)
        self.next, self.prev = spot.along(axis, 1), spot.along(axis, -1)

    def start(self, own=None):
        self.own = own or (lambda half: self.at(self.me, half))
        send, at, me = self.wires.send, self.at, self.me
        self.right0 = send(self.own(0), at(me, 0), self.next)
        self.left1 = send(self.own(1), at(me, 1), self.prev)

    def rest(self):
        send, at, me = self.wires.send, self.at, self.me
        self.right1 = send(self.own(1), at(me, 1), self.next)
        self.left0 = send(self.own(0), at(me, 0), self.prev)

    def begin(self):
        self.start()
        self.rest()

    def forward(self):
        send, at, me = self.wires.send, self.at, self.me
        self.right0.wait_recv()
        before = at(turn(me, -1), 0)
        self.pass0 = send(before, before, self.next)
        self.left1.wait_recv()
        after = at(turn(me, 1), 1)
        self.pass1 = send(after, after, self.prev)

    def near(self):
        self.right1.wait_recv()
        self.left0.wait_recv()

    def far(self):
        self.pass0.wait_recv()
        self.pass1.wait_recv()

    def close(self):
        near = [self.right0, self.left1, self.right1, self.left0]
        self.wires.done(near + [self.pass0, self.pass1])


class PairGather:
    def __init__(self, wires, spot, axis, out, own, start, size):
        self.wires, self.spot, self.out, self.own = wires, spot, out, own
        self.rows = pl.ds(start, size)
        cut = size // 2

        def half_rows(half):
            return pl.ds(start + half * cut, cut)

        self.half_rows = half_rows
        self.ring = RingGather(
            wires, spot, axis, lambda pos, half: out.at[spot.c, pos, half_rows(half)]
        )
        self.me = spot.me(axis)

    def share(self, pos):
        block = self.out.at[self.spot.c, pos, self.rows]
        return self.wires.send(block, block, self.spot.sibling)

    def start(self):
        self.ring.start(lambda half: self.own.at[self.half_rows(half)])
        mine = self.own.at[self.rows]
        place_of = self.out.at[self.spot.c, self.me, self.rows]
        self.shared = [self.wires.send(mine, place_of, self.spot.sibling)]
        self.kept = self.wires.move(mine, place_of)

    def rest(self):
        self.ring.rest()

    def forward(self):
        self.ring.forward()

    def near(self):
        self.ring.near()
        self.shared.append(self.share(turn(self.me, -1)))
        self.shared.append(self.share(turn(self.me, 1)))

    def far(self):
        self.ring.far()
        self.shared.append(self.share(turn(self.me, 2)))

    def finish(self):
        for copy in self.shared:
            copy.wait_recv()
        self.kept.wait()

    def close(self):
        self.ring.close()
        self.wires.done(self.shared)


class PairScatter:
    def __init__(self, wires, spot, axis, part, got, passed, near, start, size):
        self.wires, self.spot = wires, spot
        self.me = spot.me(axis)
        self.next, self.prev = spot.along(axis, 1), spot.along(axis, -1)
        self.part, self.got, self.passed, self.near = part, got, passed, near
        self.start_row, self.size, self.cut = start, size, size // 2
        self.shared = []

    def rows(self, half=None):
        if half is None:
            return pl.ds(self.start_row, self.size)
        return pl.ds(self.start_row + half * self.cut, self.cut)

    def share(self, half=None, start=True):
        places = slice(None) if half is None else pl.ds(half * 2, 2)
        copy = self.wires.send(
            self.part.at[self.spot.other, places, self.rows()],
            self.got.at[places, self.rows()],
            self.spot.sibling,
            start,
        )
        self.shared = (self.shared if half is not None else []) + [copy]

    def first(self):
        for copy in self.shared:
            copy.wait_recv()
        pos = turn(self.me, 2)
        mine = self.got.at[pos, self.rows()]
        add_into(mine, self.part.at[self.spot.c, pos, self.rows()], mine)
        self.pass0 = self.wires.send(
            self.got.at[pos, self.rows(0)], self.passed.at[self.rows(0)], self.next
        )
        self.pass1 = self.wires.send(
            self.got.at[pos, self.rows(1)], self.passed.at[self.rows(1)], self.prev
        )

    def left(self):
        self.wires.done([self.pass0, self.pass1])

    def gone(self):
        self.wires.done(self.arriving)

    def direct(self):
        self.arriving = []
        for by, half, who, side in ((1, 1, self.next, 0), (-1, 0, self.prev, 1)):
            pos = turn(self.me, by)
            mine = self.got.at[pos, self.rows(half)]
            add_into(mine, self.part.at[self.spot.c, pos, self.rows(half)], mine)
            self.arriving.append(self.wires.send(mine, self.near.at[side, self.rows(half)], who))

    def through(self):
        after, before = turn(self.me, 1), turn(self.me, -1)
        for pos, half, who, side, arrived in (
            (after, 0, self.next, 0, self.pass0),
            (before, 1, self.prev, 1, self.pass1),
        ):
            arrived.wait_recv()
            mine = self.got.at[pos, self.rows(half)]
            add_into(
                mine,
                self.part.at[self.spot.c, pos, self.rows(half)],
                mine,
                self.passed.at[self.rows(half)],
            )
            self.arriving.append(self.wires.send(mine, self.near.at[side, self.rows(half)], who))

    def arrive(self):
        for copy in self.arriving:
            copy.wait_recv()

    def close(self):
        self.wires.done(self.shared + [self.pass0, self.pass1] + self.arriving)

    def total(self, span):
        return (
            self.part[self.spot.c, self.me, span].astype(F32)
            + self.got[self.me, span].astype(F32)
            + self.near[0, span].astype(F32)
            + self.near[1, span].astype(F32)
        )


class LineScatter:
    def __init__(self, wires, spot, axis, at, passed, work, near):
        self.wires, self.at = wires, at
        self.me = spot.me(axis)
        self.next, self.prev = spot.along(axis, 1), spot.along(axis, -1)
        self.passed, self.work, self.near = passed, work, near

    def first(self, paced=False):
        send, me = self.wires.send, self.me
        far = turn(me, 2)
        self.pass0 = send(self.at(far, 0), self.passed(0), self.next)
        self.pass1 = send(self.at(far, 1), self.passed(1), self.prev)
        if not paced:
            self.direct()

    def direct(self):
        send, me = self.wires.send, self.me
        after, before = turn(me, 1), turn(me, -1)
        self.arriving = [
            send(self.at(after, 1), self.near(0, 1), self.next),
            send(self.at(before, 0), self.near(1, 0), self.prev),
        ]

    def second(self):
        for by, half, who, side, arrived in (
            (1, 0, self.next, 0, self.pass0),
            (-1, 1, self.prev, 1, self.pass1),
        ):
            arrived.wait_recv()
            add_into(self.work(half), self.at(turn(self.me, by), half), self.passed(half))
            self.arriving.append(self.wires.send(self.work(half), self.near(side, half), who))

    def finish(self):
        for copy in self.arriving:
            copy.wait_recv()
        for half in (0, 1):
            mine = self.at(self.me, half)
            add_into(mine, mine, self.near(0, half), self.near(1, half))


def norm_scale(values):
    return lax.rsqrt(jnp.mean(values * values, axis=-1, keepdims=True) + EPSILON)


def norm_back(upstream, values, inverse, gain):
    scaled = upstream * gain
    inner = jnp.sum(scaled * values, axis=-1, keepdims=True)
    return scaled * inverse - values * inner * (inverse * inverse * inverse) / values.shape[-1]


def over_rows(start, size, step, chunk=16):
    def body(i, carry):
        step(pl.ds(pl.multiple_of(start + i * chunk, chunk), chunk))
        return carry

    lax.fori_loop(0, size // chunk, body, 0)


def fold(total, values):
    part = values[0:8]
    for first in range(8, values.shape[0], 8):
        part = part + values[first : first + 8]
    total[...] += part


TWO = ((0, 96), (96, 96))
THREE = ((0, 64), (64, 64), (128, 64))
LOTS = ((0, 128), (128, 256))


def dot(left, right, a, b):
    return lax.dot_general(left, right, (((a,), (b,)), ((), ())), preferred_element_type=F32)


def repeat(count, step):
    def body(i, carry):
        step(i)
        return carry

    lax.fori_loop(0, count, body, 0)


def whole(i, size):
    return pl.ds(pl.multiple_of(i * size, size), size)


def grid_of(rows, columns):
    return (
        lax.broadcasted_iota(jnp.int32, (rows, columns), 0),
        lax.broadcasted_iota(jnp.int32, (rows, columns), 1),
    )


def picks(rows, columns, chosen):
    return jnp.where(chosen(*grid_of(rows, columns)), 1.0, 0.0).astype(BF16)


def quad_order(unit):
    return (((unit >> 5) & 3) << 7) + ((unit >> 7) << 5) + (unit & 31)


def swap_halves(values):
    lane = lax.broadcasted_iota(jnp.int32, values.shape, 1)
    up = pltpu.roll(values, 80, 1)
    down = pltpu.roll(values, 48, 1)
    return jnp.where(lane < 48, up, down)


def around(spot, axes):
    return [spot.along(a, by) for a in axes for by in (1, -1)] + [spot.sibling]


def layer_kernel(
    tokens, gain_attn, gain_mlp, cot, w_query, w_key, w_value, w_out, w_gate, w_up, w_down, marks,
    normed_out, result_out, token_out, gains_out, att_out, out_out, gate_out, up_out, dn_out,
    normed, cots, second, part, got, passed, near, work, att_two, own_out, aq, ao, d_att, wo,
    gu, gu_own, dn, d_gu, d_dn, own, grad_hidden, q, kv, prob, mix, cosine, sine,
    marks_two, gains, middle_all, back_all, total, grad_mix, grad_kv, far_kv,
    gu_in, dn_in, att_in, out_in, gain_c, gain_y, gain_x, gain_z,
    ready, send_sem, recv_sem,
):
    spot = Spot()
    wires = Wires(send_sem, recv_sem)
    x, y, z, c = spot.x, spot.y, spot.z, spot.c
    neighbours = (
        around(spot, "xyz")
        + [spot.along(a, 2) for a in "xyz"]
        + [spot.partner]
        + [spot.in_quad(by)[1] for by in (1, 2, 3)]
        + [device(turn(x, by), y, z, 1 - c) for by in (1, -1)]
        + [device(turn(x, 2), y, turn(z, by), 1 - c) for by in (1, -1, 2)]
    )
    greet(neighbours)

    def tell(which, devices):
        for who in devices:
            pl.semaphore_signal(ready.at[which], inc=1, device_id=who, device_id_type=MESH)

    def hear(which, count):
        pl.semaphore_wait(ready.at[which], count)

    for i, gain in enumerate((gain_attn, gain_mlp)):
        gains[i : i + 1, :] = jnp.concatenate([gain[j : j + 1, :] for j in range(12)], axis=1)

    def normalise(span):
        rows = tokens[span, :].astype(F32)
        own[span, :] = (rows * norm_scale(rows) * gains[0:1, :]).astype(BF16)

    over_rows(0, OWN, normalise)

    def three(first):
        return lambda r, k: r + first == k

    columns = (
        dot(w_query[...], picks(192, 384, three(0)), 1, 0)
        + dot(w_key[...], picks(96, 384, three(192)), 1, 0)
        + dot(w_value[...], picks(96, 384, three(288)), 1, 0)
    )
    att_two[0] = columns.astype(BF16)
    own_out[0] = jnp.zeros((16, D), BF16)
    own_out[0, 0:12] = w_out[...]
    greeted(neighbours)

    def slot_of(pos):
        return (pos % 2) * 2 + pos // 2

    slot = slot_of(x)
    low, high = pl.ds(0, 48), pl.ds(48, 48)
    stays = spot.high == c
    there_x, there_c = jnp.where(stays, x, turn(x, 2)), jnp.where(stays, c, 1 - c)
    there = slot_of(there_x)
    line_z = [device(there_x, y, turn(z, by), there_c) for by in (0, 1, -1, 2)]
    line_x = [device(turn(there_x, by), y, z, there_c) for by in (0, 1, -1, 2)]
    att_side = [
        Placed(
            wires, stays, [(att_two.at[0, low], aq.at[z, there, low], who) for who in line_z]
        ),
        Placed(
            wires, stays, [(att_two.at[0, high], aq.at[z, there, high], who) for who in line_x]
        ),
    ]
    rows_y = [PairGather(wires, spot, "y", normed, own, s, n) for s, n in TWO]
    for g in rows_y:
        g.start()
    out_side = Placed(wires, stays, [(own_out.at[0], ao.at[z, there], who) for who in line_x])
    marks_kept = wires.move(marks, marks_two.at[c])
    marks_got = wires.send(marks, marks_two.at[c], spot.sibling)

    order = picks(512, 512, lambda r, k: quad_order(r) == k)
    for shard, first in ((w_gate, 0), (w_up, 128)):
        moved = dot(shard[...], order, 1, 0).astype(BF16)
        for i in range(4):
            gu_own[i, :, first : first + 128] = moved[:, i * 128 : i * 128 + 128]
    gu_lanes = whole(y, 256)
    gu_here = gu.at[whole(z * 4 + spot.quad, 96), gu_lanes]
    gu_kept = wires.move(gu_own.at[spot.quad], gu_here)
    gu_swap = []
    for by in (1, 2, 3):
        other, who = spot.in_quad(by)
        gu_swap.append(wires.send(gu_own.at[other], gu_here, who))

    def trig(core):
        def step(i):
            span = whole(i, 128)
            row, lane = grid_of(128, 128)
            number = marks_two[core, pl.ds(spot.high * 6 + i, 1), :]
            ones = jnp.ones((128, 128), BF16)
            where = jnp.zeros((128, 128), F32)
            for digit, factor in ((number >> 5, 32.0), (number & 31, 1.0)):
                spread = jnp.where(row == lane, digit.astype(F32), 0.0).astype(BF16)
                where = where + factor * dot(spread, ones, 1, 0)
            grad_kv[core, span, 0:128] = where
            turns = jnp.where(lane < 48, lane, lane - 48).astype(F32) * (2.0 / HD)
            angle = where * jnp.exp(-math.log(ROPE_BASE) * turns)
            inside = lane < HD
            cosine[core, span, :] = jnp.where(inside, jnp.cos(angle), 0.0)
            wave = jnp.sin(angle)
            sine[core, span, :] = jnp.where(inside, jnp.where(lane < 48, -wave, wave), 0.0)

        repeat(6, step)

    marks_kept.wait()
    trig(c)
    for g in rows_y:
        g.rest()
    att_line = [
        RingGather(wires, spot, "x", lambda pos, h: aq.at[pl.ds(2 * h, 2), slot_of(pos), low]),
        RingGather(wires, spot, "z", lambda pos, h: aq.at[pos, pl.ds(2 * h, 2), high]),
    ]
    out_line = RingGather(wires, spot, "z", lambda pos, h: ao.at[pos, pl.ds(2 * h, 2)])
    cot_x = [PairGather(wires, spot, "x", cots, cot, s, n) for s, n in TWO]
    for piece in att_side:
        piece.wait()
    for line in att_line:
        line.begin()
    marks_got.wait_recv()
    trig(1 - c)
    for g in rows_y:
        g.forward()
    rows_y[0].near()
    for line in att_line:
        line.forward()
    out_side.wait()
    out_line.begin()
    dn_here = dn.at[y, z]
    dn_kept = wires.move(w_down, dn_here)
    first_rows, last_rows = pl.ds(0, 16), pl.ds(16, 16)
    dn_side = []
    for by in (1, -1, 2):
        for axis, rows in (("z", first_rows), ("y", last_rows)):
            dn_side.append(
                wires.send(w_down.at[rows], dn.at[y, z, rows], spot.along(axis, by))
            )
    cot_x[0].start()
    cot_x[0].rest()
    rows_y[1].near()
    for line in att_line:
        line.near()
        line.far()

    def out_row(r, k):
        unit = jnp.where(r < 128, r, r - 32)
        real = (r < 96) | ((r >= 128) & (r < 224))
        return real & (unit + ((unit * 5462) >> 16) * 4 == k)

    scale = HD ** (-0.5)

    def project(core, pos):
        both = dot(normed[core, pos], aq[...].reshape(D, 384), 1, 0)
        span = whole(pos, OWN)
        cos, sin = cosine[core, span, :], sine[core, span, :]
        tile = [both[:, 128 * i : 128 * i + 128] for i in range(3)]
        lane = lax.broadcasted_iota(jnp.int32, tile[0].shape, 1)

        def turned(values, factor=None):
            values = values * cos + swap_halves(values) * sin
            return (values if factor is None else values * factor).astype(BF16)

        q[core, span, 0:128] = turned(tile[0], scale)
        q[core, span, 128:256] = turned(
            jnp.where(lane < 32, pltpu.roll(tile[0], 32, 1), pltpu.roll(tile[1], 32, 1)), scale
        )
        after = pl.ds(pl.multiple_of(WIN + pos * OWN, 64), OWN)
        kv[core, after, 0:128] = turned(
            jnp.where(lane < 64, pltpu.roll(tile[1], 64, 1), pltpu.roll(tile[2], 64, 1))
        )
        kv[core, after, 128:256] = jnp.where(lane < HD, pltpu.roll(tile[2], 96, 1), 0.0).astype(
            BF16
        )

    for g in rows_y:
        g.kept.wait()
    repeat(3, lambda i: project(c, turn(y, i - 1)))
    for g in rows_y:
        for copy in g.shared[:3]:
            copy.wait_recv()
    repeat(3, lambda i: project(1 - c, turn(y, i - 1)))
    for g in rows_y:
        g.far()
    gu_kept.wait()
    for copy in gu_swap:
        copy.wait_recv()
    gu_side = RingGather(
        wires, spot, "y", lambda pos, h: gu.at[whole(z * 2 + h, 192), whole(pos, 256)]
    )
    gu_side.begin()
    out_line.forward()
    project(c, turn(y, 2))

    def send_kv(core):
        last, first = kv.at[core, pl.ds(768, WIN)], kv.at[core, pl.ds(0, WIN)]
        return wires.send(last, first, spot.along("x", 2))

    kv_got = [send_kv(c)]
    for g in rows_y:
        g.shared[3].wait_recv()
    project(1 - c, turn(y, 2))
    kv_got.append(send_kv(1 - c))
    dn_kept.wait()
    for copy in dn_side:
        copy.wait_recv()
    dn_line = [
        RingGather(wires, spot, "y", lambda pos, h: dn.at[pos, pl.ds(2 * h, 2), first_rows]),
        RingGather(wires, spot, "z", lambda pos, h: dn.at[pl.ds(2 * h, 2), pos, last_rows]),
    ]
    dn_line[1].begin()
    normed_kept = wires.move(normed, normed_out)
    for piece in att_side + [out_side]:
        piece.close()
    left = wires.started()
    cot_x[0].forward()
    cot_x[0].near()
    gu_line = RingGather(
        wires, spot, "z", lambda pos, h: gu.at[whole(pos, 384), pl.ds(h * 512, 512)]
    )

    def both_heads(ref, core, span):
        return jnp.concatenate([ref[core, span, 0:128], ref[core, span, 128:256]], axis=0)

    def attend(core, run):
        span = pl.ds(run * WIN, WIN)
        window = pl.ds(run * WIN, SEQ)
        scores = dot(both_heads(q, core, span), kv[core, window, 0:128], 1, 1)
        row, column = grid_of(2 * WIN, SEQ)
        row = row & (WIN - 1)
        spot_of = spot.high * HALF + run * WIN + row[0:WIN, 0:1]
        begin = jnp.maximum(
            (spot_of >> 9) << 9, spot_of - grad_kv[core, span, 0:1].astype(jnp.int32)
        )
        begin = begin - (spot.high * HALF + run * WIN) + WIN
        begin = jnp.concatenate([begin, begin], axis=0)
        allowed = (column >= begin) & (column <= row + WIN)
        scores = jnp.where(allowed, scores, MASKED)
        weights = jnp.exp(scores - jnp.max(scores, axis=-1, keepdims=True))
        share = weights * (1.0 / jnp.sum(weights, axis=-1, keepdims=True))
        rounded = share.astype(BF16)
        prob[core, run] = rounded
        values = dot(rounded, kv[core, window, 128:256], 1, 0).astype(BF16)
        mix[core, span, 0:128] = values[0:WIN]
        mix[core, span, 128:256] = values[WIN : 2 * WIN]

    repeat(2, lambda i: attend(i, 1))
    gu_side.forward()
    dn_line[0].begin()
    repeat(2, lambda i: attend(i, 2))
    dn_line[1].forward()
    out_line.near()
    out_line.far()
    out_rows = picks(256, 256, out_row)
    wo[...] = dot(out_rows, ao[...].reshape(256, D), 1, 0).astype(BF16).reshape(4, 4, 16, D)

    def project_out(core, half):
        rows = mix[core, half * 384 : half * 384 + 384, :]
        out = dot(rows, wo[...].reshape(256, D), 1, 0).astype(BF16)
        part[core, half * 2 : half * 2 + 2] = out.reshape(2, OWN, D)

    def share_all(sums):
        for s in sums:
            s.share()

    def back_hidden(i):
        start, size = THREE[i]

        def step(core):
            rows = cots[core, :, pl.ds(start, size)].reshape(4 * size, D)
            grad = dot(rows, dn[...].reshape(512, D), 1, 1).astype(BF16)
            grad_hidden[core, pl.ds(4 * start, 4 * size)] = grad

        repeat(2, step)

    rows_x = [PairGather(wires, spot, "x", second, own, s, n) for s, n in THREE]
    sums_y = [PairScatter(wires, spot, "y", part, got, passed, near, s, n) for s, n in THREE]
    repeat(2, lambda i: project_out(i, 1))
    sums_y[0].share(1)
    for copy in kv_got:
        copy.wait_recv()
    cot_x[1].start()
    gu_side.near()
    gu_side.far()
    gu_line.start()
    repeat(2, lambda i: attend(i, 0))
    cot_x[1].rest()
    dn_line[0].forward()
    project_out(1 - c, 0)
    sums_y[0].share(0)
    project_out(c, 0)
    for g in rows_y:
        g.close()
    normed_kept.wait()
    sums_y[0].first()
    sums_y[0].left()
    sums_y[0].direct()
    cot_x[1].forward()
    gu_line.rest()
    sums_y[1].share()
    sums_y[0].through()
    cot_x[0].far()
    cot_x[1].near()
    sums_y[0].gone()
    sums_y[1].first()
    gu_line.forward()
    cot_x[1].far()
    sums_y[2].share()
    for line in dn_line:
        line.near()
        line.far()

    def middle_rows(s):
        def use(span):
            middle = tokens[span, :].astype(F32) + s.total(span)
            middle_all[span, :] = middle
            own[span, :] = (middle * norm_scale(middle) * gains[1:2, :]).astype(BF16)

        return use

    def gather_next(i):
        s = sums_y[i]
        s.arrive()
        over_rows(s.start_row, s.size, middle_rows(s))
        s.close()
        rows_x[i].start()

    gather_next(0)
    sums_y[1].direct()
    sums_y[1].through()
    rows_x[0].rest()
    cot_x[0].finish()
    cot_x[1].finish()
    back_hidden(0)
    rows_x[0].forward()
    sums_y[1].gone()
    sums_y[2].first()
    grad_kv[...] = jnp.zeros_like(grad_kv)
    wires.done(left)
    back_hidden(1)
    gather_next(1)
    sums_y[2].direct()
    rows_x[0].near()
    sums_y[2].through()
    rows_x[1].rest()
    back_hidden(2)
    rows_x[0].far()
    rows_x[1].forward()

    def feed(core, i):
        start, part_size = THREE[i]
        span, size = pl.ds(start, part_size), 4 * part_size
        rows = second[core, :, span].reshape(size, D)
        both = dot(rows, gu[...], 1, 0)
        upstream = grad_hidden[core, pl.ds(4 * start, size)].astype(F32)
        for j in range(4):
            gate = both[:, j * 256 : j * 256 + 128]
            upward = both[:, j * 256 + 128 : j * 256 + 256]
            sent = upstream[:, j * 128 : j * 128 + 128]
            sigmoid = jax.nn.sigmoid(gate)
            silu = gate * sigmoid
            slope = sigmoid * (1.0 + gate * (1.0 - sigmoid))
            for first, values in (
                (1024 + j * 128, silu * upward),
                (j * 256, sent * upward * slope),
                (j * 256 + 128, sent * silu),
            ):
                rounded = values.astype(BF16).reshape(4, part_size, 128)
                work[core, :, span, first : first + 128] = rounded
        back = dot(work[core, :, span, 0:1024].reshape(size, 1024), gu[...], 1, 1)
        part[core, :, span] = back.astype(BF16).reshape(4, part_size, D)

    sums_x = [PairScatter(wires, spot, "x", part, got, passed, near, s, n) for s, n in THREE]
    grads_y = [PairGather(wires, spot, "y", normed, own, s, n) for s, n in THREE]

    def feed_both(i):
        sums_x[i].share(start=False)

        def step(k):
            feed(jnp.where(k == 0, spot.other, c), i)

            @pl.when(k == 0)
            def _():
                sums_x[i].shared[0].start()

        repeat(2, step)

    gather_next(2)
    gu_line.near()
    gu_line.far()
    rows_x[0].finish()
    early = wires.started()
    wires.again()

    def grad_gate_up(i, lot):
        first, size = LOTS[lot]
        lanes = pl.ds(pl.multiple_of(i * 384 + first, 128), size)
        rows = second[:, :, :, lanes].reshape(8 * OWN, size)
        sent = work[:, :, :, 0:1024].reshape(8 * OWN, 1024)
        d_gu[lanes, :] = dot(rows, sent, 0, 0).astype(BF16)

    def grad_down(i):
        lanes = pl.ds(pl.multiple_of(1024 + i * 256, 256), 256)
        rows = work[:, :, :, lanes].reshape(8 * OWN, 256)
        grad = dot(rows, cots[...].reshape(8 * OWN, D), 0, 0).astype(BF16)
        d_dn[pl.ds(i * 2, 2)] = grad.reshape(2, 4, 32, D)

    def down(i):
        rows = work[i // 2, pl.ds((i % 2) * 2, 2), :, 1024:D].reshape(384, 512)
        second[i // 2, pl.ds((i % 2) * 2, 2)] = (
            dot(rows, dn[...].reshape(512, D), 1, 0).astype(BF16).reshape(2, OWN, D)
        )

    def back_rows(s):
        def use(span):
            grad = s.total(span)
            rows = middle_all[span, :]
            inverse = norm_scale(rows)
            back = cot[span, :].astype(F32) + norm_back(grad, rows, inverse, gains[1:2, :])
            back_all[span, :] = back
            own[span, :] = back.astype(BF16)
            fold(total, grad * rows * inverse)

        return use

    def gather_back(i):
        s = sums_x[i]
        s.arrive()
        rows_x[i].close()
        over_rows(s.start_row, s.size, back_rows(s))
        s.close()
        grads_y[i].start()

    def mix_back(i):
        first, size = THREE[i]

        def step(core):
            rows = normed[core, :, pl.ds(first, size)].reshape(4 * size, D)
            grad = dot(rows, wo[...].reshape(256, D), 1, 1).astype(BF16)
            for pos in range(4):
                start = pos * OWN + first
                grad_mix[core, start : start + size, :] = grad[pos * size : pos * size + size]

        repeat(2, step)

    total[...] = jnp.zeros_like(total)

    feed_both(0)
    rows_x[2].rest()
    rows_x[2].forward()
    rows_x[1].near()
    rows_x[1].far()
    sums_x[0].first()
    rows_x[1].finish()
    feed_both(1)
    rows_x[2].near()
    sums_x[0].direct()
    rows_x[2].far()
    sums_x[0].through()
    sums_x[1].first()
    rows_x[2].finish()
    sums_x[1].direct()
    feed_both(2)
    sums_x[2].first()
    gather_back(0)
    sums_x[1].through()
    sums_x[2].direct()
    wires.done(early)
    tell(0, [spot.along("z", 1), spot.along("z", -1)])

    grads_y[0].rest()
    repeat(4, lambda i: grad_gate_up(i, 0))
    hear(0, 2)
    def lot_rows(base, lot, half=None):
        first, size = LOTS[lot]
        if half is None:
            return pl.ds(pl.multiple_of(base + first, 64), size)
        return pl.ds(pl.multiple_of(base + first + half * (size // 2), 64), size // 2)

    gu_sum = [
        LineScatter(
            wires, spot, "z",
            lambda pos, h, lot=lot: d_gu.at[lot_rows(pos * 384, lot, h)],
            lambda h, lot=lot: gu.at[lot_rows(0, lot, h)],
            lambda h, lot=lot: gu.at[lot_rows(384, lot, h)],
            lambda side, h, lot=lot: gu.at[lot_rows(768 + side * 384, lot, h)],
        )
        for lot in (0, 1)
    ]
    gu_got = []

    def gu_beside(lot):
        gu_sum[lot].finish()
        for by in (1, -1, 2):
            part_of = d_gu.at[lot_rows(z * 384, lot), whole(turn(y, by), 256)]
            into = gu_in.at[y, pl.ds(*LOTS[lot])]
            gu_got.append(wires.send(part_of, into, spot.along("y", by)))

    gu_sum[0].first()
    grads_y[0].forward()
    sums_x[2].through()
    repeat(2, lambda i: grad_gate_up(i, 1))
    gather_back(1)
    grads_y[0].near()
    repeat(2, lambda i: grad_gate_up(2 + i, 1))
    grads_y[1].rest()
    gu_sum[0].second()
    gu_sum[1].first()
    grads_y[0].far()
    gather_back(2)
    grads_y[1].forward()
    grads_y[2].rest()
    repeat(2, grad_down)
    grads_y[0].finish()
    mix_back(0)
    grads_y[1].near()
    grads_y[2].forward()
    grads_y[1].far()
    repeat(4, down)
    gu_sum[1].second()
    grads_y[2].near()
    grads_y[1].finish()
    mix_back(1)
    gu_beside(0)
    grads_y[2].far()
    tell(1, around(spot, "xy") + [spot.along("z", 1), spot.along("z", -1)])
    again = wires.move(normed_out, cots)
    gain_c[c, 1:2] = jnp.sum(total[...], axis=0, keepdims=True)
    grads_y[2].finish()
    mix_back(2)
    left = wires.started()

    def attend_back(core, run):
        span = pl.ds(run * WIN, WIN)
        window = pl.ds(run * WIN, SEQ)
        rounded = prob[core, run]
        mixed = both_heads(grad_mix, core, span)
        inner = mixed.astype(F32) * both_heads(mix, core, span).astype(F32)
        inner = jnp.sum(inner, axis=-1, keepdims=True)
        grad = dot(mixed, kv[core, window, 128:256], 1, 1)
        scored = (rounded.astype(F32) * (grad - inner)).astype(BF16)
        grad_kv[core, window, 0:128] += dot(scored, both_heads(q, core, span), 0, 0)
        grad_kv[core, window, 128:256] += dot(rounded, mixed, 0, 0)
        grad_q = dot(scored, kv[core, window, 0:128], 1, 0) * scale
        cos, sin = cosine[core, span, :], sine[core, span, :]
        for head in (0, 1):
            grad = grad_q[head * WIN : head * WIN + WIN]
            grad = (grad * cos - swap_halves(grad) * sin).astype(BF16)
            q[core, span, head * 128 : head * 128 + 128] = grad

    def send_far(core):
        far_from = grad_mix.at[core, pl.ds(0, WIN)]
        far_from[...] = grad_kv[core, 0:WIN, :].astype(BF16)
        return wires.send(far_from, far_kv.at[core], spot.along("x", 2))

    far_got = []
    for core in (0, 1):
        attend_back(core, 0)
        far_got.append(send_far(core))
    hear(1, 7)
    sums_m = [
        PairScatter(
            wires, spot, "x", second, work.at[0], work.at[1, 0], work.at[1, pl.ds(1, 2)], s, n
        )
        for s, n in TWO
    ]
    sums_m[0].share()
    repeat(2, lambda i: attend_back(i, 1))
    sums_m[0].first()
    sums_m[0].direct()
    sums_m[1].share()
    repeat(2, lambda i: attend_back(i, 2))
    sums_m[1].first()
    sums_m[1].direct()
    dn_sum = LineScatter(
        wires, spot, "z",
        lambda pos, h: d_dn.at[pl.ds(2 * h, 2), pos],
        lambda h: dn.at[0, pl.ds(2 * h, 2)],
        lambda h: dn.at[1, pl.ds(2 * h, 2)],
        lambda side, h: dn.at[2 + side, pl.ds(2 * h, 2)],
    )
    dn_sum.first()

    def turn_back(core, pos):
        after = pl.ds(pl.multiple_of(WIN + pos * OWN, 64), OWN)
        span = whole(pos, OWN)
        cos, sin = cosine[core, span, :], sine[core, span, :]
        keyed = grad_kv[core, after, 0:128]
        keyed = pltpu.roll(keyed * cos - swap_halves(keyed) * sin, 64, 1)
        valued = pltpu.roll(grad_kv[core, after, 128:256], 32, 1)
        front = q[core, span, 0:128].astype(F32)
        behind = pltpu.roll(q[core, span, 128:256].astype(F32), 96, 1)
        lane = lax.broadcasted_iota(jnp.int32, front.shape, 1)
        q[core, span, 0:128] = jnp.where(lane < 96, front, behind).astype(BF16)
        q[core, span, 128:256] = jnp.where(lane < 64, behind, keyed).astype(BF16)
        kv[core, after, 0:128] = jnp.where(lane < 32, keyed, valued).astype(BF16)


    def normed_back(core, half):
        after = pl.ds(WIN + half * 384, 384)
        span = pl.ds(half * 384, 384)
        rows = jnp.concatenate([q[core, span, :], kv[core, after, 0:128]], axis=1)
        grad = dot(rows, aq[...].reshape(D, 384), 1, 1).astype(BF16)
        part[core, half * 2 : half * 2 + 2] = grad.reshape(2, OWN, D)

    sums_n = [PairScatter(wires, spot, "y", part, got, passed, near, s, n) for s, n in THREE]
    gu_beside(1)
    repeat(4, lambda i: turn_back(i // 2, i % 2))
    repeat(2, lambda i: normed_back(i, 0))
    for s in sums_n:
        s.share(0)
    for copy in far_got:
        copy.wait_recv()
    for core in (0, 1):
        grad_kv[core, 768:1024, :] += far_kv[core].astype(F32)
    repeat(4, lambda i: turn_back(i // 2, 2 + i % 2))
    normed_back(1 - c, 1)
    for s in sums_n:
        s.share(1)
    normed_back(c, 1)
    sums_n[0].first()
    sums_n[1].first()
    sums_n[2].first()
    sums_m[0].through()
    dn_sum.second()

    def out_rows_back(r, k):
        unit = jnp.where(k < 128, k, k - 32)
        real = (k < 96) | ((k >= 128) & (k < 224))
        return real & (unit + ((unit * 5462) >> 16) * 4 == r)

    grad_out = dot(mix[...].reshape(8 * OWN, 256), normed[...].reshape(8 * OWN, D), 0, 0)
    grad_out = dot(picks(256, 256, out_rows_back), grad_out.astype(BF16), 1, 0)
    wo[...] = grad_out.astype(BF16).reshape(4, 4, 16, D)
    out_sum = LineScatter(
        wires, spot, "z",
        lambda pos, h: wo.at[pos, pl.ds(2 * h, 2)],
        lambda h: ao.at[0, pl.ds(2 * h, 2)],
        lambda h: ao.at[1, pl.ds(2 * h, 2)],
        lambda side, h: ao.at[2 + side, pl.ds(2 * h, 2)],
    )
    out_sum.first(paced=True)
    again.wait()

    def grad_columns(i):
        rows = cots[:, :, :, whole(i, 384)].reshape(8 * OWN, 384)
        asked = dot(rows, q[...].reshape(8 * OWN, 256), 0, 0)
        other = dot(rows, kv[:, pl.ds(WIN, HALF), 0:128].reshape(8 * OWN, 128), 0, 0)
        d_att[i, :, :, 0:256] = asked.astype(BF16).reshape(4, 96, 256)
        d_att[i, :, :, 256:384] = other.astype(BF16).reshape(4, 96, 128)
        held = aq[i].reshape(384, 384).astype(F32)
        folded = (
            held[:, 0:128] * asked[:, 0:128]
            + held[:, 128:256] * asked[:, 128:256]
            + held[:, 256:384] * other
        )
        gain_c[c, 0:1, whole(i, 384)] = jnp.sum(folded.T, axis=0, keepdims=True)

    repeat(4, grad_columns)
    gain_c[c, 0:1] = gain_c[c, 0:1] / gains[0:1, :]
    tell(2, [spot.along(a, by) for a in "xz" for by in (1, -1)])
    gain_got = [wires.send(gain_c.at[c], gain_c.at[c], spot.sibling)]
    for s in sums_n:
        s.direct()
    sums_m[1].through()
    out_sum.direct()
    wires.done(left)
    hear(2, 4)
    att_sum = [
        LineScatter(
            wires, spot, "x",
            lambda pos, h: d_att.at[pl.ds(2 * h, 2), slot_of(pos), low],
            lambda h: aq.at[0, pl.ds(2 * h, 2), low],
            lambda h: aq.at[1, pl.ds(2 * h, 2), low],
            lambda side, h: aq.at[2 + side, pl.ds(2 * h, 2), low],
        ),
        LineScatter(
            wires, spot, "z",
            lambda pos, h: d_att.at[pos, pl.ds(2 * h, 2), high],
            lambda h: aq.at[0, pl.ds(2 * h, 2), high],
            lambda h: aq.at[1, pl.ds(2 * h, 2), high],
            lambda side, h: aq.at[2 + side, pl.ds(2 * h, 2), high],
        ),
    ]
    for line in att_sum:
        line.first(paced=True)

    def add_gains(held, axis, into):
        for copy in gain_got:
            copy.wait_recv()
        summed = held[0]
        for i in range(1, held.shape[0]):
            summed = summed + held[i]
        if into is None:
            gains_out[...] = summed
            return []
        me = spot.me(axis)
        into[me] = summed
        return [wires.send(into.at[me], into.at[me], spot.along(axis, by)) for by in (1, -1, 2)]

    gain_got = add_gains(gain_c, "x", gain_x)
    for line in att_sum:
        line.direct()
    out_sum.second()
    for s in sums_n:
        s.through()
    dn_sum.finish()
    dn_got = [
        wires.send(d_dn.at[turn(y, by), z], dn_in.at[y], spot.along("y", by)) for by in (1, -1, 2)
    ]
    for line in (att_sum[1], att_sum[0]):
        line.second()
    for copy in gu_got:
        copy.wait_recv()
    mine = d_gu.at[whole(z, 384), whole(y, 256)]
    add_into(mine, mine, *[gu_in.at[turn(y, by)] for by in (1, -1, 2)])
    gu_done = []
    for by in (1, 2, 3):
        other, who = spot.in_quad(by)
        rows = d_gu.at[whole(z * 4 + other, 96), whole(y, 256)]
        gu_done.append(wires.send(rows, gu_own.at[spot.quad], who))
    gain_got = add_gains(gain_x, "z", gain_z)

    def token_rows(s):
        def use(span):
            grad = s.total(span)
            rows = tokens[span, :].astype(F32)
            inverse = norm_scale(rows)
            out = back_all[span, :] + norm_back(grad, rows, inverse, gains[0:1, :])
            part[c, y, span] = out.astype(BF16)

        return use

    def result_rows(s):
        def use(span):
            second[c, x, span] = (middle_all[span, :] + s.total(span)).astype(BF16)

        return use

    token_kept = []

    def token_part(i):
        s = sums_n[i]
        s.arrive()
        over_rows(s.start_row, s.size, token_rows(s))
        token_kept.append(wires.move(part.at[c, y, s.rows()], token_out.at[s.rows()]))

    def result_part(s):
        s.arrive()
        over_rows(s.start_row, s.size, result_rows(s))

    for s in sums_m:
        result_part(s)
    result_kept = wires.move(second.at[c, x], result_out)
    for line in att_sum:
        line.finish()

    def home(pos):
        stay = pos // 2 == c
        return device(jnp.where(stay, pos, turn(pos, 2)), y, z, jnp.where(stay, c, 1 - c))

    places_z = [(turn(z, by), who) for by, who in zip((0, 1, -1, 2), line_z)]
    places_x = [turn(x, by) for by in (0, 1, -1, 2)]
    att_got = [
        Placed(
            wires, stays, [(d_att.at[to, slot, low], att_in.at[z, low], w) for to, w in places_z]
        ),
        Placed(
            wires, stays,
            [(d_att.at[z, slot_of(to), high], att_in.at[x, high], home(to)) for to in places_x],
        ),
    ]
    out_sum.finish()
    out_got = Placed(
        wires, stays, [(wo.at[z, slot_of(to)], out_in.at[x], home(to)) for to in places_x]
    )
    gain_got = add_gains(gain_z, "y", gain_y)
    kept_rows = d_gu.at[whole(z * 4 + spot.quad, 96), whole(y, 256)]
    gu_own[spot.quad] = kept_rows[...]
    token_part(0)
    token_part(1)
    token_part(2)
    for copy in gu_done:
        copy.wait_recv()
    order = picks(512, 512, lambda r, k: quad_order(k) == r)
    for into, first in ((gate_out, 0), (up_out, 128)):
        moved = jnp.concatenate([gu_own[i, :, first : first + 128] for i in range(4)], axis=1)
        into[...] = dot(moved, order, 1, 0)
    for copy in dn_got:
        copy.wait_recv()
    add_into(
        dn_out, d_dn.at[y, z], *[dn_in.at[turn(y, by)] for by in (1, -1, 2)]
    )
    for piece in att_got:
        piece.wait()
    add_into(att_out, *[att_in.at[i] for i in range(4)])
    out_got.wait()
    add_into(out_out, *[out_in.at[i] for i in range(4)])
    add_gains(gain_y, None, None)
    result_kept.wait()
    for copy in token_kept:
        copy.wait()
    for piece in att_got + [out_got]:
        piece.close()
    wires.close()


def finish_kernel(
    result, token, gains, att, out, gate, up, dn,
    result_out, token_out, attn_out, mlp_out, query_out, key_out, value_out, out_out,
    gate_out, up_out, dn_out,
):
    for src, dst in (
        (result, result_out), (token, token_out), (gate, gate_out), (up, up_out), (dn, dn_out)
    ):
        dst[...] = src[...]
    for i, into in enumerate((attn_out, mlp_out)):
        for j in range(12):
            into[j : j + 1, :] = gains[i : i + 1, j * 128 : j * 128 + 128]
    rows = att[...]

    def three(first):
        return lambda r, k: r == k + first

    query_out[...] = dot(rows, picks(384, 192, three(0)), 1, 0)
    key_out[...] = dot(rows, picks(384, 96, three(192)), 1, 0)
    value_out[...] = dot(rows, picks(384, 96, three(288)), 1, 0)
    out_out[...] = out[0:12, :].astype(F32)


def layer_call(
    tokens, gain_attn, gain_mlp, cot, w_query, w_key, w_value, w_out, w_gate, w_up, w_down, marks
):
    sends, receives = 110, 174
    shape = jax.ShapeDtypeStruct
    outs = (
        (shape((2, 4, OWN, D), BF16), ANY),
        (shape((OWN, D), BF16), ANY),
        (shape((OWN, D), BF16), ANY),
        (shape((2, D), F32), VMEM),
        (shape((96, 384), BF16), VMEM),
        (shape((16, D), BF16), VMEM),
        (shape((96, 512), F32), VMEM),
        (shape((96, 512), F32), VMEM),
        (shape((32, D), F32), VMEM),
    )
    scratch = [
        ((2, 4, OWN, D), BF16),
        ((2, 4, OWN, D), BF16),
        ((2, 4, OWN, D), BF16),
        ((2, 4, OWN, D), BF16),
        ((4, OWN, D), BF16),
        ((OWN, D), BF16),
        ((2, OWN, D), BF16),
        ((2, 4, OWN, D), BF16),
        ((1, 96, 384), BF16),
        ((1, 16, D), BF16),
        ((4, 4, 96, 384), BF16),
        ((4, 4, 16, D), BF16),
        ((4, 4, 96, 384), BF16),
        ((4, 4, 16, D), BF16),
        ((D, 1024), BF16),
        ((4, 96, 256), BF16),
        ((4, 4, 32, D), BF16),
        ((D, 1024), BF16),
        ((4, 4, 32, D), BF16),
        ((OWN, D), BF16),
        ((2, 4 * OWN, 512), BF16),
        ((2, HALF, 256), BF16),
        ((2, HALF + WIN, 256), BF16),
        ((2, 3, 2 * WIN, SEQ), BF16),
        ((2, HALF, 256), BF16),
        ((2, HALF, 128), F32),
        ((2, HALF, 128), F32),
        ((2, 12, 128), jnp.int32),
        ((2, D), F32),
        ((OWN, D), F32),
        ((OWN, D), F32),
        ((8, D), F32),
        ((2, HALF, 256), BF16),
        ((2, HALF + WIN, 256), F32),
        ((2, WIN, 256), BF16),
        ((4, 384, 256), BF16),
        ((4, 32, D), BF16),
        ((4, 96, 384), BF16),
        ((4, 16, D), BF16),
        ((2, 2, D), F32),
        ((4, 2, D), F32),
        ((4, 2, D), F32),
        ((4, 2, D), F32),
    ]
    outs_raw = pl.pallas_call(
        layer_kernel,
        out_shape=tuple(o[0] for o in outs),
        in_specs=[VMEM] * 12,
        out_specs=[o[1] for o in outs],
        scratch_shapes=[pltpu.VMEM(*s) for s in scratch]
        + [
            pltpu.SemaphoreType.REGULAR((3,)),
            pltpu.SemaphoreType.DMA((sends,)),
            pltpu.SemaphoreType.DMA((receives,)),
        ],
        compiler_params=pltpu.CompilerParams(
            collective_id=1, has_side_effects=True, vmem_limit_bytes=64 << 20
        ),
        name="layer",
    )(tokens, gain_attn, gain_mlp, cot, w_query, w_key, w_value, w_out, w_gate, w_up, w_down, marks)
    finals = (
        shape((OWN, D), BF16),
        shape((OWN, D), BF16),
        shape((12, 128), F32),
        shape((12, 128), F32),
        shape((96, 192), F32),
        shape((96, 96), F32),
        shape((96, 96), F32),
        shape((12, D), F32),
        shape((96, 512), F32),
        shape((96, 512), F32),
        shape((32, D), F32),
    )
    return pl.pallas_call(
        finish_kernel,
        out_shape=finals,
        in_specs=[VMEM] * 8,
        out_specs=[VMEM] * 11,
        name="finish",
    )(*outs_raw[1:])


def shards(
    tokens,
    gain_attn,
    gain_mlp,
    w_query,
    w_key,
    w_value,
    w_out,
    w_gate,
    w_up,
    w_down,
    segments,
    positions,
    cotangent,
):
    del segments
    done = layer_call(
        tokens,
        gain_attn.reshape(12, 128),
        gain_mlp.reshape(12, 128),
        cotangent,
        w_query,
        w_key,
        w_value,
        w_out,
        w_gate,
        w_up,
        w_down,
        positions.reshape(12, 128),
    )
    return (*done[:2], done[2].reshape(D), done[3].reshape(D), *done[4:])


def solution(mesh):
    placed = (
        P(("dp", "tensor"), None),
        P(),
        P(),
        P("dp", "tensor"),
        P("dp", "tensor"),
        P("dp", "tensor"),
        P(("tensor", "dp"), None),
        P("dp", "tensor"),
        P("dp", "tensor"),
        P(("tensor", "dp"), None),
        P("dp"),
        P("dp"),
        P(("dp", "tensor"), None),
    )
    return jax.shard_map(
        shards,
        mesh=mesh,
        in_specs=placed,
        out_specs=(
            P(("dp", "tensor"), None),
            P(("dp", "tensor"), None),
            P(),
            P(),
            P("dp", "tensor"),
            P("dp", "tensor"),
            P("dp", "tensor"),
            P(("tensor", "dp"), None),
            P("dp", "tensor"),
            P("dp", "tensor"),
            P(("tensor", "dp"), None),
        ),
        check_vma=False,
    )
```
